32 devices in a mesh: gx: 4 (over y, core), gy: 8 (over z, x).
Axes of the slice: x: 2, y: 2, z: 4, core: 2. Of those that a mesh axis runs over, the one named last changes fastest.
Arguments:
- velocity: float32 [3, 384, 256, 256], P(None, 'gx', 'gy'), may hold values from -6 to 6
- inflow: float32 [3, 256, 256], P(None, 'gy'), may hold values from -5 to 5
- positions: int32 [4, 64, 3, 256], P('gx'), may hold values from 0 to 381, as said below
- tiles: int32 [4, 64, 2], P('gx'), may hold values from 0 to 7, as said below
- coefs: float32 [4, 64, 256], P('gx'), may hold values from 2 to 20
- counts: int32 [4], P('gx'), may hold values from 1 to 64, as said below
Outputs:
- velocity_next: float32 [3, 384, 256, 256], P(None, 'gx', 'gy')
- blade_force: float32 [4, 64, 3, 256], P('gx')
The draws below stay inside these ranges and needn't reach their ends.
Inputs may be any that keep to these rules, and one draw needn't show every extreme that they name: `positions`: for a record of tile row r, coordinate 0 is one value for all its points, from r * 96 + 2 to r * 96 + 93; coordinate 2 lies from 2 to 253; the points of a record lie on a straight segment in y and z. tiles[r, s, 1] is 2 or 3; the first listed y tile is the lowest y tile that holds a cell within 2 in y of some point of the record, or the tile after it. Records of row r with index below counts[r] are live; some row is full and some row has one live record.
All inputs are finite; a program needn't handle non-finite values.
Results may differ from the reference program's by a relative error of at most 0.00008.
Values sent between devices are 32-bit elements; how exact they have to be, the bound alone decides.
No kernel may reach another device: no remote copies, remote signals or barrier semaphores. Data moves between devices by JAX's collectives and lax.ppermute only.
A program may use at most 128 MiB of HBM per device.

```python
import math
import jax
import jax.numpy as jnp
from jax import lax

CX = 96
CY = 32
NZ = 256
REC_ROW = 64
PTS = 256
RAD = 2
NX = 384
NY = 256
N_GX = 4
N_GY = 8


def blade_layout(key):
    shape = (N_GX, REC_ROW)
    reach = 2 * CY - 2 * RAD
    lift = min(reach, (NZ - 2 * RAD - 2) // 2)
    rows = jnp.arange(N_GX, dtype=jnp.int32)[:, None]
    slots = jnp.arange(REC_ROW, dtype=jnp.int32)[None, :]
    hub_x = rows * CX + jax.random.randint(jax.random.fold_in(key, 31), shape, RAD, CX - RAD)
    hub_x = jnp.where(slots == 0, rows * CX + CX - RAD - 1, hub_x)
    centre = jax.random.randint(jax.random.fold_in(key, 32), (N_GX, 1), 0, NY)
    nearby = centre + jax.random.randint(jax.random.fold_in(key, 33), shape, -2 * CY, 2 * CY)
    anywhere = jax.random.randint(jax.random.fold_in(key, 34), shape, 0, NY)
    chooser = jax.random.randint(jax.random.fold_in(key, 35), shape, 0, 3)
    hub_y = jnp.where(chooser == 0, anywhere, nearby)
    third_tile = (rows * 3 + 1) % N_GY
    hub_y = jnp.where(slots == 0, NY - CY // 2, hub_y)
    hub_y = jnp.where(slots == 1, third_tile * CY + CY - 1 + RAD, hub_y)
    hub_y = jnp.where(slots == 2, RAD, hub_y)
    length = jax.random.randint(jax.random.fold_in(key, 36), shape, reach // 2, reach + 1)
    direction = 2 * jax.random.randint(jax.random.fold_in(key, 37), shape, 0, 2) - 1
    end_y = jnp.where(slots < 3, reach, length * direction)
    end_z = jax.random.randint(jax.random.fold_in(key, 38), shape, -lift, lift + 1)
    hub_z = jax.random.randint(jax.random.fold_in(key, 39), shape, RAD + lift, NZ - RAD - lift)
    along = jnp.arange(PTS, dtype=jnp.int32)
    raw_y = hub_y[:, :, None] + along[None, None, :] * end_y[:, :, None] // PTS
    cell_z = hub_z[:, :, None] + along[None, None, :] * end_z[:, :, None] // PTS
    cell_x = jnp.broadcast_to(hub_x[:, :, None], raw_y.shape)
    positions = jnp.stack([cell_x, raw_y % NY, cell_z], axis=2).astype(jnp.int32)
    low_tile = (jnp.min(raw_y, axis=2) - RAD) // CY
    first_shift = jax.random.randint(jax.random.fold_in(key, 40), shape, 0, 2)
    list_count = jax.random.randint(jax.random.fold_in(key, 41), shape, 2, 4)
    tiles = jnp.stack([(low_tile + first_shift) % N_GY, list_count], axis=2).astype(jnp.int32)
    return (positions, tiles)


def draw_positions(key, part):
    return blade_layout(key)[0]


def draw_tiles(key, part):
    return blade_layout(key)[1]


def draw_counts(key, part):
    key_count = jax.random.fold_in(key, 21)
    key_full = jax.random.fold_in(key, 22)
    drawn = jax.random.randint(key_count, (N_GX,), 1, REC_ROW + 1)
    full_row = jax.random.randint(key_full, (), 0, N_GX)
    row_index = jnp.arange(N_GX, dtype=jnp.int32)
    single = jnp.where(row_index == (full_row + 1) % N_GX, 1, drawn)
    return jnp.where(row_index == full_row, REC_ROW, single).astype(jnp.int32)


def block_scale(stream_key, shape, split, least, largest):
    level = 1.0
    for dim, shards_of in split:
        draws = jax.random.uniform(jax.random.fold_in(jax.random.fold_in(stream_key, 6), dim), (shards_of,), jnp.float32, least / len(split), largest / len(split))
        level = level * jnp.repeat(jnp.exp(draws), shape[dim] // shards_of).reshape((-1,) + (1,) * (len(shape) - 1 - dim))
    return level


def noise(rng, extent, scale, limit, pieces=(), kind=jnp.bfloat16):
    values = scale * jax.random.normal(rng, extent, jnp.float32)
    if pieces:
        values = values * block_scale(rng, extent, pieces, -0.22, 0.18)
    return jnp.clip(values, -limit, limit).astype(kind)


def setup_inputs(seed: int = 0) -> dict:
    seeds = jax.random.split(jax.random.key(seed), 7)
    velocity = noise(seeds[0], (3, NX, NY, NZ), 1.0, 6.0, ((1, 4), (2, 8)), jnp.float32)
    inflow = noise(seeds[1], (3, NY, NZ), 1.0, 5.0, ((1, 8),), jnp.float32)
    positions = draw_positions(jax.random.fold_in(seeds[6], 71), 0)
    tiles = draw_tiles(jax.random.fold_in(seeds[6], 71), 0)
    coefs = jnp.clip(jnp.exp(math.log(20.0) - 2.3025851 * jax.random.uniform(seeds[4], (N_GX, REC_ROW, PTS), jnp.float32) ** block_scale(seeds[4], (N_GX, REC_ROW, PTS), ((0, 4),), -0.2, 0.2)), 2.0, 20.0)
    counts = draw_counts(jax.random.fold_in(seeds[6], 71), 0)
    return {"velocity": velocity, "inflow": inflow, "positions": positions, "tiles": tiles, "coefs": coefs, "counts": counts}


VISCOSITY = 0.05
TIME_STEP = 0.1
WIDTH_EPS = 1.5
ROOT_PI = 1.7724538509055159

def kernel_weight(offset):
    inside = jnp.abs(offset) <= RAD
    dist = offset.astype(jnp.float32)
    value = jnp.exp(-(dist / WIDTH_EPS) ** 2) / (WIDTH_EPS * ROOT_PI)
    return jnp.where(inside, value, jnp.zeros_like(value))

def tendency(field, inflow, force):
    xpad = jnp.concatenate([inflow[:, None], field, field[:, -1:]], axis=1)
    ypad = jnp.concatenate([field[:, :, -1:], field, field[:, :, :1]], axis=2)
    zpad = jnp.pad(field, ((0, 0), (0, 0), (0, 0), (1, 1)))
    east, west = (xpad[:, 2:], xpad[:, :-2])
    north, south = (ypad[:, :, 2:], ypad[:, :, :-2])
    upper, lower = (zpad[:, :, :, 2:], zpad[:, :, :, :-2])
    advect = field[0:1] * (east - west) * 0.5 + field[1:2] * (north - south) * 0.5 + field[2:3] * (upper - lower) * 0.5
    diffuse = east + west + north + south + upper + lower - 6.0 * field
    return -advect + VISCOSITY * diffuse + force

def forcing(field, positions, tiles, coefs, counts):
    window = 2 * RAD + 1
    offsets = jnp.arange(window, dtype=jnp.int32) - RAD
    across = kernel_weight(offsets)
    padded = jnp.concatenate([field[:, :, -RAD:], field, field[:, :, :RAD]], axis=2)
    px = positions[:, :, 0, :].reshape(-1)
    py = positions[:, :, 1, :].reshape(-1)
    pz = positions[:, :, 2, :].reshape(-1)
    point_shape = (N_GX, REC_ROW, PTS)
    first_tile = jnp.broadcast_to(tiles[:, :, 0:1], point_shape).reshape(-1)
    tile_count = jnp.broadcast_to(tiles[:, :, 1:2], point_shape).reshape(-1)
    cell_y = (py[:, None] + offsets[None, :]) % NY
    listed = (cell_y // CY - first_tile[:, None]) % N_GY < tile_count[:, None]
    along_y = across[None, :] * listed.astype(jnp.float32)
    kernel_cube = across[None, :, None, None] * along_y[:, None, :, None] * across[None, None, None, :]

    def sample(xs, ys, zs, weight):
        block = lax.dynamic_slice(padded, (jnp.int32(0), xs - RAD, ys, zs - RAD), (3, window, window, window))
        return lax.optimization_barrier(jnp.sum(block * weight[None], axis=(1, 2, 3)))
    sampled = jax.vmap(sample, out_axes=1)(px, py, pz, kernel_cube)
    live_mask = jnp.arange(REC_ROW, dtype=jnp.int32)[None, :, None] < counts[:, None, None]
    strength = (coefs * live_mask.astype(jnp.float32)).reshape(-1)
    speed_norm = jnp.sqrt(lax.optimization_barrier(jnp.sum(sampled * sampled, axis=0)))
    point_force = -strength * speed_norm * sampled
    ix = px[:, None, None, None] + offsets[None, :, None, None]
    iy = (py[:, None, None, None] + offsets[None, None, :, None]) % NY
    iz = pz[:, None, None, None] + offsets[None, None, None, :]
    values = point_force[:, :, None, None, None] * kernel_cube[None]
    grid_force = jnp.zeros_like(field).at[:, ix, iy, iz].add(values)
    return (grid_force, point_force)

def reference(velocity, inflow, positions, tiles, coefs, counts):
    force_a, points_a = forcing(velocity, positions, tiles, coefs, counts)
    section = velocity + TIME_STEP * tendency(velocity, inflow, force_a)
    force_b, points_b = forcing(section, positions, tiles, coefs, counts)
    velocity_next = 0.5 * (velocity + section + TIME_STEP * tendency(section, inflow, force_b))
    mean_force = 0.5 * (points_a + points_b)
    blade_force = mean_force.reshape(3, N_GX, REC_ROW, PTS).transpose(1, 2, 0, 3)
    return (velocity_next, blade_force)
```

```python
import functools
import math

import jax
import jax.numpy as jnp
from jax import lax
from jax.experimental import pallas as pl
from jax.experimental.pallas import tpu as pltpu
from jax.sharding import PartitionSpec as P

RAD = 2
VISCOSITY = 0.05
TIME_STEP = 0.1
WIDTH_EPS = 1.5
ROOT_PI = 1.7724538509055159
TAP = [math.exp(-((d / WIDTH_EPS) ** 2)) / (WIDTH_EPS * ROOT_PI) for d in range(RAD + 1)]
LANES = 128
SUB = 8
VMEM_LIMIT = 14 * 2**20

WHOLE = pl.BlockSpec(memory_space=pltpu.VMEM)
SCALAR = pl.BlockSpec(memory_space=pltpu.SMEM)
ANYWHERE = pl.BlockSpec(memory_space=pl.ANY)


def params(limit=VMEM_LIMIT):
    return pltpu.CompilerParams(vmem_limit_bytes=limit)


def cost(flops, nbytes):
    return pl.CostEstimate(flops=flops, bytes_accessed=nbytes, transcendentals=0)


def resident(x):
    return pltpu.with_memory_space_constraint(x, pltpu.VMEM)


def smooth_z(x):
    depth = x.shape[-1]
    near = pltpu.roll(x, 1, 1) + pltpu.roll(x, depth - 1, 1)
    far = pltpu.roll(x, 2, 1) + pltpu.roll(x, depth - 2, 1)
    return TAP[0] * x + TAP[1] * near + TAP[2] * far


def split(x):
    high = x.astype(jnp.bfloat16)
    low = (x - high.astype(jnp.float32)).astype(jnp.bfloat16)
    return jnp.concatenate([high, low], axis=0)


def one_hot(point_z, depth):
    cell = lax.broadcasted_iota(jnp.int32, (depth, point_z.shape[-1]), 0)
    return jnp.where(cell == point_z, 1.0, 0.0).astype(jnp.bfloat16)


def along_y(point_y, base, cells_y, total_y):
    near = point_y - base
    near = jnp.where(near > total_y // 2, near - total_y, near)
    near = jnp.where(near < -(total_y // 2), near + total_y, near)
    dist = jnp.abs(lax.broadcasted_iota(jnp.int32, (cells_y, point_y.shape[-1]), 0) - near)
    return jnp.where(
        dist == 0, TAP[0], jnp.where(dist == 1, TAP[1], jnp.where(dist == 2, TAP[2], 0.0))
    )


def record_list(tiles, counts, active):
    tile_y, groups_y = lax.axis_index("gy"), lax.axis_size("gy")

    def step(r, found):
        offset = tile_y - tiles[r, 0]
        offset = jnp.where(offset < 0, offset + groups_y, offset)
        keep = jnp.logical_and(offset < tiles[r, 1], r < counts[0])

        @pl.when(keep)
        def _():
            active[1 + found] = r

        return found + keep.astype(jnp.int32)

    active[0] = lax.fori_loop(0, tiles.shape[0], step, jnp.int32(0))


def for_pairs(active, body):
    found = active[0]

    def step(t, carry):
        first = 2 * t
        second = jnp.minimum(first + 1, found - 1)
        body(active[1 + first], active[1 + second], first + 1 < found)
        return carry

    lax.fori_loop(0, (found + 1) // 2, step, 0)


def sample_record(field, positions, hubs, partial, r):
    cells_x, cells_y, depth = field.shape[1:]
    total_y = cells_y * lax.axis_size("gy")
    hub = hubs[r] - lax.axis_index("gx") * cells_x
    base = lax.axis_index("gy") * cells_y
    planes = []
    for c in range(3):
        plane = TAP[0] * field[c, hub]
        plane += TAP[1] * (field[c, hub - 1] + field[c, hub + 1])
        plane += TAP[2] * (field[c, hub - 2] + field[c, hub + 2])
        planes.append(plane)
    planes = smooth_z(jnp.concatenate(planes, axis=0))
    pos = positions[r]
    picked = jnp.dot(
        split(planes), one_hot(pos[2:3], depth), preferred_element_type=jnp.float32
    )
    picked = picked[: 3 * cells_y] + picked[3 * cells_y :]
    weight = along_y(pos[1:2], base, cells_y, total_y)
    rows = [
        jnp.sum(picked[c * cells_y : (c + 1) * cells_y] * weight, axis=0, keepdims=True)
        for c in range(3)
    ]
    partial[r] = jnp.concatenate(rows, axis=0)


def sample_all(field, positions, hubs, active, partial):
    partial[...] = jnp.zeros_like(partial)

    def body(first, second, both):
        sample_record(field, positions, hubs, partial, first)
        sample_record(field, positions, hubs, partial, second)

    for_pairs(active, body)


def load_sample(velocity, positions, hubs, tiles, counts, field, partial, active, sem):
    copy = pltpu.make_async_copy(velocity, field, sem)
    copy.start()
    record_list(tiles, counts, active)
    copy.wait()
    sample_all(field, positions, hubs, active, partial)


def sample(field, positions, hubs, active, partial):
    sample_all(field, positions, hubs, active, partial)


def force_law(sampled, strength):
    speed = jnp.sqrt(jnp.sum(sampled * sampled, axis=0, keepdims=True))
    return -strength * speed * sampled


def slab_of(positions, coefs, own, low, high, cells_y, depth, scale, r):
    total_y = cells_y * lax.axis_size("gy")
    base = lax.axis_index("gy") * cells_y
    pos = positions[r]
    force = force_law(own[r] + (low[r] + high[r]), coefs[r] * scale)
    weight = along_y(pos[1:2], base, cells_y, total_y)
    spread = jnp.concatenate([weight * force[c : c + 1] for c in range(3)], axis=0)
    slab = lax.dot_general(
        split(spread),
        one_hot(pos[2:3], depth),
        (((1,), (1,)), ((), ())),
        preferred_element_type=jnp.float32,
    )
    return smooth_z(slab[: 3 * cells_y] + slab[3 * cells_y :])


def add_slab(field, slab, hub, cells_y):
    for c in range(3):
        part = slab[c * cells_y : (c + 1) * cells_y]
        terms = [tap * part for tap in TAP]
        for d in range(-RAD, RAD + 1):
            field[c, hub + d] = field[c, hub + d] + terms[abs(d)]


def spread_all(field, positions, hubs, active, coefs, own, low, high, scale):
    cells_x, cells_y, depth = field.shape[1:]
    start = lax.axis_index("gx") * cells_x

    def body(first, second, both):
        slab = functools.partial(slab_of, positions, coefs, own, low, high, cells_y, depth)
        slab_a = slab(scale, first)
        slab_b = slab(jnp.where(both, scale, 0.0), second)
        add_slab(field, slab_a, hubs[first] - start, cells_y)
        add_slab(field, slab_b, hubs[second] - start, cells_y)

    for_pairs(active, body)


def spread_section(field_in, positions, hubs, active, coefs, own, low, high, field, edge_x, edge_y):
    spread_all(field, positions, hubs, active, coefs, own, low, high, TIME_STEP)
    cells_x, cells_y, depth = field.shape[1:]
    for c in range(3):
        edge_x[0, c] = field[c, 0]
        edge_x[1, c] = field[c, cells_x - 1]

    def step(t, carry):
        for c in range(3):
            for k in range(SUB):
                i = t * SUB + k
                edge_y[0, c, i] = field[c, i, pl.ds(0, 1), :]
                edge_y[1, c, i] = field[c, i, pl.ds(cells_y - 1, 1), :]
        return carry

    lax.fori_loop(0, cells_x // SUB, step, 0)


def spread_next(
    field_in, positions, hubs, active, coefs, own, low, high, field, result, sem
):
    spread_all(field, positions, hubs, active, coefs, own, low, high, 0.5 * TIME_STEP)
    copy = pltpu.make_async_copy(field, result, sem)
    copy.start()
    copy.wait()


def advance(i, factor, field, west, east, south, north, emit):
    cells_y, depth = field.shape[2:]
    groups, halves = cells_y // SUB, depth // LANES
    row = lax.broadcasted_iota(jnp.int32, (SUB, LANES), 0)
    lane = lax.broadcasted_iota(jnp.int32, (SUB, LANES), 1)
    first_row, last_row = row == 0, row == SUB - 1
    first_lane, last_lane = lane == 0, lane == LANES - 1
    spread = factor * TIME_STEP * VISCOSITY
    centre = factor * (1.0 - 6.0 * TIME_STEP * VISCOSITY)
    zero = jnp.zeros((SUB, LANES), jnp.float32)

    def cut(h):
        return pl.ds(h * LANES, LANES)

    for g in range(groups):
        rows = pl.ds(g * SUB, SUB)
        q = [[field[c, i, rows, cut(h)] for h in range(halves)] for c in range(3)]
        coef = []
        for h in range(halves):
            speeds = [(0.5 * factor * TIME_STEP) * q[c][h] for c in range(3)]
            coef.append([(spread - s, spread + s) for s in speeds])
        for c in range(3):
            up = [pltpu.roll(q[c][h], LANES - 1, 1) for h in range(halves)]
            down = [pltpu.roll(q[c][h], 1, 1) for h in range(halves)]
            for h in range(halves):
                x = q[c][h]
                upper = jnp.where(last_lane, up[h + 1] if h + 1 < halves else zero, up[h])
                lower = jnp.where(first_lane, down[h - 1] if h > 0 else zero, down[h])
                if g + 1 < groups:
                    after = pltpu.roll(field[c, i, pl.ds((g + 1) * SUB, SUB), cut(h)], SUB - 1, 0)
                else:
                    after = jnp.broadcast_to(north[c, i, :, cut(h)], (SUB, LANES))
                if g > 0:
                    before = pltpu.roll(field[c, i, pl.ds((g - 1) * SUB, SUB), cut(h)], 1, 0)
                else:
                    before = jnp.broadcast_to(south[c, i, :, cut(h)], (SUB, LANES))
                above = jnp.where(last_row, after, pltpu.roll(x, SUB - 1, 0))
                below = jnp.where(first_row, before, pltpu.roll(x, 1, 0))
                (xe, xw), (yn, ys), (zu, zl) = coef[h]
                total = centre * x
                total += east(c, rows, cut(h)) * xe + west(c, rows, cut(h)) * xw
                total += above * yn + below * ys
                total += upper * zu + lower * zl
                emit(c, rows, cut(h), total)


def advance_all(factor, field, inflow, ghost_low, ghost_high, south, north, edge, emit):
    cells_x = field.shape[1]
    is_first = lax.axis_index("gx") == 0
    is_last = lax.axis_index("gx") == lax.axis_size("gx") - 1
    for c in range(3):
        edge[0, c] = jnp.where(is_first, inflow[c], ghost_low[c])
        edge[1, c] = jnp.where(is_last, field[c, cells_x - 1], ghost_high[c])

    def inner(i):
        return lambda c, rows, cols: field[c, i, rows, cols]

    def outer(side):
        return lambda c, rows, cols: edge[side, c, rows, cols]

    def one(i, west, east):
        advance(i, factor, field, west, east, south, north, functools.partial(emit, i))

    one(0, outer(0), inner(1))

    def step(i, carry):
        one(i, inner(i - 1), inner(i + 1))
        return carry

    lax.fori_loop(1, cells_x - 1, step, 0)
    one(cells_x - 1, inner(cells_x - 2), outer(1))


def advance_first(field, inflow, ghost_low, ghost_high, south, north, section, edge):
    def emit(i, c, rows, cols, value):
        section[c, i, rows, cols] = value

    advance_all(1.0, field, inflow, ghost_low, ghost_high, south, north, edge, emit)


def advance_second(
    section, field, inflow, ghost_low, ghost_high, south, north, result, edge
):
    def emit(i, c, rows, cols, value):
        result[c, i, rows, cols] = value + 0.5 * field[c, i, rows, cols]

    advance_all(0.5, section, inflow, ghost_low, ghost_high, south, north, edge, emit)


def shifted(x, axis, step, periodic):
    count = lax.axis_size(axis)
    pairs = [(i, (i + step) % count) for i in range(count)]
    if not periodic:
        pairs = [(s, t) for s, t in pairs if t - s == step]
    return lax.ppermute(x, axis, pairs)


def local(velocity, inflow, positions, tiles, coefs, counts):
    f32 = jnp.float32
    _, cells_x, cells_y, depth = velocity.shape
    groups_y = lax.axis_size("gy")
    positions, tiles, coefs = positions[0], tiles[0], coefs[0]
    records, _, points = positions.shape
    hubs = positions[:, 0, 0]
    strengths = coefs[:, None]
    whole = velocity.shape
    size = 4 * math.prod(whole)
    held = pltpu.VMEM(whole, f32)
    partial_shape = jax.ShapeDtypeStruct((records, 3, points), f32)

    west = shifted(velocity[:, -1], "gx", 1, False)
    east = shifted(velocity[:, 0], "gx", -1, False)
    south = shifted(velocity[:, :, -1:], "gy", 1, True)
    north = shifted(velocity[:, :, :1], "gy", -1, True)

    field, partial_a, active = pl.pallas_call(
        load_sample,
        out_shape=(held, partial_shape, jax.ShapeDtypeStruct((records + 1,), jnp.int32)),
        in_specs=[ANYWHERE, WHOLE, SCALAR, SCALAR, SCALAR],
        out_specs=(WHOLE, WHOLE, SCALAR),
        scratch_shapes=[pltpu.SemaphoreType.DMA],
        compiler_params=params(),
        cost_estimate=cost(2 * 10**9, 4 * size),
        name="load_sample",
    )(velocity, positions, hubs, tiles, counts)
    low_a = shifted(partial_a, "gy", 1, True)
    high_a = shifted(partial_a, "gy", -1, True)

    edge = pltpu.VMEM((2, 3, cells_y, depth), f32)
    section = pl.pallas_call(
        advance_first,
        out_shape=held,
        in_specs=[WHOLE] * 6,
        out_specs=WHOLE,
        scratch_shapes=[edge],
        compiler_params=params(),
        cost_estimate=cost(10**9, 4 * size),
        name="advance_first",
    )(resident(field), inflow, west, east, south, north)

    section, edge_x, edge_y = pl.pallas_call(
        spread_section,
        out_shape=(
            held,
            jax.ShapeDtypeStruct((2, 3, cells_y, depth), f32),
            jax.ShapeDtypeStruct((2, 3, cells_x, 1, depth), f32),
        ),
        in_specs=[WHOLE, WHOLE, SCALAR, SCALAR, WHOLE, WHOLE, WHOLE, WHOLE],
        out_specs=(WHOLE, WHOLE, WHOLE),
        input_output_aliases={0: 0},
        compiler_params=params(),
        cost_estimate=cost(2 * 10**9, 4 * size),
        name="spread_section",
    )(resident(section), positions, hubs, active, strengths, partial_a, low_a, high_a)

    west_b = shifted(edge_x[1], "gx", 1, False)
    east_b = shifted(edge_x[0], "gx", -1, False)
    south_b = shifted(edge_y[1], "gy", 1, True)
    north_b = shifted(edge_y[0], "gy", -1, True)

    partial_b = pl.pallas_call(
        sample,
        out_shape=partial_shape,
        in_specs=[WHOLE, WHOLE, SCALAR, SCALAR],
        out_specs=WHOLE,
        compiler_params=params(),
        cost_estimate=cost(2 * 10**9, 4 * size),
        name="sample",
    )(resident(section), positions, hubs, active)
    low_b = shifted(partial_b, "gy", 1, True)
    high_b = shifted(partial_b, "gy", -1, True)

    share = records // groups_y
    both = jnp.stack([partial_a, partial_b]).reshape(2, groups_y, share, 3, points)
    both = jnp.sum(lax.all_to_all(both, "gy", 1, 1), axis=1)
    mine = lax.axis_index("gy") * share
    live = (mine + jnp.arange(share, dtype=jnp.int32) < counts[0]).astype(f32)
    strength = lax.dynamic_slice_in_dim(coefs, mine, share, 0) * live[:, None]
    speed = jnp.sqrt(jnp.sum(both * both, axis=2, keepdims=True))
    mean_force = 0.5 * jnp.sum(-strength[None, :, None] * speed * both, axis=0)
    blade_force = lax.all_gather(mean_force, "gy", axis=0, tiled=True)

    following = pl.pallas_call(
        advance_second,
        out_shape=held,
        in_specs=[WHOLE] * 7,
        out_specs=WHOLE,
        scratch_shapes=[edge],
        compiler_params=params(),
        cost_estimate=cost(10**9, 4 * size),
        name="advance_second",
    )(resident(section), resident(field), inflow, west_b, east_b, south_b, north_b)

    _, velocity_next = pl.pallas_call(
        spread_next,
        out_shape=(held, jax.ShapeDtypeStruct(whole, f32)),
        in_specs=[WHOLE, WHOLE, SCALAR, SCALAR, WHOLE, WHOLE, WHOLE, WHOLE],
        out_specs=(WHOLE, ANYWHERE),
        input_output_aliases={0: 0},
        scratch_shapes=[pltpu.SemaphoreType.DMA],
        compiler_params=params(),
        cost_estimate=cost(2 * 10**9, 4 * size),
        name="spread_next",
    )(resident(following), positions, hubs, active, strengths, partial_b, low_b, high_b)
    return (velocity_next, blade_force[None])


def solution(mesh):
    return jax.shard_map(
        local,
        mesh=mesh,
        in_specs=(
            P(None, "gx", "gy", None),
            P(None, "gy", None),
            P("gx", None, None, None),
            P("gx", None, None),
            P("gx", None, None),
            P("gx"),
        ),
        out_specs=(P(None, "gx", "gy", None), P("gx", None, None, None)),
        check_vma=False,
    )
```

```python
import functools
import math

import jax
import jax.numpy as jnp
from jax import lax
from jax.experimental import pallas as pl
from jax.experimental.pallas import tpu as pltpu
from jax.sharding import PartitionSpec as P

RAD = 2
VISCOSITY = 0.05
TIME_STEP = 0.1
WIDTH_EPS = 1.5
ROOT_PI = 1.7724538509055159
TAP = [math.exp(-((d / WIDTH_EPS) ** 2)) / (WIDTH_EPS * ROOT_PI) for d in range(RAD + 1)]
LANES = 128
SUB = 8
PACKED = 16
VMEM_LIMIT = 14 * 2**20

WHOLE = pl.BlockSpec(memory_space=pltpu.VMEM)
SCALAR = pl.BlockSpec(memory_space=pltpu.SMEM)
ANYWHERE = pl.BlockSpec(memory_space=pl.ANY)


def params():
    return pltpu.CompilerParams(vmem_limit_bytes=VMEM_LIMIT)


def cost(flops, nbytes):
    return pl.CostEstimate(flops=flops, bytes_accessed=nbytes, transcendentals=0)


def resident(x):
    return pltpu.with_memory_space_constraint(x, pltpu.VMEM)


def smooth_z(x):
    depth = x.shape[-1]
    near = pltpu.roll(x, 1, 1) + pltpu.roll(x, depth - 1, 1)
    far = pltpu.roll(x, 2, 1) + pltpu.roll(x, depth - 2, 1)
    return TAP[0] * x + TAP[1] * near + TAP[2] * far


def split(x):
    high = x.astype(jnp.bfloat16)
    low = (x - high.astype(jnp.float32)).astype(jnp.bfloat16)
    return jnp.concatenate([high, low], axis=0)


def one_hot(point_z, depth):
    points = point_z.shape[-1]
    row = lax.broadcasted_iota(jnp.int32, (PACKED, points), 0).astype(jnp.bfloat16)
    place = jnp.broadcast_to(point_z.astype(jnp.float32), (PACKED, points)).astype(jnp.bfloat16)
    one, zero = jnp.ones_like(row), jnp.zeros_like(row)
    blocks = [jnp.where(row == place - float(k), one, zero) for k in range(0, depth, PACKED)]
    return jnp.concatenate(blocks, axis=0)


def along_y(point_y, base, cells_y, total_y):
    near = point_y - base
    near = jnp.where(near > total_y // 2, near - total_y, near)
    near = jnp.where(near < -(total_y // 2), near + total_y, near)
    dist = jnp.abs(lax.broadcasted_iota(jnp.int32, (cells_y, point_y.shape[-1]), 0) - near)
    return jnp.where(
        dist == 0, TAP[0], jnp.where(dist == 1, TAP[1], jnp.where(dist == 2, TAP[2], 0.0))
    )


def make_plan(hubs, tiles, counts, start, plan, bucket, held):
    tile_y, groups_y = lax.axis_index("gy"), lax.axis_size("gy")
    records, chunks = tiles.shape[1], held.shape[0]
    for k in range(chunks):
        held[k] = 0

    def place(r, carry):
        offset = tile_y - tiles[0, r]
        offset = jnp.where(offset < 0, offset + groups_y, offset)

        @pl.when(offset < tiles[1, r])
        def _():
            k = (hubs[r, 0] - start + RAD) // SUB
            bucket[k, held[k]] = r
            held[k] = held[k] + 1

        return carry

    lax.fori_loop(0, jnp.minimum(counts[0], records), place, 0)

    def flatten(k, found):
        def move(j, found):
            r = bucket[k, j]
            plan[1 + found] = r
            plan[1 + records + found] = hubs[r, 0] - start
            return found + 1

        return lax.fori_loop(0, held[k], move, found)

    plan[0] = lax.fori_loop(0, chunks, flatten, jnp.int32(0))


def pair(plan, t):
    records = (plan.shape[0] - 1) // 2
    first = 2 * t
    second = jnp.minimum(first + 1, plan[0] - 1)
    return [(plan[1 + n], plan[1 + records + n]) for n in (first, second)], second > first


def sampled_rows(field, point_y, point_z, picks):
    cells_x, cells_y, depth = field.shape[1:]
    total_y = cells_y * lax.axis_size("gy")
    base = lax.axis_index("gy") * cells_y
    smooth = []
    for r, hub in picks:
        planes = []
        for c in range(3):
            plane = TAP[0] * field[c, hub]
            plane += TAP[1] * (field[c, hub - 1] + field[c, hub + 1])
            plane += TAP[2] * (field[c, hub - 2] + field[c, hub + 2])
            planes.append(plane)
        smooth.append(split(smooth_z(jnp.concatenate(planes, axis=0))))
    out = []
    for (r, hub), planes in zip(picks, smooth):
        picked = jnp.dot(
            planes, one_hot(point_z[r], depth), preferred_element_type=jnp.float32
        )
        picked = picked[: 3 * cells_y] + picked[3 * cells_y :]
        weight = along_y(point_y[r], base, cells_y, total_y)
        out.append(
            [
                jnp.sum(picked[c * cells_y : (c + 1) * cells_y] * weight, axis=0, keepdims=True)
                for c in range(3)
            ]
        )
    return out


def pack_edges(field, edge_x, pack_low, pack_high):
    cells_x, cells_y, depth = field.shape[1:]
    for c in range(3):
        edge_x[0, c] = field[c, 0]
        edge_x[1, c] = field[c, cells_x - 1]

    def step(t, carry):
        for c in range(3):
            for k in range(SUB):
                i = t * SUB + k
                pack_low[c * cells_x + i] = field[c, i, pl.ds(0, 1), :]
                pack_high[c * cells_x + i] = field[c, i, pl.ds(cells_y - 1, 1), :]
        return carry

    lax.fori_loop(0, cells_x // SUB, step, 0)


def load_sample(
    velocity, positions, tiles, coefs, counts,
    field, pack_low, pack_high, edge_x, point_y, point_z, strength, plan,
    hubs, bucket, held, hub_sem, sems,
):
    cells_x, cells_y, depth = field.shape[1:]
    records, points = coefs.shape
    chunks = cells_x // SUB
    first_row = 3 * cells_x
    start = lax.axis_index("gx") * cells_x

    def chunk(k):
        planes = pl.ds(k * SUB, SUB)
        return pltpu.make_async_copy(velocity.at[:, planes], field.at[:, planes], sems.at[k])

    hub_copy = pltpu.make_async_copy(positions.at[0, :, pl.ds(0, LANES)], hubs, hub_sem)
    hub_copy.start()
    for k in range(chunks):
        chunk(k).start()
    for r in range(records):
        point_y[r] = positions[1, pl.ds(r, 1), :]
        point_z[r] = positions[2, pl.ds(r, 1), :]
        strength[r] = coefs[pl.ds(r, 1), :]

    def clear(n, carry):
        for k in range(SUB):
            pack_low[first_row + n * SUB + k] = jnp.zeros((1, points), jnp.float32)
            pack_high[first_row + n * SUB + k] = jnp.zeros((1, points), jnp.float32)
        return carry

    lax.fori_loop(0, 3 * records // SUB, clear, 0)
    hub_copy.wait()
    make_plan(hubs, tiles, counts, start, plan, bucket, held)

    def wait_to(ready, wanted):
        def step(k, carry):
            chunk(k).wait()
            return carry

        lax.fori_loop(ready, wanted, step, 0)
        return jnp.maximum(ready, wanted)

    def step(t, ready):
        picks, _ = pair(plan, t)
        ready = wait_to(ready, (picks[1][1] + RAD) // SUB + 1)
        for (r, _), rows in zip(picks, sampled_rows(field, point_y, point_z, picks)):
            for c in range(3):
                pack_low[first_row + 3 * r + c] = rows[c]
                pack_high[first_row + 3 * r + c] = rows[c]
        return ready

    ready = lax.fori_loop(0, (plan[0] + 1) // 2, step, jnp.int32(0))
    wait_to(ready, chunks)
    pack_edges(field, edge_x, pack_low, pack_high)


def fix_edges(factor, target, field, inflow, ghost_low, ghost_high, got_low, got_high):
    cells_x, cells_y, depth = field.shape[1:]
    last = cells_x - 1
    is_first = lax.axis_index("gx") == 0
    is_last = lax.axis_index("gx") == lax.axis_size("gx") - 1
    spread = factor * TIME_STEP * VISCOSITY
    half = 0.5 * factor * TIME_STEP
    for c in range(3):
        west = jnp.where(is_first, inflow[c], ghost_low[c])
        east = jnp.where(is_last, field[c, last], ghost_high[c])
        target[c, 0] = target[c, 0] + west * (spread + half * field[0, 0])
        target[c, last] = target[c, last] + east * (spread - half * field[0, last])

    low, high = pl.ds(0, 1), pl.ds(cells_y - 1, 1)

    def step(t, carry):
        for k in range(SUB):
            i = t * SUB + k
            south = spread + half * field[1, i, low, :]
            north = spread - half * field[1, i, high, :]
            for c in range(3):
                n = c * cells_x + i
                target[c, i, low, :] = target[c, i, low, :] + got_low[n] * south
                target[c, i, high, :] = target[c, i, high, :] + got_high[n] * north
        return carry

    lax.fori_loop(0, cells_x // SUB, step, 0)


def slabs_of(point_y, point_z, strength, own, low, high, cells, scales, picks):
    cells_x, cells_y, depth = cells
    total_y = cells_y * lax.axis_size("gy")
    base = lax.axis_index("gy") * cells_y
    spread = []
    for (r, hub), scale in zip(picks, scales):
        rows = [3 * cells_x + 3 * r + c for c in range(3)]
        total = [own[n] + (low[n] + high[n]) for n in rows]
        speed = jnp.sqrt(total[0] * total[0] + total[1] * total[1] + total[2] * total[2])
        pull = strength[r] * (-scale) * speed
        weight = along_y(point_y[r], base, cells_y, total_y)
        spread.append(split(jnp.concatenate([weight * (pull * x) for x in total], axis=0)))
    slabs = []
    for (r, hub), part in zip(picks, spread):
        slab = lax.dot_general(
            part,
            one_hot(point_z[r], depth),
            (((1,), (1,)), ((), ())),
            preferred_element_type=jnp.float32,
        )
        slabs.append(smooth_z(slab[: 3 * cells_y] + slab[3 * cells_y :]))
    return slabs


def add_slab(field, slab, hub):
    cells_y = field.shape[2]
    for c in range(3):
        part = slab[c * cells_y : (c + 1) * cells_y]
        terms = [tap * part for tap in TAP]
        for d in range(-RAD, RAD + 1):
            field[c, hub + d] = field[c, hub + d] + terms[abs(d)]


def spread_pair(t, scale, field, plan, points, own, low, high):
    picks, both = pair(plan, t)
    scales = [scale, jnp.where(both, scale, 0.0)]
    slabs = slabs_of(*points, own, low, high, field.shape[1:], scales, picks)
    for (r, hub), slab in zip(picks, slabs):
        add_slab(field, slab, hub)


def spread_sample(
    section_in, field, inflow, ghost_low, ghost_high, own, got_low, got_high,
    plan, point_y, point_z, strength,
    section, pack_low, pack_high, edge_x, share_out,
):
    cells_x = field.shape[1]
    records = point_y.shape[0]
    share = share_out.shape[2] // 3
    first_row = 3 * cells_x
    fix_edges(1.0, section, field, inflow, ghost_low, ghost_high, got_low, got_high)

    def spread_step(t, carry):
        points = (point_y, point_z, strength)
        spread_pair(t, TIME_STEP, section, plan, points, own, got_low, got_high)
        return carry

    lax.fori_loop(0, (plan[0] + 1) // 2, spread_step, 0)
    pack_edges(section, edge_x, pack_low, pack_high)

    def clear(r, carry):
        zero = jnp.zeros_like(own[0])
        for c in range(3):
            pack_low[first_row + 3 * r + c] = zero
            pack_high[first_row + 3 * r + c] = zero
            share_out[r // share, 0, 3 * (r % share) + c] = own[first_row + 3 * r + c]
            share_out[r // share, 1, 3 * (r % share) + c] = zero
        return carry

    lax.fori_loop(0, records, clear, 0)

    def sample_step(t, carry):
        picks, _ = pair(plan, t)
        for (r, _), rows in zip(picks, sampled_rows(section, point_y, point_z, picks)):
            for c in range(3):
                pack_low[first_row + 3 * r + c] = rows[c]
                pack_high[first_row + 3 * r + c] = rows[c]
                share_out[r // share, 1, 3 * (r % share) + c] = rows[c]
        return carry

    lax.fori_loop(0, (plan[0] + 1) // 2, sample_step, 0)


def share_force(parts, strength, counts, result):
    groups, _, rows = parts.shape[:3]
    share = rows // 3
    mine = lax.axis_index("gy") * share
    for s in range(share):
        live = mine + s < counts[0]
        pull = jnp.where(live, -0.5 * strength[mine + s], 0.0)
        total = [0.0, 0.0, 0.0]
        for stage in range(2):
            value = []
            for c in range(3):
                n = 3 * s + c
                x = parts[0, stage, n]
                for g in range(1, groups):
                    x += parts[g, stage, n]
                value.append(x)
            speed = jnp.sqrt(value[0] * value[0] + value[1] * value[1] + value[2] * value[2])
            total = [acc + speed * x for acc, x in zip(total, value)]
        for c in range(3):
            for g in range(groups):
                result[g, 3 * s + c] = pull * total[c]


def spread_next(
    following_in, section, inflow, ghost_low, ghost_high, own, got_low, got_high,
    plan, point_y, point_z, strength,
    following, result, sems,
):
    chunks = section.shape[1] // SUB
    factor = 0.5

    def chunk(k):
        planes = pl.ds(k * SUB, SUB)
        return pltpu.make_async_copy(following.at[:, planes], result.at[:, planes], sems.at[k])

    def send_to(sent, ready):
        def step(k, carry):
            chunk(k).start()
            return carry

        lax.fori_loop(sent, ready, step, 0)
        return jnp.maximum(sent, ready)

    fix_edges(factor, following, section, inflow, ghost_low, ghost_high, got_low, got_high)

    def step(t, sent):
        picks, _ = pair(plan, t)
        sent = send_to(sent, (picks[0][1] + RAD) // SUB - 1)
        points = (point_y, point_z, strength)
        spread_pair(t, factor * TIME_STEP, following, plan, points, own, got_low, got_high)
        return sent

    sent = lax.fori_loop(0, (plan[0] + 1) // 2, step, jnp.int32(0))
    send_to(sent, chunks)
    for k in range(chunks):
        chunk(k).wait()


def advance(i, factor, field, west, east, emit):
    cells_y, depth = field.shape[2:]
    groups, halves = cells_y // SUB, depth // LANES
    row = lax.broadcasted_iota(jnp.int32, (SUB, LANES), 0)
    lane = lax.broadcasted_iota(jnp.int32, (SUB, LANES), 1)
    first_row, last_row = row == 0, row == SUB - 1
    first_lane, last_lane = lane == 0, lane == LANES - 1
    spread = factor * TIME_STEP * VISCOSITY
    centre = factor * (1.0 - 6.0 * TIME_STEP * VISCOSITY)
    zero = jnp.zeros((SUB, LANES), jnp.float32)

    def at(c, g, h):
        if 0 <= g < groups and 0 <= h < halves:
            return field[c, i, pl.ds(g * SUB, SUB), pl.ds(h * LANES, LANES)]
        return zero

    for g in range(groups):
        for h in range(halves):
            place = (pl.ds(g * SUB, SUB), pl.ds(h * LANES, LANES))
            q = [at(c, g, h) for c in range(3)]
            speeds = [(0.5 * factor * TIME_STEP) * x for x in q]
            less = [spread - s for s in speeds]
            more = [spread + s for s in speeds]
            for c in range(3):
                x = q[c]
                above = pltpu.roll(jnp.where(first_row, at(c, g + 1, h), x), SUB - 1, 0)
                below = pltpu.roll(jnp.where(last_row, at(c, g - 1, h), x), 1, 0)
                upper = pltpu.roll(jnp.where(first_lane, at(c, g, h + 1), x), LANES - 1, 1)
                lower = pltpu.roll(jnp.where(last_lane, at(c, g, h - 1), x), 1, 1)
                total = centre * x
                if east is not None:
                    total += field[c, east, place[0], place[1]] * less[0]
                if west is not None:
                    total += field[c, west, place[0], place[1]] * more[0]
                total += above * less[1] + below * more[1]
                total += upper * less[2] + lower * more[2]
                emit(c, place, total)


def advance_all(factor, field, emit):
    last = field.shape[1] - 1

    def one(i, west, east):
        advance(i, factor, field, west, east, functools.partial(emit, i))

    def step(i, carry):
        one(i, i - 1, i + 1)
        return carry

    one(0, None, 1)
    lax.fori_loop(1, last, step, 0)
    one(last, last - 1, None)


def advance_first(field, section):
    def emit(i, c, place, value):
        section[c, i, place[0], place[1]] = value

    advance_all(1.0, field, emit)


def advance_second(section, field, following):
    def emit(i, c, place, value):
        following[c, i, place[0], place[1]] = value + 0.5 * field[c, i, place[0], place[1]]

    advance_all(0.5, section, emit)


def shifted(x, axis, step, periodic):
    count = lax.axis_size(axis)
    pairs = [(i, (i + step) % count) for i in range(count)]
    if not periodic:
        pairs = [(s, t) for s, t in pairs if t - s == step]
    return lax.ppermute(x, axis, pairs)


def exchange(pack_low, pack_high, edge_x):
    got_low = shifted(pack_high, "gy", 1, True)
    got_high = shifted(pack_low, "gy", -1, True)
    ghost_low = shifted(edge_x[1], "gx", 1, False)
    ghost_high = shifted(edge_x[0], "gx", -1, False)
    return ghost_low, ghost_high, got_low, got_high


def local(velocity, inflow, positions, tiles, coefs, counts):
    f32, i32 = jnp.float32, jnp.int32
    whole = velocity.shape
    _, cells_x, cells_y, depth = whole
    groups_y = lax.axis_size("gy")
    positions = positions[0].transpose(1, 0, 2)
    tiles, coefs = tiles[0].T, coefs[0]
    records, points = coefs.shape
    share = records // groups_y
    chunks = cells_x // SUB
    size = 4 * math.prod(whole)
    held = pltpu.VMEM(whole, f32)
    pack = pltpu.VMEM((3 * cells_x + 3 * records, 1, points), f32)
    edge = pltpu.VMEM((2, 3, cells_y, depth), f32)
    per_record = pltpu.VMEM((records, 1, points), i32)

    field, pack_low, pack_high, edge_x, point_y, point_z, strength, plan = pl.pallas_call(
        load_sample,
        out_shape=(
            held, pack, pack, edge, per_record, per_record,
            pltpu.VMEM((records, 1, points), f32),
            jax.ShapeDtypeStruct((1 + 2 * records,), i32),
        ),
        in_specs=[ANYWHERE, WHOLE, SCALAR, WHOLE, SCALAR],
        out_specs=(WHOLE,) * 7 + (SCALAR,),
        scratch_shapes=[
            pltpu.SMEM((records, LANES), i32),
            pltpu.SMEM((chunks, records), i32),
            pltpu.SMEM((chunks,), i32),
            pltpu.SemaphoreType.DMA,
            pltpu.SemaphoreType.DMA((chunks,)),
        ],
        compiler_params=params(),
        cost_estimate=cost(2 * 10**9, 4 * size),
        name="load_sample",
    )(
        pltpu.with_memory_space_constraint(velocity, pltpu.HBM),
        positions, tiles, coefs, counts,
    )
    point_y, point_z, strength = resident(point_y), resident(point_z), resident(strength)
    field = resident(field)
    ghosts_a = exchange(pack_low, pack_high, edge_x)

    section = pl.pallas_call(
        advance_first,
        out_shape=held,
        in_specs=[WHOLE],
        out_specs=WHOLE,
        compiler_params=params(),
        cost_estimate=cost(10**9, 4 * size),
        name="advance_first",
    )(field)

    section, pack_low_b, pack_high_b, edge_x, shares = pl.pallas_call(
        spread_sample,
        out_shape=(
            held, pack, pack, edge,
            pltpu.VMEM((groups_y, 2, 3 * share, 1, points), f32),
        ),
        in_specs=[WHOLE] * 8 + [SCALAR] + [WHOLE] * 3,
        out_specs=(WHOLE,) * 5,
        input_output_aliases={0: 0},
        compiler_params=params(),
        cost_estimate=cost(2 * 10**9, 4 * size),
        name="spread_sample",
    )(
        resident(section), field, inflow, *ghosts_a[:2], resident(pack_low), *ghosts_a[2:],
        plan, point_y, point_z, strength,
    )
    section = resident(section)
    ghosts_b = exchange(pack_low_b, pack_high_b, edge_x)
    shares = lax.all_to_all(shares, "gy", 0, 0)

    following = pl.pallas_call(
        advance_second,
        out_shape=held,
        in_specs=[WHOLE] * 2,
        out_specs=WHOLE,
        compiler_params=params(),
        cost_estimate=cost(10**9, 4 * size),
        name="advance_second",
    )(section, field)

    forces = pl.pallas_call(
        share_force,
        out_shape=pltpu.VMEM((groups_y, 3 * share, 1, points), f32),
        in_specs=[WHOLE, WHOLE, SCALAR],
        out_specs=WHOLE,
        compiler_params=params(),
        cost_estimate=cost(10**6, 10**6),
        name="share_force",
    )(shares, strength, counts)
    forces = lax.all_to_all(forces, "gy", 0, 0)

    _, velocity_next = pl.pallas_call(
        spread_next,
        out_shape=(held, jax.ShapeDtypeStruct(whole, f32)),
        in_specs=[WHOLE] * 8 + [SCALAR] + [WHOLE] * 3,
        out_specs=(WHOLE, ANYWHERE),
        input_output_aliases={0: 0},
        scratch_shapes=[pltpu.SemaphoreType.DMA((chunks,))],
        compiler_params=params(),
        cost_estimate=cost(2 * 10**9, 4 * size),
        name="spread_next",
    )(
        resident(following), section, inflow, *ghosts_b[:2], resident(pack_low_b), *ghosts_b[2:],
        plan, point_y, point_z, strength,
    )
    return (velocity_next, forces.reshape(1, records, 3, points))


def solution(mesh):
    return jax.shard_map(
        local,
        mesh=mesh,
        in_specs=(
            P(None, "gx", "gy", None),
            P(None, "gy", None),
            P("gx", None, None, None),
            P("gx", None, None),
            P("gx", None, None),
            P("gx"),
        ),
        out_specs=(P(None, "gx", "gy", None), P("gx", None, None, None)),
        check_vma=False,
    )
```

```python
import functools
import math

import jax
import jax.numpy as jnp
from jax import lax
from jax.experimental import pallas as pl
from jax.experimental.pallas import tpu as pltpu
from jax.sharding import PartitionSpec as P

RAD = 2
VISCOSITY = 0.05
TIME_STEP = 0.1
WIDTH_EPS = 1.5
ROOT_PI = 1.7724538509055159
TAP = [math.exp(-((d / WIDTH_EPS) ** 2)) / (WIDTH_EPS * ROOT_PI) for d in range(RAD + 1)]
LANES = 128
SUB = 8
PACKED = 16
VMEM_LIMIT = 14 * 2**20

WHOLE = pl.BlockSpec(memory_space=pltpu.VMEM)
SCALAR = pl.BlockSpec(memory_space=pltpu.SMEM)
ANYWHERE = pl.BlockSpec(memory_space=pl.ANY)


def params(limit=VMEM_LIMIT):
    return pltpu.CompilerParams(vmem_limit_bytes=limit)


def cost(flops, nbytes):
    return pl.CostEstimate(flops=flops, bytes_accessed=nbytes, transcendentals=0)


def resident(x):
    return pltpu.with_memory_space_constraint(x, pltpu.VMEM)


def streamed(x):
    return pltpu.with_memory_space_constraint(x, pltpu.HBM)


def smooth_z(x):
    depth = x.shape[-1]
    near = pltpu.roll(x, 1, 1) + pltpu.roll(x, depth - 1, 1)
    far = pltpu.roll(x, 2, 1) + pltpu.roll(x, depth - 2, 1)
    return TAP[0] * x + TAP[1] * near + TAP[2] * far


def split(x):
    high = x.astype(jnp.bfloat16)
    low = (x - high.astype(jnp.float32)).astype(jnp.bfloat16)
    return jnp.concatenate([high, low], axis=0)


def one_hot(point_z, depth):
    points = point_z.shape[-1]
    row = lax.broadcasted_iota(jnp.int32, (PACKED, points), 0).astype(jnp.bfloat16)
    place = jnp.broadcast_to(point_z.astype(jnp.float32), (PACKED, points)).astype(jnp.bfloat16)
    one, zero = jnp.ones_like(row), jnp.zeros_like(row)
    blocks = [jnp.where(row == place - float(k), one, zero) for k in range(0, depth, PACKED)]
    return jnp.concatenate(blocks, axis=0)


def along_y(point_y, base, cells_y, total_y):
    near = point_y - base
    near = jnp.where(near > total_y // 2, near - total_y, near)
    near = jnp.where(near < -(total_y // 2), near + total_y, near)
    dist = jnp.abs(lax.broadcasted_iota(jnp.int32, (cells_y, point_y.shape[-1]), 0) - near)
    return jnp.where(
        dist == 0, TAP[0], jnp.where(dist == 1, TAP[1], jnp.where(dist == 2, TAP[2], 0.0))
    )


def make_plan(hubs, tiles, counts, start, plan, bucket, held):
    tile_y, groups_y = lax.axis_index("gy"), lax.axis_size("gy")
    records, chunks = tiles.shape[1], held.shape[0]
    for k in range(chunks):
        held[k] = 0

    def place(r, carry):
        offset = tile_y - tiles[0, r]
        offset = jnp.where(offset < 0, offset + groups_y, offset)

        @pl.when(offset < tiles[1, r])
        def _():
            k = (hubs[r, 0] - start + RAD) // SUB
            bucket[k, held[k]] = r
            held[k] = held[k] + 1

        return carry

    lax.fori_loop(0, jnp.minimum(counts[0], records), place, 0)

    def flatten(k, found):
        def move(j, found):
            r = bucket[k, j]
            plan[1 + found] = r
            plan[1 + records + found] = hubs[r, 0] - start
            return found + 1

        return lax.fori_loop(0, held[k], move, found)

    plan[0] = lax.fori_loop(0, chunks, flatten, jnp.int32(0))


def pair(plan, t):
    records = (plan.shape[0] - 1) // 2
    first = 2 * t
    second = jnp.minimum(first + 1, plan[0] - 1)
    return [(plan[1 + n], plan[1 + records + n]) for n in (first, second)], second > first


def sampled_rows(field, point_y, point_z, picks):
    cells_x, cells_y, depth = field.shape[1:]
    total_y = cells_y * lax.axis_size("gy")
    base = lax.axis_index("gy") * cells_y
    smooth = []
    for r, hub in picks:
        planes = []
        for c in range(3):
            plane = TAP[0] * field[c, hub]
            plane += TAP[1] * (field[c, hub - 1] + field[c, hub + 1])
            plane += TAP[2] * (field[c, hub - 2] + field[c, hub + 2])
            planes.append(plane)
        smooth.append(split(smooth_z(jnp.concatenate(planes, axis=0))))
    out = []
    for (r, hub), planes in zip(picks, smooth):
        picked = jnp.dot(
            planes, one_hot(point_z[r], depth), preferred_element_type=jnp.float32
        )
        picked = picked[: 3 * cells_y] + picked[3 * cells_y :]
        weight = along_y(point_y[r], base, cells_y, total_y)
        out.append(
            [
                jnp.sum(picked[c * cells_y : (c + 1) * cells_y] * weight, axis=0, keepdims=True)
                for c in range(3)
            ]
        )
    return out


def pack_edges(field, edge_west, edge_east, pack_low, pack_high):
    cells_x, cells_y, depth = field.shape[1:]
    for c in range(3):
        edge_west[c] = field[c, 0]
        edge_east[c] = field[c, cells_x - 1]

    def step(t, carry):
        for c in range(3):
            for k in range(SUB):
                i = t * SUB + k
                pack_low[c * cells_x + i] = field[c, i, pl.ds(0, 1), :]
                pack_high[c * cells_x + i] = field[c, i, pl.ds(cells_y - 1, 1), :]
        return carry

    lax.fori_loop(0, cells_x // SUB, step, 0)


def load_sample(
    velocity, positions, tiles_hbm, coefs_hbm, counts,
    field, pack_low, pack_high, edge_west, edge_east, point_y, point_z, strength, plan,
    hubs, tiles, places, coefs, bucket, held, small_sems, sems,
):
    cells_x, cells_y, depth = field.shape[1:]
    records, points = coefs.shape
    chunks = cells_x // SUB
    first_row = 3 * cells_x
    start = lax.axis_index("gx") * cells_x

    def chunk(k):
        planes = pl.ds(k * SUB, SUB)
        return pltpu.make_async_copy(velocity.at[:, planes], field.at[:, planes], sems.at[k])

    small = [
        (positions.at[0, :, pl.ds(0, LANES)], hubs),
        (tiles_hbm, tiles),
        (positions.at[pl.ds(1, 2)], places),
        (coefs_hbm, coefs),
    ]
    small = [
        pltpu.make_async_copy(source, target, small_sems.at[n])
        for n, (source, target) in enumerate(small)
    ]
    for copy in small:
        copy.start()
    for k in range(chunks):
        chunk(k).start()

    def clear(n, carry):
        for k in range(SUB):
            pack_low[first_row + n * SUB + k] = jnp.zeros((1, points), jnp.float32)
            pack_high[first_row + n * SUB + k] = jnp.zeros((1, points), jnp.float32)
        return carry

    lax.fori_loop(0, 3 * records // SUB, clear, 0)
    for copy in small:
        copy.wait()
    make_plan(hubs, tiles, counts, start, plan, bucket, held)
    for r in range(records):
        point_y[r] = places[0, pl.ds(r, 1), :]
        point_z[r] = places[1, pl.ds(r, 1), :]
        strength[r] = coefs[pl.ds(r, 1), :]

    def wait_to(ready, wanted):
        def step(k, carry):
            chunk(k).wait()
            return carry

        lax.fori_loop(ready, wanted, step, 0)
        return jnp.maximum(ready, wanted)

    def step(t, ready):
        picks, _ = pair(plan, t)
        ready = wait_to(ready, (picks[1][1] + RAD) // SUB + 1)
        for (r, _), rows in zip(picks, sampled_rows(field, point_y, point_z, picks)):
            for c in range(3):
                pack_low[first_row + 3 * r + c] = rows[c]
                pack_high[first_row + 3 * r + c] = rows[c]
        return ready

    ready = lax.fori_loop(0, (plan[0] + 1) // 2, step, jnp.int32(0))
    wait_to(ready, chunks)
    pack_edges(field, edge_west, edge_east, pack_low, pack_high)


def fix_west(factor, target, own, inflow, ghost):
    first = lax.axis_index("gx") == 0
    for c in range(3):
        west = jnp.where(first, inflow[c], ghost[c])
        coef = factor * TIME_STEP * VISCOSITY + (0.5 * factor * TIME_STEP) * own[0]
        target[c, 0] = target[c, 0] + west * coef


def fix_east(factor, target, own, ghost):
    last = lax.axis_index("gx") == lax.axis_size("gx") - 1
    end = target.shape[1] - 1
    for c in range(3):
        east = jnp.where(last, own[c], ghost[c])
        coef = factor * TIME_STEP * VISCOSITY - (0.5 * factor * TIME_STEP) * own[0]
        target[c, end] = target[c, end] + east * coef


def fix_rows(factor, target, own_low, own_high, got_low, got_high, t):
    cells_x, cells_y = target.shape[1:3]
    spread = factor * TIME_STEP * VISCOSITY
    half = 0.5 * factor * TIME_STEP
    low, high = pl.ds(0, 1), pl.ds(cells_y - 1, 1)
    for k in range(SUB):
        i = t * SUB + k
        south = spread + half * own_low[cells_x + i]
        north = spread - half * own_high[cells_x + i]
        for c in range(3):
            n = c * cells_x + i
            target[c, i, low, :] = target[c, i, low, :] + got_low[n] * south
            target[c, i, high, :] = target[c, i, high, :] + got_high[n] * north


def slabs_of(point_y, point_z, strength, own, low, high, cells, scales, picks):
    cells_x, cells_y, depth = cells
    total_y = cells_y * lax.axis_size("gy")
    base = lax.axis_index("gy") * cells_y
    spread = []
    for (r, hub), scale in zip(picks, scales):
        rows = [3 * cells_x + 3 * r + c for c in range(3)]
        total = [own[n] + (low[n] + high[n]) for n in rows]
        speed = jnp.sqrt(total[0] * total[0] + total[1] * total[1] + total[2] * total[2])
        pull = strength[r] * (-scale) * speed
        weight = along_y(point_y[r], base, cells_y, total_y)
        spread.append(split(jnp.concatenate([weight * (pull * x) for x in total], axis=0)))
    slabs = []
    for (r, hub), part in zip(picks, spread):
        slab = lax.dot_general(
            part,
            one_hot(point_z[r], depth),
            (((1,), (1,)), ((), ())),
            preferred_element_type=jnp.float32,
        )
        slabs.append(smooth_z(slab[: 3 * cells_y] + slab[3 * cells_y :]))
    return slabs


def add_slab(field, slab, hub):
    cells_y = field.shape[2]
    for c in range(3):
        part = slab[c * cells_y : (c + 1) * cells_y]
        terms = [tap * part for tap in TAP]
        for d in range(-RAD, RAD + 1):
            field[c, hub + d] = field[c, hub + d] + terms[abs(d)]


def spread_pair(t, scale, field, plan, points, own, low, high):
    picks, both = pair(plan, t)
    scales = [scale, jnp.where(both, scale, 0.0)]
    slabs = slabs_of(*points, own, low, high, field.shape[1:], scales, picks)
    for (r, hub), slab in zip(picks, slabs):
        add_slab(field, slab, hub)


def spread_sample(
    section_in, inflow, ghost_low, ghost_high, own_low, own_high, own_west, own_east, got_low, got_high,
    plan, point_y, point_z, strength,
    section, section_out, pack_low, pack_high, edge_west, edge_east, share_out, sem,
):
    cells_x = section.shape[1]
    records = point_y.shape[0]
    share = share_out.shape[2] // 3
    first_row = 3 * cells_x

    def fix_step(t, carry):
        fix_rows(1.0, section, own_low, own_high, got_low, got_high, t)
        return carry

    fix_west(1.0, section, own_west, inflow, ghost_low)
    fix_east(1.0, section, own_east, ghost_high)
    lax.fori_loop(0, cells_x // SUB, fix_step, 0)

    def spread_step(t, carry):
        points = (point_y, point_z, strength)
        spread_pair(t, TIME_STEP, section, plan, points, own_low, got_low, got_high)
        return carry

    lax.fori_loop(0, (plan[0] + 1) // 2, spread_step, 0)
    copy = pltpu.make_async_copy(section, section_out, sem)
    copy.start()
    pack_edges(section, edge_west, edge_east, pack_low, pack_high)

    def clear(r, carry):
        zero = jnp.zeros_like(own_low[0])
        for c in range(3):
            pack_low[first_row + 3 * r + c] = zero
            pack_high[first_row + 3 * r + c] = zero
            share_out[r // share, 0, 3 * (r % share) + c] = own_low[first_row + 3 * r + c]
            share_out[r // share, 1, 3 * (r % share) + c] = zero
        return carry

    lax.fori_loop(0, records, clear, 0)

    def sample_step(t, carry):
        picks, _ = pair(plan, t)
        for (r, _), rows in zip(picks, sampled_rows(section, point_y, point_z, picks)):
            for c in range(3):
                pack_low[first_row + 3 * r + c] = rows[c]
                pack_high[first_row + 3 * r + c] = rows[c]
                share_out[r // share, 1, 3 * (r % share) + c] = rows[c]
        return carry

    lax.fori_loop(0, (plan[0] + 1) // 2, sample_step, 0)
    copy.wait()


def share_force(parts, strength, counts, after, after_low, after_high, result):
    groups, _, rows = parts.shape[:3]
    share = rows // 3
    mine = lax.axis_index("gy") * share
    for s in range(share):
        live = mine + s < counts[0]
        pull = jnp.where(live, -0.5 * strength[mine + s], 0.0)
        total = [0.0, 0.0, 0.0]
        for stage in range(2):
            value = []
            for c in range(3):
                n = 3 * s + c
                x = parts[0, stage, n]
                for g in range(1, groups):
                    x += parts[g, stage, n]
                value.append(x)
            speed = jnp.sqrt(value[0] * value[0] + value[1] * value[1] + value[2] * value[2])
            total = [acc + speed * x for acc, x in zip(total, value)]
        for c in range(3):
            for g in range(groups):
                result[g, 3 * s + c] = pull * total[c]


def spread_next(
    following, inflow, ghost_low, ghost_high, own_low, own_high, own_west, own_east, got_low, got_high,
    plan, point_y, point_z, strength, after,
    result, field, in_sems, out_sems,
):
    chunks = field.shape[1] // SUB
    factor = 0.5

    def chunk_in(k):
        planes = pl.ds(k * SUB, SUB)
        return pltpu.make_async_copy(following.at[:, planes], field.at[:, planes], in_sems.at[k])

    def chunk_out(k):
        planes = pl.ds(k * SUB, SUB)
        return pltpu.make_async_copy(field.at[:, planes], result.at[:, planes], out_sems.at[k])

    def wait_to(ready, wanted):
        def step(k, carry):
            chunk_in(k).wait()
            fix_rows(factor, field, own_low, own_high, got_low, got_high, k)

            @pl.when(k == 0)
            def _():
                fix_west(factor, field, own_west, inflow, ghost_low)

            @pl.when(k == chunks - 1)
            def _():
                fix_east(factor, field, own_east, ghost_high)

            return carry

        lax.fori_loop(ready, wanted, step, 0)
        return jnp.maximum(ready, wanted)

    def send_to(sent, done):
        def step(k, carry):
            chunk_out(k).start()
            return carry

        lax.fori_loop(sent, done, step, 0)
        return jnp.maximum(sent, done)

    for k in range(chunks):
        chunk_in(k).start()

    def step(t, carry):
        ready, sent = carry
        picks, _ = pair(plan, t)
        ready = wait_to(ready, (picks[1][1] + RAD) // SUB + 1)
        sent = send_to(sent, (picks[0][1] + RAD) // SUB - 1)
        points = (point_y, point_z, strength)
        spread_pair(t, factor * TIME_STEP, field, plan, points, own_low, got_low, got_high)
        return ready, sent

    zero = jnp.int32(0)
    ready, sent = lax.fori_loop(0, (plan[0] + 1) // 2, step, (zero, zero))
    sent = send_to(sent, ready)

    def finish(k, carry):
        wait_to(k, k + 1)
        chunk_out(k).start()
        return carry

    lax.fori_loop(ready, chunks, finish, 0)
    for k in range(chunks):
        chunk_out(k).wait()


def advance(i, factor, field, west, east, emit):
    cells_y, depth = field.shape[2:]
    groups, halves = cells_y // SUB, depth // LANES
    row = lax.broadcasted_iota(jnp.int32, (SUB, LANES), 0)
    lane = lax.broadcasted_iota(jnp.int32, (SUB, LANES), 1)
    first_row, last_row = row == 0, row == SUB - 1
    first_lane, last_lane = lane == 0, lane == LANES - 1
    spread = factor * TIME_STEP * VISCOSITY
    centre = factor * (1.0 - 6.0 * TIME_STEP * VISCOSITY)
    zero = jnp.zeros((SUB, LANES), jnp.float32)

    loaded = {}

    def at(c, g, h):
        if not (0 <= g < groups and 0 <= h < halves):
            return zero
        if (c, g, h) not in loaded:
            loaded[c, g, h] = field[c, i, pl.ds(g * SUB, SUB), pl.ds(h * LANES, LANES)]
        return loaded[c, g, h]

    for g in range(groups):
        for h in range(halves):
            place = (pl.ds(g * SUB, SUB), pl.ds(h * LANES, LANES))
            q = [at(c, g, h) for c in range(3)]
            speeds = [(0.5 * factor * TIME_STEP) * x for x in q]
            less = [spread - s for s in speeds]
            more = [spread + s for s in speeds]
            for c in range(3):
                x = q[c]
                above = pltpu.roll(jnp.where(first_row, at(c, g + 1, h), x), SUB - 1, 0)
                below = pltpu.roll(jnp.where(last_row, at(c, g - 1, h), x), 1, 0)
                upper = pltpu.roll(jnp.where(first_lane, at(c, g, h + 1), x), LANES - 1, 1)
                lower = pltpu.roll(jnp.where(last_lane, at(c, g, h - 1), x), 1, 1)
                total = centre * x
                if east is not None:
                    total += field[c, east, place[0], place[1]] * less[0]
                if west is not None:
                    total += field[c, west, place[0], place[1]] * more[0]
                total += above * less[1] + below * more[1]
                total += upper * less[2] + lower * more[2]
                emit(c, place, total)


def advance_all(factor, field, emit):
    last = field.shape[1] - 1

    def one(i, west, east):
        advance(i, factor, field, west, east, functools.partial(emit, i))

    def step(i, carry):
        one(i, i - 1, i + 1)
        return carry

    one(0, None, 1)
    lax.fori_loop(1, last, step, 0)
    one(last, last - 1, None)


def advance_first(field, section):
    def emit(i, c, place, value):
        section[c, i, place[0], place[1]] = value

    advance_all(1.0, field, emit)


def advance_second(
    section_hbm, velocity, following, token, section, field, result, in_sems, old_sems, out_sems
):
    cells_x = section.shape[1]
    chunks = cells_x // SUB

    def planes(k):
        return pl.ds(k * SUB, SUB)

    def chunk_in(k):
        return pltpu.make_async_copy(
            section_hbm.at[:, planes(k)], section.at[:, planes(k)], in_sems.at[k]
        )

    def chunk_old(k):
        return pltpu.make_async_copy(
            velocity.at[:, planes(k)], field.at[:, planes(k)], old_sems.at[k]
        )

    def chunk_out(k):
        return pltpu.make_async_copy(
            result.at[:, planes(k)], following.at[:, planes(k)], out_sems.at[k]
        )

    def emit(i, c, place, value):
        result[c, i, place[0], place[1]] = value + 0.5 * field[c, i, place[0], place[1]]

    def one(i, west, east):
        advance(i, 0.5, section, west, east, functools.partial(emit, i))

    def step(i, carry):
        one(i, i - 1, i + 1)
        return carry

    token[...] = jnp.zeros_like(token)
    for k in range(chunks):
        chunk_in(k).start()
        chunk_old(k).start()
    chunk_in(0).wait()
    chunk_in(1).wait()
    chunk_old(0).wait()
    one(0, None, 1)
    lax.fori_loop(1, SUB, step, 0)
    chunk_out(0).start()

    def middle(k, carry):
        chunk_in(k + 1).wait()
        chunk_old(k).wait()
        lax.fori_loop(k * SUB, (k + 1) * SUB, step, 0)
        chunk_out(k).start()
        return carry

    lax.fori_loop(1, chunks - 1, middle, 0)
    chunk_old(chunks - 1).wait()
    lax.fori_loop(cells_x - SUB, cells_x - 1, step, 0)
    one(cells_x - 1, cells_x - 2, None)
    chunk_out(chunks - 1).start()
    for k in range(chunks):
        chunk_out(k).wait()


def shifted(x, axis, step, periodic):
    count = lax.axis_size(axis)
    pairs = [(i, (i + step) % count) for i in range(count)]
    if not periodic:
        pairs = [(s, t) for s, t in pairs if t - s == step]
    return lax.ppermute(x, axis, pairs)


def exchange(pack_low, pack_high, edge_west, edge_east):
    got_low = shifted(pack_high, "gy", 1, True)
    got_high = shifted(pack_low, "gy", -1, True)
    ghost_low = shifted(edge_east, "gx", 1, False)
    ghost_high = shifted(edge_west, "gx", -1, False)
    return ghost_low, ghost_high, got_low, got_high


def local(velocity, inflow, positions, tiles, coefs, counts):
    f32, i32 = jnp.float32, jnp.int32
    whole = velocity.shape
    _, cells_x, cells_y, depth = whole
    groups_y = lax.axis_size("gy")
    positions = positions[0].transpose(1, 0, 2)
    tiles, coefs = tiles[0].T, coefs[0]
    records, points = coefs.shape
    share = records // groups_y
    chunks = cells_x // SUB
    size = 4 * math.prod(whole)
    held = pltpu.VMEM(whole, f32)
    stored = pltpu.HBM(whole, f32)
    array = jax.ShapeDtypeStruct
    pack = array((3 * cells_x + 3 * records, 1, points), f32)
    edge = array((3, cells_y, depth), f32)
    per_record = array((records, 1, points), i32)
    chunk_sems = pltpu.SemaphoreType.DMA((chunks,))

    field, *own_a, point_y, point_z, strength, plan = pl.pallas_call(
        load_sample,
        out_shape=(
            held, pack, pack, edge, edge, per_record, per_record,
            array((records, 1, points), f32),
            array((1 + 2 * records,), i32),
        ),
        in_specs=[ANYWHERE] * 4 + [SCALAR],
        out_specs=(WHOLE,) * 8 + (SCALAR,),
        scratch_shapes=[
            pltpu.SMEM((records, LANES), i32),
            pltpu.SMEM((2, records), i32),
            pltpu.VMEM((2, records, points), i32),
            pltpu.VMEM((records, points), f32),
            pltpu.SMEM((chunks, records), i32),
            pltpu.SMEM((chunks,), i32),
            pltpu.SemaphoreType.DMA((4,)),
            chunk_sems,
        ],
        compiler_params=params(),
        cost_estimate=cost(2 * 10**9, 4 * size),
        name="load_sample",
    )(streamed(velocity), streamed(positions), streamed(tiles), streamed(coefs), counts)
    points_of = (plan, point_y, point_z, strength)
    ghosts_a = exchange(*own_a)

    section = pl.pallas_call(
        advance_first,
        out_shape=held,
        in_specs=[WHOLE],
        out_specs=WHOLE,
        compiler_params=params(),
        cost_estimate=cost(10**9, 4 * size),
        name="advance_first",
    )(resident(field))

    _, section, *own_b, shares = pl.pallas_call(
        spread_sample,
        out_shape=(
            held, stored, pack, pack, edge, edge,
            array((groups_y, 2, 3 * share, 1, points), f32),
        ),
        in_specs=[WHOLE] * 10 + [SCALAR] + [WHOLE] * 3,
        out_specs=(WHOLE, ANYWHERE) + (WHOLE,) * 5,
        input_output_aliases={0: 0},
        scratch_shapes=[pltpu.SemaphoreType.DMA],
        compiler_params=params(),
        cost_estimate=cost(2 * 10**9, 4 * size),
        name="spread_sample",
    )(
        resident(section), inflow, *ghosts_a[:2], *own_a, *ghosts_a[2:], *points_of,
    )
    shares = lax.all_to_all(shares, "gy", 0, 0)
    ghosts_b = exchange(*own_b)

    following, token = pl.pallas_call(
        advance_second,
        out_shape=(stored, array((SUB, LANES), f32)),
        in_specs=[ANYWHERE] * 2,
        out_specs=(ANYWHERE, WHOLE),
        scratch_shapes=[pltpu.VMEM(whole, f32)] * 3 + [chunk_sems] * 3,
        compiler_params=params(VMEM_LIMIT + 3 * size),
        cost_estimate=cost(10**9, 4 * size),
        name="advance_second",
    )(streamed(section), streamed(velocity))

    forces = pl.pallas_call(
        share_force,
        out_shape=array((groups_y, 3 * share, 1, points), f32),
        in_specs=[WHOLE, WHOLE, SCALAR] + [ANYWHERE] * 3,
        out_specs=WHOLE,
        compiler_params=params(),
        cost_estimate=cost(10**6, 10**6),
        name="share_force",
    )(shares, strength, counts, token, *ghosts_b[:2])
    all_forces = lax.all_to_all(forces, "gy", 0, 0)

    velocity_next = pl.pallas_call(
        spread_next,
        out_shape=stored,
        in_specs=[ANYWHERE] + [WHOLE] * 9 + [SCALAR] + [WHOLE] * 3 + [ANYWHERE],
        out_specs=ANYWHERE,
        scratch_shapes=[pltpu.VMEM(whole, f32)] + [chunk_sems] * 2,
        compiler_params=params(VMEM_LIMIT + size),
        cost_estimate=cost(2 * 10**9, 4 * size),
        name="spread_next",
    )(
        streamed(following), inflow, *ghosts_b[:2], *own_b, *ghosts_b[2:], *points_of, forces,
    )
    return (velocity_next, all_forces.reshape(1, records, 3, points))


def solution(mesh):
    return jax.shard_map(
        local,
        mesh=mesh,
        in_specs=(
            P(None, "gx", "gy", None),
            P(None, "gy", None),
            P("gx", None, None, None),
            P("gx", None, None),
            P("gx", None, None),
            P("gx"),
        ),
        out_specs=(P(None, "gx", "gy", None), P("gx", None, None, None)),
        check_vma=False,
    )
```

```python
import functools
import math

import jax
import jax.numpy as jnp
from jax import lax
from jax.experimental import pallas as pl
from jax.experimental.pallas import tpu as pltpu
from jax.sharding import PartitionSpec as P

RAD = 2
VISCOSITY = 0.05
TIME_STEP = 0.1
WIDTH_EPS = 1.5
ROOT_PI = 1.7724538509055159
TAP = [math.exp(-((d / WIDTH_EPS) ** 2)) / (WIDTH_EPS * ROOT_PI) for d in range(RAD + 1)]
HIGH = [float(jnp.bfloat16(tap)) for tap in TAP]
LOW = [float(jnp.bfloat16(tap - high)) for tap, high in zip(TAP, HIGH)]
LANES = 128
SUB = 8
PACKED = 16
VMEM_LIMIT = 14 * 2**20

WHOLE = pl.BlockSpec(memory_space=pltpu.VMEM)
SCALAR = pl.BlockSpec(memory_space=pltpu.SMEM)
ANYWHERE = pl.BlockSpec(memory_space=pl.ANY)


def params(limit=VMEM_LIMIT):
    return pltpu.CompilerParams(vmem_limit_bytes=limit)


def cost(flops, nbytes):
    return pl.CostEstimate(flops=flops, bytes_accessed=nbytes, transcendentals=0)


def resident(x):
    return pltpu.with_memory_space_constraint(x, pltpu.VMEM)


def streamed(x):
    return pltpu.with_memory_space_constraint(x, pltpu.HBM)


def split(x):
    high = x.astype(jnp.bfloat16)
    low = (x - high.astype(jnp.float32)).astype(jnp.bfloat16)
    return jnp.concatenate([high, low], axis=0)


def along_z(point_z, depth):
    points = point_z.shape[-1]
    row = lax.broadcasted_iota(jnp.int32, (PACKED, points), 0).astype(jnp.bfloat16)
    place = jnp.broadcast_to(point_z.astype(jnp.float32), (PACKED, points)).astype(jnp.bfloat16)
    zero = jnp.zeros_like(row)
    high, low = [], []
    for k in range(0, depth, PACKED):
        dist = jnp.abs(row - (place - float(k)))
        near = [dist == float(d) for d in range(RAD + 1)]
        for taps, out in ((HIGH, high), (LOW, low)):
            value = zero
            for d in range(RAD, -1, -1):
                value = jnp.where(near[d], jnp.full_like(row, taps[d]), value)
            out.append(value)
    return jnp.concatenate(high, axis=0), jnp.concatenate(low, axis=0)


def wrapped(point_y, base, total_y):
    near = point_y - base
    near = jnp.where(near > total_y // 2, near - total_y, near)
    return jnp.where(near < -(total_y // 2), near + total_y, near)


def along_y(point_y, base, cells_y, total_y):
    near = wrapped(point_y, base, total_y)
    dist = jnp.abs(lax.broadcasted_iota(jnp.int32, (cells_y, point_y.shape[-1]), 0) - near)
    return jnp.where(
        dist == 0, TAP[0], jnp.where(dist == 1, TAP[1], jnp.where(dist == 2, TAP[2], 0.0))
    )


def make_plan(hubs, tiles, touch, counts, start, plan, bucket, held):
    tile_y, groups_y = lax.axis_index("gy"), lax.axis_size("gy")
    records, chunks = tiles.shape[1], held.shape[0]
    for k in range(chunks):
        held[k] = 0

    def place(r, carry):
        offset = tile_y - tiles[0, r]
        offset = jnp.where(offset < 0, offset + groups_y, offset)

        @pl.when(jnp.logical_and(offset < tiles[1, r], touch[r, 0] > 0))
        def _():
            k = (hubs[r, 0] - start + RAD) // SUB
            bucket[k, held[k]] = r
            held[k] = held[k] + 1

        return carry

    lax.fori_loop(0, jnp.minimum(counts[0], records), place, 0)

    def flatten(k, found):
        def move(j, found):
            r = bucket[k, j]
            plan[1 + found] = r
            plan[1 + records + found] = hubs[r, 0] - start
            return found + 1

        return lax.fori_loop(0, held[k], move, found)

    plan[0] = lax.fori_loop(0, chunks, flatten, jnp.int32(0))


def pair(plan, t):
    records = (plan.shape[0] - 1) // 2
    first = 2 * t
    second = jnp.minimum(first + 1, plan[0] - 1)
    return [(n, plan[1 + n], plan[1 + records + n]) for n in (first, second)], second > first


def sampled_rows(field, weight_y, weight_z, picks):
    cells_y = field.shape[2]
    rows = 3 * cells_y
    parts = []
    for t, r, hub in picks:
        planes = []
        for c in range(3):
            plane = TAP[0] * field[c, hub]
            plane += TAP[1] * (field[c, hub - 1] + field[c, hub + 1])
            plane += TAP[2] * (field[c, hub - 2] + field[c, hub + 2])
            planes.append(plane)
        parts.append(split(jnp.concatenate(planes, axis=0)))
    out = []
    for (t, r, hub), part in zip(picks, parts):
        picked = jnp.dot(part, weight_z[t, 0], preferred_element_type=jnp.float32)
        rest = jnp.dot(part[:rows], weight_z[t, 1], preferred_element_type=jnp.float32)
        picked = picked[:rows] + (picked[rows:] + rest)
        weight = weight_y[t]
        out.append(
            [
                jnp.sum(picked[c * cells_y : (c + 1) * cells_y] * weight, axis=0, keepdims=True)
                for c in range(3)
            ]
        )
    return out


def pack_edges(field, edge_west, edge_east, pack_low, pack_high):
    cells_x, cells_y, depth = field.shape[1:]
    for c in range(3):
        edge_west[c] = field[c, 0]
        edge_east[c] = field[c, cells_x - 1]

    def step(t, carry):
        for c in range(3):
            for k in range(SUB):
                i = t * SUB + k
                pack_low[c * cells_x + i] = field[c, i, pl.ds(0, 1), :]
                pack_high[c * cells_x + i] = field[c, i, pl.ds(cells_y - 1, 1), :]
        return carry

    lax.fori_loop(0, cells_x // SUB, step, 0)


def load_sample(
    velocity, positions, tiles_hbm, coefs_hbm, counts,
    field, pack_low, pack_high, edge_west, edge_east, weight_y, weight_z, strength, plan,
    point_y, point_z, hubs, tiles, places, coefs, flags, touch, bucket, held, small_sems, touch_sem, sems,
):
    cells_x, cells_y, depth = field.shape[1:]
    records, points = coefs.shape
    chunks = cells_x // SUB
    first_row = 3 * cells_x
    start = lax.axis_index("gx") * cells_x

    def chunk(k):
        planes = pl.ds(k * SUB, SUB)
        return pltpu.make_async_copy(velocity.at[:, planes], field.at[:, planes], sems.at[k])

    small = [
        (positions.at[pl.ds(1, 2)], places),
        (positions.at[0, :, pl.ds(0, LANES)], hubs),
        (tiles_hbm, tiles),
        (coefs_hbm, coefs),
    ]
    small = [
        pltpu.make_async_copy(source, target, small_sems.at[n])
        for n, (source, target) in enumerate(small)
    ]
    total_y = cells_y * lax.axis_size("gy")
    base = lax.axis_index("gy") * cells_y
    for copy in small:
        copy.start()
    for k in range(chunks):
        chunk(k).start()
    small[0].wait()
    near = wrapped(places[0], base, total_y)
    inside = jnp.logical_and(near >= -RAD, near < cells_y + RAD)
    inside = jnp.max(jnp.where(inside, 1.0, 0.0), axis=1, keepdims=True)
    flags[...] = jnp.broadcast_to(inside, flags.shape).astype(jnp.int32)
    touch_copy = pltpu.make_async_copy(flags, touch, touch_sem)
    touch_copy.start()

    def clear(n, carry):
        for k in range(SUB):
            pack_low[first_row + n * SUB + k] = jnp.zeros((1, points), jnp.float32)
            pack_high[first_row + n * SUB + k] = jnp.zeros((1, points), jnp.float32)
        return carry

    lax.fori_loop(0, 3 * records // SUB, clear, 0)
    for copy in small[1:]:
        copy.wait()
    for r in range(records):
        point_y[r] = places[0, pl.ds(r, 1), :]
        point_z[r] = places[1, pl.ds(r, 1), :]
        strength[r] = coefs[pl.ds(r, 1), :]
    touch_copy.wait()
    make_plan(hubs, tiles, touch, counts, start, plan, bucket, held)

    def weigh(t, carry):
        r = plan[1 + t]
        weight_y[t] = along_y(point_y[r], base, cells_y, total_y)
        weight_z[t, 0], weight_z[t, 1] = along_z(point_z[r], depth)
        return carry

    lax.fori_loop(0, plan[0], weigh, 0)

    def wait_to(ready, wanted):
        def step(k, carry):
            chunk(k).wait()
            return carry

        lax.fori_loop(ready, wanted, step, 0)
        return jnp.maximum(ready, wanted)

    def step(t, ready):
        picks, _ = pair(plan, t)
        ready = wait_to(ready, (picks[1][2] + RAD) // SUB + 1)
        for (_, r, _), rows in zip(picks, sampled_rows(field, weight_y, weight_z, picks)):
            for c in range(3):
                pack_low[first_row + 3 * r + c] = rows[c]
                pack_high[first_row + 3 * r + c] = rows[c]
        return ready

    ready = lax.fori_loop(0, (plan[0] + 1) // 2, step, jnp.int32(0))
    wait_to(ready, chunks)
    pack_edges(field, edge_west, edge_east, pack_low, pack_high)


def fix_west(factor, target, own, inflow, ghost):
    first = lax.axis_index("gx") == 0
    for c in range(3):
        west = jnp.where(first, inflow[c], ghost[c])
        coef = factor * TIME_STEP * VISCOSITY + (0.5 * factor * TIME_STEP) * own[0]
        target[c, 0] = target[c, 0] + west * coef


def fix_east(factor, target, own, ghost):
    last = lax.axis_index("gx") == lax.axis_size("gx") - 1
    end = target.shape[1] - 1
    for c in range(3):
        east = jnp.where(last, own[c], ghost[c])
        coef = factor * TIME_STEP * VISCOSITY - (0.5 * factor * TIME_STEP) * own[0]
        target[c, end] = target[c, end] + east * coef


def fix_rows(factor, target, own_low, own_high, got_low, got_high, t):
    cells_x, cells_y = target.shape[1:3]
    spread = factor * TIME_STEP * VISCOSITY
    half = 0.5 * factor * TIME_STEP
    low, high = pl.ds(0, 1), pl.ds(cells_y - 1, 1)
    for k in range(SUB):
        i = t * SUB + k
        south = spread + half * own_low[cells_x + i]
        north = spread - half * own_high[cells_x + i]
        for c in range(3):
            n = c * cells_x + i
            target[c, i, low, :] = target[c, i, low, :] + got_low[n] * south
            target[c, i, high, :] = target[c, i, high, :] + got_high[n] * north


def slabs_of(weight_y, weight_z, strength, own, low, high, cells, scales, picks):
    cells_x, cells_y, depth = cells
    count = 3 * cells_y
    across = (((1,), (1,)), ((), ()))
    spread = []
    for (t, r, hub), scale in zip(picks, scales):
        rows = [3 * cells_x + 3 * r + c for c in range(3)]
        total = [own[n] + (low[n] + high[n]) for n in rows]
        speed = jnp.sqrt(total[0] * total[0] + total[1] * total[1] + total[2] * total[2])
        pull = strength[r] * (-scale) * speed
        weight = weight_y[t]
        spread.append(split(jnp.concatenate([weight * (pull * x) for x in total], axis=0)))
    slabs = []
    for (t, r, hub), part in zip(picks, spread):
        slab = lax.dot_general(part, weight_z[t, 0], across, preferred_element_type=jnp.float32)
        rest = lax.dot_general(
            part[:count], weight_z[t, 1], across, preferred_element_type=jnp.float32
        )
        slabs.append(slab[:count] + (slab[count:] + rest))
    return slabs


def add_slab(field, slab, hub):
    cells_y = field.shape[2]
    for c in range(3):
        part = slab[c * cells_y : (c + 1) * cells_y]
        terms = [tap * part for tap in TAP]
        for d in range(-RAD, RAD + 1):
            field[c, hub + d] = field[c, hub + d] + terms[abs(d)]


def spread_pair(t, scale, field, plan, points, own, low, high):
    picks, both = pair(plan, t)
    scales = [scale, jnp.where(both, scale, 0.0)]
    slabs = slabs_of(*points, own, low, high, field.shape[1:], scales, picks)
    for (_, _, hub), slab in zip(picks, slabs):
        add_slab(field, slab, hub)


def spread_sample(
    section_in, inflow, ghost_low, ghost_high, own_low, own_high, own_west, own_east, got_low, got_high,
    plan, weight_y, weight_z, strength,
    section, section_out, pack_low, pack_high, edge_west, edge_east, share_out, sem,
):
    cells_x = section.shape[1]
    records = strength.shape[0]
    share = share_out.shape[2] // 3
    first_row = 3 * cells_x

    def fix_step(t, carry):
        fix_rows(1.0, section, own_low, own_high, got_low, got_high, t)
        return carry

    fix_west(1.0, section, own_west, inflow, ghost_low)
    fix_east(1.0, section, own_east, ghost_high)
    lax.fori_loop(0, cells_x // SUB, fix_step, 0)

    def spread_step(t, carry):
        points = (weight_y, weight_z, strength)
        spread_pair(t, TIME_STEP, section, plan, points, own_low, got_low, got_high)
        return carry

    lax.fori_loop(0, (plan[0] + 1) // 2, spread_step, 0)
    copy = pltpu.make_async_copy(section, section_out, sem)
    copy.start()
    pack_edges(section, edge_west, edge_east, pack_low, pack_high)

    def clear(r, carry):
        zero = jnp.zeros_like(own_low[0])
        for c in range(3):
            pack_low[first_row + 3 * r + c] = zero
            pack_high[first_row + 3 * r + c] = zero
            share_out[r // share, 0, 3 * (r % share) + c] = own_low[first_row + 3 * r + c]
            share_out[r // share, 1, 3 * (r % share) + c] = zero
        return carry

    lax.fori_loop(0, records, clear, 0)

    def sample_step(t, carry):
        picks, _ = pair(plan, t)
        for (_, r, _), rows in zip(picks, sampled_rows(section, weight_y, weight_z, picks)):
            for c in range(3):
                pack_low[first_row + 3 * r + c] = rows[c]
                pack_high[first_row + 3 * r + c] = rows[c]
                share_out[r // share, 1, 3 * (r % share) + c] = rows[c]
        return carry

    lax.fori_loop(0, (plan[0] + 1) // 2, sample_step, 0)
    copy.wait()


def share_force(parts, strength, counts, after, after_low, after_high, result):
    groups, _, rows = parts.shape[:3]
    share = rows // 3
    mine = lax.axis_index("gy") * share
    for s in range(share):
        live = mine + s < counts[0]
        pull = jnp.where(live, -0.5 * strength[mine + s], 0.0)
        total = [0.0, 0.0, 0.0]
        for stage in range(2):
            value = []
            for c in range(3):
                n = 3 * s + c
                x = parts[0, stage, n]
                for g in range(1, groups):
                    x += parts[g, stage, n]
                value.append(x)
            speed = jnp.sqrt(value[0] * value[0] + value[1] * value[1] + value[2] * value[2])
            total = [acc + speed * x for acc, x in zip(total, value)]
        for c in range(3):
            for g in range(groups):
                result[g, 3 * s + c] = pull * total[c]


def spread_next(
    following, inflow, ghost_low, ghost_high, own_low, own_high, own_west, own_east, got_low, got_high,
    plan, stored_y, stored_z, strength, after,
    result, field, weight_y, weight_z, in_sems, out_sems, sem_y, sem_z,
):
    chunks = field.shape[1] // SUB
    factor = 0.5

    def chunk_in(k):
        planes = pl.ds(k * SUB, SUB)
        return pltpu.make_async_copy(following.at[:, planes], field.at[:, planes], in_sems.at[k])

    def chunk_out(k):
        planes = pl.ds(k * SUB, SUB)
        return pltpu.make_async_copy(field.at[:, planes], result.at[:, planes], out_sems.at[k])

    def wait_to(ready, wanted):
        def step(k, carry):
            chunk_in(k).wait()
            fix_rows(factor, field, own_low, own_high, got_low, got_high, k)

            @pl.when(k == 0)
            def _():
                fix_west(factor, field, own_west, inflow, ghost_low)

            @pl.when(k == chunks - 1)
            def _():
                fix_east(factor, field, own_east, ghost_high)

            return carry

        lax.fori_loop(ready, wanted, step, 0)
        return jnp.maximum(ready, wanted)

    def send_to(sent, done):
        def step(k, carry):
            chunk_out(k).start()
            return carry

        lax.fori_loop(sent, done, step, 0)
        return jnp.maximum(sent, done)

    def weights(t):
        return (
            pltpu.make_async_copy(stored_y.at[t], weight_y.at[t], sem_y.at[t]),
            pltpu.make_async_copy(stored_z.at[t], weight_z.at[t], sem_z.at[t]),
        )

    def start_weights(t, carry):
        for copy in weights(t):
            copy.start()
        return carry

    found = plan[0]
    for k in range(chunks):
        chunk_in(k).start()
        lax.fori_loop(k * found // chunks, (k + 1) * found // chunks, start_weights, 0)

    def step(t, carry):
        ready, sent = carry
        picks, both = pair(plan, t)
        for copy in weights(picks[0][0]):
            copy.wait()

        @pl.when(both)
        def _():
            for copy in weights(picks[1][0]):
                copy.wait()

        ready = wait_to(ready, (picks[1][2] + RAD) // SUB + 1)
        sent = send_to(sent, (picks[0][2] + RAD) // SUB - 1)
        points = (weight_y, weight_z, strength)
        spread_pair(t, factor * TIME_STEP, field, plan, points, own_low, got_low, got_high)
        return ready, sent

    zero = jnp.int32(0)
    ready, sent = lax.fori_loop(0, (plan[0] + 1) // 2, step, (zero, zero))
    sent = send_to(sent, ready)

    def finish(k, carry):
        wait_to(k, k + 1)
        chunk_out(k).start()
        return carry

    lax.fori_loop(ready, chunks, finish, 0)
    for k in range(chunks):
        chunk_out(k).wait()


def advance(i, factor, field, west, east, emit):
    cells_y, depth = field.shape[2:]
    groups, halves = cells_y // SUB, depth // LANES
    row = lax.broadcasted_iota(jnp.int32, (SUB, LANES), 0)
    lane = lax.broadcasted_iota(jnp.int32, (SUB, LANES), 1)
    first_row, last_row = row == 0, row == SUB - 1
    first_lane, last_lane = lane == 0, lane == LANES - 1
    spread = factor * TIME_STEP * VISCOSITY
    centre = factor * (1.0 - 6.0 * TIME_STEP * VISCOSITY)
    zero = jnp.zeros((SUB, LANES), jnp.float32)

    loaded = {}

    def at(c, g, h):
        if not (0 <= g < groups and 0 <= h < halves):
            return zero
        if (c, g, h) not in loaded:
            loaded[c, g, h] = field[c, i, pl.ds(g * SUB, SUB), pl.ds(h * LANES, LANES)]
        return loaded[c, g, h]

    for g in range(groups):
        for h in range(halves):
            place = (pl.ds(g * SUB, SUB), pl.ds(h * LANES, LANES))
            q = [at(c, g, h) for c in range(3)]
            speeds = [(0.5 * factor * TIME_STEP) * x for x in q]
            less = [spread - s for s in speeds]
            more = [spread + s for s in speeds]
            for c in range(3):
                x = q[c]
                above = pltpu.roll(jnp.where(first_row, at(c, g + 1, h), x), SUB - 1, 0)
                below = pltpu.roll(jnp.where(last_row, at(c, g - 1, h), x), 1, 0)
                upper = pltpu.roll(jnp.where(first_lane, at(c, g, h + 1), x), LANES - 1, 1)
                lower = pltpu.roll(jnp.where(last_lane, at(c, g, h - 1), x), 1, 1)
                total = centre * x
                if east is not None:
                    total += field[c, east, place[0], place[1]] * less[0]
                if west is not None:
                    total += field[c, west, place[0], place[1]] * more[0]
                total += above * less[1] + below * more[1]
                total += upper * less[2] + lower * more[2]
                emit(c, place, total)


def advance_all(factor, field, emit):
    last = field.shape[1] - 1

    def one(i, west, east):
        advance(i, factor, field, west, east, functools.partial(emit, i))

    def step(i, carry):
        one(i, i - 1, i + 1)
        return carry

    one(0, None, 1)
    lax.fori_loop(1, last, step, 0)
    one(last, last - 1, None)


def advance_first(field, plan, weight_y, weight_z, section, stored_y, stored_z, sem_y, sem_z):
    def emit(i, c, place, value):
        section[c, i, place[0], place[1]] = value

    def copies(t):
        return (
            pltpu.make_async_copy(weight_y.at[t], stored_y.at[t], sem_y.at[t]),
            pltpu.make_async_copy(weight_z.at[t], stored_z.at[t], sem_z.at[t]),
        )

    def start(t, carry):
        for copy in copies(t):
            copy.start()
        return carry

    def wait(t, carry):
        for copy in copies(t):
            copy.wait()
        return carry

    lax.fori_loop(0, plan[0], start, 0)
    advance_all(1.0, field, emit)
    lax.fori_loop(0, plan[0], wait, 0)


def advance_second(
    section_hbm, velocity, following, token, section, field, result, in_sems, old_sems, out_sems
):
    cells_x = section.shape[1]
    chunks = cells_x // SUB

    def planes(k):
        return pl.ds(k * SUB, SUB)

    def chunk_in(k):
        return pltpu.make_async_copy(
            section_hbm.at[:, planes(k)], section.at[:, planes(k)], in_sems.at[k]
        )

    def chunk_old(k):
        return pltpu.make_async_copy(
            velocity.at[:, planes(k)], field.at[:, planes(k)], old_sems.at[k]
        )

    def chunk_out(k):
        return pltpu.make_async_copy(
            result.at[:, planes(k)], following.at[:, planes(k)], out_sems.at[k]
        )

    def emit(i, c, place, value):
        result[c, i, place[0], place[1]] = value + 0.5 * field[c, i, place[0], place[1]]

    def one(i, west, east):
        advance(i, 0.5, section, west, east, functools.partial(emit, i))

    def step(i, carry):
        one(i, i - 1, i + 1)
        return carry

    token[...] = jnp.zeros_like(token)
    for k in range(chunks):
        chunk_in(k).start()
        chunk_old(k).start()
    chunk_in(0).wait()
    chunk_in(1).wait()
    chunk_old(0).wait()
    one(0, None, 1)
    lax.fori_loop(1, SUB, step, 0)
    chunk_out(0).start()

    def middle(k, carry):
        chunk_in(k + 1).wait()
        chunk_old(k).wait()
        lax.fori_loop(k * SUB, (k + 1) * SUB, step, 0)
        chunk_out(k).start()
        return carry

    lax.fori_loop(1, chunks - 1, middle, 0)
    chunk_old(chunks - 1).wait()
    lax.fori_loop(cells_x - SUB, cells_x - 1, step, 0)
    one(cells_x - 1, cells_x - 2, None)
    chunk_out(chunks - 1).start()
    for k in range(chunks):
        chunk_out(k).wait()


def shifted(x, axis, step, periodic):
    count = lax.axis_size(axis)
    pairs = [(i, (i + step) % count) for i in range(count)]
    if not periodic:
        pairs = [(s, t) for s, t in pairs if t - s == step]
    return lax.ppermute(x, axis, pairs)


def exchange(pack_low, pack_high, edge_west, edge_east):
    got_low = shifted(pack_high, "gy", 1, True)
    got_high = shifted(pack_low, "gy", -1, True)
    ghost_low = shifted(edge_east, "gx", 1, False)
    ghost_high = shifted(edge_west, "gx", -1, False)
    return ghost_low, ghost_high, got_low, got_high


def local(velocity, inflow, positions, tiles, coefs, counts):
    f32, i32 = jnp.float32, jnp.int32
    whole = velocity.shape
    _, cells_x, cells_y, depth = whole
    groups_y = lax.axis_size("gy")
    positions = positions[0].transpose(1, 0, 2)
    tiles, coefs = tiles[0].T, coefs[0]
    records, points = coefs.shape
    share = records // groups_y
    chunks = cells_x // SUB
    size = 4 * math.prod(whole)
    held = pltpu.VMEM(whole, f32)
    stored = pltpu.HBM(whole, f32)
    array = jax.ShapeDtypeStruct
    pack = array((3 * cells_x + 3 * records, 1, points), f32)
    edge = array((3, cells_y, depth), f32)
    per_record = (records, 1, points)
    y_shape, z_shape = (records, cells_y, points), (records, 2, depth, points)
    y_bytes, z_bytes = 4 * math.prod(y_shape), 2 * math.prod(z_shape)
    record_sems = pltpu.SemaphoreType.DMA((records,))
    chunk_sems = pltpu.SemaphoreType.DMA((chunks,))

    field, *own_a, weight_y, weight_z, strength, plan = pl.pallas_call(
        load_sample,
        out_shape=(
            held, pack, pack, edge, edge,
            pltpu.VMEM(y_shape, f32), pltpu.VMEM(z_shape, jnp.bfloat16),
            array(per_record, f32),
            array((1 + 2 * records,), i32),
        ),
        in_specs=[ANYWHERE] * 4 + [SCALAR],
        out_specs=(WHOLE,) * 8 + (SCALAR,),
        scratch_shapes=[
            pltpu.VMEM(per_record, i32),
            pltpu.VMEM(per_record, i32),
            pltpu.SMEM((records, LANES), i32),
            pltpu.SMEM((2, records), i32),
            pltpu.VMEM((2, records, points), i32),
            pltpu.VMEM((records, points), f32),
            pltpu.VMEM((records, LANES), i32),
            pltpu.SMEM((records, LANES), i32),
            pltpu.SMEM((chunks, records), i32),
            pltpu.SMEM((chunks,), i32),
            pltpu.SemaphoreType.DMA((4,)),
            pltpu.SemaphoreType.DMA,
            chunk_sems,
        ],
        compiler_params=params(),
        cost_estimate=cost(2 * 10**9, 4 * size),
        name="load_sample",
    )(streamed(velocity), streamed(positions), streamed(tiles), streamed(coefs), counts)
    weight_y, weight_z = resident(weight_y), resident(weight_z)
    ghosts_a = exchange(*own_a)

    section, stored_y, stored_z = pl.pallas_call(
        advance_first,
        out_shape=(held, pltpu.HBM(y_shape, f32), pltpu.HBM(z_shape, jnp.bfloat16)),
        in_specs=[WHOLE, SCALAR, WHOLE, WHOLE],
        out_specs=(WHOLE, ANYWHERE, ANYWHERE),
        scratch_shapes=[record_sems] * 2,
        compiler_params=params(),
        cost_estimate=cost(10**9, 4 * size),
        name="advance_first",
    )(resident(field), plan, weight_y, weight_z)

    _, section, *own_b, shares = pl.pallas_call(
        spread_sample,
        out_shape=(
            held, stored, pack, pack, edge, edge,
            array((groups_y, 2, 3 * share, 1, points), f32),
        ),
        in_specs=[WHOLE] * 10 + [SCALAR] + [WHOLE] * 3,
        out_specs=(WHOLE, ANYWHERE) + (WHOLE,) * 5,
        input_output_aliases={0: 0},
        scratch_shapes=[pltpu.SemaphoreType.DMA],
        compiler_params=params(),
        cost_estimate=cost(2 * 10**9, 4 * size),
        name="spread_sample",
    )(
        resident(section), inflow, *ghosts_a[:2], *own_a, *ghosts_a[2:],
        plan, weight_y, weight_z, strength,
    )
    shares = lax.all_to_all(shares, "gy", 0, 0)
    ghosts_b = exchange(*own_b)

    following, token = pl.pallas_call(
        advance_second,
        out_shape=(stored, array((SUB, LANES), f32)),
        in_specs=[ANYWHERE] * 2,
        out_specs=(ANYWHERE, WHOLE),
        scratch_shapes=[pltpu.VMEM(whole, f32)] * 3 + [chunk_sems] * 3,
        compiler_params=params(VMEM_LIMIT + 3 * size),
        cost_estimate=cost(10**9, 4 * size),
        name="advance_second",
    )(streamed(section), streamed(velocity))

    forces = pl.pallas_call(
        share_force,
        out_shape=array((groups_y, 3 * share, 1, points), f32),
        in_specs=[WHOLE, WHOLE, SCALAR] + [ANYWHERE] * 3,
        out_specs=WHOLE,
        compiler_params=params(),
        cost_estimate=cost(10**6, 10**6),
        name="share_force",
    )(shares, strength, counts, token, *ghosts_b[:2])
    all_forces = lax.all_to_all(forces, "gy", 0, 0)

    velocity_next = pl.pallas_call(
        spread_next,
        out_shape=stored,
        in_specs=[ANYWHERE] + [WHOLE] * 9 + [SCALAR, ANYWHERE, ANYWHERE, WHOLE, ANYWHERE],
        out_specs=ANYWHERE,
        scratch_shapes=[
            pltpu.VMEM(whole, f32),
            pltpu.VMEM(y_shape, f32),
            pltpu.VMEM(z_shape, jnp.bfloat16),
            chunk_sems, chunk_sems, record_sems, record_sems,
        ],
        compiler_params=params(VMEM_LIMIT + size + y_bytes + z_bytes),
        cost_estimate=cost(2 * 10**9, 4 * size),
        name="spread_next",
    )(
        streamed(following), inflow, *ghosts_b[:2], *own_b, *ghosts_b[2:],
        plan, streamed(stored_y), streamed(stored_z), strength, forces,
    )
    return (velocity_next, all_forces.reshape(1, records, 3, points))


def solution(mesh):
    return jax.shard_map(
        local,
        mesh=mesh,
        in_specs=(
            P(None, "gx", "gy", None),
            P(None, "gy", None),
            P("gx", None, None, None),
            P("gx", None, None),
            P("gx", None, None),
            P("gx"),
        ),
        out_specs=(P(None, "gx", "gy", None), P("gx", None, None, None)),
        check_vma=False,
    )
```

```python
import functools
import math

import jax
import jax.numpy as jnp
from jax import lax
from jax.experimental import pallas as pl
from jax.experimental.pallas import tpu as pltpu
from jax.sharding import PartitionSpec as P

RAD = 2
VISCOSITY = 0.05
TIME_STEP = 0.1
WIDTH_EPS = 1.5
ROOT_PI = 1.7724538509055159
TAP = [math.exp(-((d / WIDTH_EPS) ** 2)) / (WIDTH_EPS * ROOT_PI) for d in range(RAD + 1)]
HIGH = [float(jnp.bfloat16(tap)) for tap in TAP]
LOW = [float(jnp.bfloat16(tap - high)) for tap, high in zip(TAP, HIGH)]
LANES = 128
SUB = 8
PACKED = 32
VMEM_LIMIT = 5 * 2**20

WHOLE = pl.BlockSpec(memory_space=pltpu.VMEM)
SCALAR = pl.BlockSpec(memory_space=pltpu.SMEM)
ANYWHERE = pl.BlockSpec(memory_space=pl.ANY)


def params(limit=VMEM_LIMIT):
    return pltpu.CompilerParams(vmem_limit_bytes=limit)


def cost(flops, nbytes):
    return pl.CostEstimate(flops=flops, bytes_accessed=nbytes, transcendentals=0)


def resident(x):
    return pltpu.with_memory_space_constraint(x, pltpu.VMEM)


def streamed(x):
    return pltpu.with_memory_space_constraint(x, pltpu.HBM)


def split(x):
    high = x.astype(jnp.bfloat16)
    low = (x - high.astype(jnp.float32)).astype(jnp.bfloat16)
    return jnp.concatenate([high, low], axis=0)


def along_z(point_z, start):
    points = point_z.shape[-1]
    row = lax.broadcasted_iota(jnp.int32, (PACKED, points), 0).astype(jnp.bfloat16)
    place = (point_z - start).astype(jnp.float32)
    place = jnp.broadcast_to(place, (PACKED, points)).astype(jnp.bfloat16)
    dist = jnp.abs(row - place)
    near = [dist == float(d) for d in range(RAD + 1)]
    out = []
    for taps in (HIGH, LOW):
        value = jnp.zeros_like(row)
        for d in range(RAD, -1, -1):
            value = jnp.where(near[d], jnp.full_like(row, taps[d]), value)
        out.append(value)
    return out


def wrapped(point_y, base, total_y):
    near = point_y - base
    near = jnp.where(near > total_y // 2, near - total_y, near)
    return jnp.where(near < -(total_y // 2), near + total_y, near)


def along_y(point_y, base, cells_y, total_y):
    near = wrapped(point_y, base, total_y)
    dist = jnp.abs(lax.broadcasted_iota(jnp.int32, (cells_y, point_y.shape[-1]), 0) - near)
    return jnp.where(
        dist == 0, TAP[0], jnp.where(dist == 1, TAP[1], jnp.where(dist == 2, TAP[2], 0.0))
    )


def make_plan(hubs, tiles, touch, counts, start, plan, bucket, held):
    tile_y, groups_y = lax.axis_index("gy"), lax.axis_size("gy")
    records, chunks = tiles.shape[1], held.shape[0]
    for k in range(chunks):
        held[k] = 0

    def place(r, carry):
        offset = tile_y - tiles[0, r]
        offset = jnp.where(offset < 0, offset + groups_y, offset)

        @pl.when(jnp.logical_and(offset < tiles[1, r], touch[r, 1] >= 0))
        def _():
            k = (hubs[r, 0] - start + RAD) // SUB
            bucket[k, held[k]] = r
            held[k] = held[k] + 1

        return carry

    lax.fori_loop(0, jnp.minimum(counts[0], records), place, 0)

    def flatten(k, found):
        def move(j, found):
            r = bucket[k, j]
            plan[1 + found] = r
            plan[1 + records + found] = hubs[r, 0] - start
            return found + 1

        return lax.fori_loop(0, held[k], move, found)

    plan[0] = lax.fori_loop(0, chunks, flatten, jnp.int32(0))


def pair(plan, t):
    records = (plan.shape[0] - 1) // 2
    first = 2 * t
    second = jnp.minimum(first + 1, plan[0] - 1)
    return [(n, plan[1 + n], plan[1 + records + n]) for n in (first, second)], second > first


def sampled_rows(field, weight_y, weight_z, picks):
    cells_y = field.shape[2]
    rows = 3 * cells_y
    parts = []
    for t, r, hub in picks:
        planes = []
        for c in range(3):
            plane = TAP[0] * field[c, hub]
            plane += TAP[1] * (field[c, hub - 1] + field[c, hub + 1])
            plane += TAP[2] * (field[c, hub - 2] + field[c, hub + 2])
            planes.append(plane)
        parts.append(split(jnp.concatenate(planes, axis=0)))
    out = []
    for (t, r, hub), part in zip(picks, parts):
        picked = jnp.dot(part, weight_z[t, 0], preferred_element_type=jnp.float32)
        rest = jnp.dot(part[:rows], weight_z[t, 1], preferred_element_type=jnp.float32)
        picked = picked[:rows] + (picked[rows:] + rest)
        weight = weight_y[t]
        out.append(
            [
                jnp.sum(picked[c * cells_y : (c + 1) * cells_y] * weight, axis=0, keepdims=True)
                for c in range(3)
            ]
        )
    return out


def pack_edges(field, edge_west, edge_east, pack_low, pack_high):
    cells_x, cells_y, depth = field.shape[1:]
    for c in range(3):
        edge_west[c] = field[c, 0]
        edge_east[c] = field[c, cells_x - 1]

    def step(t, carry):
        for c in range(3):
            for k in range(SUB):
                i = t * SUB + k
                pack_low[c * cells_x + i] = field[c, i, pl.ds(0, 1), :]
                pack_high[c * cells_x + i] = field[c, i, pl.ds(cells_y - 1, 1), :]
        return carry

    lax.fori_loop(0, cells_x // SUB, step, 0)


def load_sample(
    velocity, positions, tiles_hbm, coefs_hbm, counts,
    field, pack_low, pack_high, edge_west, edge_east, weight_y, weight_z, strength, plan,
    point_y, point_z, hubs, tiles, places, coefs, flags, touch, bucket, held, small_sems, touch_sem, sems,
):
    cells_x, cells_y, depth = field.shape[1:]
    records, points = coefs.shape
    chunks = cells_x // SUB
    first_row = 3 * cells_x
    start = lax.axis_index("gx") * cells_x

    def chunk(k):
        planes = pl.ds(k * SUB, SUB)
        return pltpu.make_async_copy(velocity.at[:, planes], field.at[:, planes], sems.at[k])

    small = [
        (positions.at[pl.ds(1, 2)], places),
        (positions.at[0, :, pl.ds(0, LANES)], hubs),
        (tiles_hbm, tiles),
        (coefs_hbm, coefs),
    ]
    small = [
        pltpu.make_async_copy(source, target, small_sems.at[n])
        for n, (source, target) in enumerate(small)
    ]
    total_y = cells_y * lax.axis_size("gy")
    base = lax.axis_index("gy") * cells_y
    for copy in small:
        copy.start()
    for k in range(chunks):
        chunk(k).start()
    small[0].wait()
    near = wrapped(places[0], base, total_y)
    inside = jnp.logical_and(near >= -RAD, near < cells_y + RAD)
    height = places[1].astype(jnp.float32)
    lowest = jnp.min(jnp.where(inside, height, float(depth)), axis=1, keepdims=True)
    highest = jnp.max(jnp.where(inside, height, -1.0), axis=1, keepdims=True)
    column = lax.broadcasted_iota(jnp.int32, flags.shape, 1)
    flags[...] = jnp.where(column == 0, lowest, highest).astype(jnp.int32)
    touch_copy = pltpu.make_async_copy(flags, touch, touch_sem)
    touch_copy.start()

    def clear(n, carry):
        for k in range(SUB):
            pack_low[first_row + n * SUB + k] = jnp.zeros((1, points), jnp.float32)
            pack_high[first_row + n * SUB + k] = jnp.zeros((1, points), jnp.float32)
        return carry

    lax.fori_loop(0, 3 * records // SUB, clear, 0)
    for copy in small[1:]:
        copy.wait()
    for r in range(records):
        point_y[r] = places[0, pl.ds(r, 1), :]
        point_z[r] = places[1, pl.ds(r, 1), :]
        strength[r] = coefs[pl.ds(r, 1), :]
    touch_copy.wait()
    make_plan(hubs, tiles, touch, counts, start, plan, bucket, held)

    def weigh(t, carry):
        r = plan[1 + t]
        weight_y[t] = along_y(point_y[r], base, cells_y, total_y)
        weight_z[t] = jnp.zeros(weight_z.shape[1:], weight_z.dtype)

        def block(k, carry):
            rows = pl.ds(pl.multiple_of(k * PACKED, PACKED), PACKED)
            weight_z[t, 0, rows], weight_z[t, 1, rows] = along_z(point_z[r], k * PACKED)
            return carry

        first = (touch[r, 0] - RAD) // PACKED
        lax.fori_loop(first, (touch[r, 1] + RAD) // PACKED + 1, block, 0)
        return carry

    lax.fori_loop(0, plan[0], weigh, 0)

    def wait_to(ready, wanted):
        def step(k, carry):
            chunk(k).wait()
            return carry

        lax.fori_loop(ready, wanted, step, 0)
        return jnp.maximum(ready, wanted)

    def step(t, ready):
        picks, _ = pair(plan, t)
        ready = wait_to(ready, (picks[1][2] + RAD) // SUB + 1)
        for (_, r, _), rows in zip(picks, sampled_rows(field, weight_y, weight_z, picks)):
            for c in range(3):
                pack_low[first_row + 3 * r + c] = rows[c]
                pack_high[first_row + 3 * r + c] = rows[c]
        return ready

    ready = lax.fori_loop(0, (plan[0] + 1) // 2, step, jnp.int32(0))
    wait_to(ready, chunks)
    pack_edges(field, edge_west, edge_east, pack_low, pack_high)


def fix_west(factor, target, own, inflow, ghost):
    first = lax.axis_index("gx") == 0
    for c in range(3):
        west = jnp.where(first, inflow[c], ghost[c])
        coef = factor * TIME_STEP * VISCOSITY + (0.5 * factor * TIME_STEP) * own[0]
        target[c, 0] = target[c, 0] + west * coef


def fix_east(factor, target, own, ghost):
    last = lax.axis_index("gx") == lax.axis_size("gx") - 1
    end = target.shape[1] - 1
    for c in range(3):
        east = jnp.where(last, own[c], ghost[c])
        coef = factor * TIME_STEP * VISCOSITY - (0.5 * factor * TIME_STEP) * own[0]
        target[c, end] = target[c, end] + east * coef


def fix_rows(factor, target, own_low, own_high, got_low, got_high, t):
    cells_x, cells_y = target.shape[1:3]
    spread = factor * TIME_STEP * VISCOSITY
    half = 0.5 * factor * TIME_STEP
    low, high = pl.ds(0, 1), pl.ds(cells_y - 1, 1)
    for k in range(SUB):
        i = t * SUB + k
        south = spread + half * own_low[cells_x + i]
        north = spread - half * own_high[cells_x + i]
        for c in range(3):
            n = c * cells_x + i
            target[c, i, low, :] = target[c, i, low, :] + got_low[n] * south
            target[c, i, high, :] = target[c, i, high, :] + got_high[n] * north


def slabs_of(weight_y, weight_z, strength, own, low, high, cells, scales, picks):
    cells_x, cells_y, depth = cells
    count = 3 * cells_y
    across = (((1,), (1,)), ((), ()))
    spread = []
    for (t, r, hub), scale in zip(picks, scales):
        rows = [3 * cells_x + 3 * r + c for c in range(3)]
        total = [own[n] + (low[n] + high[n]) for n in rows]
        speed = jnp.sqrt(total[0] * total[0] + total[1] * total[1] + total[2] * total[2])
        pull = strength[r] * (-scale) * speed
        weight = weight_y[t]
        spread.append(split(jnp.concatenate([weight * (pull * x) for x in total], axis=0)))
    slabs = []
    for (t, r, hub), part in zip(picks, spread):
        slab = lax.dot_general(part, weight_z[t, 0], across, preferred_element_type=jnp.float32)
        rest = lax.dot_general(
            part[:count], weight_z[t, 1], across, preferred_element_type=jnp.float32
        )
        slabs.append(slab[:count] + (slab[count:] + rest))
    return slabs


def add_slab(field, slab, hub):
    cells_y = field.shape[2]
    for c in range(3):
        part = slab[c * cells_y : (c + 1) * cells_y]
        terms = [tap * part for tap in TAP]
        for d in range(-RAD, RAD + 1):
            field[c, hub + d] = field[c, hub + d] + terms[abs(d)]


def spread_pair(t, scale, field, plan, points, own, low, high):
    picks, both = pair(plan, t)
    scales = [scale, jnp.where(both, scale, 0.0)]
    slabs = slabs_of(*points, own, low, high, field.shape[1:], scales, picks)
    for (_, _, hub), slab in zip(picks, slabs):
        add_slab(field, slab, hub)


def spread_sample(
    section_in, inflow, ghost_low, ghost_high, own_low, own_high, own_west, own_east, got_low, got_high,
    plan, weight_y, weight_z, strength,
    section, section_out, stored_y, stored_z, pack_low, pack_high, edge_west, edge_east,
    share_out, sem, sem_y, sem_z,
):
    cells_x = section.shape[1]
    records = strength.shape[0]
    share = share_out.shape[2] // 3
    first_row = 3 * cells_x

    def copies(t):
        return (
            pltpu.make_async_copy(weight_y.at[t], stored_y.at[t], sem_y.at[t]),
            pltpu.make_async_copy(weight_z.at[t], stored_z.at[t], sem_z.at[t]),
        )

    def start_store(t, carry):
        for copy in copies(t):
            copy.start()
        return carry

    def wait_store(t, carry):
        for copy in copies(t):
            copy.wait()
        return carry

    lax.fori_loop(0, plan[0], start_store, 0)

    def fix_step(t, carry):
        fix_rows(1.0, section, own_low, own_high, got_low, got_high, t)
        return carry

    fix_west(1.0, section, own_west, inflow, ghost_low)
    fix_east(1.0, section, own_east, ghost_high)
    lax.fori_loop(0, cells_x // SUB, fix_step, 0)

    def spread_step(t, carry):
        points = (weight_y, weight_z, strength)
        spread_pair(t, TIME_STEP, section, plan, points, own_low, got_low, got_high)
        return carry

    lax.fori_loop(0, (plan[0] + 1) // 2, spread_step, 0)
    copy = pltpu.make_async_copy(section, section_out, sem)
    copy.start()
    pack_edges(section, edge_west, edge_east, pack_low, pack_high)

    def clear(r, carry):
        zero = jnp.zeros_like(own_low[0])
        for c in range(3):
            pack_low[first_row + 3 * r + c] = zero
            pack_high[first_row + 3 * r + c] = zero
            share_out[r // share, 0, 3 * (r % share) + c] = own_low[first_row + 3 * r + c]
            share_out[r // share, 1, 3 * (r % share) + c] = zero
        return carry

    lax.fori_loop(0, records, clear, 0)

    def sample_step(t, carry):
        picks, _ = pair(plan, t)
        for (_, r, _), rows in zip(picks, sampled_rows(section, weight_y, weight_z, picks)):
            for c in range(3):
                pack_low[first_row + 3 * r + c] = rows[c]
                pack_high[first_row + 3 * r + c] = rows[c]
                share_out[r // share, 1, 3 * (r % share) + c] = rows[c]
        return carry

    lax.fori_loop(0, (plan[0] + 1) // 2, sample_step, 0)
    lax.fori_loop(0, plan[0], wait_store, 0)
    copy.wait()


def share_force(parts, strength, counts, after, after_low, after_high, result):
    groups, _, rows = parts.shape[:3]
    share = rows // 3
    mine = lax.axis_index("gy") * share
    for s in range(share):
        live = mine + s < counts[0]
        pull = jnp.where(live, -0.5 * strength[mine + s], 0.0)
        total = [0.0, 0.0, 0.0]
        for stage in range(2):
            value = []
            for c in range(3):
                n = 3 * s + c
                x = parts[0, stage, n]
                for g in range(1, groups):
                    x += parts[g, stage, n]
                value.append(x)
            speed = jnp.sqrt(value[0] * value[0] + value[1] * value[1] + value[2] * value[2])
            total = [acc + speed * x for acc, x in zip(total, value)]
        for c in range(3):
            for g in range(groups):
                result[g, 3 * s + c] = pull * total[c]


def spread_next(
    following, inflow, ghost_low, ghost_high, own_low, own_high, own_west, own_east, got_low, got_high,
    plan, stored_y, stored_z, strength, after,
    result, field, weight_y, weight_z, in_sems, out_sems, sem_y, sem_z,
):
    chunks = field.shape[1] // SUB
    factor = 0.5

    def chunk_in(k):
        planes = pl.ds(k * SUB, SUB)
        return pltpu.make_async_copy(following.at[:, planes], field.at[:, planes], in_sems.at[k])

    def chunk_out(k):
        planes = pl.ds(k * SUB, SUB)
        return pltpu.make_async_copy(field.at[:, planes], result.at[:, planes], out_sems.at[k])

    def wait_to(ready, wanted):
        def step(k, carry):
            chunk_in(k).wait()
            fix_rows(factor, field, own_low, own_high, got_low, got_high, k)

            @pl.when(k == 0)
            def _():
                fix_west(factor, field, own_west, inflow, ghost_low)

            @pl.when(k == chunks - 1)
            def _():
                fix_east(factor, field, own_east, ghost_high)

            return carry

        lax.fori_loop(ready, wanted, step, 0)
        return jnp.maximum(ready, wanted)

    def send_to(sent, done):
        def step(k, carry):
            chunk_out(k).start()
            return carry

        lax.fori_loop(sent, done, step, 0)
        return jnp.maximum(sent, done)

    def weights(t):
        return (
            pltpu.make_async_copy(stored_y.at[t], weight_y.at[t], sem_y.at[t]),
            pltpu.make_async_copy(stored_z.at[t], weight_z.at[t], sem_z.at[t]),
        )

    def start_weights(t, carry):
        for copy in weights(t):
            copy.start()
        return carry

    found = plan[0]
    for k in range(chunks):
        chunk_in(k).start()
        lax.fori_loop(k * found // chunks, (k + 1) * found // chunks, start_weights, 0)

    def step(t, carry):
        ready, sent = carry
        picks, both = pair(plan, t)
        for copy in weights(picks[0][0]):
            copy.wait()

        @pl.when(both)
        def _():
            for copy in weights(picks[1][0]):
                copy.wait()

        ready = wait_to(ready, (picks[1][2] + RAD) // SUB + 1)
        sent = send_to(sent, (picks[0][2] + RAD) // SUB - 1)
        points = (weight_y, weight_z, strength)
        spread_pair(t, factor * TIME_STEP, field, plan, points, own_low, got_low, got_high)
        return ready, sent

    zero = jnp.int32(0)
    ready, sent = lax.fori_loop(0, (plan[0] + 1) // 2, step, (zero, zero))
    sent = send_to(sent, ready)

    def finish(k, carry):
        wait_to(k, k + 1)
        chunk_out(k).start()
        return carry

    lax.fori_loop(ready, chunks, finish, 0)
    for k in range(chunks):
        chunk_out(k).wait()


def advance(i, factor, field, west, east, emit):
    cells_y, depth = field.shape[2:]
    groups, halves = cells_y // SUB, depth // LANES
    row = lax.broadcasted_iota(jnp.int32, (SUB, LANES), 0)
    lane = lax.broadcasted_iota(jnp.int32, (SUB, LANES), 1)
    first_row, last_row = row == 0, row == SUB - 1
    first_lane, last_lane = lane == 0, lane == LANES - 1
    spread = factor * TIME_STEP * VISCOSITY
    centre = factor * (1.0 - 6.0 * TIME_STEP * VISCOSITY)
    zero = jnp.zeros((SUB, LANES), jnp.float32)

    loaded = {}

    def at(c, g, h):
        if (c, g, h) not in loaded:
            loaded[c, g, h] = field[c, i, pl.ds(g * SUB, SUB), pl.ds(h * LANES, LANES)]
        return loaded[c, g, h]

    for g in range(groups):
        for h in range(halves):
            place = (pl.ds(g * SUB, SUB), pl.ds(h * LANES, LANES))
            q = [at(c, g, h) for c in range(3)]
            speeds = [(0.5 * factor * TIME_STEP) * x for x in q]
            less = [spread - s for s in speeds]
            more = [spread + s for s in speeds]
            if g == 0:
                more[1] = jnp.where(first_row, zero, more[1])
            if g == groups - 1:
                less[1] = jnp.where(last_row, zero, less[1])
            if h == 0:
                more[2] = jnp.where(first_lane, zero, more[2])
            if h == halves - 1:
                less[2] = jnp.where(last_lane, zero, less[2])
            for c in range(3):
                x = q[c]
                above, below, upper, lower = x, x, x, x
                if g + 1 < groups:
                    above = jnp.where(first_row, at(c, g + 1, h), x)
                if g > 0:
                    below = jnp.where(last_row, at(c, g - 1, h), x)
                if h + 1 < halves:
                    upper = jnp.where(first_lane, at(c, g, h + 1), x)
                if h > 0:
                    lower = jnp.where(last_lane, at(c, g, h - 1), x)
                above, below = pltpu.roll(above, SUB - 1, 0), pltpu.roll(below, 1, 0)
                upper, lower = pltpu.roll(upper, LANES - 1, 1), pltpu.roll(lower, 1, 1)
                total = centre * x
                if east is not None:
                    total += field[c, east, place[0], place[1]] * less[0]
                if west is not None:
                    total += field[c, west, place[0], place[1]] * more[0]
                total += above * less[1] + below * more[1]
                total += upper * less[2] + lower * more[2]
                emit(c, place, total)


def advance_all(factor, field, emit):
    last = field.shape[1] - 1

    def one(i, west, east):
        advance(i, factor, field, west, east, functools.partial(emit, i))

    def step(i, carry):
        one(i, i - 1, i + 1)
        return carry

    one(0, None, 1)
    lax.fori_loop(1, last, step, 0)
    one(last, last - 1, None)


def advance_first(field, section):
    def emit(i, c, place, value):
        section[c, i, place[0], place[1]] = value

    advance_all(1.0, field, emit)


def advance_second(
    section_hbm, velocity, following, token, section, field, result, in_sems, old_sems, out_sems
):
    cells_x = section.shape[1]
    chunks = cells_x // SUB

    def planes(k):
        return pl.ds(k * SUB, SUB)

    def chunk_in(k):
        return pltpu.make_async_copy(
            section_hbm.at[:, planes(k)], section.at[:, planes(k)], in_sems.at[k]
        )

    def chunk_old(k):
        return pltpu.make_async_copy(
            velocity.at[:, planes(k)], field.at[:, planes(k)], old_sems.at[k]
        )

    def chunk_out(k):
        return pltpu.make_async_copy(
            result.at[:, planes(k)], following.at[:, planes(k)], out_sems.at[k]
        )

    def emit(i, c, place, value):
        result[c, i, place[0], place[1]] = value + 0.5 * field[c, i, place[0], place[1]]

    def one(i, west, east):
        advance(i, 0.5, section, west, east, functools.partial(emit, i))

    def step(i, carry):
        one(i, i - 1, i + 1)
        return carry

    token[...] = jnp.zeros_like(token)
    for k in range(chunks):
        chunk_in(k).start()
        chunk_old(k).start()
    chunk_in(0).wait()
    chunk_in(1).wait()
    chunk_old(0).wait()
    one(0, None, 1)
    lax.fori_loop(1, SUB, step, 0)
    chunk_out(0).start()

    def middle(k, carry):
        chunk_in(k + 1).wait()
        chunk_old(k).wait()
        lax.fori_loop(k * SUB, (k + 1) * SUB, step, 0)
        chunk_out(k).start()
        return carry

    lax.fori_loop(1, chunks - 1, middle, 0)
    chunk_old(chunks - 1).wait()
    lax.fori_loop(cells_x - SUB, cells_x - 1, step, 0)
    one(cells_x - 1, cells_x - 2, None)
    chunk_out(chunks - 1).start()
    for k in range(chunks):
        chunk_out(k).wait()


def shifted(x, axis, step, periodic):
    count = lax.axis_size(axis)
    pairs = [(i, (i + step) % count) for i in range(count)]
    if not periodic:
        pairs = [(s, t) for s, t in pairs if t - s == step]
    return lax.ppermute(x, axis, pairs)


def exchange(pack_low, pack_high, edge_west, edge_east):
    got_low = shifted(pack_high, "gy", 1, True)
    got_high = shifted(pack_low, "gy", -1, True)
    ghost_low = shifted(edge_east, "gx", 1, False)
    ghost_high = shifted(edge_west, "gx", -1, False)
    return ghost_low, ghost_high, got_low, got_high


def local(velocity, inflow, positions, tiles, coefs, counts):
    f32, i32 = jnp.float32, jnp.int32
    whole = velocity.shape
    _, cells_x, cells_y, depth = whole
    groups_y = lax.axis_size("gy")
    positions = positions[0].transpose(1, 0, 2)
    tiles, coefs = tiles[0].T, coefs[0]
    records, points = coefs.shape
    share = records // groups_y
    chunks = cells_x // SUB
    size = 4 * math.prod(whole)
    held = pltpu.VMEM(whole, f32)
    stored = pltpu.HBM(whole, f32)
    array = jax.ShapeDtypeStruct
    pack = array((3 * cells_x + 3 * records, 1, points), f32)
    edge = array((3, cells_y, depth), f32)
    per_record = (records, 1, points)
    y_shape, z_shape = (records, cells_y, points), (records, 2, depth, points)
    y_bytes, z_bytes = 4 * math.prod(y_shape), 2 * math.prod(z_shape)
    record_sems = pltpu.SemaphoreType.DMA((records,))
    chunk_sems = pltpu.SemaphoreType.DMA((chunks,))

    field, *own_a, weight_y, weight_z, strength, plan = pl.pallas_call(
        load_sample,
        out_shape=(
            held, pack, pack, edge, edge,
            pltpu.VMEM(y_shape, f32), pltpu.VMEM(z_shape, jnp.bfloat16),
            array(per_record, f32),
            array((1 + 2 * records,), i32),
        ),
        in_specs=[ANYWHERE] * 4 + [SCALAR],
        out_specs=(WHOLE,) * 8 + (SCALAR,),
        scratch_shapes=[
            pltpu.VMEM(per_record, i32),
            pltpu.VMEM(per_record, i32),
            pltpu.SMEM((records, LANES), i32),
            pltpu.SMEM((2, records), i32),
            pltpu.VMEM((2, records, points), i32),
            pltpu.VMEM((records, points), f32),
            pltpu.VMEM((records, LANES), i32),
            pltpu.SMEM((records, LANES), i32),
            pltpu.SMEM((chunks, records), i32),
            pltpu.SMEM((chunks,), i32),
            pltpu.SemaphoreType.DMA((4,)),
            pltpu.SemaphoreType.DMA,
            chunk_sems,
        ],
        compiler_params=params(),
        cost_estimate=cost(2 * 10**9, 4 * size),
        name="load_sample",
    )(streamed(velocity), streamed(positions), streamed(tiles), streamed(coefs), counts)
    weight_y, weight_z = resident(weight_y), resident(weight_z)
    ghosts_a = exchange(*own_a)

    section = pl.pallas_call(
        advance_first,
        out_shape=held,
        in_specs=[WHOLE],
        out_specs=WHOLE,
        compiler_params=params(),
        cost_estimate=cost(10**9, 4 * size),
        name="advance_first",
    )(resident(field))

    _, section, stored_y, stored_z, *own_b, shares = pl.pallas_call(
        spread_sample,
        out_shape=(
            held, stored, pltpu.HBM(y_shape, f32), pltpu.HBM(z_shape, jnp.bfloat16),
            pack, pack, edge, edge,
            array((groups_y, 2, 3 * share, 1, points), f32),
        ),
        in_specs=[WHOLE] * 10 + [SCALAR] + [WHOLE] * 3,
        out_specs=(WHOLE,) + (ANYWHERE,) * 3 + (WHOLE,) * 5,
        input_output_aliases={0: 0},
        scratch_shapes=[pltpu.SemaphoreType.DMA, record_sems, record_sems],
        compiler_params=params(),
        cost_estimate=cost(2 * 10**9, 4 * size),
        name="spread_sample",
    )(
        resident(section), inflow, *ghosts_a[:2], *own_a, *ghosts_a[2:],
        plan, weight_y, weight_z, strength,
    )
    shares = lax.all_to_all(shares, "gy", 0, 0)
    ghosts_b = exchange(*own_b)

    following, token = pl.pallas_call(
        advance_second,
        out_shape=(stored, array((SUB, LANES), f32)),
        in_specs=[ANYWHERE] * 2,
        out_specs=(ANYWHERE, WHOLE),
        scratch_shapes=[pltpu.VMEM(whole, f32)] * 3 + [chunk_sems] * 3,
        compiler_params=params(VMEM_LIMIT + 3 * size),
        cost_estimate=cost(10**9, 4 * size),
        name="advance_second",
    )(streamed(section), streamed(velocity))

    forces = pl.pallas_call(
        share_force,
        out_shape=array((groups_y, 3 * share, 1, points), f32),
        in_specs=[WHOLE, WHOLE, SCALAR] + [ANYWHERE] * 3,
        out_specs=WHOLE,
        compiler_params=params(),
        cost_estimate=cost(10**6, 10**6),
        name="share_force",
    )(shares, strength, counts, token, *ghosts_b[:2])
    all_forces = lax.all_to_all(forces, "gy", 0, 0)

    velocity_next = pl.pallas_call(
        spread_next,
        out_shape=stored,
        in_specs=[ANYWHERE] + [WHOLE] * 9 + [SCALAR, ANYWHERE, ANYWHERE, WHOLE, ANYWHERE],
        out_specs=ANYWHERE,
        scratch_shapes=[
            pltpu.VMEM(whole, f32),
            pltpu.VMEM(y_shape, f32),
            pltpu.VMEM(z_shape, jnp.bfloat16),
            chunk_sems, chunk_sems, record_sems, record_sems,
        ],
        compiler_params=params(VMEM_LIMIT + size + y_bytes + z_bytes),
        cost_estimate=cost(2 * 10**9, 4 * size),
        name="spread_next",
    )(
        streamed(following), inflow, *ghosts_b[:2], *own_b, *ghosts_b[2:],
        plan, streamed(stored_y), streamed(stored_z), strength, forces,
    )
    return (velocity_next, all_forces.reshape(1, records, 3, points))


def solution(mesh):
    return jax.shard_map(
        local,
        mesh=mesh,
        in_specs=(
            P(None, "gx", "gy", None),
            P(None, "gy", None),
            P("gx", None, None, None),
            P("gx", None, None),
            P("gx", None, None),
            P("gx"),
        ),
        out_specs=(P(None, "gx", "gy", None), P("gx", None, None, None)),
        check_vma=False,
    )
```

```python
import math

import jax
import jax.numpy as jnp
from jax import lax
from jax.experimental import pallas as pl
from jax.experimental.pallas import tpu as pltpu
from jax.sharding import PartitionSpec as P

RAD = 2
VISCOSITY = 0.05
TIME_STEP = 0.1
WIDTH_EPS = 1.5
ROOT_PI = 1.7724538509055159
TAP = [math.exp(-((d / WIDTH_EPS) ** 2)) / (WIDTH_EPS * ROOT_PI) for d in range(RAD + 1)]
HIGH = [float(jnp.bfloat16(tap)) for tap in TAP]
LOW = [float(jnp.bfloat16(tap - high)) for tap, high in zip(TAP, HIGH)]
LANES = 128
SUB = 8
PACKED = 32
BATCH = 4
VMEM_LIMIT = 5 * 2**20

WHOLE = pl.BlockSpec(memory_space=pltpu.VMEM)
SCALAR = pl.BlockSpec(memory_space=pltpu.SMEM)
ANYWHERE = pl.BlockSpec(memory_space=pl.ANY)


def params(limit=VMEM_LIMIT):
    return pltpu.CompilerParams(vmem_limit_bytes=limit)


def cost(flops, nbytes):
    return pl.CostEstimate(flops=flops, bytes_accessed=nbytes, transcendentals=0)


def resident(x):
    return pltpu.with_memory_space_constraint(x, pltpu.VMEM)


def streamed(x):
    return pltpu.with_memory_space_constraint(x, pltpu.HBM)


def split(x):
    high = x.astype(jnp.bfloat16)
    low = (x - high.astype(jnp.float32)).astype(jnp.bfloat16)
    return jnp.concatenate([high, low], axis=0)


def along_z(point_z, start):
    points = point_z.shape[-1]
    row = lax.broadcasted_iota(jnp.int32, (PACKED, points), 0).astype(jnp.bfloat16)
    place = (point_z - start).astype(jnp.float32)
    place = jnp.broadcast_to(place, (PACKED, points)).astype(jnp.bfloat16)
    dist = jnp.abs(row - place)
    near = [dist == float(d) for d in range(RAD + 1)]
    out = []
    for taps in (HIGH, LOW):
        value = jnp.zeros_like(row)
        for d in range(RAD, -1, -1):
            value = jnp.where(near[d], jnp.full_like(row, taps[d]), value)
        out.append(value)
    return out


def wrapped(point_y, base, total_y):
    near = point_y - base
    near = jnp.where(near > total_y // 2, near - total_y, near)
    return jnp.where(near < -(total_y // 2), near + total_y, near)


def along_y(point_y, base, cells_y, total_y):
    near = wrapped(point_y, base, total_y)
    dist = jnp.abs(lax.broadcasted_iota(jnp.int32, (cells_y, point_y.shape[-1]), 0) - near)
    return jnp.where(
        dist == 0, TAP[0], jnp.where(dist == 1, TAP[1], jnp.where(dist == 2, TAP[2], 0.0))
    )


def make_plan(hubs, tiles, touch, counts, start, plan, bucket, held):
    tile_y, groups_y = lax.axis_index("gy"), lax.axis_size("gy")
    records, chunks = tiles.shape[1], held.shape[0]
    for k in range(chunks):
        held[k] = 0

    def place(r, carry):
        offset = tile_y - tiles[0, r]
        offset = jnp.where(offset < 0, offset + groups_y, offset)

        @pl.when(jnp.logical_and(offset < tiles[1, r], touch[r, 1] >= 0))
        def _():
            k = (hubs[r, 0] - start + RAD) // SUB
            bucket[k, held[k]] = r
            held[k] = held[k] + 1

        return carry

    lax.fori_loop(0, jnp.minimum(counts[0], records), place, 0)

    def flatten(k, found):
        def move(j, found):
            r = bucket[k, j]
            plan[1 + found] = r
            plan[1 + records + found] = hubs[r, 0] - start
            return found + 1

        return lax.fori_loop(0, held[k], move, found)

    plan[0] = lax.fori_loop(0, chunks, flatten, jnp.int32(0))


def pair(plan, t):
    records = (plan.shape[0] - 1) // 2
    first = 2 * t
    second = jnp.minimum(first + 1, plan[0] - 1)
    return [(n, plan[1 + n], plan[1 + records + n]) for n in (first, second)], second > first


def sampled_rows(field, weight_y, weight_z, picks):
    cells_y = field.shape[2]
    rows = 3 * cells_y
    parts = []
    for t, r, hub in picks:
        planes = []
        for c in range(3):
            plane = TAP[0] * field[c, hub]
            plane += TAP[1] * (field[c, hub - 1] + field[c, hub + 1])
            plane += TAP[2] * (field[c, hub - 2] + field[c, hub + 2])
            planes.append(plane)
        parts.append(split(jnp.concatenate(planes, axis=0)))
    out = []
    for (t, r, hub), part in zip(picks, parts):
        picked = jnp.dot(part, weight_z[t, 0], preferred_element_type=jnp.float32)
        rest = jnp.dot(part[:rows], weight_z[t, 1], preferred_element_type=jnp.float32)
        picked = picked[:rows] + (picked[rows:] + rest)
        weight = weight_y[t]
        out.append(
            [
                jnp.sum(picked[c * cells_y : (c + 1) * cells_y] * weight, axis=0, keepdims=True)
                for c in range(3)
            ]
        )
    return out


def pack_edges(field, edge_west, edge_east, pack_low, pack_high):
    cells_x, cells_y, depth = field.shape[1:]
    for c in range(3):
        edge_west[c] = field[c, 0]
        edge_east[c] = field[c, cells_x - 1]

    def step(t, carry):
        cells = [(c, t * BATCH + k) for k in range(BATCH) for c in range(3)]
        rows = [
            (field[c, i, pl.ds(0, 1), :], field[c, i, pl.ds(cells_y - 1, 1), :]) for c, i in cells
        ]
        for (c, i), (low, high) in zip(cells, rows):
            pack_low[c * cells_x + i] = low
            pack_high[c * cells_x + i] = high
        return carry

    lax.fori_loop(0, cells_x // BATCH, step, 0)


def load_sample(
    velocity, positions, tiles_hbm, coefs_hbm, counts,
    field, pack_low, pack_high, edge_west, edge_east, weight_y, weight_z, strength, plan,
    point_y, point_z, hubs, tiles, places, coefs, flags, touch, bucket, held, small_sems, touch_sem, sems,
):
    cells_x, cells_y, depth = field.shape[1:]
    records, points = coefs.shape
    chunks = cells_x // SUB
    first_row = 3 * cells_x
    start = lax.axis_index("gx") * cells_x

    def chunk(k):
        planes = pl.ds(k * SUB, SUB)
        return pltpu.make_async_copy(velocity.at[:, planes], field.at[:, planes], sems.at[k])

    small = [
        (positions.at[pl.ds(1, 2)], places),
        (positions.at[0, :, pl.ds(0, LANES)], hubs),
        (tiles_hbm, tiles),
        (coefs_hbm, coefs),
    ]
    small = [
        pltpu.make_async_copy(source, target, small_sems.at[n])
        for n, (source, target) in enumerate(small)
    ]
    total_y = cells_y * lax.axis_size("gy")
    base = lax.axis_index("gy") * cells_y
    for copy in small:
        copy.start()
    for k in range(chunks):
        chunk(k).start()
    small[0].wait()
    near = wrapped(places[0], base, total_y)
    inside = jnp.logical_and(near >= -RAD, near < cells_y + RAD)
    height = places[1].astype(jnp.float32)
    lowest = jnp.min(jnp.where(inside, height, float(depth)), axis=1, keepdims=True)
    highest = jnp.max(jnp.where(inside, height, -1.0), axis=1, keepdims=True)
    column = lax.broadcasted_iota(jnp.int32, flags.shape, 1)
    flags[...] = jnp.where(column == 0, lowest, highest).astype(jnp.int32)
    touch_copy = pltpu.make_async_copy(flags, touch, touch_sem)
    touch_copy.start()

    def clear(n, carry):
        for k in range(SUB):
            pack_low[first_row + n * SUB + k] = jnp.zeros((1, points), jnp.float32)
            pack_high[first_row + n * SUB + k] = jnp.zeros((1, points), jnp.float32)
        return carry

    lax.fori_loop(0, 3 * records // SUB, clear, 0)
    for copy in small[1:]:
        copy.wait()
    for first in range(0, records, SUB):
        here = range(first, first + SUB)
        rows = [
            (places[0, pl.ds(r, 1), :], places[1, pl.ds(r, 1), :], coefs[pl.ds(r, 1), :])
            for r in here
        ]
        for r, (y, z, coef) in zip(here, rows):
            point_y[r], point_z[r], strength[r] = y, z, coef
    touch_copy.wait()
    make_plan(hubs, tiles, touch, counts, start, plan, bucket, held)

    def weigh(t, carry):
        r = plan[1 + t]
        weight_y[t] = along_y(point_y[r], base, cells_y, total_y)
        weight_z[t] = jnp.zeros(weight_z.shape[1:], weight_z.dtype)

        def block(k, carry):
            rows = pl.ds(pl.multiple_of(k * PACKED, PACKED), PACKED)
            weight_z[t, 0, rows], weight_z[t, 1, rows] = along_z(point_z[r], k * PACKED)
            return carry

        first = (touch[r, 0] - RAD) // PACKED
        lax.fori_loop(first, (touch[r, 1] + RAD) // PACKED + 1, block, 0)
        return carry

    lax.fori_loop(0, plan[0], weigh, 0)

    def wait_to(ready, wanted):
        def step(k, carry):
            chunk(k).wait()
            return carry

        lax.fori_loop(ready, wanted, step, 0)
        return jnp.maximum(ready, wanted)

    def step(t, ready):
        picks, _ = pair(plan, t)
        ready = wait_to(ready, (picks[1][2] + RAD) // SUB + 1)
        for (_, r, _), rows in zip(picks, sampled_rows(field, weight_y, weight_z, picks)):
            for c in range(3):
                pack_low[first_row + 3 * r + c] = rows[c]
                pack_high[first_row + 3 * r + c] = rows[c]
        return ready

    ready = lax.fori_loop(0, (plan[0] + 1) // 2, step, jnp.int32(0))
    wait_to(ready, chunks)
    pack_edges(field, edge_west, edge_east, pack_low, pack_high)


def fix_west(factor, target, own, inflow, ghost):
    first = lax.axis_index("gx") == 0
    for c in range(3):
        west = jnp.where(first, inflow[c], ghost[c])
        coef = factor * TIME_STEP * VISCOSITY + (0.5 * factor * TIME_STEP) * own[0]
        target[c, 0] = target[c, 0] + west * coef


def fix_east(factor, target, own, ghost):
    last = lax.axis_index("gx") == lax.axis_size("gx") - 1
    end = target.shape[1] - 1
    for c in range(3):
        east = jnp.where(last, own[c], ghost[c])
        coef = factor * TIME_STEP * VISCOSITY - (0.5 * factor * TIME_STEP) * own[0]
        target[c, end] = target[c, end] + east * coef


def fix_rows(factor, target, own_low, own_high, got_low, got_high, t):
    cells_x, cells_y = target.shape[1:3]
    spread = factor * TIME_STEP * VISCOSITY
    half = 0.5 * factor * TIME_STEP
    low, high = pl.ds(0, 1), pl.ds(cells_y - 1, 1)
    for first in range(0, SUB, 2):
        values = []
        for k in range(first, first + 2):
            i = t * SUB + k
            south = spread + half * own_low[cells_x + i]
            north = spread - half * own_high[cells_x + i]
            for c in range(3):
                n = c * cells_x + i
                values.append((c, i, low, target[c, i, low, :] + got_low[n] * south))
                values.append((c, i, high, target[c, i, high, :] + got_high[n] * north))
        for c, i, row, value in values:
            target[c, i, row, :] = value


def slabs_of(weight_y, weight_z, strength, own, low, high, cells, scales, picks):
    cells_x, cells_y, depth = cells
    count = 3 * cells_y
    across = (((1,), (1,)), ((), ()))
    spread = []
    for (t, r, hub), scale in zip(picks, scales):
        rows = [3 * cells_x + 3 * r + c for c in range(3)]
        total = [own[n] + (low[n] + high[n]) for n in rows]
        speed = jnp.sqrt(total[0] * total[0] + total[1] * total[1] + total[2] * total[2])
        pull = strength[r] * (-scale) * speed
        weight = weight_y[t]
        spread.append(split(jnp.concatenate([weight * (pull * x) for x in total], axis=0)))
    slabs = []
    for (t, r, hub), part in zip(picks, spread):
        slab = lax.dot_general(part, weight_z[t, 0], across, preferred_element_type=jnp.float32)
        rest = lax.dot_general(
            part[:count], weight_z[t, 1], across, preferred_element_type=jnp.float32
        )
        slabs.append(slab[:count] + (slab[count:] + rest))
    return slabs


def add_slab(field, slab, hub):
    cells_y = field.shape[2]
    for c in range(3):
        part = slab[c * cells_y : (c + 1) * cells_y]
        terms = [tap * part for tap in TAP]
        reach = range(-RAD, RAD + 1)
        values = [field[c, hub + d] + terms[abs(d)] for d in reach]
        for d, value in zip(reach, values):
            field[c, hub + d] = value


def spread_pair(t, scale, field, plan, points, own, low, high):
    picks, both = pair(plan, t)
    scales = [scale, jnp.where(both, scale, 0.0)]
    slabs = slabs_of(*points, own, low, high, field.shape[1:], scales, picks)
    for (_, _, hub), slab in zip(picks, slabs):
        add_slab(field, slab, hub)


def spread_sample(
    section_in, inflow, ghost_low, ghost_high, own_low, own_high, own_west, own_east, got_low, got_high,
    plan, weight_y, weight_z, strength,
    section, section_out, stored_y, stored_z, pack_low, pack_high, edge_west, edge_east,
    share_out, sem, sem_y, sem_z,
):
    cells_x = section.shape[1]
    records = strength.shape[0]
    share = share_out.shape[2] // 3
    first_row = 3 * cells_x

    def copies(t):
        return (
            pltpu.make_async_copy(weight_y.at[t], stored_y.at[t], sem_y.at[t]),
            pltpu.make_async_copy(weight_z.at[t], stored_z.at[t], sem_z.at[t]),
        )

    def start_store(t, carry):
        for copy in copies(t):
            copy.start()
        return carry

    def wait_store(t, carry):
        for copy in copies(t):
            copy.wait()
        return carry

    lax.fori_loop(0, plan[0], start_store, 0)

    def fix_step(t, carry):
        fix_rows(1.0, section, own_low, own_high, got_low, got_high, t)
        return carry

    fix_west(1.0, section, own_west, inflow, ghost_low)
    fix_east(1.0, section, own_east, ghost_high)
    lax.fori_loop(0, cells_x // SUB, fix_step, 0)

    def spread_step(t, carry):
        points = (weight_y, weight_z, strength)
        spread_pair(t, TIME_STEP, section, plan, points, own_low, got_low, got_high)
        return carry

    lax.fori_loop(0, (plan[0] + 1) // 2, spread_step, 0)
    copy = pltpu.make_async_copy(section, section_out, sem)
    copy.start()
    pack_edges(section, edge_west, edge_east, pack_low, pack_high)

    def clear(r, carry):
        rows = [own_low[first_row + 3 * r + c] for c in range(3)]
        zero = jnp.zeros_like(rows[0])
        for c in range(3):
            pack_low[first_row + 3 * r + c] = zero
            pack_high[first_row + 3 * r + c] = zero
            share_out[r // share, 0, 3 * (r % share) + c] = rows[c]
            share_out[r // share, 1, 3 * (r % share) + c] = zero
        return carry

    lax.fori_loop(0, records, clear, 0)

    def sample_step(t, carry):
        picks, _ = pair(plan, t)
        for (_, r, _), rows in zip(picks, sampled_rows(section, weight_y, weight_z, picks)):
            for c in range(3):
                pack_low[first_row + 3 * r + c] = rows[c]
                pack_high[first_row + 3 * r + c] = rows[c]
                share_out[r // share, 1, 3 * (r % share) + c] = rows[c]
        return carry

    lax.fori_loop(0, (plan[0] + 1) // 2, sample_step, 0)
    lax.fori_loop(0, plan[0], wait_store, 0)
    copy.wait()


def share_force(parts, strength, counts, after, after_low, after_high, result):
    groups, _, rows = parts.shape[:3]
    share = rows // 3
    mine = lax.axis_index("gy") * share
    values = []
    for s in range(share):
        live = mine + s < counts[0]
        pull = jnp.where(live, -0.5 * strength[mine + s], 0.0)
        total = [0.0, 0.0, 0.0]
        for stage in range(2):
            value = []
            for c in range(3):
                n = 3 * s + c
                x = parts[0, stage, n]
                for g in range(1, groups):
                    x += parts[g, stage, n]
                value.append(x)
            speed = jnp.sqrt(value[0] * value[0] + value[1] * value[1] + value[2] * value[2])
            total = [acc + speed * x for acc, x in zip(total, value)]
        values.extend((3 * s + c, pull * total[c]) for c in range(3))
        if s % 2 == 1 or s + 1 == share:
            for n, value in values:
                for g in range(groups):
                    result[g, n] = value
            values = []


def spread_next(
    following, inflow, ghost_low, ghost_high, own_low, own_high, own_west, own_east, got_low, got_high,
    plan, stored_y, stored_z, strength, after,
    result, field, weight_y, weight_z, in_sems, out_sems, sem_y, sem_z,
):
    chunks = field.shape[1] // SUB
    factor = 0.5

    def chunk_in(k):
        planes = pl.ds(k * SUB, SUB)
        return pltpu.make_async_copy(following.at[:, planes], field.at[:, planes], in_sems.at[k])

    def chunk_out(k):
        planes = pl.ds(k * SUB, SUB)
        return pltpu.make_async_copy(field.at[:, planes], result.at[:, planes], out_sems.at[k])

    def wait_to(ready, wanted):
        def step(k, carry):
            chunk_in(k).wait()
            fix_rows(factor, field, own_low, own_high, got_low, got_high, k)

            @pl.when(k == 0)
            def _():
                fix_west(factor, field, own_west, inflow, ghost_low)

            @pl.when(k == chunks - 1)
            def _():
                fix_east(factor, field, own_east, ghost_high)

            return carry

        lax.fori_loop(ready, wanted, step, 0)
        return jnp.maximum(ready, wanted)

    def send_to(sent, done):
        def step(k, carry):
            chunk_out(k).start()
            return carry

        lax.fori_loop(sent, done, step, 0)
        return jnp.maximum(sent, done)

    def weights(t):
        return (
            pltpu.make_async_copy(stored_y.at[t], weight_y.at[t], sem_y.at[t]),
            pltpu.make_async_copy(stored_z.at[t], weight_z.at[t], sem_z.at[t]),
        )

    def start_weights(t, carry):
        for copy in weights(t):
            copy.start()
        return carry

    found = plan[0]
    for k in range(chunks):
        chunk_in(k).start()
        lax.fori_loop(k * found // chunks, (k + 1) * found // chunks, start_weights, 0)

    def step(t, carry):
        ready, sent = carry
        picks, both = pair(plan, t)
        for copy in weights(picks[0][0]):
            copy.wait()

        @pl.when(both)
        def _():
            for copy in weights(picks[1][0]):
                copy.wait()

        ready = wait_to(ready, (picks[1][2] + RAD) // SUB + 1)
        sent = send_to(sent, (picks[0][2] + RAD) // SUB - 1)
        points = (weight_y, weight_z, strength)
        spread_pair(t, factor * TIME_STEP, field, plan, points, own_low, got_low, got_high)
        return ready, sent

    zero = jnp.int32(0)
    ready, sent = lax.fori_loop(0, (plan[0] + 1) // 2, step, (zero, zero))
    sent = send_to(sent, ready)

    def finish(k, carry):
        wait_to(k, k + 1)
        chunk_out(k).start()
        return carry

    lax.fori_loop(ready, chunks, finish, 0)
    for k in range(chunks):
        chunk_out(k).wait()


def advance(i, factor, field, west, east, target, finish):
    cells_y, depth = field.shape[2:]
    groups, halves = cells_y // SUB, depth // LANES
    row = lax.broadcasted_iota(jnp.int32, (SUB, LANES), 0)
    lane = lax.broadcasted_iota(jnp.int32, (SUB, LANES), 1)
    first_row, last_row = row == 0, row == SUB - 1
    first_lane, last_lane = lane == 0, lane == LANES - 1
    spread = factor * TIME_STEP * VISCOSITY
    centre = factor * (1.0 - 6.0 * TIME_STEP * VISCOSITY)
    zero = jnp.zeros((SUB, LANES), jnp.float32)

    loaded = {}

    def at(c, g, h):
        if (c, g, h) not in loaded:
            loaded[c, g, h] = field[c, i, pl.ds(g * SUB, SUB), pl.ds(h * LANES, LANES)]
        return loaded[c, g, h]

    values = []
    for g in range(groups):
        for h in range(halves):
            place = (pl.ds(g * SUB, SUB), pl.ds(h * LANES, LANES))
            q = [at(c, g, h) for c in range(3)]
            speeds = [(0.5 * factor * TIME_STEP) * x for x in q]
            less = [spread - s for s in speeds]
            more = [spread + s for s in speeds]
            if g == 0:
                more[1] = jnp.where(first_row, zero, more[1])
            if g == groups - 1:
                less[1] = jnp.where(last_row, zero, less[1])
            if h == 0:
                more[2] = jnp.where(first_lane, zero, more[2])
            if h == halves - 1:
                less[2] = jnp.where(last_lane, zero, less[2])
            for c in range(3):
                x = q[c]
                above, below, upper, lower = x, x, x, x
                if g + 1 < groups:
                    above = jnp.where(first_row, at(c, g + 1, h), x)
                if g > 0:
                    below = jnp.where(last_row, at(c, g - 1, h), x)
                if h + 1 < halves:
                    upper = jnp.where(first_lane, at(c, g, h + 1), x)
                if h > 0:
                    lower = jnp.where(last_lane, at(c, g, h - 1), x)
                above, below = pltpu.roll(above, SUB - 1, 0), pltpu.roll(below, 1, 0)
                upper, lower = pltpu.roll(upper, LANES - 1, 1), pltpu.roll(lower, 1, 1)
                total = centre * x
                if east is not None:
                    total += field[c, east, place[0], place[1]] * less[0]
                if west is not None:
                    total += field[c, west, place[0], place[1]] * more[0]
                total += above * less[1] + below * more[1]
                total += upper * less[2] + lower * more[2]
                values.append((c, place, finish(c, i, place, total)))
        if g % 2 == 1 or g + 1 == groups:
            for c, place, value in values:
                target[c, i, place[0], place[1]] = value
            values = []


def advance_all(factor, field, target, finish):
    last = field.shape[1] - 1

    def one(i, west, east):
        advance(i, factor, field, west, east, target, finish)

    def step(i, carry):
        one(i, i - 1, i + 1)
        return carry

    one(0, None, 1)
    lax.fori_loop(1, last, step, 0)
    one(last, last - 1, None)


def advance_first(field, section):
    advance_all(1.0, field, section, lambda c, i, place, value: value)


def advance_second(
    section_hbm, velocity, following, token, section, field, result, in_sems, old_sems, out_sems
):
    cells_x = section.shape[1]
    chunks = cells_x // SUB

    def planes(k):
        return pl.ds(k * SUB, SUB)

    def chunk_in(k):
        return pltpu.make_async_copy(
            section_hbm.at[:, planes(k)], section.at[:, planes(k)], in_sems.at[k]
        )

    def chunk_old(k):
        return pltpu.make_async_copy(
            velocity.at[:, planes(k)], field.at[:, planes(k)], old_sems.at[k]
        )

    def chunk_out(k):
        return pltpu.make_async_copy(
            result.at[:, planes(k)], following.at[:, planes(k)], out_sems.at[k]
        )

    def finish(c, i, place, value):
        return value + 0.5 * field[c, i, place[0], place[1]]

    def one(i, west, east):
        advance(i, 0.5, section, west, east, result, finish)

    def step(i, carry):
        one(i, i - 1, i + 1)
        return carry

    token[...] = jnp.zeros_like(token)
    for k in range(chunks):
        chunk_in(k).start()
        chunk_old(k).start()
    chunk_in(0).wait()
    chunk_in(1).wait()
    chunk_old(0).wait()
    one(0, None, 1)
    lax.fori_loop(1, SUB, step, 0)
    chunk_out(0).start()

    def middle(k, carry):
        chunk_in(k + 1).wait()
        chunk_old(k).wait()
        lax.fori_loop(k * SUB, (k + 1) * SUB, step, 0)
        chunk_out(k).start()
        return carry

    lax.fori_loop(1, chunks - 1, middle, 0)
    chunk_old(chunks - 1).wait()
    lax.fori_loop(cells_x - SUB, cells_x - 1, step, 0)
    one(cells_x - 1, cells_x - 2, None)
    chunk_out(chunks - 1).start()
    for k in range(chunks):
        chunk_out(k).wait()


def shifted(x, axis, step, periodic):
    count = lax.axis_size(axis)
    pairs = [(i, (i + step) % count) for i in range(count)]
    if not periodic:
        pairs = [(s, t) for s, t in pairs if t - s == step]
    return lax.ppermute(x, axis, pairs)


def exchange(pack_low, pack_high, edge_west, edge_east):
    got_low = shifted(pack_high, "gy", 1, True)
    got_high = shifted(pack_low, "gy", -1, True)
    ghost_low = shifted(edge_east, "gx", 1, False)
    ghost_high = shifted(edge_west, "gx", -1, False)
    return ghost_low, ghost_high, got_low, got_high


def local(velocity, inflow, positions, tiles, coefs, counts):
    f32, i32 = jnp.float32, jnp.int32
    whole = velocity.shape
    _, cells_x, cells_y, depth = whole
    groups_y = lax.axis_size("gy")
    positions = positions[0].transpose(1, 0, 2)
    tiles, coefs = tiles[0].T, coefs[0]
    records, points = coefs.shape
    share = records // groups_y
    chunks = cells_x // SUB
    size = 4 * math.prod(whole)
    held = pltpu.VMEM(whole, f32)
    stored = pltpu.HBM(whole, f32)
    array = jax.ShapeDtypeStruct
    pack = array((3 * cells_x + 3 * records, 1, points), f32)
    edge = array((3, cells_y, depth), f32)
    per_record = (records, 1, points)
    y_shape, z_shape = (records, cells_y, points), (records, 2, depth, points)
    y_bytes, z_bytes = 4 * math.prod(y_shape), 2 * math.prod(z_shape)
    record_sems = pltpu.SemaphoreType.DMA((records,))
    chunk_sems = pltpu.SemaphoreType.DMA((chunks,))

    field, *own_a, weight_y, weight_z, strength, plan = pl.pallas_call(
        load_sample,
        out_shape=(
            held, pack, pack, edge, edge,
            pltpu.VMEM(y_shape, f32), pltpu.VMEM(z_shape, jnp.bfloat16),
            array(per_record, f32),
            array((1 + 2 * records,), i32),
        ),
        in_specs=[ANYWHERE] * 4 + [SCALAR],
        out_specs=(WHOLE,) * 8 + (SCALAR,),
        scratch_shapes=[
            pltpu.VMEM(per_record, i32),
            pltpu.VMEM(per_record, i32),
            pltpu.SMEM((records, LANES), i32),
            pltpu.SMEM((2, records), i32),
            pltpu.VMEM((2, records, points), i32),
            pltpu.VMEM((records, points), f32),
            pltpu.VMEM((records, LANES), i32),
            pltpu.SMEM((records, LANES), i32),
            pltpu.SMEM((chunks, records), i32),
            pltpu.SMEM((chunks,), i32),
            pltpu.SemaphoreType.DMA((4,)),
            pltpu.SemaphoreType.DMA,
            chunk_sems,
        ],
        compiler_params=params(),
        cost_estimate=cost(2 * 10**9, 4 * size),
        name="load_sample",
    )(streamed(velocity), streamed(positions), streamed(tiles), streamed(coefs), counts)
    weight_y, weight_z = resident(weight_y), resident(weight_z)
    ghosts_a = exchange(*own_a)

    section = pl.pallas_call(
        advance_first,
        out_shape=held,
        in_specs=[WHOLE],
        out_specs=WHOLE,
        compiler_params=params(),
        cost_estimate=cost(10**9, 4 * size),
        name="advance_first",
    )(resident(field))

    _, section, stored_y, stored_z, *own_b, shares = pl.pallas_call(
        spread_sample,
        out_shape=(
            held, stored, pltpu.HBM(y_shape, f32), pltpu.HBM(z_shape, jnp.bfloat16),
            pack, pack, edge, edge,
            array((groups_y, 2, 3 * share, 1, points), f32),
        ),
        in_specs=[WHOLE] * 10 + [SCALAR] + [WHOLE] * 3,
        out_specs=(WHOLE,) + (ANYWHERE,) * 3 + (WHOLE,) * 5,
        input_output_aliases={0: 0},
        scratch_shapes=[pltpu.SemaphoreType.DMA, record_sems, record_sems],
        compiler_params=params(),
        cost_estimate=cost(2 * 10**9, 4 * size),
        name="spread_sample",
    )(
        resident(section), inflow, *ghosts_a[:2], *own_a, *ghosts_a[2:],
        plan, weight_y, weight_z, strength,
    )
    shares = lax.all_to_all(shares, "gy", 0, 0)
    ghosts_b = exchange(*own_b)

    following, token = pl.pallas_call(
        advance_second,
        out_shape=(stored, array((SUB, LANES), f32)),
        in_specs=[ANYWHERE] * 2,
        out_specs=(ANYWHERE, WHOLE),
        scratch_shapes=[pltpu.VMEM(whole, f32)] * 3 + [chunk_sems] * 3,
        compiler_params=params(VMEM_LIMIT + 3 * size),
        cost_estimate=cost(10**9, 4 * size),
        name="advance_second",
    )(streamed(section), streamed(velocity))

    forces = pl.pallas_call(
        share_force,
        out_shape=array((groups_y, 3 * share, 1, points), f32),
        in_specs=[WHOLE, WHOLE, SCALAR] + [ANYWHERE] * 3,
        out_specs=WHOLE,
        compiler_params=params(),
        cost_estimate=cost(10**6, 10**6),
        name="share_force",
    )(shares, strength, counts, token, *ghosts_b[:2])
    all_forces = lax.all_to_all(forces, "gy", 0, 0)

    velocity_next = pl.pallas_call(
        spread_next,
        out_shape=stored,
        in_specs=[ANYWHERE] + [WHOLE] * 9 + [SCALAR, ANYWHERE, ANYWHERE, WHOLE, ANYWHERE],
        out_specs=ANYWHERE,
        scratch_shapes=[
            pltpu.VMEM(whole, f32),
            pltpu.VMEM(y_shape, f32),
            pltpu.VMEM(z_shape, jnp.bfloat16),
            chunk_sems, chunk_sems, record_sems, record_sems,
        ],
        compiler_params=params(VMEM_LIMIT + size + y_bytes + z_bytes),
        cost_estimate=cost(2 * 10**9, 4 * size),
        name="spread_next",
    )(
        streamed(following), inflow, *ghosts_b[:2], *own_b, *ghosts_b[2:],
        plan, streamed(stored_y), streamed(stored_z), strength, forces,
    )
    return (velocity_next, all_forces.reshape(1, records, 3, points))


def solution(mesh):
    return jax.shard_map(
        local,
        mesh=mesh,
        in_specs=(
            P(None, "gx", "gy", None),
            P(None, "gy", None),
            P("gx", None, None, None),
            P("gx", None, None),
            P("gx", None, None),
            P("gx"),
        ),
        out_specs=(P(None, "gx", "gy", None), P("gx", None, None, None)),
        check_vma=False,
    )
```

```python
import math

import jax
import jax.numpy as jnp
from jax import lax
from jax.experimental import pallas as pl
from jax.experimental.pallas import tpu as pltpu
from jax.sharding import PartitionSpec as P

RAD = 2
VISCOSITY = 0.05
TIME_STEP = 0.1
WIDTH_EPS = 1.5
ROOT_PI = 1.7724538509055159
TAP = [math.exp(-((d / WIDTH_EPS) ** 2)) / (WIDTH_EPS * ROOT_PI) for d in range(RAD + 1)]
HIGH = [float(jnp.bfloat16(tap)) for tap in TAP]
LOW = [float(jnp.bfloat16(tap - high)) for tap, high in zip(TAP, HIGH)]
LANES = 128
SUB = 8
PACKED = 32
BATCH = 4
VMEM_LIMIT = 5 * 2**20

WHOLE = pl.BlockSpec(memory_space=pltpu.VMEM)
SCALAR = pl.BlockSpec(memory_space=pltpu.SMEM)
ANYWHERE = pl.BlockSpec(memory_space=pl.ANY)


def params(limit=VMEM_LIMIT):
    return pltpu.CompilerParams(vmem_limit_bytes=limit)


def cost(flops, nbytes):
    return pl.CostEstimate(flops=flops, bytes_accessed=nbytes, transcendentals=0)


def resident(x):
    return pltpu.with_memory_space_constraint(x, pltpu.VMEM)


def streamed(x):
    return pltpu.with_memory_space_constraint(x, pltpu.HBM)


def split(x):
    high = x.astype(jnp.bfloat16)
    low = (x - high.astype(jnp.float32)).astype(jnp.bfloat16)
    return jnp.concatenate([high, low], axis=0)


def along_z(point_z, start):
    points = point_z.shape[-1]
    row = lax.broadcasted_iota(jnp.int32, (PACKED, points), 0).astype(jnp.bfloat16)
    place = (point_z - start).astype(jnp.float32)
    place = jnp.broadcast_to(place, (PACKED, points)).astype(jnp.bfloat16)
    dist = jnp.abs(row - place)
    near = [dist == float(d) for d in range(RAD + 1)]
    out = []
    for taps in (HIGH, LOW):
        value = jnp.zeros_like(row)
        for d in range(RAD, -1, -1):
            value = jnp.where(near[d], jnp.full_like(row, taps[d]), value)
        out.append(value)
    return out


def wrapped(point_y, base, total_y):
    near = point_y - base
    near = jnp.where(near > total_y // 2, near - total_y, near)
    return jnp.where(near < -(total_y // 2), near + total_y, near)


def along_y(point_y, base, cells_y, total_y):
    near = wrapped(point_y, base, total_y)
    dist = jnp.abs(lax.broadcasted_iota(jnp.int32, (cells_y, point_y.shape[-1]), 0) - near)
    return jnp.where(
        dist == 0, TAP[0], jnp.where(dist == 1, TAP[1], jnp.where(dist == 2, TAP[2], 0.0))
    )


def make_plan(hubs, tiles, touch, counts, start, plan, bucket, held):
    tile_y, groups_y = lax.axis_index("gy"), lax.axis_size("gy")
    records, chunks = tiles.shape[1], held.shape[0]
    for k in range(chunks):
        held[k] = 0

    def place(r, carry):
        offset = tile_y - tiles[0, r]
        offset = jnp.where(offset < 0, offset + groups_y, offset)

        @pl.when(jnp.logical_and(offset < tiles[1, r], touch[r, 1] >= 0))
        def _():
            k = (hubs[r, 0] - start + RAD) // SUB
            bucket[k, held[k]] = r
            held[k] = held[k] + 1

        return carry

    lax.fori_loop(0, jnp.minimum(counts[0], records), place, 0)

    def flatten(k, found):
        def move(j, found):
            r = bucket[k, j]
            plan[1 + found] = r
            plan[1 + records + found] = hubs[r, 0] - start
            return found + 1

        return lax.fori_loop(0, held[k], move, found)

    plan[0] = lax.fori_loop(0, chunks, flatten, jnp.int32(0))


def pair(plan, t):
    records = (plan.shape[0] - 1) // 2
    first = 2 * t
    second = jnp.minimum(first + 1, plan[0] - 1)
    return [(n, plan[1 + n], plan[1 + records + n]) for n in (first, second)], second > first


def sampled_rows(field, weight_y, weight_z, picks):
    cells_y = field.shape[2]
    rows = 3 * cells_y
    parts = []
    for t, r, hub in picks:
        planes = []
        for c in range(3):
            plane = TAP[0] * field[c, hub]
            plane += TAP[1] * (field[c, hub - 1] + field[c, hub + 1])
            plane += TAP[2] * (field[c, hub - 2] + field[c, hub + 2])
            planes.append(plane)
        parts.append(split(jnp.concatenate(planes, axis=0)))
    out = []
    for (t, r, hub), part in zip(picks, parts):
        picked = jnp.dot(part, weight_z[t, 0], preferred_element_type=jnp.float32)
        rest = jnp.dot(part[:rows], weight_z[t, 1], preferred_element_type=jnp.float32)
        picked = picked[:rows] + (picked[rows:] + rest)
        weight = weight_y[t]
        out.append(
            [
                jnp.sum(picked[c * cells_y : (c + 1) * cells_y] * weight, axis=0, keepdims=True)
                for c in range(3)
            ]
        )
    return out


def pack_edges(field, edge_west, edge_east, pack_low, pack_high):
    cells_x, cells_y, depth = field.shape[1:]
    for c in range(3):
        edge_west[c] = field[c, 0]
        edge_east[c] = field[c, cells_x - 1]

    def step(t, carry):
        cells = [(c, t * BATCH + k) for k in range(BATCH) for c in range(3)]
        rows = [
            (field[c, i, pl.ds(0, 1), :], field[c, i, pl.ds(cells_y - 1, 1), :]) for c, i in cells
        ]
        for (c, i), (low, high) in zip(cells, rows):
            pack_low[c * cells_x + i] = low
            pack_high[c * cells_x + i] = high
        return carry

    lax.fori_loop(0, cells_x // BATCH, step, 0)


def load_sample(
    velocity, positions, tiles_hbm, coefs_hbm, counts,
    field, pack_low, pack_high, edge_west, edge_east, weight_y, weight_z, strength, plan,
    point_y, point_z, hubs, tiles, places, coefs, flags, touch, bucket, held, small_sems, touch_sem, sems,
):
    cells_x, cells_y, depth = field.shape[1:]
    records, points = coefs.shape
    chunks = cells_x // SUB
    first_row = 3 * cells_x
    start = lax.axis_index("gx") * cells_x

    def chunk(k):
        planes = pl.ds(k * SUB, SUB)
        return pltpu.make_async_copy(velocity.at[:, planes], field.at[:, planes], sems.at[k])

    small = [
        (positions.at[pl.ds(1, 2)], places),
        (positions.at[0, :, pl.ds(0, LANES)], hubs),
        (tiles_hbm, tiles),
        (coefs_hbm, coefs),
    ]
    small = [
        pltpu.make_async_copy(source, target, small_sems.at[n])
        for n, (source, target) in enumerate(small)
    ]
    total_y = cells_y * lax.axis_size("gy")
    base = lax.axis_index("gy") * cells_y
    for copy in small:
        copy.start()
    for k in range(chunks):
        chunk(k).start()
    small[0].wait()
    near = wrapped(places[0], base, total_y)
    inside = jnp.logical_and(near >= -RAD, near < cells_y + RAD)
    height = places[1].astype(jnp.float32)
    lowest = jnp.min(jnp.where(inside, height, float(depth)), axis=1, keepdims=True)
    highest = jnp.max(jnp.where(inside, height, -1.0), axis=1, keepdims=True)
    column = lax.broadcasted_iota(jnp.int32, flags.shape, 1)
    flags[...] = jnp.where(column == 0, lowest, highest).astype(jnp.int32)
    touch_copy = pltpu.make_async_copy(flags, touch, touch_sem)
    touch_copy.start()

    def clear(n, carry):
        for k in range(SUB):
            pack_low[first_row + n * SUB + k] = jnp.zeros((1, points), jnp.float32)
            pack_high[first_row + n * SUB + k] = jnp.zeros((1, points), jnp.float32)
        return carry

    lax.fori_loop(0, 3 * records // SUB, clear, 0)
    for copy in small[1:]:
        copy.wait()
    for first in range(0, records, SUB):
        here = range(first, first + SUB)
        rows = [
            (places[0, pl.ds(r, 1), :], places[1, pl.ds(r, 1), :], coefs[pl.ds(r, 1), :])
            for r in here
        ]
        for r, (y, z, coef) in zip(here, rows):
            point_y[r], point_z[r], strength[r] = y, z, coef
    touch_copy.wait()
    make_plan(hubs, tiles, touch, counts, start, plan, bucket, held)

    def weigh(t, carry):
        r = plan[1 + t]
        weight_y[t] = along_y(point_y[r], base, cells_y, total_y)
        weight_z[t] = jnp.zeros(weight_z.shape[1:], weight_z.dtype)

        def block(k, carry):
            rows = pl.ds(pl.multiple_of(k * PACKED, PACKED), PACKED)
            weight_z[t, 0, rows], weight_z[t, 1, rows] = along_z(point_z[r], k * PACKED)
            return carry

        first = (touch[r, 0] - RAD) // PACKED
        lax.fori_loop(first, (touch[r, 1] + RAD) // PACKED + 1, block, 0)
        return carry

    lax.fori_loop(0, plan[0], weigh, 0)

    def wait_to(ready, wanted):
        def step(k, carry):
            chunk(k).wait()
            return carry

        lax.fori_loop(ready, wanted, step, 0)
        return jnp.maximum(ready, wanted)

    def step(t, ready):
        picks, _ = pair(plan, t)
        ready = wait_to(ready, (picks[1][2] + RAD) // SUB + 1)
        for (_, r, _), rows in zip(picks, sampled_rows(field, weight_y, weight_z, picks)):
            for c in range(3):
                pack_low[first_row + 3 * r + c] = rows[c]
                pack_high[first_row + 3 * r + c] = rows[c]
        return ready

    ready = lax.fori_loop(0, (plan[0] + 1) // 2, step, jnp.int32(0))
    wait_to(ready, chunks)
    pack_edges(field, edge_west, edge_east, pack_low, pack_high)


def fix_west(factor, target, own, inflow, ghost):
    first = lax.axis_index("gx") == 0
    for c in range(3):
        west = jnp.where(first, inflow[c], ghost[c])
        coef = factor * TIME_STEP * VISCOSITY + (0.5 * factor * TIME_STEP) * own[0]
        target[c, 0] = target[c, 0] + (west - own[c]) * coef


def fix_east(factor, target, own, ghost):
    last = lax.axis_index("gx") == lax.axis_size("gx") - 1
    end = target.shape[1] - 1
    for c in range(3):
        east = jnp.where(last, own[c], ghost[c])
        coef = factor * TIME_STEP * VISCOSITY - (0.5 * factor * TIME_STEP) * own[0]
        target[c, end] = target[c, end] + (east - own[c]) * coef


def fix_rows(factor, target, own_low, own_high, got_low, got_high, t):
    cells_x, cells_y = target.shape[1:3]
    spread = factor * TIME_STEP * VISCOSITY
    half = 0.5 * factor * TIME_STEP
    shape = (SUB, target.shape[3])
    row = lax.broadcasted_iota(jnp.int32, shape, 0)
    low, high = pl.ds(0, SUB), pl.ds(cells_y - SUB, SUB)

    def wide(x):
        return jnp.broadcast_to(x, shape)

    for first in range(0, SUB, 2):
        values = []
        for k in range(first, first + 2):
            i = t * SUB + k
            south = jnp.where(row == 0, spread + half * wide(own_low[cells_x + i]), 0.0)
            north = jnp.where(row == SUB - 1, spread - half * wide(own_high[cells_x + i]), 0.0)
            for c in range(3):
                n = c * cells_x + i
                values.append((c, i, low, target[c, i, low, :] + wide(got_low[n]) * south))
                values.append((c, i, high, target[c, i, high, :] + wide(got_high[n]) * north))
        for c, i, rows, value in values:
            target[c, i, rows, :] = value


def slabs_of(weight_y, weight_z, strength, own, low, high, cells, scales, picks):
    cells_x, cells_y, depth = cells
    count = 3 * cells_y
    across = (((1,), (1,)), ((), ()))
    spread = []
    for (t, r, hub), scale in zip(picks, scales):
        rows = [3 * cells_x + 3 * r + c for c in range(3)]
        total = [own[n] + (low[n] + high[n]) for n in rows]
        speed = jnp.sqrt(total[0] * total[0] + total[1] * total[1] + total[2] * total[2])
        pull = strength[r] * (-scale) * speed
        weight = weight_y[t]
        spread.append(split(jnp.concatenate([weight * (pull * x) for x in total], axis=0)))
    slabs = []
    for (t, r, hub), part in zip(picks, spread):
        slab = lax.dot_general(part, weight_z[t, 0], across, preferred_element_type=jnp.float32)
        rest = lax.dot_general(
            part[:count], weight_z[t, 1], across, preferred_element_type=jnp.float32
        )
        slabs.append(slab[:count] + (slab[count:] + rest))
    return slabs


def add_slab(field, slab, hub):
    cells_y = field.shape[2]
    for c in range(3):
        part = slab[c * cells_y : (c + 1) * cells_y]
        terms = [tap * part for tap in TAP]
        reach = range(-RAD, RAD + 1)
        values = [field[c, hub + d] + terms[abs(d)] for d in reach]
        for d, value in zip(reach, values):
            field[c, hub + d] = value


def spread_pair(t, scale, field, plan, points, own, low, high):
    picks, both = pair(plan, t)
    scales = [scale, jnp.where(both, scale, 0.0)]
    slabs = slabs_of(*points, own, low, high, field.shape[1:], scales, picks)
    for (_, _, hub), slab in zip(picks, slabs):
        add_slab(field, slab, hub)


def spread_sample(
    section_in, inflow, ghost_low, ghost_high, own_low, own_high, own_west, own_east, got_low, got_high,
    plan, weight_y, weight_z, strength,
    section, section_out, stored_y, stored_z, pack_low, pack_high, edge_west, edge_east,
    share_out, sem, sem_y, sem_z,
):
    cells_x = section.shape[1]
    records = strength.shape[0]
    share = share_out.shape[2] // 3
    first_row = 3 * cells_x

    def copies(t):
        return (
            pltpu.make_async_copy(weight_y.at[t], stored_y.at[t], sem_y.at[t]),
            pltpu.make_async_copy(weight_z.at[t], stored_z.at[t], sem_z.at[t]),
        )

    def start_store(t, carry):
        for copy in copies(t):
            copy.start()
        return carry

    def wait_store(t, carry):
        for copy in copies(t):
            copy.wait()
        return carry

    lax.fori_loop(0, plan[0], start_store, 0)

    def fix_step(t, carry):
        fix_rows(1.0, section, own_low, own_high, got_low, got_high, t)
        return carry

    fix_west(1.0, section, own_west, inflow, ghost_low)
    fix_east(1.0, section, own_east, ghost_high)
    lax.fori_loop(0, cells_x // SUB, fix_step, 0)

    def spread_step(t, carry):
        points = (weight_y, weight_z, strength)
        spread_pair(t, TIME_STEP, section, plan, points, own_low, got_low, got_high)
        return carry

    lax.fori_loop(0, (plan[0] + 1) // 2, spread_step, 0)
    copy = pltpu.make_async_copy(section, section_out, sem)
    copy.start()
    pack_edges(section, edge_west, edge_east, pack_low, pack_high)

    def clear(r, carry):
        rows = [own_low[first_row + 3 * r + c] for c in range(3)]
        zero = jnp.zeros_like(rows[0])
        for c in range(3):
            pack_low[first_row + 3 * r + c] = zero
            pack_high[first_row + 3 * r + c] = zero
            share_out[r // share, 0, 3 * (r % share) + c] = rows[c]
            share_out[r // share, 1, 3 * (r % share) + c] = zero
        return carry

    lax.fori_loop(0, records, clear, 0)

    def sample_step(t, carry):
        picks, _ = pair(plan, t)
        for (_, r, _), rows in zip(picks, sampled_rows(section, weight_y, weight_z, picks)):
            for c in range(3):
                pack_low[first_row + 3 * r + c] = rows[c]
                pack_high[first_row + 3 * r + c] = rows[c]
                share_out[r // share, 1, 3 * (r % share) + c] = rows[c]
        return carry

    lax.fori_loop(0, (plan[0] + 1) // 2, sample_step, 0)
    lax.fori_loop(0, plan[0], wait_store, 0)
    copy.wait()


def share_force(parts, strength, counts, after, after_low, after_high, result):
    groups, _, rows = parts.shape[:3]
    share = rows // 3
    mine = lax.axis_index("gy") * share
    values = []
    for s in range(share):
        live = mine + s < counts[0]
        pull = jnp.where(live, -0.5 * strength[mine + s], 0.0)
        total = [0.0, 0.0, 0.0]
        for stage in range(2):
            value = []
            for c in range(3):
                n = 3 * s + c
                x = parts[0, stage, n]
                for g in range(1, groups):
                    x += parts[g, stage, n]
                value.append(x)
            speed = jnp.sqrt(value[0] * value[0] + value[1] * value[1] + value[2] * value[2])
            total = [acc + speed * x for acc, x in zip(total, value)]
        values.extend((3 * s + c, pull * total[c]) for c in range(3))
        if s % 2 == 1 or s + 1 == share:
            for n, value in values:
                for g in range(groups):
                    result[g, n] = value
            values = []


def spread_next(
    following, inflow, ghost_low, ghost_high, own_low, own_high, own_west, own_east, got_low, got_high,
    plan, stored_y, stored_z, strength, after,
    result, field, weight_y, weight_z, in_sems, out_sems, sem_y, sem_z,
):
    chunks = field.shape[1] // SUB
    factor = 0.5

    def chunk_in(k):
        planes = pl.ds(k * SUB, SUB)
        return pltpu.make_async_copy(following.at[:, planes], field.at[:, planes], in_sems.at[k])

    def chunk_out(k):
        planes = pl.ds(k * SUB, SUB)
        return pltpu.make_async_copy(field.at[:, planes], result.at[:, planes], out_sems.at[k])

    def wait_to(ready, wanted):
        def step(k, carry):
            chunk_in(k).wait()
            fix_rows(factor, field, own_low, own_high, got_low, got_high, k)

            @pl.when(k == 0)
            def _():
                fix_west(factor, field, own_west, inflow, ghost_low)

            @pl.when(k == chunks - 1)
            def _():
                fix_east(factor, field, own_east, ghost_high)

            return carry

        lax.fori_loop(ready, wanted, step, 0)
        return jnp.maximum(ready, wanted)

    def send_to(sent, done):
        def step(k, carry):
            chunk_out(k).start()
            return carry

        lax.fori_loop(sent, done, step, 0)
        return jnp.maximum(sent, done)

    def weights(t):
        return (
            pltpu.make_async_copy(stored_y.at[t], weight_y.at[t], sem_y.at[t]),
            pltpu.make_async_copy(stored_z.at[t], weight_z.at[t], sem_z.at[t]),
        )

    def start_weights(t, carry):
        for copy in weights(t):
            copy.start()
        return carry

    found = plan[0]
    for k in range(chunks):
        chunk_in(k).start()
        lax.fori_loop(k * found // chunks, (k + 1) * found // chunks, start_weights, 0)

    def step(t, carry):
        ready, sent = carry
        picks, both = pair(plan, t)
        for copy in weights(picks[0][0]):
            copy.wait()

        @pl.when(both)
        def _():
            for copy in weights(picks[1][0]):
                copy.wait()

        ready = wait_to(ready, (picks[1][2] + RAD) // SUB + 1)
        sent = send_to(sent, (picks[0][2] + RAD) // SUB - 1)
        points = (weight_y, weight_z, strength)
        spread_pair(t, factor * TIME_STEP, field, plan, points, own_low, got_low, got_high)
        return ready, sent

    zero = jnp.int32(0)
    ready, sent = lax.fori_loop(0, (plan[0] + 1) // 2, step, (zero, zero))
    sent = send_to(sent, ready)

    def finish(k, carry):
        wait_to(k, k + 1)
        chunk_out(k).start()
        return carry

    lax.fori_loop(ready, chunks, finish, 0)
    for k in range(chunks):
        chunk_out(k).wait()


def fill_shifts(shifts):
    depth = shifts.shape[1]
    source = lax.broadcasted_iota(jnp.int32, (depth, depth), 0)
    cell = lax.broadcasted_iota(jnp.int32, (depth, depth), 1)
    upper = jnp.where(source == cell + 1, 1.0, 0.0)
    lower = jnp.where(source == cell - 1, 1.0, 0.0)
    difference = (upper - lower).astype(shifts.dtype)
    shifts[0:depth] = difference
    shifts[depth : 2 * depth] = difference
    shifts[2 * depth : 3 * depth] = (upper + lower).astype(shifts.dtype)


def along_depth(i, field, shifts, slot):
    depth = shifts.shape[1]
    x = jnp.concatenate([field[c, i + k] for k in range(2) for c in range(3)], axis=0)
    high = x.astype(jnp.bfloat16)
    low = (x - high.astype(jnp.float32)).astype(jnp.bfloat16)
    slot[0] = jnp.dot(
        jnp.concatenate([high, low], axis=1),
        shifts[0 : 2 * depth],
        preferred_element_type=jnp.float32,
    )
    slot[1] = jnp.dot(
        high, shifts[2 * depth : 3 * depth], preferred_element_type=jnp.float32
    )


def advance(i, k, factor, field, slot, target, finish):
    cells_x, cells_y, depth = field.shape[1:]
    groups, halves = cells_y // SUB, depth // LANES
    row = lax.broadcasted_iota(jnp.int32, (SUB, LANES), 0)
    first_row, last_row = row == 0, row == SUB - 1
    spread = factor * TIME_STEP * VISCOSITY
    centre = factor * (1.0 - 6.0 * TIME_STEP * VISCOSITY)
    zero = jnp.zeros((SUB, LANES), jnp.float32)
    loaded = {}
    here = i + k
    west, east = jnp.maximum(here - 1, 0), jnp.minimum(here + 1, cells_x - 1)

    def at(c, g, h):
        if (c, g, h) not in loaded:
            loaded[c, g, h] = field[c, here, pl.ds(g * SUB, SUB), pl.ds(h * LANES, LANES)]
        return loaded[c, g, h]

    values = []
    for g in range(groups):
        for h in range(halves):
            rows, cols = pl.ds(g * SUB, SUB), pl.ds(h * LANES, LANES)
            q = [at(c, g, h) for c in range(3)]
            speeds = [(0.5 * factor * TIME_STEP) * x for x in q]
            less = [spread - s for s in speeds[:2]]
            more = [spread + s for s in speeds[:2]]
            if g == 0:
                more[1] = jnp.where(first_row, zero, more[1])
            if g == groups - 1:
                less[1] = jnp.where(last_row, zero, less[1])
            for c in range(3):
                x = q[c]
                above, below = x, x
                if g + 1 < groups:
                    above = jnp.where(first_row, at(c, g + 1, h), x)
                if g > 0:
                    below = jnp.where(last_row, at(c, g - 1, h), x)
                above, below = pltpu.roll(above, SUB - 1, 0), pltpu.roll(below, 1, 0)
                place = pl.ds((3 * k + c) * cells_y + g * SUB, SUB)
                total = centre * x
                total += field[c, east, rows, cols] * less[0]
                total += field[c, west, rows, cols] * more[0]
                total += above * less[1] + below * more[1]
                total += spread * slot[1, place, cols] - speeds[2] * slot[0, place, cols]
                values.append((c, rows, cols, finish(c, here, rows, cols, total)))
        if g % 2 == 1 or g + 1 == groups:
            for c, rows, cols, value in values:
                target[c, here, rows, cols] = value
            values = []


def advance_four(i, factor, field, shifts, slots, target, finish):
    last = field.shape[1] - 2
    for n in range(2):
        now, later = slots[n], slots[1 - n]
        along_depth(jnp.minimum(i + 2, last), field, shifts, later)
        for k in range(2):
            advance(i, k, factor, field, now, target, finish)
        i = i + 2


def advance_first(field, section, shifts, slot_a, slot_b):
    fill_shifts(shifts)
    along_depth(0, field, shifts, slot_a)

    def step(t, carry):
        advance_four(
            4 * t, 1.0, field, shifts, (slot_a, slot_b), section,
            lambda c, i, rows, cols, value: value,
        )
        return carry

    lax.fori_loop(0, field.shape[1] // 4, step, 0)


def advance_second(
    section_hbm, velocity, following, token,
    section, field, result, shifts, slot_a, slot_b, in_sems, old_sems, out_sems,
):
    chunks = section.shape[1] // SUB

    def planes(k):
        return pl.ds(k * SUB, SUB)

    def chunk_in(k):
        return pltpu.make_async_copy(
            section_hbm.at[:, planes(k)], section.at[:, planes(k)], in_sems.at[k]
        )

    def chunk_old(k):
        return pltpu.make_async_copy(
            velocity.at[:, planes(k)], field.at[:, planes(k)], old_sems.at[k]
        )

    def chunk_out(k):
        return pltpu.make_async_copy(
            result.at[:, planes(k)], following.at[:, planes(k)], out_sems.at[k]
        )

    def finish(c, i, rows, cols, value):
        return value + 0.5 * field[c, i, rows, cols]

    for k in range(chunks):
        chunk_in(k).start()
        chunk_old(k).start()
    token[...] = jnp.zeros_like(token)
    fill_shifts(shifts)
    chunk_in(0).wait()
    along_depth(0, section, shifts, slot_a)

    def step(k, carry):
        @pl.when(k + 1 < chunks)
        def _():
            chunk_in(k + 1).wait()

        chunk_old(k).wait()
        for n in range(0, SUB, 4):
            advance_four(
                k * SUB + n, 0.5, section, shifts, (slot_a, slot_b), result, finish
            )
        chunk_out(k).start()
        return carry

    lax.fori_loop(0, chunks, step, 0)
    for k in range(chunks):
        chunk_out(k).wait()


def shifted(x, axis, step, periodic):
    count = lax.axis_size(axis)
    pairs = [(i, (i + step) % count) for i in range(count)]
    if not periodic:
        pairs = [(s, t) for s, t in pairs if t - s == step]
    return lax.ppermute(x, axis, pairs)


def exchange(pack_low, pack_high, edge_west, edge_east):
    got_low = shifted(pack_high, "gy", 1, True)
    got_high = shifted(pack_low, "gy", -1, True)
    ghost_low = shifted(edge_east, "gx", 1, False)
    ghost_high = shifted(edge_west, "gx", -1, False)
    return ghost_low, ghost_high, got_low, got_high


def local(velocity, inflow, positions, tiles, coefs, counts):
    f32, i32 = jnp.float32, jnp.int32
    whole = velocity.shape
    _, cells_x, cells_y, depth = whole
    groups_y = lax.axis_size("gy")
    positions = positions[0].transpose(1, 0, 2)
    tiles, coefs = tiles[0].T, coefs[0]
    records, points = coefs.shape
    share = records // groups_y
    chunks = cells_x // SUB
    size = 4 * math.prod(whole)
    held = pltpu.VMEM(whole, f32)
    stored = pltpu.HBM(whole, f32)
    array = jax.ShapeDtypeStruct
    pack = array((3 * cells_x + 3 * records, 1, points), f32)
    edge = array((3, cells_y, depth), f32)
    per_record = (records, 1, points)
    y_shape, z_shape = (records, cells_y, points), (records, 2, depth, points)
    y_bytes, z_bytes = 4 * math.prod(y_shape), 2 * math.prod(z_shape)
    products = [pltpu.VMEM((3 * depth, depth), jnp.bfloat16)]
    products += [pltpu.VMEM((2, 6 * cells_y, depth), f32)] * 2
    record_sems = pltpu.SemaphoreType.DMA((records,))
    chunk_sems = pltpu.SemaphoreType.DMA((chunks,))

    field, *own_a, weight_y, weight_z, strength, plan = pl.pallas_call(
        load_sample,
        out_shape=(
            held, pack, pack, edge, edge,
            pltpu.VMEM(y_shape, f32), pltpu.VMEM(z_shape, jnp.bfloat16),
            array(per_record, f32),
            array((1 + 2 * records,), i32),
        ),
        in_specs=[ANYWHERE] * 4 + [SCALAR],
        out_specs=(WHOLE,) * 8 + (SCALAR,),
        scratch_shapes=[
            pltpu.VMEM(per_record, i32),
            pltpu.VMEM(per_record, i32),
            pltpu.SMEM((records, LANES), i32),
            pltpu.SMEM((2, records), i32),
            pltpu.VMEM((2, records, points), i32),
            pltpu.VMEM((records, points), f32),
            pltpu.VMEM((records, LANES), i32),
            pltpu.SMEM((records, LANES), i32),
            pltpu.SMEM((chunks, records), i32),
            pltpu.SMEM((chunks,), i32),
            pltpu.SemaphoreType.DMA((4,)),
            pltpu.SemaphoreType.DMA,
            chunk_sems,
        ],
        compiler_params=params(),
        cost_estimate=cost(2 * 10**9, 4 * size),
        name="load_sample",
    )(streamed(velocity), streamed(positions), streamed(tiles), streamed(coefs), counts)
    weight_y, weight_z = resident(weight_y), resident(weight_z)
    ghosts_a = exchange(*own_a)

    section = pl.pallas_call(
        advance_first,
        out_shape=held,
        in_specs=[WHOLE],
        out_specs=WHOLE,
        scratch_shapes=products,
        compiler_params=params(),
        cost_estimate=cost(10**9, 4 * size),
        name="advance_first",
    )(resident(field))

    _, section, stored_y, stored_z, *own_b, shares = pl.pallas_call(
        spread_sample,
        out_shape=(
            held, stored, pltpu.HBM(y_shape, f32), pltpu.HBM(z_shape, jnp.bfloat16),
            pack, pack, edge, edge,
            array((groups_y, 2, 3 * share, 1, points), f32),
        ),
        in_specs=[WHOLE] * 10 + [SCALAR] + [WHOLE] * 3,
        out_specs=(WHOLE,) + (ANYWHERE,) * 3 + (WHOLE,) * 5,
        input_output_aliases={0: 0},
        scratch_shapes=[pltpu.SemaphoreType.DMA, record_sems, record_sems],
        compiler_params=params(),
        cost_estimate=cost(2 * 10**9, 4 * size),
        name="spread_sample",
    )(
        resident(section), inflow, *ghosts_a[:2], *own_a, *ghosts_a[2:],
        plan, weight_y, weight_z, strength,
    )
    shares = lax.all_to_all(shares, "gy", 0, 0)
    ghosts_b = exchange(*own_b)

    following, token = pl.pallas_call(
        advance_second,
        out_shape=(stored, array((SUB, LANES), f32)),
        in_specs=[ANYWHERE] * 2,
        out_specs=(ANYWHERE, WHOLE),
        scratch_shapes=[pltpu.VMEM(whole, f32)] * 3 + products + [chunk_sems] * 3,
        compiler_params=params(VMEM_LIMIT + 3 * size),
        cost_estimate=cost(10**9, 4 * size),
        name="advance_second",
    )(streamed(section), streamed(velocity))

    forces = pl.pallas_call(
        share_force,
        out_shape=array((groups_y, 3 * share, 1, points), f32),
        in_specs=[WHOLE, WHOLE, SCALAR] + [ANYWHERE] * 3,
        out_specs=WHOLE,
        compiler_params=params(),
        cost_estimate=cost(10**6, 10**6),
        name="share_force",
    )(shares, strength, counts, token, *ghosts_b[:2])
    all_forces = lax.all_to_all(forces, "gy", 0, 0)

    velocity_next = pl.pallas_call(
        spread_next,
        out_shape=stored,
        in_specs=[ANYWHERE] + [WHOLE] * 9 + [SCALAR, ANYWHERE, ANYWHERE, WHOLE, ANYWHERE],
        out_specs=ANYWHERE,
        scratch_shapes=[
            pltpu.VMEM(whole, f32),
            pltpu.VMEM(y_shape, f32),
            pltpu.VMEM(z_shape, jnp.bfloat16),
            chunk_sems, chunk_sems, record_sems, record_sems,
        ],
        compiler_params=params(VMEM_LIMIT + size + y_bytes + z_bytes),
        cost_estimate=cost(2 * 10**9, 4 * size),
        name="spread_next",
    )(
        streamed(following), inflow, *ghosts_b[:2], *own_b, *ghosts_b[2:],
        plan, streamed(stored_y), streamed(stored_z), strength, forces,
    )
    return (velocity_next, all_forces.reshape(1, records, 3, points))


def solution(mesh):
    return jax.shard_map(
        local,
        mesh=mesh,
        in_specs=(
            P(None, "gx", "gy", None),
            P(None, "gy", None),
            P("gx", None, None, None),
            P("gx", None, None),
            P("gx", None, None),
            P("gx"),
        ),
        out_specs=(P(None, "gx", "gy", None), P("gx", None, None, None)),
        check_vma=False,
    )
```

```python
import math

import jax
import jax.numpy as jnp
from jax import lax
from jax.experimental import pallas as pl
from jax.experimental.pallas import tpu as pltpu
from jax.sharding import PartitionSpec as P

RAD = 2
VISCOSITY = 0.05
TIME_STEP = 0.1
WIDTH_EPS = 1.5
ROOT_PI = 1.7724538509055159
TAP = [math.exp(-((d / WIDTH_EPS) ** 2)) / (WIDTH_EPS * ROOT_PI) for d in range(RAD + 1)]
HIGH = [float(jnp.bfloat16(tap)) for tap in TAP]
LOW = [float(jnp.bfloat16(tap - high)) for tap, high in zip(TAP, HIGH)]
LANES = 128
SUB = 8
PACKED = 32
BATCH = 4
HEAD = 1
VMEM_LIMIT = 6 * 2**20

WHOLE = pl.BlockSpec(memory_space=pltpu.VMEM)
SCALAR = pl.BlockSpec(memory_space=pltpu.SMEM)
ANYWHERE = pl.BlockSpec(memory_space=pl.ANY)


def params(limit=VMEM_LIMIT):
    return pltpu.CompilerParams(vmem_limit_bytes=limit)


def cost(flops, nbytes):
    return pl.CostEstimate(flops=flops, bytes_accessed=nbytes, transcendentals=0)


def resident(x):
    return pltpu.with_memory_space_constraint(x, pltpu.VMEM)


def streamed(x):
    return pltpu.with_memory_space_constraint(x, pltpu.HBM)


def split(x):
    high = x.astype(jnp.bfloat16)
    low = (x - high.astype(jnp.float32)).astype(jnp.bfloat16)
    return jnp.concatenate([high, low], axis=0)


def along_z(point_z, start):
    points = point_z.shape[-1]
    row = lax.broadcasted_iota(jnp.int32, (PACKED, points), 0).astype(jnp.bfloat16)
    place = (point_z - start).astype(jnp.float32)
    place = jnp.broadcast_to(place, (PACKED, points)).astype(jnp.bfloat16)
    dist = jnp.abs(row - place)
    near = [dist == float(d) for d in range(RAD + 1)]
    out = []
    for taps in (HIGH, LOW):
        value = jnp.zeros_like(row)
        for d in range(RAD, -1, -1):
            value = jnp.where(near[d], jnp.full_like(row, taps[d]), value)
        out.append(value)
    return out


def wrapped(point_y, base, total_y):
    near = point_y - base
    near = jnp.where(near > total_y // 2, near - total_y, near)
    return jnp.where(near < -(total_y // 2), near + total_y, near)


def along_y(point_y, base, cells_y, total_y):
    near = wrapped(point_y, base, total_y)
    dist = jnp.abs(lax.broadcasted_iota(jnp.int32, (cells_y, point_y.shape[-1]), 0) - near)
    return jnp.where(
        dist == 0, TAP[0], jnp.where(dist == 1, TAP[1], jnp.where(dist == 2, TAP[2], 0.0))
    )


def make_plan(hubs, tiles, touch, counts, start, plan, bucket, held):
    tile_y, groups_y = lax.axis_index("gy"), lax.axis_size("gy")
    records, chunks = tiles.shape[1], held.shape[0]
    for k in range(chunks):
        held[k] = 0

    def place(r, carry):
        offset = tile_y - tiles[0, r]
        offset = jnp.where(offset < 0, offset + groups_y, offset)

        @pl.when(jnp.logical_and(offset < tiles[1, r], touch[r, 1] >= 0))
        def _():
            k = (hubs[r, 0] - start + RAD) // SUB
            bucket[k, held[k]] = r
            held[k] = held[k] + 1

        return carry

    lax.fori_loop(0, jnp.minimum(counts[0], records), place, 0)

    units = (plan.shape[0] - HEAD) // 3

    def flatten(k, found):
        def move(j, found):
            r = bucket[k, j]

            def add(half, found):
                plan[HEAD + found] = r
                plan[HEAD + units + found] = hubs[r, 0] - start
                plan[HEAD + 2 * units + found] = half
                return found + 1

            first = (touch[r, 0] - RAD) // LANES
            return lax.fori_loop(first, (touch[r, 1] + RAD) // LANES + 1, add, found)

        return lax.fori_loop(0, held[k], move, found)

    plan[0] = lax.fori_loop(0, chunks, flatten, jnp.int32(0))


def pair(plan, t):
    units = (plan.shape[0] - HEAD) // 3
    first = 2 * t
    second = jnp.minimum(first + 1, plan[0] - 1)
    picks = []
    for n in (first, second):
        record, hub, half = [plan[HEAD + k * units + n] for k in range(3)]
        picks.append((n, record, hub, pl.ds(pl.multiple_of(half * LANES, LANES), LANES)))
    return picks, second > first


def sampled_rows(field, weight_y, weight_z, picks):
    cells_y = field.shape[2]
    rows = 3 * cells_y
    parts = []
    for t, r, hub, cols in picks:
        planes = []
        for c in range(3):
            plane = TAP[0] * field[c, hub, :, cols]
            plane += TAP[1] * (field[c, hub - 1, :, cols] + field[c, hub + 1, :, cols])
            plane += TAP[2] * (field[c, hub - 2, :, cols] + field[c, hub + 2, :, cols])
            planes.append(plane)
        part = split(jnp.concatenate(planes, axis=0))
        parts.append(jnp.concatenate([part, part], axis=1))
    out = []
    for (t, r, hub, cols), part in zip(picks, parts):
        picked = jnp.dot(part, weight_z[t], preferred_element_type=jnp.float32)
        picked = picked[:rows] + picked[rows:]
        weight = weight_y[t]
        out.append(
            [
                jnp.sum(picked[c * cells_y : (c + 1) * cells_y] * weight, axis=0, keepdims=True)
                for c in range(3)
            ]
        )
    return out


def add_rows(pack, first_row, picks, sampled, both):
    for (t, r, hub, cols), rows, keep in zip(picks, sampled, (None, both)):
        for c in range(3):
            n = first_row + 3 * r + c
            value = rows[c] if keep is None else jnp.where(keep, rows[c], 0.0)
            pack[n] = pack[n] + value


def pack_edges(field, edge_west, edge_east, pack_low, pack_high):
    cells_x, cells_y, depth = field.shape[1:]
    for c in range(3):
        edge_west[c] = field[c, 0]
        edge_east[c] = field[c, cells_x - 1]

    def step(t, carry):
        cells = [(c, t * BATCH + k) for k in range(BATCH) for c in range(3)]
        rows = [
            (field[c, i, pl.ds(0, 1), :], field[c, i, pl.ds(cells_y - 1, 1), :]) for c, i in cells
        ]
        for (c, i), (low, high) in zip(cells, rows):
            pack_low[c * cells_x + i] = low
            pack_high[c * cells_x + i] = high
        return carry

    lax.fori_loop(0, cells_x // BATCH, step, 0)


def load_sample(
    velocity, positions, tiles_hbm, coefs_hbm, counts,
    field, pack_low, pack_high, edge_west, edge_east, weight_y, weight_z, strength, plan,
    point_y, point_z, hubs, tiles, places, coefs, flags, touch, bucket, held, small_sems, touch_sem, sems,
):
    cells_x, cells_y, depth = field.shape[1:]
    records, points = coefs.shape
    chunks = cells_x // SUB
    first_row = 3 * cells_x
    start = lax.axis_index("gx") * cells_x

    def chunk(k):
        planes = pl.ds(k * SUB, SUB)
        return pltpu.make_async_copy(velocity.at[:, planes], field.at[:, planes], sems.at[k])

    small = [
        (positions.at[pl.ds(1, 2)], places),
        (positions.at[0, :, pl.ds(0, LANES)], hubs),
        (tiles_hbm, tiles),
        (coefs_hbm, coefs),
    ]
    small = [
        pltpu.make_async_copy(source, target, small_sems.at[n])
        for n, (source, target) in enumerate(small)
    ]
    total_y = cells_y * lax.axis_size("gy")
    base = lax.axis_index("gy") * cells_y
    for copy in small:
        copy.start()
    for k in range(chunks):
        chunk(k).start()
    small[0].wait()
    near = wrapped(places[0], base, total_y)
    inside = jnp.logical_and(near >= -RAD, near < cells_y + RAD)
    height = places[1].astype(jnp.float32)
    lowest = jnp.min(jnp.where(inside, height, float(depth)), axis=1, keepdims=True)
    highest = jnp.max(jnp.where(inside, height, -1.0), axis=1, keepdims=True)
    column = lax.broadcasted_iota(jnp.int32, flags.shape, 1)
    flags[...] = jnp.where(column == 0, lowest, highest).astype(jnp.int32)
    touch_copy = pltpu.make_async_copy(flags, touch, touch_sem)
    touch_copy.start()

    def clear(n, carry):
        for k in range(SUB):
            pack_low[first_row + n * SUB + k] = jnp.zeros((1, points), jnp.float32)
        return carry

    lax.fori_loop(0, 3 * records // SUB, clear, 0)
    for copy in small[1:]:
        copy.wait()
    for first in range(0, records, SUB):
        here = range(first, first + SUB)
        rows = [
            (places[0, pl.ds(r, 1), :], places[1, pl.ds(r, 1), :], coefs[pl.ds(r, 1), :])
            for r in here
        ]
        for r, (y, z, coef) in zip(here, rows):
            point_y[r], point_z[r], strength[r] = y, z, coef
    touch_copy.wait()
    make_plan(hubs, tiles, touch, counts, start, plan, bucket, held)

    def weigh(t, carry):
        units = weight_z.shape[0]
        r, half = plan[HEAD + t], plan[HEAD + 2 * units + t]
        weight_y[t] = along_y(point_y[r], base, cells_y, total_y)
        weight_z[t] = jnp.zeros(weight_z.shape[1:], weight_z.dtype)

        def block(k, carry):
            rows = pl.ds(pl.multiple_of(k * PACKED, PACKED), PACKED)
            rest = pl.ds(pl.multiple_of(LANES + k * PACKED, PACKED), PACKED)
            high, low = along_z(point_z[r], half * LANES + k * PACKED)
            weight_z[t, rows] = high
            weight_z[t, rest] = low
            return carry

        blocks = LANES // PACKED
        first = (touch[r, 0] - RAD) // PACKED - half * blocks
        last = (touch[r, 1] + RAD) // PACKED - half * blocks
        lax.fori_loop(jnp.maximum(first, 0), jnp.minimum(last + 1, blocks), block, 0)
        return carry

    lax.fori_loop(0, plan[0], weigh, 0)

    def wait_to(ready, wanted):
        def step(k, carry):
            chunk(k).wait()
            return carry

        lax.fori_loop(ready, wanted, step, 0)
        return jnp.maximum(ready, wanted)

    def step(t, ready):
        picks, both = pair(plan, t)
        ready = wait_to(ready, (picks[1][2] + RAD) // SUB + 1)
        rows = sampled_rows(field, weight_y, weight_z, picks)
        add_rows(pack_low, first_row, picks, rows, both)
        return ready

    ready = lax.fori_loop(0, (plan[0] + 1) // 2, step, jnp.int32(0))
    wait_to(ready, chunks)

    def copy_rows(t, carry):
        rows = [first_row + t * SUB + k for k in range(SUB)]
        values = [pack_low[n] for n in rows]
        for n, value in zip(rows, values):
            pack_high[n] = value
        return carry

    lax.fori_loop(0, 3 * records // SUB, copy_rows, 0)
    pack_edges(field, edge_west, edge_east, pack_low, pack_high)


def fix_west(factor, target, own, inflow, ghost):
    first = lax.axis_index("gx") == 0
    for c in range(3):
        west = jnp.where(first, inflow[c], ghost[c])
        coef = factor * TIME_STEP * VISCOSITY + (0.5 * factor * TIME_STEP) * own[0]
        target[c, 0] = target[c, 0] + (west - own[c]) * coef


def fix_east(factor, target, own, ghost):
    last = lax.axis_index("gx") == lax.axis_size("gx") - 1
    end = target.shape[1] - 1
    for c in range(3):
        east = jnp.where(last, own[c], ghost[c])
        coef = factor * TIME_STEP * VISCOSITY - (0.5 * factor * TIME_STEP) * own[0]
        target[c, end] = target[c, end] + (east - own[c]) * coef


def fix_rows(factor, target, own_low, own_high, got_low, got_high, t):
    cells_x, cells_y = target.shape[1:3]
    spread = factor * TIME_STEP * VISCOSITY
    half = 0.5 * factor * TIME_STEP
    shape = (SUB, target.shape[3])
    row = lax.broadcasted_iota(jnp.int32, shape, 0)
    low, high = pl.ds(0, SUB), pl.ds(cells_y - SUB, SUB)

    def wide(x):
        return jnp.broadcast_to(x, shape)

    for first in range(0, SUB, 2):
        values = []
        for k in range(first, first + 2):
            i = t * SUB + k
            south = jnp.where(row == 0, spread + half * wide(own_low[cells_x + i]), 0.0)
            north = jnp.where(row == SUB - 1, spread - half * wide(own_high[cells_x + i]), 0.0)
            for c in range(3):
                n = c * cells_x + i
                values.append((c, i, low, target[c, i, low, :] + wide(got_low[n]) * south))
                values.append((c, i, high, target[c, i, high, :] + wide(got_high[n]) * north))
        for c, i, rows, value in values:
            target[c, i, rows, :] = value


def slabs_of(weight_y, weight_z, strength, own, low, high, cells, scales, picks):
    cells_x, cells_y, depth = cells
    count = 3 * cells_y
    across = (((1,), (1,)), ((), ()))
    spread = []
    for (t, r, hub, cols), scale in zip(picks, scales):
        rows = [3 * cells_x + 3 * r + c for c in range(3)]
        total = [own[n] + (low[n] + high[n]) for n in rows]
        speed = jnp.sqrt(total[0] * total[0] + total[1] * total[1] + total[2] * total[2])
        pull = strength[r] * (-scale) * speed
        weight = weight_y[t]
        spread.append(split(jnp.concatenate([weight * (pull * x) for x in total], axis=0)))
    slabs = []
    for (t, r, hub, cols), part in zip(picks, spread):
        slab = lax.dot_general(part, weight_z[t], across, preferred_element_type=jnp.float32)
        slab = slab[:count] + slab[count:]
        slabs.append(slab[:, :LANES] + slab[:, LANES:])
    return slabs


def add_slab(field, slab, hub, cols):
    cells_y = field.shape[2]
    for c in range(3):
        part = slab[c * cells_y : (c + 1) * cells_y]
        terms = [tap * part for tap in TAP]
        reach = range(-RAD, RAD + 1)
        values = [field[c, hub + d, :, cols] + terms[abs(d)] for d in reach]
        for d, value in zip(reach, values):
            field[c, hub + d, :, cols] = value


def spread_pair(t, scale, field, plan, points, own, low, high):
    picks, both = pair(plan, t)
    scales = [scale, jnp.where(both, scale, 0.0)]
    slabs = slabs_of(*points, own, low, high, field.shape[1:], scales, picks)
    for (_, _, hub, cols), slab in zip(picks, slabs):
        add_slab(field, slab, hub, cols)


def spread_sample(
    section_in, inflow, ghost_low, ghost_high, own_low, own_high, own_west, own_east, got_low, got_high,
    plan, weight_y, weight_z, strength,
    section, section_out, stored_y, stored_z, pack_low, pack_high, edge_west, edge_east,
    share_out, sem, sem_y, sem_z,
):
    cells_x = section.shape[1]
    records = strength.shape[0]
    share = share_out.shape[2] // 3
    first_row = 3 * cells_x

    def copies(t):
        return (
            pltpu.make_async_copy(weight_y.at[t], stored_y.at[t], sem_y.at[t]),
            pltpu.make_async_copy(weight_z.at[t], stored_z.at[t], sem_z.at[t]),
        )

    def start_store(t, carry):
        for copy in copies(t):
            copy.start()
        return carry

    def wait_store(t, carry):
        for copy in copies(t):
            copy.wait()
        return carry

    lax.fori_loop(0, plan[0], start_store, 0)

    def fix_step(t, carry):
        fix_rows(1.0, section, own_low, own_high, got_low, got_high, t)
        return carry

    fix_west(1.0, section, own_west, inflow, ghost_low)
    fix_east(1.0, section, own_east, ghost_high)
    lax.fori_loop(0, cells_x // SUB, fix_step, 0)

    def spread_step(t, carry):
        points = (weight_y, weight_z, strength)
        spread_pair(t, TIME_STEP, section, plan, points, own_low, got_low, got_high)
        return carry

    lax.fori_loop(0, (plan[0] + 1) // 2, spread_step, 0)
    copy = pltpu.make_async_copy(section, section_out, sem)
    copy.start()
    pack_edges(section, edge_west, edge_east, pack_low, pack_high)

    def clear(n, carry):
        for k in range(SUB):
            pack_low[first_row + n * SUB + k] = jnp.zeros_like(own_low[0])
        return carry

    lax.fori_loop(0, 3 * records // SUB, clear, 0)

    def sample_step(t, carry):
        picks, both = pair(plan, t)
        rows = sampled_rows(section, weight_y, weight_z, picks)
        add_rows(pack_low, first_row, picks, rows, both)
        return carry

    lax.fori_loop(0, (plan[0] + 1) // 2, sample_step, 0)

    def copy_rows(r, carry):
        old = [own_low[first_row + 3 * r + c] for c in range(3)]
        new = [pack_low[first_row + 3 * r + c] for c in range(3)]
        for c in range(3):
            pack_high[first_row + 3 * r + c] = new[c]
            share_out[r // share, 0, 3 * (r % share) + c] = old[c]
            share_out[r // share, 1, 3 * (r % share) + c] = new[c]
        return carry

    lax.fori_loop(0, records, copy_rows, 0)
    lax.fori_loop(0, plan[0], wait_store, 0)
    copy.wait()


def share_force(parts, strength, counts, after, after_low, after_high, result):
    groups, _, rows = parts.shape[:3]
    share = rows // 3
    mine = lax.axis_index("gy") * share
    values = []
    for s in range(share):
        live = mine + s < counts[0]
        pull = jnp.where(live, -0.5 * strength[mine + s], 0.0)
        total = [0.0, 0.0, 0.0]
        for stage in range(2):
            value = []
            for c in range(3):
                n = 3 * s + c
                x = parts[0, stage, n]
                for g in range(1, groups):
                    x += parts[g, stage, n]
                value.append(x)
            speed = jnp.sqrt(value[0] * value[0] + value[1] * value[1] + value[2] * value[2])
            total = [acc + speed * x for acc, x in zip(total, value)]
        values.extend((3 * s + c, pull * total[c]) for c in range(3))
        if s % 2 == 1 or s + 1 == share:
            for n, value in values:
                for g in range(groups):
                    result[g, n] = value
            values = []


def spread_next(
    following, inflow, ghost_low, ghost_high, own_low, own_high, own_west, own_east, got_low, got_high,
    plan, stored_y, stored_z, strength, after,
    result, field, weight_y, weight_z, in_sems, out_sems, sem_y, sem_z,
):
    chunks = field.shape[1] // SUB
    factor = 0.5

    def chunk_in(k):
        planes = pl.ds(k * SUB, SUB)
        return pltpu.make_async_copy(following.at[:, planes], field.at[:, planes], in_sems.at[k])

    def chunk_out(k):
        planes = pl.ds(k * SUB, SUB)
        return pltpu.make_async_copy(field.at[:, planes], result.at[:, planes], out_sems.at[k])

    def wait_to(ready, wanted):
        def step(k, carry):
            chunk_in(k).wait()
            fix_rows(factor, field, own_low, own_high, got_low, got_high, k)

            @pl.when(k == 0)
            def _():
                fix_west(factor, field, own_west, inflow, ghost_low)

            @pl.when(k == chunks - 1)
            def _():
                fix_east(factor, field, own_east, ghost_high)

            return carry

        lax.fori_loop(ready, wanted, step, 0)
        return jnp.maximum(ready, wanted)

    def send_to(sent, done):
        def step(k, carry):
            chunk_out(k).start()
            return carry

        lax.fori_loop(sent, done, step, 0)
        return jnp.maximum(sent, done)

    def weights(t):
        return (
            pltpu.make_async_copy(stored_y.at[t], weight_y.at[t], sem_y.at[t]),
            pltpu.make_async_copy(stored_z.at[t], weight_z.at[t], sem_z.at[t]),
        )

    def start_weights(t, carry):
        for copy in weights(t):
            copy.start()
        return carry

    found = plan[0]
    for k in range(chunks):
        chunk_in(k).start()
        lax.fori_loop(k * found // chunks, (k + 1) * found // chunks, start_weights, 0)

    def step(t, carry):
        ready, sent = carry
        picks, both = pair(plan, t)
        for copy in weights(picks[0][0]):
            copy.wait()

        @pl.when(both)
        def _():
            for copy in weights(picks[1][0]):
                copy.wait()

        ready = wait_to(ready, (picks[1][2] + RAD) // SUB + 1)
        sent = send_to(sent, (picks[0][2] + RAD) // SUB - 1)
        points = (weight_y, weight_z, strength)
        spread_pair(t, factor * TIME_STEP, field, plan, points, own_low, got_low, got_high)
        return ready, sent

    zero = jnp.int32(0)
    ready, sent = lax.fori_loop(0, (plan[0] + 1) // 2, step, (zero, zero))
    sent = send_to(sent, ready)

    def finish(k, carry):
        wait_to(k, k + 1)
        chunk_out(k).start()
        return carry

    lax.fori_loop(ready, chunks, finish, 0)
    for k in range(chunks):
        chunk_out(k).wait()


def fill_shifts(shifts):
    depth = shifts.shape[1]
    source = lax.broadcasted_iota(jnp.int32, (depth, depth), 0)
    cell = lax.broadcasted_iota(jnp.int32, (depth, depth), 1)
    upper = jnp.where(source == cell + 1, 1.0, 0.0)
    lower = jnp.where(source == cell - 1, 1.0, 0.0)
    difference = (upper - lower).astype(shifts.dtype)
    shifts[0:depth] = difference
    shifts[depth : 2 * depth] = difference
    shifts[2 * depth : 3 * depth] = (upper + lower).astype(shifts.dtype)


def along_depth(i, field, shifts, slot):
    depth = shifts.shape[1]
    x = jnp.concatenate([field[c, i + k] for k in range(BATCH) for c in range(3)], axis=0)
    high = x.astype(jnp.bfloat16)
    low = (x - high.astype(jnp.float32)).astype(jnp.bfloat16)
    slot[0] = jnp.dot(
        jnp.concatenate([high, low], axis=1),
        shifts[0 : 2 * depth],
        preferred_element_type=jnp.float32,
    )
    slot[1] = jnp.dot(
        high, shifts[2 * depth : 3 * depth], preferred_element_type=jnp.float32
    )


def advance(i, k, factor, field, slot, target, finish):
    cells_x, cells_y, depth = field.shape[1:]
    groups, halves = cells_y // SUB, depth // LANES
    row = lax.broadcasted_iota(jnp.int32, (SUB, LANES), 0)
    first_row, last_row = row == 0, row == SUB - 1
    spread = factor * TIME_STEP * VISCOSITY
    centre = factor * (1.0 - 6.0 * TIME_STEP * VISCOSITY)
    zero = jnp.zeros((SUB, LANES), jnp.float32)
    loaded = {}
    here = i + k
    west, east = jnp.maximum(here - 1, 0), jnp.minimum(here + 1, cells_x - 1)

    def at(c, g, h):
        if (c, g, h) not in loaded:
            loaded[c, g, h] = field[c, here, pl.ds(g * SUB, SUB), pl.ds(h * LANES, LANES)]
        return loaded[c, g, h]

    values = []
    for g in range(groups):
        for h in range(halves):
            rows, cols = pl.ds(g * SUB, SUB), pl.ds(h * LANES, LANES)
            q = [at(c, g, h) for c in range(3)]
            speeds = [(0.5 * factor * TIME_STEP) * x for x in q]
            less = [spread - s for s in speeds[:2]]
            more = [spread + s for s in speeds[:2]]
            if g == 0:
                more[1] = jnp.where(first_row, zero, more[1])
            if g == groups - 1:
                less[1] = jnp.where(last_row, zero, less[1])
            for c in range(3):
                x = q[c]
                above, below = x, x
                if g + 1 < groups:
                    above = jnp.where(first_row, at(c, g + 1, h), x)
                if g > 0:
                    below = jnp.where(last_row, at(c, g - 1, h), x)
                above, below = pltpu.roll(above, SUB - 1, 0), pltpu.roll(below, 1, 0)
                place = pl.ds((3 * k + c) * cells_y + g * SUB, SUB)
                total = centre * x
                total += field[c, east, rows, cols] * less[0]
                total += field[c, west, rows, cols] * more[0]
                total += above * less[1] + below * more[1]
                total += spread * slot[1, place, cols] - speeds[2] * slot[0, place, cols]
                values.append((c, rows, cols, finish(c, here, rows, cols, total)))
        if g % 2 == 1 or g + 1 == groups:
            for c, rows, cols, value in values:
                target[c, here, rows, cols] = value
            values = []


def advance_chunk(i, factor, field, shifts, slots, target, finish):
    last = field.shape[1] - BATCH
    for n in range(SUB // BATCH):
        now, later = slots[n % 2], slots[1 - n % 2]
        along_depth(jnp.minimum(i + BATCH, last), field, shifts, later)
        for k in range(BATCH):
            advance(i, k, factor, field, now, target, finish)
        i = i + BATCH


def advance_first(field, section, shifts, slot_a, slot_b):
    fill_shifts(shifts)
    along_depth(0, field, shifts, slot_a)

    def step(t, carry):
        advance_chunk(
            SUB * t, 1.0, field, shifts, (slot_a, slot_b), section,
            lambda c, i, rows, cols, value: value,
        )
        return carry

    lax.fori_loop(0, field.shape[1] // SUB, step, 0)


def advance_second(
    section_hbm, velocity, following, token,
    section, field, result, shifts, slot_a, slot_b, in_sems, old_sems, out_sems,
):
    chunks = section.shape[1] // SUB

    def planes(k):
        return pl.ds(k * SUB, SUB)

    def chunk_in(k):
        return pltpu.make_async_copy(
            section_hbm.at[:, planes(k)], section.at[:, planes(k)], in_sems.at[k]
        )

    def chunk_old(k):
        return pltpu.make_async_copy(
            velocity.at[:, planes(k)], field.at[:, planes(k)], old_sems.at[k]
        )

    def chunk_out(k):
        return pltpu.make_async_copy(
            result.at[:, planes(k)], following.at[:, planes(k)], out_sems.at[k]
        )

    def finish(c, i, rows, cols, value):
        return value + 0.5 * field[c, i, rows, cols]

    for k in range(chunks):
        chunk_in(k).start()
        chunk_old(k).start()
    token[...] = jnp.zeros_like(token)
    fill_shifts(shifts)
    chunk_in(0).wait()
    along_depth(0, section, shifts, slot_a)

    def step(k, carry):
        @pl.when(k + 1 < chunks)
        def _():
            chunk_in(k + 1).wait()

        chunk_old(k).wait()
        advance_chunk(SUB * k, 0.5, section, shifts, (slot_a, slot_b), result, finish)
        chunk_out(k).start()
        return carry

    lax.fori_loop(0, chunks, step, 0)
    for k in range(chunks):
        chunk_out(k).wait()


def shifted(x, axis, step, periodic):
    count = lax.axis_size(axis)
    pairs = [(i, (i + step) % count) for i in range(count)]
    if not periodic:
        pairs = [(s, t) for s, t in pairs if t - s == step]
    return lax.ppermute(x, axis, pairs)


def exchange(pack_low, pack_high, edge_west, edge_east):
    got_low = shifted(pack_high, "gy", 1, True)
    got_high = shifted(pack_low, "gy", -1, True)
    ghost_low = shifted(edge_east, "gx", 1, False)
    ghost_high = shifted(edge_west, "gx", -1, False)
    return ghost_low, ghost_high, got_low, got_high


def local(velocity, inflow, positions, tiles, coefs, counts):
    f32, i32 = jnp.float32, jnp.int32
    whole = velocity.shape
    _, cells_x, cells_y, depth = whole
    groups_y = lax.axis_size("gy")
    positions = positions[0].transpose(1, 0, 2)
    tiles, coefs = tiles[0].T, coefs[0]
    records, points = coefs.shape
    share = records // groups_y
    chunks = cells_x // SUB
    size = 4 * math.prod(whole)
    held = pltpu.VMEM(whole, f32)
    stored = pltpu.HBM(whole, f32)
    array = jax.ShapeDtypeStruct
    pack = array((3 * cells_x + 3 * records, 1, points), f32)
    edge = array((3, cells_y, depth), f32)
    per_record = (records, 1, points)
    units = records * (depth // LANES)
    y_shape, z_shape = (units, cells_y, points), (units, 2 * LANES, points)
    y_bytes, z_bytes = 4 * math.prod(y_shape), 2 * math.prod(z_shape)
    products = [pltpu.VMEM((3 * depth, depth), jnp.bfloat16)]
    products += [pltpu.VMEM((2, 3 * BATCH * cells_y, depth), f32)] * 2
    unit_sems = pltpu.SemaphoreType.DMA((units,))
    chunk_sems = pltpu.SemaphoreType.DMA((chunks,))

    field, *own_a, weight_y, weight_z, strength, plan = pl.pallas_call(
        load_sample,
        out_shape=(
            held, pack, pack, edge, edge,
            pltpu.VMEM(y_shape, f32), pltpu.VMEM(z_shape, jnp.bfloat16),
            array(per_record, f32),
            array((HEAD + 3 * units,), i32),
        ),
        in_specs=[ANYWHERE] * 4 + [SCALAR],
        out_specs=(WHOLE,) * 8 + (SCALAR,),
        scratch_shapes=[
            pltpu.VMEM(per_record, i32),
            pltpu.VMEM(per_record, i32),
            pltpu.SMEM((records, LANES), i32),
            pltpu.SMEM((2, records), i32),
            pltpu.VMEM((2, records, points), i32),
            pltpu.VMEM((records, points), f32),
            pltpu.VMEM((records, LANES), i32),
            pltpu.SMEM((records, LANES), i32),
            pltpu.SMEM((chunks, records), i32),
            pltpu.SMEM((chunks,), i32),
            pltpu.SemaphoreType.DMA((4,)),
            pltpu.SemaphoreType.DMA,
            chunk_sems,
        ],
        compiler_params=params(),
        cost_estimate=cost(2 * 10**9, 4 * size),
        name="load_sample",
    )(streamed(velocity), streamed(positions), streamed(tiles), streamed(coefs), counts)
    weight_y, weight_z = resident(weight_y), resident(weight_z)
    ghosts_a = exchange(*own_a)

    section = pl.pallas_call(
        advance_first,
        out_shape=held,
        in_specs=[WHOLE],
        out_specs=WHOLE,
        scratch_shapes=products,
        compiler_params=params(),
        cost_estimate=cost(10**9, 4 * size),
        name="advance_first",
    )(resident(field))

    _, section, stored_y, stored_z, *own_b, shares = pl.pallas_call(
        spread_sample,
        out_shape=(
            held, stored, pltpu.HBM(y_shape, f32), pltpu.HBM(z_shape, jnp.bfloat16),
            pack, pack, edge, edge,
            array((groups_y, 2, 3 * share, 1, points), f32),
        ),
        in_specs=[WHOLE] * 10 + [SCALAR] + [WHOLE] * 3,
        out_specs=(WHOLE,) + (ANYWHERE,) * 3 + (WHOLE,) * 5,
        input_output_aliases={0: 0},
        scratch_shapes=[pltpu.SemaphoreType.DMA, unit_sems, unit_sems],
        compiler_params=params(),
        cost_estimate=cost(2 * 10**9, 4 * size),
        name="spread_sample",
    )(
        resident(section), inflow, *ghosts_a[:2], *own_a, *ghosts_a[2:],
        plan, weight_y, weight_z, strength,
    )
    shares = lax.all_to_all(shares, "gy", 0, 0)
    ghosts_b = exchange(*own_b)

    following, token = pl.pallas_call(
        advance_second,
        out_shape=(stored, array((SUB, LANES), f32)),
        in_specs=[ANYWHERE] * 2,
        out_specs=(ANYWHERE, WHOLE),
        scratch_shapes=[pltpu.VMEM(whole, f32)] * 3 + products + [chunk_sems] * 3,
        compiler_params=params(VMEM_LIMIT + 3 * size),
        cost_estimate=cost(10**9, 4 * size),
        name="advance_second",
    )(streamed(section), streamed(velocity))

    forces = pl.pallas_call(
        share_force,
        out_shape=array((groups_y, 3 * share, 1, points), f32),
        in_specs=[WHOLE, WHOLE, SCALAR] + [ANYWHERE] * 3,
        out_specs=WHOLE,
        compiler_params=params(),
        cost_estimate=cost(10**6, 10**6),
        name="share_force",
    )(shares, strength, counts, token, *ghosts_b[:2])
    all_forces = lax.all_to_all(forces, "gy", 0, 0)

    velocity_next = pl.pallas_call(
        spread_next,
        out_shape=stored,
        in_specs=[ANYWHERE] + [WHOLE] * 9 + [SCALAR, ANYWHERE, ANYWHERE, WHOLE, ANYWHERE],
        out_specs=ANYWHERE,
        scratch_shapes=[
            pltpu.VMEM(whole, f32),
            pltpu.VMEM(y_shape, f32),
            pltpu.VMEM(z_shape, jnp.bfloat16),
            chunk_sems, chunk_sems, unit_sems, unit_sems,
        ],
        compiler_params=params(VMEM_LIMIT + size + y_bytes + z_bytes),
        cost_estimate=cost(2 * 10**9, 4 * size),
        name="spread_next",
    )(
        streamed(following), inflow, *ghosts_b[:2], *own_b, *ghosts_b[2:],
        plan, streamed(stored_y), streamed(stored_z), strength, forces,
    )
    return (velocity_next, all_forces.reshape(1, records, 3, points))


def solution(mesh):
    return jax.shard_map(
        local,
        mesh=mesh,
        in_specs=(
            P(None, "gx", "gy", None),
            P(None, "gy", None),
            P("gx", None, None, None),
            P("gx", None, None),
            P("gx", None, None),
            P("gx"),
        ),
        out_specs=(P(None, "gx", "gy", None), P("gx", None, None, None)),
        check_vma=False,
    )
```

```python
import math

import jax
import jax.numpy as jnp
from jax import lax
from jax.experimental import pallas as pl
from jax.experimental.pallas import tpu as pltpu
from jax.sharding import PartitionSpec as P

RAD = 2
VISCOSITY = 0.05
TIME_STEP = 0.1
WIDTH_EPS = 1.5
ROOT_PI = 1.7724538509055159
TAP = [math.exp(-((d / WIDTH_EPS) ** 2)) / (WIDTH_EPS * ROOT_PI) for d in range(RAD + 1)]
HIGH = [float(jnp.bfloat16(tap)) for tap in TAP]
LOW = [float(jnp.bfloat16(tap - high)) for tap, high in zip(TAP, HIGH)]
LANES = 128
SUB = 8
GROUP = 4
BATCH = 4
HEAD = 1
VMEM_LIMIT = 6 * 2**20

WHOLE = pl.BlockSpec(memory_space=pltpu.VMEM)
SCALAR = pl.BlockSpec(memory_space=pltpu.SMEM)
ANYWHERE = pl.BlockSpec(memory_space=pl.ANY)


def params(limit=VMEM_LIMIT):
    return pltpu.CompilerParams(vmem_limit_bytes=limit)


def cost(flops, nbytes):
    return pl.CostEstimate(flops=flops, bytes_accessed=nbytes, transcendentals=0)


def resident(x):
    return pltpu.with_memory_space_constraint(x, pltpu.VMEM)


def streamed(x):
    return pltpu.with_memory_space_constraint(x, pltpu.HBM)


def split(x):
    high = x.astype(jnp.bfloat16)
    low = (x - high.astype(jnp.float32)).astype(jnp.bfloat16)
    return jnp.concatenate([high, low], axis=0)


def along_z(point_z, start):
    points = point_z.shape[-1]
    row = lax.broadcasted_iota(jnp.int32, (LANES, points), 0).astype(jnp.bfloat16)
    place = (point_z - start).astype(jnp.float32)
    place = jnp.broadcast_to(place, (LANES, points)).astype(jnp.bfloat16)
    dist = jnp.abs(row - place)
    near = [dist == float(d) for d in range(RAD + 1)]
    out = []
    for taps in (HIGH, LOW):
        value = jnp.zeros_like(row)
        for d in range(RAD, -1, -1):
            value = jnp.where(near[d], jnp.full_like(row, taps[d]), value)
        out.append(value)
    return out


def wrapped(point_y, base, total_y):
    near = point_y - base
    near = jnp.where(near > total_y // 2, near - total_y, near)
    return jnp.where(near < -(total_y // 2), near + total_y, near)


def along_y(point_y, base, cells_y, total_y):
    near = wrapped(point_y, base, total_y)
    dist = jnp.abs(lax.broadcasted_iota(jnp.int32, (cells_y, point_y.shape[-1]), 0) - near)
    return jnp.where(
        dist == 0, TAP[0], jnp.where(dist == 1, TAP[1], jnp.where(dist == 2, TAP[2], 0.0))
    )


def make_plan(hubs, tiles, touch, counts, start, plan, bucket, held):
    tile_y, groups_y = lax.axis_index("gy"), lax.axis_size("gy")
    records, chunks = tiles.shape[1], held.shape[0]
    for k in range(chunks):
        held[k] = 0

    def place(r, carry):
        offset = tile_y - tiles[0, r]
        offset = jnp.where(offset < 0, offset + groups_y, offset)

        @pl.when(jnp.logical_and(offset < tiles[1, r], touch[r, 1] >= 0))
        def _():
            k = (hubs[r, 0] - start + RAD) // SUB
            bucket[k, held[k]] = r
            held[k] = held[k] + 1

        return carry

    lax.fori_loop(0, jnp.minimum(counts[0], records), place, 0)

    units = (plan.shape[0] - HEAD) // 3

    def flatten(k, found):
        def move(j, found):
            r = bucket[k, j]

            def add(half, found):
                plan[HEAD + found] = r
                plan[HEAD + units + found] = hubs[r, 0] - start
                plan[HEAD + 2 * units + found] = half
                return found + 1

            first = (touch[r, 0] - RAD) // LANES
            return lax.fori_loop(first, (touch[r, 1] + RAD) // LANES + 1, add, found)

        return lax.fori_loop(0, held[k], move, found)

    plan[0] = lax.fori_loop(0, chunks, flatten, jnp.int32(0))


def group(plan, t):
    units = (plan.shape[0] - HEAD) // 3
    picks, keeps = [], []
    for k in range(GROUP):
        wanted = GROUP * t + k
        n = jnp.minimum(wanted, plan[0] - 1)
        record, hub, half = [plan[HEAD + k * units + n] for k in range(3)]
        picks.append((n, record, hub, pl.ds(pl.multiple_of(half * LANES, LANES), LANES)))
        keeps.append(wanted == n)
    return picks, keeps


def groups_of(plan):
    return (plan[0] + GROUP - 1) // GROUP


def sampled_rows(field, weight_y, weight_z, picks):
    cells_y = field.shape[2]
    rows = 3 * cells_y
    parts = []
    for t, r, hub, cols in picks:
        planes = []
        for c in range(3):
            plane = TAP[0] * field[c, hub, :, cols]
            plane += TAP[1] * (field[c, hub - 1, :, cols] + field[c, hub + 1, :, cols])
            plane += TAP[2] * (field[c, hub - 2, :, cols] + field[c, hub + 2, :, cols])
            planes.append(plane)
        part = split(jnp.concatenate(planes, axis=0))
        parts.append(jnp.concatenate([part, part], axis=1))
    out = []
    for (t, r, hub, cols), part in zip(picks, parts):
        picked = jnp.dot(part, weight_z[t], preferred_element_type=jnp.float32)
        picked = picked[:rows] + picked[rows:]
        weight = weight_y[t]
        out.append(
            [
                jnp.sum(picked[c * cells_y : (c + 1) * cells_y] * weight, axis=0, keepdims=True)
                for c in range(3)
            ]
        )
    return out


def add_rows(pack, first_row, picks, sampled, keeps):
    for (t, r, hub, cols), rows, keep in zip(picks, sampled, keeps):
        for c in range(3):
            n = first_row + 3 * r + c
            pack[n] = pack[n] + jnp.where(keep, rows[c], 0.0)


def pack_edges(field, edge_west, edge_east, pack_low, pack_high):
    cells_x, cells_y, depth = field.shape[1:]
    for c in range(3):
        edge_west[c] = field[c, 0]
        edge_east[c] = field[c, cells_x - 1]

    def step(t, carry):
        cells = [(c, t * BATCH + k) for k in range(BATCH) for c in range(3)]
        rows = [
            (field[c, i, pl.ds(0, 1), :], field[c, i, pl.ds(cells_y - 1, 1), :]) for c, i in cells
        ]
        for (c, i), (low, high) in zip(cells, rows):
            pack_low[c * cells_x + i] = low
            pack_high[c * cells_x + i] = high
        return carry

    lax.fori_loop(0, cells_x // BATCH, step, 0)


def load_sample(
    velocity, positions, tiles_hbm, coefs_hbm, counts,
    field, pack_low, pack_high, edge_west, edge_east, weight_y, weight_z, strength, point_y, plan,
    point_z, hubs, tiles, places, coefs, flags, touch, bucket, held, small_sems, touch_sem, sems,
):
    cells_x, cells_y, depth = field.shape[1:]
    records, points = coefs.shape
    chunks = cells_x // SUB
    first_row = 3 * cells_x
    start = lax.axis_index("gx") * cells_x

    def chunk(k):
        planes = pl.ds(k * SUB, SUB)
        return pltpu.make_async_copy(velocity.at[:, planes], field.at[:, planes], sems.at[k])

    small = [
        (positions.at[pl.ds(1, 2)], places),
        (positions.at[0, :, pl.ds(0, LANES)], hubs),
        (tiles_hbm, tiles),
        (coefs_hbm, coefs),
    ]
    small = [
        pltpu.make_async_copy(source, target, small_sems.at[n])
        for n, (source, target) in enumerate(small)
    ]
    total_y = cells_y * lax.axis_size("gy")
    base = lax.axis_index("gy") * cells_y
    for copy in small:
        copy.start()
    for k in range(chunks):
        chunk(k).start()
    small[0].wait()
    near = wrapped(places[0], base, total_y)
    inside = jnp.logical_and(near >= -RAD, near < cells_y + RAD)
    height = places[1].astype(jnp.float32)
    lowest = jnp.min(jnp.where(inside, height, float(depth)), axis=1, keepdims=True)
    highest = jnp.max(jnp.where(inside, height, -1.0), axis=1, keepdims=True)
    column = lax.broadcasted_iota(jnp.int32, flags.shape, 1)
    flags[...] = jnp.where(column == 0, lowest, highest).astype(jnp.int32)
    touch_copy = pltpu.make_async_copy(flags, touch, touch_sem)
    touch_copy.start()

    def clear(n, carry):
        for k in range(SUB):
            pack_low[first_row + n * SUB + k] = jnp.zeros((1, points), jnp.float32)
        return carry

    lax.fori_loop(0, 3 * records // SUB, clear, 0)
    for copy in small[1:]:
        copy.wait()
    for first in range(0, records, SUB):
        here = range(first, first + SUB)
        rows = [
            (places[0, pl.ds(r, 1), :], places[1, pl.ds(r, 1), :], coefs[pl.ds(r, 1), :])
            for r in here
        ]
        for r, (y, z, coef) in zip(here, rows):
            point_y[r], point_z[r], strength[r] = y, z, coef
    touch_copy.wait()
    make_plan(hubs, tiles, touch, counts, start, plan, bucket, held)

    def weigh(t, carry):
        units = weight_z.shape[0]
        made = []
        for k in range(2):
            n = jnp.minimum(2 * t + k, plan[0] - 1)
            r, half = plan[HEAD + n], plan[HEAD + 2 * units + n]
            high, low = along_z(point_z[r], half * LANES)
            made.append((n, along_y(point_y[r], base, cells_y, total_y), high, low))
        for n, across, high, low in made:
            weight_y[n] = across
            weight_z[n, 0:LANES] = high
            weight_z[n, LANES:] = low
        return carry

    lax.fori_loop(0, (plan[0] + 1) // 2, weigh, 0)

    def wait_to(ready, wanted):
        def step(k, carry):
            chunk(k).wait()
            return carry

        lax.fori_loop(ready, wanted, step, 0)
        return jnp.maximum(ready, wanted)

    def step(t, ready):
        picks, keeps = group(plan, t)
        ready = wait_to(ready, (picks[-1][2] + RAD) // SUB + 1)
        rows = sampled_rows(field, weight_y, weight_z, picks)
        add_rows(pack_low, first_row, picks, rows, keeps)
        return ready

    ready = lax.fori_loop(0, groups_of(plan), step, jnp.int32(0))
    wait_to(ready, chunks)

    def copy_rows(t, carry):
        rows = [first_row + t * SUB + k for k in range(SUB)]
        values = [pack_low[n] for n in rows]
        for n, value in zip(rows, values):
            pack_high[n] = value
        return carry

    lax.fori_loop(0, 3 * records // SUB, copy_rows, 0)
    pack_edges(field, edge_west, edge_east, pack_low, pack_high)


def fix_west(factor, target, own, inflow, ghost):
    first = lax.axis_index("gx") == 0
    for c in range(3):
        west = jnp.where(first, inflow[c], ghost[c])
        coef = factor * TIME_STEP * VISCOSITY + (0.5 * factor * TIME_STEP) * own[0]
        target[c, 0] = target[c, 0] + (west - own[c]) * coef


def fix_east(factor, target, own, ghost):
    last = lax.axis_index("gx") == lax.axis_size("gx") - 1
    end = target.shape[1] - 1
    for c in range(3):
        east = jnp.where(last, own[c], ghost[c])
        coef = factor * TIME_STEP * VISCOSITY - (0.5 * factor * TIME_STEP) * own[0]
        target[c, end] = target[c, end] + (east - own[c]) * coef


def fix_rows(factor, target, own_low, own_high, got_low, got_high, t):
    cells_x, cells_y = target.shape[1:3]
    spread = factor * TIME_STEP * VISCOSITY
    half = 0.5 * factor * TIME_STEP
    shape = (SUB, target.shape[3])
    row = lax.broadcasted_iota(jnp.int32, shape, 0)
    low, high = pl.ds(0, SUB), pl.ds(cells_y - SUB, SUB)

    def wide(x):
        return jnp.broadcast_to(x, shape)

    for first in range(0, SUB, 2):
        values = []
        for k in range(first, first + 2):
            i = t * SUB + k
            south = jnp.where(row == 0, spread + half * wide(own_low[cells_x + i]), 0.0)
            north = jnp.where(row == SUB - 1, spread - half * wide(own_high[cells_x + i]), 0.0)
            for c in range(3):
                n = c * cells_x + i
                values.append((c, i, low, target[c, i, low, :] + wide(got_low[n]) * south))
                values.append((c, i, high, target[c, i, high, :] + wide(got_high[n]) * north))
        for c, i, rows, value in values:
            target[c, i, rows, :] = value


def slabs_of(weight_of, weight_z, strength, own, low, high, cells, scales, picks):
    cells_x, cells_y, depth = cells
    count = 3 * cells_y
    across = (((1,), (1,)), ((), ()))
    spread = []
    for (t, r, hub, cols), scale in zip(picks, scales):
        rows = [3 * cells_x + 3 * r + c for c in range(3)]
        total = [own[n] + (low[n] + high[n]) for n in rows]
        speed = jnp.sqrt(total[0] * total[0] + total[1] * total[1] + total[2] * total[2])
        pull = strength[r] * (-scale) * speed
        weight = weight_of(t, r)
        spread.append(split(jnp.concatenate([weight * (pull * x) for x in total], axis=0)))
    slabs = []
    for (t, r, hub, cols), part in zip(picks, spread):
        slab = lax.dot_general(part, weight_z[t], across, preferred_element_type=jnp.float32)
        slab = slab[:count] + slab[count:]
        slabs.append(slab[:, :LANES] + slab[:, LANES:])
    return slabs


def add_slab(field, slab, hub, cols):
    cells_y = field.shape[2]
    for c in range(3):
        part = slab[c * cells_y : (c + 1) * cells_y]
        terms = [tap * part for tap in TAP]
        reach = range(-RAD, RAD + 1)
        values = [field[c, hub + d, :, cols] + terms[abs(d)] for d in reach]
        for d, value in zip(reach, values):
            field[c, hub + d, :, cols] = value


def spread_group(t, scale, field, plan, points, own, low, high):
    picks, keeps = group(plan, t)
    scales = [jnp.where(keep, scale, 0.0) for keep in keeps]
    slabs = slabs_of(*points, own, low, high, field.shape[1:], scales, picks)
    for (_, _, hub, cols), slab in zip(picks, slabs):
        add_slab(field, slab, hub, cols)


def spread_sample(
    section_in, inflow, ghost_low, ghost_high, own_low, own_high, own_west, own_east, got_low, got_high,
    plan, weight_y, weight_z, strength,
    section, section_out, stored_z, pack_low, pack_high, edge_west, edge_east,
    share_out, sem, sem_z,
):
    cells_x = section.shape[1]
    records = strength.shape[0]
    share = share_out.shape[2] // 3
    first_row = 3 * cells_x

    def store(t):
        return pltpu.make_async_copy(weight_z.at[t], stored_z.at[t], sem_z.at[t])

    def start_store(t, carry):
        store(t).start()
        return carry

    def wait_store(t, carry):
        store(t).wait()
        return carry

    lax.fori_loop(0, plan[0], start_store, 0)

    def fix_step(t, carry):
        fix_rows(1.0, section, own_low, own_high, got_low, got_high, t)
        return carry

    fix_west(1.0, section, own_west, inflow, ghost_low)
    fix_east(1.0, section, own_east, ghost_high)
    lax.fori_loop(0, cells_x // SUB, fix_step, 0)

    def spread_step(t, carry):
        points = (lambda n, r: weight_y[n], weight_z, strength)
        spread_group(t, TIME_STEP, section, plan, points, own_low, got_low, got_high)
        return carry

    lax.fori_loop(0, groups_of(plan), spread_step, 0)
    copy = pltpu.make_async_copy(section, section_out, sem)
    copy.start()
    pack_edges(section, edge_west, edge_east, pack_low, pack_high)

    def clear(n, carry):
        for k in range(SUB):
            pack_low[first_row + n * SUB + k] = jnp.zeros_like(own_low[0])
        return carry

    lax.fori_loop(0, 3 * records // SUB, clear, 0)

    def sample_step(t, carry):
        picks, keeps = group(plan, t)
        rows = sampled_rows(section, weight_y, weight_z, picks)
        add_rows(pack_low, first_row, picks, rows, keeps)
        return carry

    lax.fori_loop(0, groups_of(plan), sample_step, 0)

    def copy_rows(r, carry):
        old = [own_low[first_row + 3 * r + c] for c in range(3)]
        new = [pack_low[first_row + 3 * r + c] for c in range(3)]
        for c in range(3):
            pack_high[first_row + 3 * r + c] = new[c]
            share_out[r // share, 0, 3 * (r % share) + c] = old[c]
            share_out[r // share, 1, 3 * (r % share) + c] = new[c]
        return carry

    lax.fori_loop(0, records, copy_rows, 0)
    lax.fori_loop(0, plan[0], wait_store, 0)
    copy.wait()


def share_force(parts, strength, counts, after, after_low, after_high, result):
    groups, _, rows = parts.shape[:3]
    share = rows // 3
    mine = lax.axis_index("gy") * share
    values = []
    for s in range(share):
        live = mine + s < counts[0]
        pull = jnp.where(live, -0.5 * strength[mine + s], 0.0)
        total = [0.0, 0.0, 0.0]
        for stage in range(2):
            value = []
            for c in range(3):
                n = 3 * s + c
                x = parts[0, stage, n]
                for g in range(1, groups):
                    x += parts[g, stage, n]
                value.append(x)
            speed = jnp.sqrt(value[0] * value[0] + value[1] * value[1] + value[2] * value[2])
            total = [acc + speed * x for acc, x in zip(total, value)]
        values.extend((3 * s + c, pull * total[c]) for c in range(3))
        if s % 2 == 1 or s + 1 == share:
            for n, value in values:
                for g in range(groups):
                    result[g, n] = value
            values = []


def spread_next(
    following, inflow, ghost_low, ghost_high, own_low, own_high, own_west, own_east, got_low, got_high,
    plan, point_y, stored_z, strength, after,
    result, field, weight_z, in_sems, out_sems, sem_z,
):
    chunks = field.shape[1] // SUB
    factor = 0.5

    def chunk_in(k):
        planes = pl.ds(k * SUB, SUB)
        return pltpu.make_async_copy(following.at[:, planes], field.at[:, planes], in_sems.at[k])

    def chunk_out(k):
        planes = pl.ds(k * SUB, SUB)
        return pltpu.make_async_copy(field.at[:, planes], result.at[:, planes], out_sems.at[k])

    def wait_to(ready, wanted):
        def step(k, carry):
            chunk_in(k).wait()
            fix_rows(factor, field, own_low, own_high, got_low, got_high, k)

            @pl.when(k == 0)
            def _():
                fix_west(factor, field, own_west, inflow, ghost_low)

            @pl.when(k == chunks - 1)
            def _():
                fix_east(factor, field, own_east, ghost_high)

            return carry

        lax.fori_loop(ready, wanted, step, 0)
        return jnp.maximum(ready, wanted)

    def send_to(sent, done):
        def step(k, carry):
            chunk_out(k).start()
            return carry

        lax.fori_loop(sent, done, step, 0)
        return jnp.maximum(sent, done)

    def weights(t):
        return pltpu.make_async_copy(stored_z.at[t], weight_z.at[t], sem_z.at[t])

    def start_weights(t, carry):
        weights(t).start()
        return carry

    def weight_of(t, r):
        cells_y = field.shape[2]
        base = lax.axis_index("gy") * cells_y
        return along_y(point_y[r], base, cells_y, cells_y * lax.axis_size("gy"))

    found = plan[0]
    for k in range(chunks):
        chunk_in(k).start()
        lax.fori_loop(k * found // chunks, (k + 1) * found // chunks, start_weights, 0)

    def step(t, carry):
        ready, sent = carry
        picks, keeps = group(plan, t)
        for (n, _, _, _), keep in zip(picks, keeps):

            @pl.when(keep)
            def _(n=n):
                weights(n).wait()

        ready = wait_to(ready, (picks[-1][2] + RAD) // SUB + 1)
        sent = send_to(sent, (picks[0][2] + RAD) // SUB - 1)
        points = (weight_of, weight_z, strength)
        spread_group(t, factor * TIME_STEP, field, plan, points, own_low, got_low, got_high)
        return ready, sent

    zero = jnp.int32(0)
    ready, sent = lax.fori_loop(0, groups_of(plan), step, (zero, zero))
    sent = send_to(sent, ready)

    def finish(k, carry):
        wait_to(k, k + 1)
        chunk_out(k).start()
        return carry

    lax.fori_loop(ready, chunks, finish, 0)
    for k in range(chunks):
        chunk_out(k).wait()


def fill_shifts(shifts):
    depth = shifts.shape[1]
    source = lax.broadcasted_iota(jnp.int32, (depth, depth), 0)
    cell = lax.broadcasted_iota(jnp.int32, (depth, depth), 1)
    upper = jnp.where(source == cell + 1, 1.0, 0.0)
    lower = jnp.where(source == cell - 1, 1.0, 0.0)
    difference = (upper - lower).astype(shifts.dtype)
    shifts[0:depth] = difference
    shifts[depth : 2 * depth] = difference
    shifts[2 * depth : 3 * depth] = (upper + lower).astype(shifts.dtype)


def along_depth(i, field, shifts, slot):
    depth = shifts.shape[1]
    x = jnp.concatenate([field[c, i + k] for k in range(BATCH) for c in range(3)], axis=0)
    high = x.astype(jnp.bfloat16)
    low = (x - high.astype(jnp.float32)).astype(jnp.bfloat16)
    slot[0] = jnp.dot(
        jnp.concatenate([high, low], axis=1),
        shifts[0 : 2 * depth],
        preferred_element_type=jnp.float32,
    )
    slot[1] = jnp.dot(
        high, shifts[2 * depth : 3 * depth], preferred_element_type=jnp.float32
    )


def advance(i, k, factor, field, slot, target, finish):
    cells_x, cells_y, depth = field.shape[1:]
    groups, halves = cells_y // SUB, depth // LANES
    row = lax.broadcasted_iota(jnp.int32, (SUB, LANES), 0)
    first_row, last_row = row == 0, row == SUB - 1
    spread = factor * TIME_STEP * VISCOSITY
    centre = factor * (1.0 - 6.0 * TIME_STEP * VISCOSITY)
    zero = jnp.zeros((SUB, LANES), jnp.float32)
    loaded = {}
    here = i + k
    west, east = jnp.maximum(here - 1, 0), jnp.minimum(here + 1, cells_x - 1)

    def at(c, g, h):
        if (c, g, h) not in loaded:
            loaded[c, g, h] = field[c, here, pl.ds(g * SUB, SUB), pl.ds(h * LANES, LANES)]
        return loaded[c, g, h]

    values = []
    for g in range(groups):
        for h in range(halves):
            rows, cols = pl.ds(g * SUB, SUB), pl.ds(h * LANES, LANES)
            q = [at(c, g, h) for c in range(3)]
            speeds = [(0.5 * factor * TIME_STEP) * x for x in q]
            less = [spread - s for s in speeds[:2]]
            more = [spread + s for s in speeds[:2]]
            if g == 0:
                more[1] = jnp.where(first_row, zero, more[1])
            if g == groups - 1:
                less[1] = jnp.where(last_row, zero, less[1])
            for c in range(3):
                x = q[c]
                above, below = x, x
                if g + 1 < groups:
                    above = jnp.where(first_row, at(c, g + 1, h), x)
                if g > 0:
                    below = jnp.where(last_row, at(c, g - 1, h), x)
                above, below = pltpu.roll(above, SUB - 1, 0), pltpu.roll(below, 1, 0)
                place = pl.ds((3 * k + c) * cells_y + g * SUB, SUB)
                total = centre * x
                total += field[c, east, rows, cols] * less[0]
                total += field[c, west, rows, cols] * more[0]
                total += above * less[1] + below * more[1]
                total += spread * slot[1, place, cols] - speeds[2] * slot[0, place, cols]
                values.append((c, rows, cols, finish(c, here, rows, cols, total)))
        if g % 2 == 1 or g + 1 == groups:
            for c, rows, cols, value in values:
                target[c, here, rows, cols] = value
            values = []


def advance_batch(i, n, factor, field, shifts, slots, target, finish):
    now, later = slots[n % 2], slots[1 - n % 2]
    along_depth(jnp.minimum(i + BATCH, field.shape[1] - BATCH), field, shifts, later)
    for k in range(BATCH):
        advance(i, k, factor, field, now, target, finish)


def advance_first(field, section, shifts, slot_a, slot_b):
    fill_shifts(shifts)
    along_depth(0, field, shifts, slot_a)

    def step(t, carry):
        for n in range(SUB // BATCH):
            advance_batch(
                SUB * t + BATCH * n, n, 1.0, field, shifts, (slot_a, slot_b), section,
                lambda c, i, rows, cols, value: value,
            )
        return carry

    lax.fori_loop(0, field.shape[1] // SUB, step, 0)


def advance_second(
    section_hbm, velocity, following, token,
    section, field, result, shifts, slot_a, slot_b, in_sems, old_sems, out_sems,
):
    chunks = section.shape[1] // BATCH

    def planes(k):
        return pl.ds(k * BATCH, BATCH)

    def chunk_in(k):
        return pltpu.make_async_copy(
            section_hbm.at[:, planes(k)], section.at[:, planes(k)], in_sems.at[k]
        )

    def chunk_old(k):
        return pltpu.make_async_copy(
            velocity.at[:, planes(k)], field.at[:, planes(k)], old_sems.at[k]
        )

    def chunk_out(k):
        return pltpu.make_async_copy(
            result.at[:, planes(k)], following.at[:, planes(k)], out_sems.at[k]
        )

    def finish(c, i, rows, cols, value):
        return value + 0.5 * field[c, i, rows, cols]

    for k in range(chunks):
        chunk_in(k).start()
        chunk_old(k).start()
    token[...] = jnp.zeros_like(token)
    fill_shifts(shifts)
    chunk_in(0).wait()
    along_depth(0, section, shifts, slot_a)

    def step(t, carry):
        slots = (slot_a, slot_b)
        for n in range(SUB // BATCH):
            k = t * (SUB // BATCH) + n

            @pl.when(k + 1 < chunks)
            def _(k=k):
                chunk_in(k + 1).wait()

            chunk_old(k).wait()
            advance_batch(k * BATCH, n, 0.5, section, shifts, slots, result, finish)
            chunk_out(k).start()
        return carry

    lax.fori_loop(0, section.shape[1] // SUB, step, 0)
    for k in range(chunks):
        chunk_out(k).wait()


def shifted(x, axis, step, periodic):
    count = lax.axis_size(axis)
    pairs = [(i, (i + step) % count) for i in range(count)]
    if not periodic:
        pairs = [(s, t) for s, t in pairs if t - s == step]
    return lax.ppermute(x, axis, pairs)


def exchange(pack_low, pack_high, edge_west, edge_east):
    got_low = shifted(pack_high, "gy", 1, True)
    got_high = shifted(pack_low, "gy", -1, True)
    ghost_low = shifted(edge_east, "gx", 1, False)
    ghost_high = shifted(edge_west, "gx", -1, False)
    return ghost_low, ghost_high, got_low, got_high


def local(velocity, inflow, positions, tiles, coefs, counts):
    f32, i32 = jnp.float32, jnp.int32
    whole = velocity.shape
    _, cells_x, cells_y, depth = whole
    groups_y = lax.axis_size("gy")
    positions = positions[0].transpose(1, 0, 2)
    tiles, coefs = tiles[0].T, coefs[0]
    records, points = coefs.shape
    share = records // groups_y
    chunks = cells_x // SUB
    size = 4 * math.prod(whole)
    held = pltpu.VMEM(whole, f32)
    stored = pltpu.HBM(whole, f32)
    array = jax.ShapeDtypeStruct
    pack = array((3 * cells_x + 3 * records, 1, points), f32)
    edge = array((3, cells_y, depth), f32)
    per_record = (records, 1, points)
    units = records * (depth // LANES)
    y_shape, z_shape = (units, cells_y, points), (units, 2 * LANES, points)
    z_bytes = 2 * math.prod(z_shape)
    products = [pltpu.VMEM((3 * depth, depth), jnp.bfloat16)]
    products += [pltpu.VMEM((2, 3 * BATCH * cells_y, depth), f32)] * 2
    unit_sems = pltpu.SemaphoreType.DMA((units,))
    chunk_sems = pltpu.SemaphoreType.DMA((chunks,))

    field, *own_a, weight_y, weight_z, strength, point_y, plan = pl.pallas_call(
        load_sample,
        out_shape=(
            held, pack, pack, edge, edge,
            pltpu.VMEM(y_shape, f32), pltpu.VMEM(z_shape, jnp.bfloat16),
            array(per_record, f32), array(per_record, i32),
            array((HEAD + 3 * units,), i32),
        ),
        in_specs=[ANYWHERE] * 4 + [SCALAR],
        out_specs=(WHOLE,) * 9 + (SCALAR,),
        scratch_shapes=[
            pltpu.VMEM(per_record, i32),
            pltpu.SMEM((records, LANES), i32),
            pltpu.SMEM((2, records), i32),
            pltpu.VMEM((2, records, points), i32),
            pltpu.VMEM((records, points), f32),
            pltpu.VMEM((records, LANES), i32),
            pltpu.SMEM((records, LANES), i32),
            pltpu.SMEM((chunks, records), i32),
            pltpu.SMEM((chunks,), i32),
            pltpu.SemaphoreType.DMA((4,)),
            pltpu.SemaphoreType.DMA,
            chunk_sems,
        ],
        compiler_params=params(),
        cost_estimate=cost(2 * 10**9, 4 * size),
        name="load_sample",
    )(streamed(velocity), streamed(positions), streamed(tiles), streamed(coefs), counts)
    weight_y, weight_z = resident(weight_y), resident(weight_z)
    ghosts_a = exchange(*own_a)

    section = pl.pallas_call(
        advance_first,
        out_shape=held,
        in_specs=[WHOLE],
        out_specs=WHOLE,
        scratch_shapes=products,
        compiler_params=params(),
        cost_estimate=cost(10**9, 4 * size),
        name="advance_first",
    )(resident(field))

    _, section, stored_z, *own_b, shares = pl.pallas_call(
        spread_sample,
        out_shape=(
            held, stored, pltpu.HBM(z_shape, jnp.bfloat16),
            pack, pack, edge, edge,
            array((groups_y, 2, 3 * share, 1, points), f32),
        ),
        in_specs=[WHOLE] * 10 + [SCALAR] + [WHOLE] * 3,
        out_specs=(WHOLE,) + (ANYWHERE,) * 2 + (WHOLE,) * 5,
        input_output_aliases={0: 0},
        scratch_shapes=[pltpu.SemaphoreType.DMA, unit_sems],
        compiler_params=params(),
        cost_estimate=cost(2 * 10**9, 4 * size),
        name="spread_sample",
    )(
        resident(section), inflow, *ghosts_a[:2], *own_a, *ghosts_a[2:],
        plan, weight_y, weight_z, strength,
    )
    shares = lax.all_to_all(shares, "gy", 0, 0)
    ghosts_b = exchange(*own_b)

    following, token = pl.pallas_call(
        advance_second,
        out_shape=(stored, array((SUB, LANES), f32)),
        in_specs=[ANYWHERE] * 2,
        out_specs=(ANYWHERE, WHOLE),
        scratch_shapes=[pltpu.VMEM(whole, f32)] * 3
        + products
        + [pltpu.SemaphoreType.DMA((cells_x // BATCH,))] * 3,
        compiler_params=params(VMEM_LIMIT + 3 * size),
        cost_estimate=cost(10**9, 4 * size),
        name="advance_second",
    )(streamed(section), streamed(velocity))

    forces = pl.pallas_call(
        share_force,
        out_shape=array((groups_y, 3 * share, 1, points), f32),
        in_specs=[WHOLE, WHOLE, SCALAR] + [ANYWHERE] * 3,
        out_specs=WHOLE,
        compiler_params=params(),
        cost_estimate=cost(10**6, 10**6),
        name="share_force",
    )(shares, strength, counts, token, *ghosts_b[:2])
    all_forces = lax.all_to_all(forces, "gy", 0, 0)

    velocity_next = pl.pallas_call(
        spread_next,
        out_shape=stored,
        in_specs=[ANYWHERE] + [WHOLE] * 9 + [SCALAR, WHOLE, ANYWHERE, WHOLE, ANYWHERE],
        out_specs=ANYWHERE,
        scratch_shapes=[
            pltpu.VMEM(whole, f32),
            pltpu.VMEM(z_shape, jnp.bfloat16),
            chunk_sems, chunk_sems, unit_sems,
        ],
        compiler_params=params(VMEM_LIMIT + size + z_bytes),
        cost_estimate=cost(2 * 10**9, 4 * size),
        name="spread_next",
    )(
        streamed(following), inflow, *ghosts_b[:2], *own_b, *ghosts_b[2:],
        plan, point_y, streamed(stored_z), strength, forces,
    )
    return (velocity_next, all_forces.reshape(1, records, 3, points))


def solution(mesh):
    return jax.shard_map(
        local,
        mesh=mesh,
        in_specs=(
            P(None, "gx", "gy", None),
            P(None, "gy", None),
            P("gx", None, None, None),
            P("gx", None, None),
            P("gx", None, None),
            P("gx"),
        ),
        out_specs=(P(None, "gx", "gy", None), P("gx", None, None, None)),
        check_vma=False,
    )
```

```python
import math

import jax
import jax.numpy as jnp
from jax import lax
from jax.experimental import pallas as pl
from jax.experimental.pallas import tpu as pltpu
from jax.sharding import PartitionSpec as P

RAD = 2
VISCOSITY = 0.05
TIME_STEP = 0.1
WIDTH_EPS = 1.5
ROOT_PI = 1.7724538509055159
TAP = [math.exp(-((d / WIDTH_EPS) ** 2)) / (WIDTH_EPS * ROOT_PI) for d in range(RAD + 1)]
HIGH = [float(jnp.bfloat16(tap)) for tap in TAP]
LOW = [float(jnp.bfloat16(tap - high)) for tap, high in zip(TAP, HIGH)]
LANES = 128
SUB = 8
GROUP = 4
BATCH = 4
PLANES = 8
BLOCK = 2 * PLANES
HEAD = 1
VMEM_LIMIT = 8 * 2**20

WHOLE = pl.BlockSpec(memory_space=pltpu.VMEM)
SCALAR = pl.BlockSpec(memory_space=pltpu.SMEM)
ANYWHERE = pl.BlockSpec(memory_space=pl.ANY)


def params(limit=VMEM_LIMIT):
    return pltpu.CompilerParams(vmem_limit_bytes=limit)


def cost(flops, nbytes):
    return pl.CostEstimate(flops=flops, bytes_accessed=nbytes, transcendentals=0)


def resident(x):
    return pltpu.with_memory_space_constraint(x, pltpu.VMEM)


def streamed(x):
    return pltpu.with_memory_space_constraint(x, pltpu.HBM)


def split(x):
    high = x.astype(jnp.bfloat16)
    low = (x - high.astype(jnp.float32)).astype(jnp.bfloat16)
    return jnp.concatenate([high, low], axis=0)


def along_z(point_z, start):
    shape = (LANES, point_z.shape[-1])
    dist = jnp.abs(lax.broadcasted_iota(jnp.int32, shape, 0) - (point_z - start))
    near = [dist == d for d in range(RAD + 1)]
    out = []
    for taps in (HIGH, LOW):
        value = 0.0
        for d in range(RAD, -1, -1):
            value = jnp.where(near[d], taps[d], value)
        out.append(value.astype(jnp.bfloat16))
    return out


def wrapped(point_y, base, total_y):
    near = point_y - base
    near = jnp.where(near > total_y // 2, near - total_y, near)
    return jnp.where(near < -(total_y // 2), near + total_y, near)


def along_y(point_y, base, cells_y, total_y):
    near = wrapped(point_y, base, total_y)
    dist = jnp.abs(lax.broadcasted_iota(jnp.int32, (cells_y, point_y.shape[-1]), 0) - near)
    return jnp.where(
        dist == 0, TAP[0], jnp.where(dist == 1, TAP[1], jnp.where(dist == 2, TAP[2], 0.0))
    )


def make_plan(hubs, tiles, touch, counts, start, plan, bucket, held):
    tile_y, groups_y = lax.axis_index("gy"), lax.axis_size("gy")
    records, chunks = tiles.shape[1], held.shape[0]
    for k in range(chunks):
        held[k] = 0

    def place(r, carry):
        offset = tile_y - tiles[0, r]
        offset = jnp.where(offset < 0, offset + groups_y, offset)

        @pl.when(jnp.logical_and(offset < tiles[1, r], touch[r, 1] >= 0))
        def _():
            k = (hubs[r, 0] - start + RAD) // SUB
            bucket[k, held[k]] = r
            held[k] = held[k] + 1

        return carry

    lax.fori_loop(0, jnp.minimum(counts[0], records), place, 0)

    units = (plan.shape[0] - HEAD) // 3

    def flatten(k, found):
        def move(j, found):
            r = bucket[k, j]

            def add(half, found):
                plan[HEAD + found] = r
                plan[HEAD + units + found] = hubs[r, 0] - start
                plan[HEAD + 2 * units + found] = half
                return found + 1

            first = (touch[r, 0] - RAD) // LANES
            return lax.fori_loop(first, (touch[r, 1] + RAD) // LANES + 1, add, found)

        return lax.fori_loop(0, held[k], move, found)

    plan[0] = lax.fori_loop(0, chunks, flatten, jnp.int32(0))


def group(plan, t):
    units = (plan.shape[0] - HEAD) // 3
    picks, keeps = [], []
    for k in range(GROUP):
        wanted = GROUP * t + k
        n = jnp.minimum(wanted, plan[0] - 1)
        record, hub, half = [plan[HEAD + k * units + n] for k in range(3)]
        picks.append((n, record, hub, pl.ds(pl.multiple_of(half * LANES, LANES), LANES)))
        keeps.append(wanted == n)
    return picks, keeps


def groups_of(plan):
    return (plan[0] + GROUP - 1) // GROUP


def sampled_rows(field, weight_y, weight_z, picks):
    cells_y = field.shape[2]
    rows = 3 * cells_y
    parts = []
    for t, r, hub, cols in picks:
        planes = []
        for c in range(3):
            plane = TAP[0] * field[c, hub, :, cols]
            plane += TAP[1] * (field[c, hub - 1, :, cols] + field[c, hub + 1, :, cols])
            plane += TAP[2] * (field[c, hub - 2, :, cols] + field[c, hub + 2, :, cols])
            planes.append(plane)
        part = split(jnp.concatenate(planes, axis=0))
        parts.append(jnp.concatenate([part, part], axis=1))
    out = []
    for (t, r, hub, cols), part in zip(picks, parts):
        picked = jnp.dot(part, weight_z[t], preferred_element_type=jnp.float32)
        picked = picked[:rows] + picked[rows:]
        weight = weight_y[t]
        out.append(
            [
                jnp.sum(picked[c * cells_y : (c + 1) * cells_y] * weight, axis=0, keepdims=True)
                for c in range(3)
            ]
        )
    return out


def add_rows(pack, first_row, picks, sampled, keeps):
    for (t, r, hub, cols), rows, keep in zip(picks, sampled, keeps):
        for c in range(3):
            n = first_row + 3 * r + c
            pack[n] = pack[n] + jnp.where(keep, rows[c], 0.0)


def pack_edges(field, edge_west, edge_east, pack_low, pack_high):
    cells_x, cells_y, depth = field.shape[1:]
    for c in range(3):
        edge_west[c] = field[c, 0]
        edge_east[c] = field[c, cells_x - 1]

    def step(t, carry):
        cells = [(c, t * BATCH + k) for k in range(BATCH) for c in range(3)]
        rows = [
            (field[c, i, pl.ds(0, 1), :], field[c, i, pl.ds(cells_y - 1, 1), :]) for c, i in cells
        ]
        for (c, i), (low, high) in zip(cells, rows):
            pack_low[c * cells_x + i] = low
            pack_high[c * cells_x + i] = high
        return carry

    lax.fori_loop(0, cells_x // BATCH, step, 0)


def load_sample(
    velocity, positions, tiles_hbm, coefs_hbm, counts,
    field, pack_low, pack_high, edge_west, edge_east, weight_y, weight_z, strength, point_y, plan,
    point_z, hubs, tiles, places, coefs, flags, touch, bucket, held, small_sems, touch_sem, sems,
):
    cells_x, cells_y, depth = field.shape[1:]
    records, points = coefs.shape
    chunks = cells_x // SUB
    first_row = 3 * cells_x
    start = lax.axis_index("gx") * cells_x

    def chunk(k):
        planes = pl.ds(k * SUB, SUB)
        return pltpu.make_async_copy(velocity.at[:, planes], field.at[:, planes], sems.at[k])

    small = [
        (positions.at[pl.ds(1, 2)], places),
        (positions.at[0, :, pl.ds(0, LANES)], hubs),
        (tiles_hbm, tiles),
        (coefs_hbm, coefs),
    ]
    small = [
        pltpu.make_async_copy(source, target, small_sems.at[n])
        for n, (source, target) in enumerate(small)
    ]
    total_y = cells_y * lax.axis_size("gy")
    base = lax.axis_index("gy") * cells_y
    for copy in small:
        copy.start()
    for k in range(chunks):
        chunk(k).start()
    small[0].wait()
    near = wrapped(places[0], base, total_y)
    inside = jnp.logical_and(near >= -RAD, near < cells_y + RAD)
    height = places[1].astype(jnp.float32)
    lowest = jnp.min(jnp.where(inside, height, float(depth)), axis=1, keepdims=True)
    highest = jnp.max(jnp.where(inside, height, -1.0), axis=1, keepdims=True)
    column = lax.broadcasted_iota(jnp.int32, flags.shape, 1)
    flags[...] = jnp.where(column == 0, lowest, highest).astype(jnp.int32)
    touch_copy = pltpu.make_async_copy(flags, touch, touch_sem)
    touch_copy.start()

    def clear(n, carry):
        for k in range(SUB):
            pack_low[first_row + n * SUB + k] = jnp.zeros((1, points), jnp.float32)
        return carry

    lax.fori_loop(0, 3 * records // SUB, clear, 0)
    for copy in small[1:]:
        copy.wait()
    for first in range(0, records, SUB):
        here = range(first, first + SUB)
        rows = [
            (places[0, pl.ds(r, 1), :], places[1, pl.ds(r, 1), :], coefs[pl.ds(r, 1), :])
            for r in here
        ]
        for r, (y, z, coef) in zip(here, rows):
            point_y[r], point_z[r], strength[r] = y, z, coef
    touch_copy.wait()
    make_plan(hubs, tiles, touch, counts, start, plan, bucket, held)

    def weigh(t, carry):
        units = weight_z.shape[0]
        made = []
        for k in range(2):
            n = jnp.minimum(2 * t + k, plan[0] - 1)
            r, half = plan[HEAD + n], plan[HEAD + 2 * units + n]
            high, low = along_z(point_z[r], half * LANES)
            made.append((n, along_y(point_y[r], base, cells_y, total_y), high, low))
        for n, across, high, low in made:
            weight_y[n] = across
            weight_z[n, 0:LANES] = high
            weight_z[n, LANES:] = low
        return carry

    lax.fori_loop(0, (plan[0] + 1) // 2, weigh, 0)

    def wait_to(ready, wanted):
        def step(k, carry):
            chunk(k).wait()
            return carry

        lax.fori_loop(ready, wanted, step, 0)
        return jnp.maximum(ready, wanted)

    def step(t, ready):
        picks, keeps = group(plan, t)
        ready = wait_to(ready, (picks[-1][2] + RAD) // SUB + 1)
        rows = sampled_rows(field, weight_y, weight_z, picks)
        add_rows(pack_low, first_row, picks, rows, keeps)
        return ready

    ready = lax.fori_loop(0, groups_of(plan), step, jnp.int32(0))
    wait_to(ready, chunks)

    def copy_rows(t, carry):
        rows = [first_row + t * SUB + k for k in range(SUB)]
        values = [pack_low[n] for n in rows]
        for n, value in zip(rows, values):
            pack_high[n] = value
        return carry

    lax.fori_loop(0, 3 * records // SUB, copy_rows, 0)
    pack_edges(field, edge_west, edge_east, pack_low, pack_high)


def fix_west(factor, target, own, inflow, ghost):
    first = lax.axis_index("gx") == 0
    for c in range(3):
        west = jnp.where(first, inflow[c], ghost[c])
        coef = factor * TIME_STEP * VISCOSITY + (0.5 * factor * TIME_STEP) * own[0]
        target[c, 0] = target[c, 0] + (west - own[c]) * coef


def fix_east(factor, target, own, ghost):
    last = lax.axis_index("gx") == lax.axis_size("gx") - 1
    end = target.shape[1] - 1
    for c in range(3):
        east = jnp.where(last, own[c], ghost[c])
        coef = factor * TIME_STEP * VISCOSITY - (0.5 * factor * TIME_STEP) * own[0]
        target[c, end] = target[c, end] + (east - own[c]) * coef


def fix_rows(factor, target, own_low, own_high, got_low, got_high, t):
    cells_x, cells_y = target.shape[1:3]
    spread = factor * TIME_STEP * VISCOSITY
    half = 0.5 * factor * TIME_STEP
    shape = (SUB, target.shape[3])
    row = lax.broadcasted_iota(jnp.int32, shape, 0)
    low, high = pl.ds(0, SUB), pl.ds(cells_y - SUB, SUB)

    def wide(x):
        return jnp.broadcast_to(x, shape)

    for first in range(0, SUB, 2):
        values = []
        for k in range(first, first + 2):
            i = t * SUB + k
            south = jnp.where(row == 0, spread + half * wide(own_low[cells_x + i]), 0.0)
            north = jnp.where(row == SUB - 1, spread - half * wide(own_high[cells_x + i]), 0.0)
            for c in range(3):
                n = c * cells_x + i
                values.append((c, i, low, target[c, i, low, :] + wide(got_low[n]) * south))
                values.append((c, i, high, target[c, i, high, :] + wide(got_high[n]) * north))
        for c, i, rows, value in values:
            target[c, i, rows, :] = value


def slabs_of(weight_of, weight_z, strength, own, low, high, cells, scales, picks):
    cells_x, cells_y, depth = cells
    count = 3 * cells_y
    across = (((1,), (1,)), ((), ()))
    spread = []
    for (t, r, hub, cols), scale in zip(picks, scales):
        rows = [3 * cells_x + 3 * r + c for c in range(3)]
        total = [own[n] + (low[n] + high[n]) for n in rows]
        speed = jnp.sqrt(total[0] * total[0] + total[1] * total[1] + total[2] * total[2])
        pull = strength[r] * (-scale) * speed
        weight = weight_of(t, r)
        spread.append(split(jnp.concatenate([weight * (pull * x) for x in total], axis=0)))
    slabs = []
    for (t, r, hub, cols), part in zip(picks, spread):
        slab = lax.dot_general(part, weight_z[t], across, preferred_element_type=jnp.float32)
        slab = slab[:count] + slab[count:]
        slabs.append(slab[:, :LANES] + slab[:, LANES:])
    return slabs


def add_slab(field, slab, hub, cols):
    cells_y = field.shape[2]
    for c in range(3):
        part = slab[c * cells_y : (c + 1) * cells_y]
        terms = [tap * part for tap in TAP]
        reach = range(-RAD, RAD + 1)
        values = [field[c, hub + d, :, cols] + terms[abs(d)] for d in reach]
        for d, value in zip(reach, values):
            field[c, hub + d, :, cols] = value


def spread_group(t, scale, field, plan, points, own, low, high):
    picks, keeps = group(plan, t)
    scales = [jnp.where(keep, scale, 0.0) for keep in keeps]
    slabs = slabs_of(*points, own, low, high, field.shape[1:], scales, picks)
    for (_, _, hub, cols), slab in zip(picks, slabs):
        add_slab(field, slab, hub, cols)


def spread_sample(
    section_in, inflow, ghost_low, ghost_high, own_low, own_high, own_west, own_east, got_low, got_high,
    plan, weight_y, weight_z, strength,
    section, section_out, stored_z, pack_low, pack_high, edge_west, edge_east,
    share_out, sem, sem_z,
):
    cells_x = section.shape[1]
    records = strength.shape[0]
    share = share_out.shape[2] // 3
    first_row = 3 * cells_x

    def store(t):
        return pltpu.make_async_copy(weight_z.at[t], stored_z.at[t], sem_z.at[t])

    def start_store(t, carry):
        store(t).start()
        return carry

    def wait_store(t, carry):
        store(t).wait()
        return carry

    lax.fori_loop(0, plan[0], start_store, 0)

    def fix_step(t, carry):
        fix_rows(1.0, section, own_low, own_high, got_low, got_high, t)
        return carry

    fix_west(1.0, section, own_west, inflow, ghost_low)
    fix_east(1.0, section, own_east, ghost_high)
    lax.fori_loop(0, cells_x // SUB, fix_step, 0)

    def spread_step(t, carry):
        points = (lambda n, r: weight_y[n], weight_z, strength)
        spread_group(t, TIME_STEP, section, plan, points, own_low, got_low, got_high)
        return carry

    lax.fori_loop(0, groups_of(plan), spread_step, 0)
    copy = pltpu.make_async_copy(section, section_out, sem)
    copy.start()
    pack_edges(section, edge_west, edge_east, pack_low, pack_high)

    def clear(n, carry):
        for k in range(SUB):
            pack_low[first_row + n * SUB + k] = jnp.zeros_like(own_low[0])
        return carry

    lax.fori_loop(0, 3 * records // SUB, clear, 0)

    def sample_step(t, carry):
        picks, keeps = group(plan, t)
        rows = sampled_rows(section, weight_y, weight_z, picks)
        add_rows(pack_low, first_row, picks, rows, keeps)
        return carry

    lax.fori_loop(0, groups_of(plan), sample_step, 0)

    def copy_rows(r, carry):
        old = [own_low[first_row + 3 * r + c] for c in range(3)]
        new = [pack_low[first_row + 3 * r + c] for c in range(3)]
        for c in range(3):
            pack_high[first_row + 3 * r + c] = new[c]
            share_out[r // share, 0, 3 * (r % share) + c] = old[c]
            share_out[r // share, 1, 3 * (r % share) + c] = new[c]
        return carry

    lax.fori_loop(0, records, copy_rows, 0)
    lax.fori_loop(0, plan[0], wait_store, 0)
    copy.wait()


def share_force(parts, strength, counts, after, after_low, after_high, result):
    groups, _, rows = parts.shape[:3]
    share = rows // 3
    mine = lax.axis_index("gy") * share
    values = []
    for s in range(share):
        live = mine + s < counts[0]
        pull = jnp.where(live, -0.5 * strength[mine + s], 0.0)
        total = [0.0, 0.0, 0.0]
        for stage in range(2):
            value = []
            for c in range(3):
                n = 3 * s + c
                x = parts[0, stage, n]
                for g in range(1, groups):
                    x += parts[g, stage, n]
                value.append(x)
            speed = jnp.sqrt(value[0] * value[0] + value[1] * value[1] + value[2] * value[2])
            total = [acc + speed * x for acc, x in zip(total, value)]
        values.extend((3 * s + c, pull * total[c]) for c in range(3))
        if s % 2 == 1 or s + 1 == share:
            for n, value in values:
                for g in range(groups):
                    result[g, n] = value
            values = []


def spread_next(
    following, inflow, ghost_low, ghost_high, own_low, own_high, own_west, own_east, got_low, got_high,
    plan, point_y, stored_z, strength, after,
    result, field, weight_z, in_sems, out_sems, sem_z,
):
    chunks = field.shape[1] // SUB
    factor = 0.5

    def chunk_in(k):
        planes = pl.ds(k * SUB, SUB)
        return pltpu.make_async_copy(following.at[:, planes], field.at[:, planes], in_sems.at[k])

    def chunk_out(k):
        planes = pl.ds(k * SUB, SUB)
        return pltpu.make_async_copy(field.at[:, planes], result.at[:, planes], out_sems.at[k])

    def wait_to(ready, wanted):
        def step(k, carry):
            chunk_in(k).wait()
            fix_rows(factor, field, own_low, own_high, got_low, got_high, k)

            @pl.when(k == 0)
            def _():
                fix_west(factor, field, own_west, inflow, ghost_low)

            @pl.when(k == chunks - 1)
            def _():
                fix_east(factor, field, own_east, ghost_high)

            return carry

        lax.fori_loop(ready, wanted, step, 0)
        return jnp.maximum(ready, wanted)

    def send_to(sent, done):
        def step(k, carry):
            chunk_out(k).start()
            return carry

        lax.fori_loop(sent, done, step, 0)
        return jnp.maximum(sent, done)

    def weights(t):
        return pltpu.make_async_copy(stored_z.at[t], weight_z.at[t], sem_z.at[t])

    def start_weights(t, carry):
        weights(t).start()
        return carry

    def weight_of(t, r):
        cells_y = field.shape[2]
        base = lax.axis_index("gy") * cells_y
        return along_y(point_y[r], base, cells_y, cells_y * lax.axis_size("gy"))

    found = plan[0]
    for k in range(chunks):
        chunk_in(k).start()
        lax.fori_loop(k * found // chunks, (k + 1) * found // chunks, start_weights, 0)

    def step(t, carry):
        ready, sent = carry
        picks, keeps = group(plan, t)
        for (n, _, _, _), keep in zip(picks, keeps):

            @pl.when(keep)
            def _(n=n):
                weights(n).wait()

        ready = wait_to(ready, (picks[-1][2] + RAD) // SUB + 1)
        sent = send_to(sent, (picks[0][2] + RAD) // SUB - 1)
        points = (weight_of, weight_z, strength)
        spread_group(t, factor * TIME_STEP, field, plan, points, own_low, got_low, got_high)
        return ready, sent

    zero = jnp.int32(0)
    ready, sent = lax.fori_loop(0, groups_of(plan), step, (zero, zero))
    sent = send_to(sent, ready)

    def finish(k, carry):
        wait_to(k, k + 1)
        chunk_out(k).start()
        return carry

    lax.fori_loop(ready, chunks, finish, 0)
    for k in range(chunks):
        chunk_out(k).wait()


def fill_shifts(shifts):
    depth = shifts.shape[1]
    source = lax.broadcasted_iota(jnp.int32, (depth, depth), 0)
    cell = lax.broadcasted_iota(jnp.int32, (depth, depth), 1)
    upper = jnp.where(source == cell + 1, 1.0, 0.0)
    lower = jnp.where(source == cell - 1, 1.0, 0.0)
    difference = (upper - lower).astype(shifts.dtype)
    shifts[0:depth] = difference
    shifts[depth : 2 * depth] = difference
    shifts[2 * depth : 3 * depth] = (upper + lower).astype(shifts.dtype)


def along_depth(i, field, shifts, slot):
    depth = shifts.shape[1]
    x = jnp.concatenate([field[c, i + k] for k in range(PLANES) for c in range(3)], axis=0)
    high = x.astype(jnp.bfloat16)
    low = (x - high.astype(jnp.float32)).astype(jnp.bfloat16)
    slot[0] = jnp.dot(
        jnp.concatenate([high, low], axis=1),
        shifts[0 : 2 * depth],
        preferred_element_type=jnp.float32,
    )
    slot[1] = jnp.dot(
        high, shifts[2 * depth : 3 * depth], preferred_element_type=jnp.float32
    )


def advance(i, k, factor, field, slot, target, finish):
    cells_x, cells_y, depth = field.shape[1:]
    groups, halves = cells_y // SUB, depth // LANES
    row = lax.broadcasted_iota(jnp.int32, (SUB, LANES), 0)
    first_row, last_row = row == 0, row == SUB - 1
    spread = factor * TIME_STEP * VISCOSITY
    centre = factor * (1.0 - 6.0 * TIME_STEP * VISCOSITY)
    zero = jnp.zeros((SUB, LANES), jnp.float32)
    loaded = {}
    here = i + k
    west, east = jnp.maximum(here - 1, 0), jnp.minimum(here + 1, cells_x - 1)

    def at(c, g, h):
        if (c, g, h) not in loaded:
            loaded[c, g, h] = field[c, here, pl.ds(g * SUB, SUB), pl.ds(h * LANES, LANES)]
        return loaded[c, g, h]

    values = []
    for g in range(groups):
        for h in range(halves):
            rows, cols = pl.ds(g * SUB, SUB), pl.ds(h * LANES, LANES)
            q = [at(c, g, h) for c in range(3)]
            speeds = [(0.5 * factor * TIME_STEP) * x for x in q]
            less = [spread - s for s in speeds[:2]]
            more = [spread + s for s in speeds[:2]]
            if g == 0:
                more[1] = jnp.where(first_row, zero, more[1])
            if g == groups - 1:
                less[1] = jnp.where(last_row, zero, less[1])
            for c in range(3):
                x = q[c]
                above, below = x, x
                if g + 1 < groups:
                    above = jnp.where(first_row, at(c, g + 1, h), x)
                if g > 0:
                    below = jnp.where(last_row, at(c, g - 1, h), x)
                above, below = pltpu.roll(above, SUB - 1, 0), pltpu.roll(below, 1, 0)
                place = pl.ds((3 * k + c) * cells_y + g * SUB, SUB)
                total = centre * x
                total += field[c, east, rows, cols] * less[0]
                total += field[c, west, rows, cols] * more[0]
                total += above * less[1] + below * more[1]
                total += spread * slot[1, place, cols] - speeds[2] * slot[0, place, cols]
                values.append((c, rows, cols, finish(c, here, rows, cols, total)))
        if g % 2 == 1 or g + 1 == groups:
            for c, rows, cols, value in values:
                target[c, here, rows, cols] = value
            values = []


def advance_batch(i, n, factor, field, shifts, slots, target, finish):
    now, later = slots[n % 2], slots[1 - n % 2]
    along_depth(jnp.minimum(i + PLANES, field.shape[1] - PLANES), field, shifts, later)
    for k in range(PLANES):
        advance(i, k, factor, field, now, target, finish)


def advance_first(field, section, shifts, slot_a, slot_b):
    fill_shifts(shifts)
    along_depth(0, field, shifts, slot_a)

    def step(t, carry):
        for n in range(BLOCK // PLANES):
            advance_batch(
                BLOCK * t + PLANES * n, n, 1.0, field, shifts, (slot_a, slot_b), section,
                lambda c, i, rows, cols, value: value,
            )
        return carry

    lax.fori_loop(0, field.shape[1] // BLOCK, step, 0)


def advance_second(
    section_hbm, velocity, following, token,
    section, field, result, shifts, slot_a, slot_b, in_sems, old_sems, out_sems,
):
    chunks = section.shape[1] // PLANES

    def planes(k):
        return pl.ds(k * PLANES, PLANES)

    def chunk_in(k):
        return pltpu.make_async_copy(
            section_hbm.at[:, planes(k)], section.at[:, planes(k)], in_sems.at[k]
        )

    def chunk_old(k):
        return pltpu.make_async_copy(
            velocity.at[:, planes(k)], field.at[:, planes(k)], old_sems.at[k]
        )

    def chunk_out(k):
        return pltpu.make_async_copy(
            result.at[:, planes(k)], following.at[:, planes(k)], out_sems.at[k]
        )

    def finish(c, i, rows, cols, value):
        return value + 0.5 * field[c, i, rows, cols]

    for k in range(chunks):
        chunk_in(k).start()
        chunk_old(k).start()
    token[...] = jnp.zeros_like(token)
    fill_shifts(shifts)
    chunk_in(0).wait()
    along_depth(0, section, shifts, slot_a)

    def step(t, carry):
        slots = (slot_a, slot_b)
        per = BLOCK // PLANES
        for n in range(per):
            k = t * per + n

            @pl.when(k + 1 < chunks)
            def _(k=k):
                chunk_in(k + 1).wait()

            chunk_old(k).wait()
        for n in range(per):
            advance_batch(
                t * BLOCK + n * PLANES, n, 0.5, section, shifts, slots, result, finish
            )
        for n in range(per):
            chunk_out(t * per + n).start()
        return carry

    lax.fori_loop(0, chunks * PLANES // BLOCK, step, 0)
    for k in range(chunks):
        chunk_out(k).wait()


def shifted(x, axis, step, periodic):
    count = lax.axis_size(axis)
    pairs = [(i, (i + step) % count) for i in range(count)]
    if not periodic:
        pairs = [(s, t) for s, t in pairs if t - s == step]
    return lax.ppermute(x, axis, pairs)


def exchange(pack_low, pack_high, edge_west, edge_east):
    got_low = shifted(pack_high, "gy", 1, True)
    got_high = shifted(pack_low, "gy", -1, True)
    ghost_low = shifted(edge_east, "gx", 1, False)
    ghost_high = shifted(edge_west, "gx", -1, False)
    return ghost_low, ghost_high, got_low, got_high


def local(velocity, inflow, positions, tiles, coefs, counts):
    f32, i32 = jnp.float32, jnp.int32
    whole = velocity.shape
    _, cells_x, cells_y, depth = whole
    groups_y = lax.axis_size("gy")
    positions = positions[0].transpose(1, 0, 2)
    tiles, coefs = tiles[0].T, coefs[0]
    records, points = coefs.shape
    share = records // groups_y
    chunks = cells_x // SUB
    size = 4 * math.prod(whole)
    held = pltpu.VMEM(whole, f32)
    stored = pltpu.HBM(whole, f32)
    array = jax.ShapeDtypeStruct
    pack = array((3 * cells_x + 3 * records, 1, points), f32)
    edge = array((3, cells_y, depth), f32)
    per_record = (records, 1, points)
    units = records * (depth // LANES)
    y_shape, z_shape = (units, cells_y, points), (units, 2 * LANES, points)
    z_bytes = 2 * math.prod(z_shape)
    products = [pltpu.VMEM((3 * depth, depth), jnp.bfloat16)]
    products += [pltpu.VMEM((2, 3 * PLANES * cells_y, depth), f32)] * 2
    unit_sems = pltpu.SemaphoreType.DMA((units,))
    chunk_sems = pltpu.SemaphoreType.DMA((chunks,))

    field, *own_a, weight_y, weight_z, strength, point_y, plan = pl.pallas_call(
        load_sample,
        out_shape=(
            held, pack, pack, edge, edge,
            pltpu.VMEM(y_shape, f32), pltpu.VMEM(z_shape, jnp.bfloat16),
            array(per_record, f32), array(per_record, i32),
            array((HEAD + 3 * units,), i32),
        ),
        in_specs=[ANYWHERE] * 4 + [SCALAR],
        out_specs=(WHOLE,) * 9 + (SCALAR,),
        scratch_shapes=[
            pltpu.VMEM(per_record, i32),
            pltpu.SMEM((records, LANES), i32),
            pltpu.SMEM((2, records), i32),
            pltpu.VMEM((2, records, points), i32),
            pltpu.VMEM((records, points), f32),
            pltpu.VMEM((records, LANES), i32),
            pltpu.SMEM((records, LANES), i32),
            pltpu.SMEM((chunks, records), i32),
            pltpu.SMEM((chunks,), i32),
            pltpu.SemaphoreType.DMA((4,)),
            pltpu.SemaphoreType.DMA,
            chunk_sems,
        ],
        compiler_params=params(),
        cost_estimate=cost(2 * 10**9, 4 * size),
        name="load_sample",
    )(streamed(velocity), streamed(positions), streamed(tiles), streamed(coefs), counts)
    weight_y, weight_z = resident(weight_y), resident(weight_z)
    ghosts_a = exchange(*own_a)

    section = pl.pallas_call(
        advance_first,
        out_shape=held,
        in_specs=[WHOLE],
        out_specs=WHOLE,
        scratch_shapes=products,
        compiler_params=params(),
        cost_estimate=cost(10**9, 4 * size),
        name="advance_first",
    )(resident(field))

    _, section, stored_z, *own_b, shares = pl.pallas_call(
        spread_sample,
        out_shape=(
            held, stored, pltpu.HBM(z_shape, jnp.bfloat16),
            pack, pack, edge, edge,
            array((groups_y, 2, 3 * share, 1, points), f32),
        ),
        in_specs=[WHOLE] * 10 + [SCALAR] + [WHOLE] * 3,
        out_specs=(WHOLE,) + (ANYWHERE,) * 2 + (WHOLE,) * 5,
        input_output_aliases={0: 0},
        scratch_shapes=[pltpu.SemaphoreType.DMA, unit_sems],
        compiler_params=params(),
        cost_estimate=cost(2 * 10**9, 4 * size),
        name="spread_sample",
    )(
        resident(section), inflow, *ghosts_a[:2], *own_a, *ghosts_a[2:],
        plan, weight_y, weight_z, strength,
    )
    shares = lax.all_to_all(shares, "gy", 0, 0)
    ghosts_b = exchange(*own_b)

    following, token = pl.pallas_call(
        advance_second,
        out_shape=(stored, array((SUB, LANES), f32)),
        in_specs=[ANYWHERE] * 2,
        out_specs=(ANYWHERE, WHOLE),
        scratch_shapes=[pltpu.VMEM(whole, f32)] * 3
        + products
        + [pltpu.SemaphoreType.DMA((cells_x // PLANES,))] * 3,
        compiler_params=params(VMEM_LIMIT + 3 * size),
        cost_estimate=cost(10**9, 4 * size),
        name="advance_second",
    )(streamed(section), streamed(velocity))

    forces = pl.pallas_call(
        share_force,
        out_shape=array((groups_y, 3 * share, 1, points), f32),
        in_specs=[WHOLE, WHOLE, SCALAR] + [ANYWHERE] * 3,
        out_specs=WHOLE,
        compiler_params=params(),
        cost_estimate=cost(10**6, 10**6),
        name="share_force",
    )(shares, strength, counts, token, *ghosts_b[:2])
    all_forces = lax.all_to_all(forces, "gy", 0, 0)

    velocity_next = pl.pallas_call(
        spread_next,
        out_shape=stored,
        in_specs=[ANYWHERE] + [WHOLE] * 9 + [SCALAR, WHOLE, ANYWHERE, WHOLE, ANYWHERE],
        out_specs=ANYWHERE,
        scratch_shapes=[
            pltpu.VMEM(whole, f32),
            pltpu.VMEM(z_shape, jnp.bfloat16),
            chunk_sems, chunk_sems, unit_sems,
        ],
        compiler_params=params(VMEM_LIMIT + size + z_bytes),
        cost_estimate=cost(2 * 10**9, 4 * size),
        name="spread_next",
    )(
        streamed(following), inflow, *ghosts_b[:2], *own_b, *ghosts_b[2:],
        plan, point_y, streamed(stored_z), strength, forces,
    )
    return (velocity_next, all_forces.reshape(1, records, 3, points))


def solution(mesh):
    return jax.shard_map(
        local,
        mesh=mesh,
        in_specs=(
            P(None, "gx", "gy", None),
            P(None, "gy", None),
            P("gx", None, None, None),
            P("gx", None, None),
            P("gx", None, None),
            P("gx"),
        ),
        out_specs=(P(None, "gx", "gy", None), P("gx", None, None, None)),
        check_vma=False,
    )
```

```python
import math

import jax
import jax.numpy as jnp
from jax import lax
from jax.experimental import pallas as pl
from jax.experimental.pallas import tpu as pltpu
from jax.sharding import PartitionSpec as P

RAD = 2
VISCOSITY = 0.05
TIME_STEP = 0.1
WIDTH_EPS = 1.5
ROOT_PI = 1.7724538509055159
TAP = [math.exp(-((d / WIDTH_EPS) ** 2)) / (WIDTH_EPS * ROOT_PI) for d in range(RAD + 1)]
HIGH = [float(jnp.bfloat16(tap)) for tap in TAP]
LOW = [float(jnp.bfloat16(tap - high)) for tap, high in zip(TAP, HIGH)]
LANES = 128
SUB = 8
GROUP = 4
BATCH = 4
PLANES = 8
BLOCK = 2 * PLANES
CHUNK = 16
TILES = 8
VMEM_LIMIT = 8 * 2**20

WHOLE = pl.BlockSpec(memory_space=pltpu.VMEM)
SCALAR = pl.BlockSpec(memory_space=pltpu.SMEM)
ANYWHERE = pl.BlockSpec(memory_space=pl.ANY)


def params(limit=VMEM_LIMIT):
    return pltpu.CompilerParams(vmem_limit_bytes=limit)


def cost(flops, nbytes):
    return pl.CostEstimate(flops=flops, bytes_accessed=nbytes, transcendentals=0)


def resident(x):
    return pltpu.with_memory_space_constraint(x, pltpu.VMEM)


def streamed(x):
    return pltpu.with_memory_space_constraint(x, pltpu.HBM)


def split(x):
    high = x.astype(jnp.bfloat16)
    low = (x - high.astype(jnp.float32)).astype(jnp.bfloat16)
    return jnp.concatenate([high, low], axis=0)


def along_z(point_z, start):
    points = point_z.shape[-1]
    row = lax.broadcasted_iota(jnp.int32, (LANES, points), 0).astype(jnp.bfloat16)
    place = (point_z - start).astype(jnp.float32)
    place = jnp.broadcast_to(place, (LANES, points)).astype(jnp.bfloat16)
    dist = jnp.abs(row - place)
    near = [dist == float(d) for d in range(RAD + 1)]
    out = []
    for taps in (HIGH, LOW):
        value = jnp.zeros_like(row)
        for d in range(RAD, -1, -1):
            value = jnp.where(near[d], jnp.full_like(row, taps[d]), value)
        out.append(value)
    return out


def wrapped(point_y, base, total_y):
    near = point_y - base
    near = jnp.where(near > total_y // 2, near - total_y, near)
    return jnp.where(near < -(total_y // 2), near + total_y, near)


def along_y(point_y, base, cells_y, total_y):
    near = wrapped(point_y, base, total_y)
    dist = jnp.abs(lax.broadcasted_iota(jnp.int32, (cells_y, point_y.shape[-1]), 0) - near)
    return jnp.where(
        dist == 0, TAP[0], jnp.where(dist == 1, TAP[1], jnp.where(dist == 2, TAP[2], 0.0))
    )


def make_plan(hub, lowest, highest, tiles, live, table):
    f32, i32 = jnp.float32, jnp.int32
    tile_y = lax.axis_index("gy").astype(f32)
    groups_y = float(lax.axis_size("gy"))
    records, units = hub.shape[0], table.shape[1]
    square = (records, records)
    diagonal = lax.broadcasted_iota(i32, square, 0) == lax.broadcasted_iota(i32, square, 1)

    def turned(x, axis):
        kept = jnp.where(diagonal, jnp.broadcast_to(x, square), 0.0)
        return jnp.sum(kept, axis=axis, keepdims=True)

    first, count = turned(tiles[0:1].astype(f32), 1), turned(tiles[1:2].astype(f32), 1)
    offset = tile_y - first
    offset = jnp.where(offset < 0.0, offset + groups_y, offset)
    order = lax.broadcasted_iota(i32, (records, 1), 0).astype(f32)
    valid = jnp.logical_and(offset < count, order < live)
    valid = jnp.logical_and(valid, highest >= 0.0)
    low = jnp.right_shift(lowest.astype(i32) - RAD, 7)
    high = jnp.right_shift(highest.astype(i32) + RAD, 7)
    number = jnp.where(valid, (high - low + 1).astype(f32), 0.0)
    key = hub * float(records) + order
    before = turned(key, 0) < key
    place = jnp.sum(jnp.where(before, turned(number, 0), 0.0), axis=1, keepdims=True)
    lane = lax.broadcasted_iota(i32, (records, units), 1).astype(f32)
    mine = jnp.logical_and(lane >= place, lane < place + number)

    def pick(value):
        return jnp.sum(jnp.where(mine, value, 0.0), axis=0, keepdims=True).astype(i32)

    table[0:1] = pick(order)
    table[1:2] = pick(hub)
    table[2:3] = pick(low.astype(f32) + lane - place)
    total = jnp.sum(number, axis=0, keepdims=True).astype(i32)
    table[3:4] = jnp.broadcast_to(total, (1, units))


def found(plan):
    return plan[3, 0]


def group(plan, t):
    picks, keeps = [], []
    for k in range(GROUP):
        wanted = GROUP * t + k
        n = jnp.minimum(wanted, found(plan) - 1)
        cols = pl.ds(pl.multiple_of(plan[2, n] * LANES, LANES), LANES)
        picks.append((n, plan[0, n], plan[1, n], cols))
        keeps.append(wanted == n)
    return picks, keeps


def groups_of(plan):
    return (found(plan) + GROUP - 1) // GROUP


def sampled_rows(field, weight_y, weight_z, picks):
    cells_y = field.shape[2]
    rows = 3 * cells_y
    parts = []
    for t, r, hub, cols in picks:
        planes = []
        for c in range(3):
            plane = TAP[0] * field[c, hub, :, cols]
            plane += TAP[1] * (field[c, hub - 1, :, cols] + field[c, hub + 1, :, cols])
            plane += TAP[2] * (field[c, hub - 2, :, cols] + field[c, hub + 2, :, cols])
            planes.append(plane)
        part = split(jnp.concatenate(planes, axis=0))
        parts.append(jnp.concatenate([part, part], axis=1))
    out = []
    for (t, r, hub, cols), part in zip(picks, parts):
        picked = jnp.dot(part, weight_z[t], preferred_element_type=jnp.float32)
        picked = picked[:rows] + picked[rows:]
        weight = weight_y[t]
        out.append(
            [
                jnp.sum(picked[c * cells_y : (c + 1) * cells_y] * weight, axis=0, keepdims=True)
                for c in range(3)
            ]
        )
    return out


def add_rows(pack, first_row, picks, sampled, keeps):
    for (t, r, hub, cols), rows, keep in zip(picks, sampled, keeps):
        for c in range(3):
            n = first_row + 3 * r + c
            pack[n] = pack[n] + jnp.where(keep, rows[c], 0.0)


def pack_edges(field, edge_west, edge_east, pack_low, pack_high):
    cells_x, cells_y, depth = field.shape[1:]
    for c in range(3):
        edge_west[c] = field[c, 0]
        edge_east[c] = field[c, cells_x - 1]

    def step(t, carry):
        cells = [(c, t * BATCH + k) for k in range(BATCH) for c in range(3)]
        rows = [
            (field[c, i, pl.ds(0, 1), :], field[c, i, pl.ds(cells_y - 1, 1), :]) for c, i in cells
        ]
        for (c, i), (low, high) in zip(cells, rows):
            pack_low[c * cells_x + i] = low
            pack_high[c * cells_x + i] = high
        return carry

    lax.fori_loop(0, cells_x // BATCH, step, 0)


def load_sample(
    velocity, positions, tiles_hbm, coefs_hbm, counts,
    field, pack_low, pack_high, edge_west, edge_east, weight_y, weight_z, strength, point_y, plan,
    point_z, hubs, tiles, places, coefs, table, small_sems, plan_sem, sems,
):
    cells_x, cells_y, depth = field.shape[1:]
    records, points = coefs.shape
    chunks = cells_x // CHUNK
    first_row = 3 * cells_x
    start = lax.axis_index("gx") * cells_x

    def chunk(k):
        planes = pl.ds(k * CHUNK, CHUNK)
        return pltpu.make_async_copy(velocity.at[:, planes], field.at[:, planes], sems.at[k])

    small = [
        (positions.at[pl.ds(1, 2)], places),
        (positions.at[0, :, pl.ds(0, LANES)], hubs),
        (tiles_hbm, tiles),
        (coefs_hbm, coefs),
    ]
    small = [
        pltpu.make_async_copy(source, target, small_sems.at[n])
        for n, (source, target) in enumerate(small)
    ]
    total_y = cells_y * lax.axis_size("gy")
    base = lax.axis_index("gy") * cells_y
    for copy in small:
        copy.start()
    for k in range(chunks):
        chunk(k).start()
    for copy in small[:3]:
        copy.wait()
    near = wrapped(places[0], base, total_y)
    inside = jnp.logical_and(near >= -RAD, near < cells_y + RAD)
    height = places[1].astype(jnp.float32)
    lowest = jnp.min(jnp.where(inside, height, float(depth)), axis=1, keepdims=True)
    highest = jnp.max(jnp.where(inside, height, -1.0), axis=1, keepdims=True)
    hub = (hubs[:, 0:1] - start).astype(jnp.float32)
    make_plan(hub, lowest, highest, tiles, counts[0].astype(jnp.float32), table)
    plan_copy = pltpu.make_async_copy(table, plan, plan_sem)
    plan_copy.start()

    def clear(n, carry):
        for k in range(SUB):
            pack_low[first_row + n * SUB + k] = jnp.zeros((1, points), jnp.float32)
        return carry

    lax.fori_loop(0, 3 * records // SUB, clear, 0)
    small[3].wait()
    for first in range(0, records, SUB):
        here = range(first, first + SUB)
        rows = [
            (places[0, pl.ds(r, 1), :], places[1, pl.ds(r, 1), :], coefs[pl.ds(r, 1), :])
            for r in here
        ]
        for r, (y, z, coef) in zip(here, rows):
            point_y[r], point_z[r], strength[r] = y, z, coef
    plan_copy.wait()

    def weigh(t, carry):
        made = []
        for k in range(2):
            n = jnp.minimum(2 * t + k, found(plan) - 1)
            r, half = plan[0, n], plan[2, n]
            high, low = along_z(point_z[r], half * LANES)
            made.append((n, along_y(point_y[r], base, cells_y, total_y), high, low))
        for n, across, high, low in made:
            weight_y[n] = across
            weight_z[n, 0:LANES] = high
            weight_z[n, LANES:] = low
        return carry

    lax.fori_loop(0, (found(plan) + 1) // 2, weigh, 0)

    def wait_to(ready, wanted):
        def step(k, carry):
            chunk(k).wait()
            return carry

        lax.fori_loop(ready, wanted, step, 0)
        return jnp.maximum(ready, wanted)

    def step(t, ready):
        picks, keeps = group(plan, t)
        ready = wait_to(ready, (picks[-1][2] + RAD) // CHUNK + 1)
        rows = sampled_rows(field, weight_y, weight_z, picks)
        add_rows(pack_low, first_row, picks, rows, keeps)
        return ready

    ready = lax.fori_loop(0, groups_of(plan), step, jnp.int32(0))
    wait_to(ready, chunks)

    def copy_rows(t, carry):
        rows = [first_row + t * SUB + k for k in range(SUB)]
        values = [pack_low[n] for n in rows]
        for n, value in zip(rows, values):
            pack_high[n] = value
        return carry

    lax.fori_loop(0, 3 * records // SUB, copy_rows, 0)
    pack_edges(field, edge_west, edge_east, pack_low, pack_high)


def fix_west(factor, target, own, inflow, ghost):
    first = lax.axis_index("gx") == 0
    for c in range(3):
        west = jnp.where(first, inflow[c], ghost[c])
        coef = factor * TIME_STEP * VISCOSITY + (0.5 * factor * TIME_STEP) * own[0]
        target[c, 0] = target[c, 0] + (west - own[c]) * coef


def fix_east(factor, target, own, ghost):
    last = lax.axis_index("gx") == lax.axis_size("gx") - 1
    end = target.shape[1] - 1
    for c in range(3):
        east = jnp.where(last, own[c], ghost[c])
        coef = factor * TIME_STEP * VISCOSITY - (0.5 * factor * TIME_STEP) * own[0]
        target[c, end] = target[c, end] + (east - own[c]) * coef


def fix_rows(factor, target, own_low, own_high, got_low, got_high, t):
    cells_x, cells_y = target.shape[1:3]
    spread = factor * TIME_STEP * VISCOSITY
    half = 0.5 * factor * TIME_STEP
    shape = (SUB, target.shape[3])
    row = lax.broadcasted_iota(jnp.int32, shape, 0)
    low, high = pl.ds(0, SUB), pl.ds(cells_y - SUB, SUB)

    def wide(x):
        return jnp.broadcast_to(x, shape)

    for first in range(0, SUB, 2):
        values = []
        for k in range(first, first + 2):
            i = t * SUB + k
            south = jnp.where(row == 0, spread + half * wide(own_low[cells_x + i]), 0.0)
            north = jnp.where(row == SUB - 1, spread - half * wide(own_high[cells_x + i]), 0.0)
            for c in range(3):
                n = c * cells_x + i
                values.append((c, i, low, target[c, i, low, :] + wide(got_low[n]) * south))
                values.append((c, i, high, target[c, i, high, :] + wide(got_high[n]) * north))
        for c, i, rows, value in values:
            target[c, i, rows, :] = value


def slabs_of(weight_of, weight_z, strength, own, low, high, cells, scales, picks):
    cells_x, cells_y, depth = cells
    count = 3 * cells_y
    across = (((1,), (1,)), ((), ()))
    spread = []
    for (t, r, hub, cols), scale in zip(picks, scales):
        rows = [3 * cells_x + 3 * r + c for c in range(3)]
        total = [own[n] + (low[n] + high[n]) for n in rows]
        speed = jnp.sqrt(total[0] * total[0] + total[1] * total[1] + total[2] * total[2])
        pull = strength[r] * (-scale) * speed
        weight = weight_of(t, r)
        spread.append(split(jnp.concatenate([weight * (pull * x) for x in total], axis=0)))
    slabs = []
    for (t, r, hub, cols), part in zip(picks, spread):
        slab = lax.dot_general(part, weight_z[t], across, preferred_element_type=jnp.float32)
        slab = slab[:count] + slab[count:]
        slabs.append(slab[:, :LANES] + slab[:, LANES:])
    return slabs


def add_slab(field, slab, hub, cols):
    cells_y = field.shape[2]
    for c in range(3):
        part = slab[c * cells_y : (c + 1) * cells_y]
        terms = [tap * part for tap in TAP]
        reach = range(-RAD, RAD + 1)
        values = [field[c, hub + d, :, cols] + terms[abs(d)] for d in reach]
        for d, value in zip(reach, values):
            field[c, hub + d, :, cols] = value


def spread_group(t, scale, field, plan, points, own, low, high):
    picks, keeps = group(plan, t)
    scales = [jnp.where(keep, scale, 0.0) for keep in keeps]
    slabs = slabs_of(*points, own, low, high, field.shape[1:], scales, picks)
    for (_, _, hub, cols), slab in zip(picks, slabs):
        add_slab(field, slab, hub, cols)


def spread_sample(
    section_in, inflow, ghost_low, ghost_high, own_low, own_high, own_west, own_east, got_low, got_high,
    plan, weight_y, weight_z, strength,
    section, section_out, stored_z, pack_low, pack_high, edge_west, edge_east,
    share_out, sem, sem_z,
):
    cells_x = section.shape[1]
    records = strength.shape[0]
    share = share_out.shape[2] // 3
    first_row = 3 * cells_x

    def store(t):
        some = pl.ds(t * TILES, TILES)
        return pltpu.make_async_copy(weight_z.at[some], stored_z.at[some], sem_z.at[t])

    def start_store(t, carry):
        store(t).start()
        return carry

    def wait_store(t, carry):
        store(t).wait()
        return carry

    stores = (found(plan) + TILES - 1) // TILES
    lax.fori_loop(0, stores, start_store, 0)

    def fix_step(t, carry):
        fix_rows(1.0, section, own_low, own_high, got_low, got_high, t)
        return carry

    fix_west(1.0, section, own_west, inflow, ghost_low)
    fix_east(1.0, section, own_east, ghost_high)
    lax.fori_loop(0, cells_x // SUB, fix_step, 0)

    def spread_step(t, carry):
        points = (lambda n, r: weight_y[n], weight_z, strength)
        spread_group(t, TIME_STEP, section, plan, points, own_low, got_low, got_high)
        return carry

    lax.fori_loop(0, groups_of(plan), spread_step, 0)
    copy = pltpu.make_async_copy(section, section_out, sem)
    copy.start()
    pack_edges(section, edge_west, edge_east, pack_low, pack_high)

    def clear(n, carry):
        for k in range(SUB):
            pack_low[first_row + n * SUB + k] = jnp.zeros_like(own_low[0])
        return carry

    lax.fori_loop(0, 3 * records // SUB, clear, 0)

    def sample_step(t, carry):
        picks, keeps = group(plan, t)
        rows = sampled_rows(section, weight_y, weight_z, picks)
        add_rows(pack_low, first_row, picks, rows, keeps)
        return carry

    lax.fori_loop(0, groups_of(plan), sample_step, 0)

    def copy_rows(r, carry):
        old = [own_low[first_row + 3 * r + c] for c in range(3)]
        new = [pack_low[first_row + 3 * r + c] for c in range(3)]
        for c in range(3):
            pack_high[first_row + 3 * r + c] = new[c]
            share_out[r // share, 0, 3 * (r % share) + c] = old[c]
            share_out[r // share, 1, 3 * (r % share) + c] = new[c]
        return carry

    lax.fori_loop(0, records, copy_rows, 0)
    lax.fori_loop(0, stores, wait_store, 0)
    copy.wait()


def share_force(parts, strength, counts, after, after_low, after_high, result):
    groups, _, rows = parts.shape[:3]
    share = rows // 3
    mine = lax.axis_index("gy") * share
    values = []
    for s in range(share):
        live = mine + s < counts[0]
        pull = jnp.where(live, -0.5 * strength[mine + s], 0.0)
        total = [0.0, 0.0, 0.0]
        for stage in range(2):
            value = []
            for c in range(3):
                n = 3 * s + c
                x = parts[0, stage, n]
                for g in range(1, groups):
                    x += parts[g, stage, n]
                value.append(x)
            speed = jnp.sqrt(value[0] * value[0] + value[1] * value[1] + value[2] * value[2])
            total = [acc + speed * x for acc, x in zip(total, value)]
        values.extend((3 * s + c, pull * total[c]) for c in range(3))
        if s % 2 == 1 or s + 1 == share:
            for n, value in values:
                for g in range(groups):
                    result[g, n] = value
            values = []


def spread_next(
    following, inflow, ghost_low, ghost_high, own_low, own_high, own_west, own_east, got_low, got_high,
    plan, point_y, stored_z, strength, after,
    result, field, weight_z, in_sems, out_sems, sem_z,
):
    chunks = field.shape[1] // CHUNK
    factor = 0.5

    def chunk_in(k):
        planes = pl.ds(k * CHUNK, CHUNK)
        return pltpu.make_async_copy(following.at[:, planes], field.at[:, planes], in_sems.at[k])

    def chunk_out(k):
        planes = pl.ds(k * CHUNK, CHUNK)
        return pltpu.make_async_copy(field.at[:, planes], result.at[:, planes], out_sems.at[k])

    def wait_to(ready, wanted):
        def step(k, carry):
            chunk_in(k).wait()
            for n in range(CHUNK // SUB):
                t = k * (CHUNK // SUB) + n
                fix_rows(factor, field, own_low, own_high, got_low, got_high, t)

            @pl.when(k == 0)
            def _():
                fix_west(factor, field, own_west, inflow, ghost_low)

            @pl.when(k == chunks - 1)
            def _():
                fix_east(factor, field, own_east, ghost_high)

            return carry

        lax.fori_loop(ready, wanted, step, 0)
        return jnp.maximum(ready, wanted)

    def send_to(sent, done):
        def step(k, carry):
            chunk_out(k).start()
            return carry

        lax.fori_loop(sent, done, step, 0)
        return jnp.maximum(sent, done)

    def weights(t):
        some = pl.ds(t * TILES, TILES)
        return pltpu.make_async_copy(stored_z.at[some], weight_z.at[some], sem_z.at[t])

    def start_weights(t, carry):
        weights(t).start()
        return carry

    def weight_of(t, r):
        cells_y = field.shape[2]
        base = lax.axis_index("gy") * cells_y
        return along_y(point_y[r], base, cells_y, cells_y * lax.axis_size("gy"))

    loads = (found(plan) + TILES - 1) // TILES
    for k in range(chunks):
        chunk_in(k).start()
        lax.fori_loop(k * loads // chunks, (k + 1) * loads // chunks, start_weights, 0)

    def step(t, carry):
        ready, sent = carry
        picks, keeps = group(plan, t)
        @pl.when(t * GROUP % TILES == 0)
        def _():
            weights(t * GROUP // TILES).wait()

        ready = wait_to(ready, (picks[-1][2] + RAD) // CHUNK + 1)
        sent = send_to(sent, (picks[0][2] - RAD) // CHUNK)
        points = (weight_of, weight_z, strength)
        spread_group(t, factor * TIME_STEP, field, plan, points, own_low, got_low, got_high)
        return ready, sent

    zero = jnp.int32(0)
    ready, sent = lax.fori_loop(0, groups_of(plan), step, (zero, zero))
    sent = send_to(sent, ready)

    def finish(k, carry):
        wait_to(k, k + 1)
        chunk_out(k).start()
        return carry

    lax.fori_loop(ready, chunks, finish, 0)
    for k in range(chunks):
        chunk_out(k).wait()


def fill_shifts(shifts):
    depth = shifts.shape[1]
    source = lax.broadcasted_iota(jnp.int32, (depth, depth), 0)
    cell = lax.broadcasted_iota(jnp.int32, (depth, depth), 1)
    upper = jnp.where(source == cell + 1, 1.0, 0.0)
    lower = jnp.where(source == cell - 1, 1.0, 0.0)
    difference = (upper - lower).astype(shifts.dtype)
    shifts[0:depth] = difference
    shifts[depth : 2 * depth] = difference
    shifts[2 * depth : 3 * depth] = (upper + lower).astype(shifts.dtype)


def along_depth(i, field, shifts, slot):
    depth = shifts.shape[1]
    x = jnp.concatenate([field[c, i + k] for k in range(PLANES) for c in range(3)], axis=0)
    high = x.astype(jnp.bfloat16)
    low = (x - high.astype(jnp.float32)).astype(jnp.bfloat16)
    slot[0] = jnp.dot(
        jnp.concatenate([high, low], axis=1),
        shifts[0 : 2 * depth],
        preferred_element_type=jnp.float32,
    )
    slot[1] = jnp.dot(
        high, shifts[2 * depth : 3 * depth], preferred_element_type=jnp.float32
    )


def advance(i, k, factor, field, slot, target, finish):
    cells_x, cells_y, depth = field.shape[1:]
    groups, halves = cells_y // SUB, depth // LANES
    row = lax.broadcasted_iota(jnp.int32, (SUB, LANES), 0)
    first_row, last_row = row == 0, row == SUB - 1
    spread = factor * TIME_STEP * VISCOSITY
    centre = factor * (1.0 - 6.0 * TIME_STEP * VISCOSITY)
    zero = jnp.zeros((SUB, LANES), jnp.float32)
    loaded = {}
    here = i + k
    west, east = jnp.maximum(here - 1, 0), jnp.minimum(here + 1, cells_x - 1)

    def at(c, g, h):
        if (c, g, h) not in loaded:
            loaded[c, g, h] = field[c, here, pl.ds(g * SUB, SUB), pl.ds(h * LANES, LANES)]
        return loaded[c, g, h]

    values = []
    for g in range(groups):
        for h in range(halves):
            rows, cols = pl.ds(g * SUB, SUB), pl.ds(h * LANES, LANES)
            q = [at(c, g, h) for c in range(3)]
            speeds = [(0.5 * factor * TIME_STEP) * x for x in q]
            less = [spread - s for s in speeds[:2]]
            more = [spread + s for s in speeds[:2]]
            if g == 0:
                more[1] = jnp.where(first_row, zero, more[1])
            if g == groups - 1:
                less[1] = jnp.where(last_row, zero, less[1])
            for c in range(3):
                x = q[c]
                above, below = x, x
                if g + 1 < groups:
                    above = jnp.where(first_row, at(c, g + 1, h), x)
                if g > 0:
                    below = jnp.where(last_row, at(c, g - 1, h), x)
                above, below = pltpu.roll(above, SUB - 1, 0), pltpu.roll(below, 1, 0)
                place = pl.ds((3 * k + c) * cells_y + g * SUB, SUB)
                total = centre * x
                total += field[c, east, rows, cols] * less[0]
                total += field[c, west, rows, cols] * more[0]
                total += above * less[1] + below * more[1]
                total += spread * slot[1, place, cols] - speeds[2] * slot[0, place, cols]
                values.append((c, rows, cols, finish(c, here, rows, cols, total)))
        if g % 2 == 1 or g + 1 == groups:
            for c, rows, cols, value in values:
                target[c, here, rows, cols] = value
            values = []


def advance_batch(i, n, factor, field, shifts, slots, target, finish):
    now, later = slots[n % 2], slots[1 - n % 2]
    along_depth(jnp.minimum(i + PLANES, field.shape[1] - PLANES), field, shifts, later)
    for k in range(PLANES):
        advance(i, k, factor, field, now, target, finish)


def advance_first(field, section, shifts, slot_a, slot_b):
    fill_shifts(shifts)
    along_depth(0, field, shifts, slot_a)

    def step(t, carry):
        for n in range(BLOCK // PLANES):
            advance_batch(
                BLOCK * t + PLANES * n, n, 1.0, field, shifts, (slot_a, slot_b), section,
                lambda c, i, rows, cols, value: value,
            )
        return carry

    lax.fori_loop(0, field.shape[1] // BLOCK, step, 0)


def advance_second(
    section_hbm, velocity, following, token,
    section, field, result, shifts, slot_a, slot_b, in_sems, old_sems, out_sems,
):
    cells_x = section.shape[1]
    blocks = cells_x // BLOCK

    def planes(k):
        return pl.ds(k * BLOCK, BLOCK)

    def section_in(k):
        if isinstance(k, int) and k in (0, blocks):
            some = pl.ds(0 if k == 0 else cells_x - PLANES, PLANES)
        else:
            some = pl.ds(k * BLOCK - PLANES, BLOCK)
        return pltpu.make_async_copy(section_hbm.at[:, some], section.at[:, some], in_sems.at[k])

    def old_in(k):
        return pltpu.make_async_copy(
            velocity.at[:, planes(k)], field.at[:, planes(k)], old_sems.at[k]
        )

    def block_out(k):
        return pltpu.make_async_copy(
            result.at[:, planes(k)], following.at[:, planes(k)], out_sems.at[k]
        )

    def finish(c, i, rows, cols, value):
        return value + 0.5 * field[c, i, rows, cols]

    for k in range(blocks + 1):
        section_in(k).start()
        if k > 0:
            old_in(k - 1).start()
    token[...] = jnp.zeros_like(token)
    fill_shifts(shifts)
    section_in(0).wait()
    along_depth(0, section, shifts, slot_a)

    def step(t, carry):
        @pl.when(t + 1 < blocks)
        def _():
            section_in(t + 1).wait()

        @pl.when(t + 1 == blocks)
        def _():
            section_in(blocks).wait()

        old_in(t).wait()
        for n in range(BLOCK // PLANES):
            advance_batch(
                t * BLOCK + n * PLANES, n, 0.5, section, shifts, (slot_a, slot_b), result, finish
            )
        block_out(t).start()
        return carry

    lax.fori_loop(0, blocks, step, 0)
    for k in range(blocks):
        block_out(k).wait()


def shifted(x, axis, step, periodic):
    count = lax.axis_size(axis)
    pairs = [(i, (i + step) % count) for i in range(count)]
    if not periodic:
        pairs = [(s, t) for s, t in pairs if t - s == step]
    return lax.ppermute(x, axis, pairs)


def exchange(pack_low, pack_high, edge_west, edge_east):
    got_low = shifted(pack_high, "gy", 1, True)
    got_high = shifted(pack_low, "gy", -1, True)
    ghost_low = shifted(edge_east, "gx", 1, False)
    ghost_high = shifted(edge_west, "gx", -1, False)
    return ghost_low, ghost_high, got_low, got_high


def local(velocity, inflow, positions, tiles, coefs, counts):
    f32, i32 = jnp.float32, jnp.int32
    whole = velocity.shape
    _, cells_x, cells_y, depth = whole
    groups_y = lax.axis_size("gy")
    positions = positions[0].transpose(1, 0, 2)
    tiles, coefs = tiles[0].T, coefs[0]
    records, points = coefs.shape
    share = records // groups_y
    chunks = cells_x // CHUNK
    size = 4 * math.prod(whole)
    held = pltpu.VMEM(whole, f32)
    stored = pltpu.HBM(whole, f32)
    array = jax.ShapeDtypeStruct
    pack = array((3 * cells_x + 3 * records, 1, points), f32)
    edge = array((3, cells_y, depth), f32)
    per_record = (records, 1, points)
    units = records * (depth // LANES)
    y_shape, z_shape = (units, cells_y, points), (units, 2 * LANES, points)
    z_bytes = 2 * math.prod(z_shape)
    products = [pltpu.VMEM((3 * depth, depth), jnp.bfloat16)]
    products += [pltpu.VMEM((2, 3 * PLANES * cells_y, depth), f32)] * 2
    unit_sems = pltpu.SemaphoreType.DMA((units // TILES,))
    chunk_sems = pltpu.SemaphoreType.DMA((chunks,))

    field, *own_a, weight_y, weight_z, strength, point_y, plan = pl.pallas_call(
        load_sample,
        out_shape=(
            held, pack, pack, edge, edge,
            pltpu.VMEM(y_shape, f32), pltpu.VMEM(z_shape, jnp.bfloat16),
            array(per_record, f32), array(per_record, i32),
            array((SUB, units), i32),
        ),
        in_specs=[ANYWHERE] * 4 + [SCALAR],
        out_specs=(WHOLE,) * 9 + (SCALAR,),
        scratch_shapes=[
            pltpu.VMEM(per_record, i32),
            pltpu.VMEM((records, LANES), i32),
            pltpu.VMEM((2, records), i32),
            pltpu.VMEM((2, records, points), i32),
            pltpu.VMEM((records, points), f32),
            pltpu.VMEM((SUB, units), i32),
            pltpu.SemaphoreType.DMA((4,)),
            pltpu.SemaphoreType.DMA,
            chunk_sems,
        ],
        compiler_params=params(),
        cost_estimate=cost(2 * 10**9, 4 * size),
        name="load_sample",
    )(streamed(velocity), streamed(positions), streamed(tiles), streamed(coefs), counts)
    weight_y, weight_z = resident(weight_y), resident(weight_z)
    ghosts_a = exchange(*own_a)

    section = pl.pallas_call(
        advance_first,
        out_shape=held,
        in_specs=[WHOLE],
        out_specs=WHOLE,
        scratch_shapes=products,
        compiler_params=params(),
        cost_estimate=cost(10**9, 4 * size),
        name="advance_first",
    )(resident(field))

    _, section, stored_z, *own_b, shares = pl.pallas_call(
        spread_sample,
        out_shape=(
            held, stored, pltpu.HBM(z_shape, jnp.bfloat16),
            pack, pack, edge, edge,
            array((groups_y, 2, 3 * share, 1, points), f32),
        ),
        in_specs=[WHOLE] * 10 + [SCALAR] + [WHOLE] * 3,
        out_specs=(WHOLE,) + (ANYWHERE,) * 2 + (WHOLE,) * 5,
        input_output_aliases={0: 0},
        scratch_shapes=[pltpu.SemaphoreType.DMA, unit_sems],
        compiler_params=params(),
        cost_estimate=cost(2 * 10**9, 4 * size),
        name="spread_sample",
    )(
        resident(section), inflow, *ghosts_a[:2], *own_a, *ghosts_a[2:],
        plan, weight_y, weight_z, strength,
    )
    shares = lax.all_to_all(shares, "gy", 0, 0)
    ghosts_b = exchange(*own_b)

    following, token = pl.pallas_call(
        advance_second,
        out_shape=(stored, array((SUB, LANES), f32)),
        in_specs=[ANYWHERE] * 2,
        out_specs=(ANYWHERE, WHOLE),
        scratch_shapes=[pltpu.VMEM(whole, f32)] * 3
        + products
        + [pltpu.SemaphoreType.DMA((cells_x // BLOCK + 1,))] * 3,
        compiler_params=params(VMEM_LIMIT + 3 * size),
        cost_estimate=cost(10**9, 4 * size),
        name="advance_second",
    )(streamed(section), streamed(velocity))

    forces = pl.pallas_call(
        share_force,
        out_shape=array((groups_y, 3 * share, 1, points), f32),
        in_specs=[WHOLE, WHOLE, SCALAR] + [ANYWHERE] * 3,
        out_specs=WHOLE,
        compiler_params=params(),
        cost_estimate=cost(10**6, 10**6),
        name="share_force",
    )(shares, strength, counts, token, *ghosts_b[:2])
    all_forces = lax.all_to_all(forces, "gy", 0, 0)

    velocity_next = pl.pallas_call(
        spread_next,
        out_shape=stored,
        in_specs=[ANYWHERE] + [WHOLE] * 9 + [SCALAR, WHOLE, ANYWHERE, WHOLE, ANYWHERE],
        out_specs=ANYWHERE,
        scratch_shapes=[
            pltpu.VMEM(whole, f32),
            pltpu.VMEM(z_shape, jnp.bfloat16),
            chunk_sems, chunk_sems, unit_sems,
        ],
        compiler_params=params(VMEM_LIMIT + size + z_bytes),
        cost_estimate=cost(2 * 10**9, 4 * size),
        name="spread_next",
    )(
        streamed(following), inflow, *ghosts_b[:2], *own_b, *ghosts_b[2:],
        plan, point_y, streamed(stored_z), strength, forces,
    )
    return (velocity_next, all_forces.reshape(1, records, 3, points))


def solution(mesh):
    return jax.shard_map(
        local,
        mesh=mesh,
        in_specs=(
            P(None, "gx", "gy", None),
            P(None, "gy", None),
            P("gx", None, None, None),
            P("gx", None, None),
            P("gx", None, None),
            P("gx"),
        ),
        out_specs=(P(None, "gx", "gy", None), P("gx", None, None, None)),
        check_vma=False,
    )
```

```python
import math

import jax
import jax.numpy as jnp
from jax import lax
from jax.experimental import pallas as pl
from jax.experimental.pallas import tpu as pltpu
from jax.sharding import PartitionSpec as P

RAD = 2
VISCOSITY = 0.05
TIME_STEP = 0.1
WIDTH_EPS = 1.5
ROOT_PI = 1.7724538509055159
TAP = [math.exp(-((d / WIDTH_EPS) ** 2)) / (WIDTH_EPS * ROOT_PI) for d in range(RAD + 1)]
HIGH = [float(jnp.bfloat16(tap)) for tap in TAP]
LOW = [float(jnp.bfloat16(tap - high)) for tap, high in zip(TAP, HIGH)]
LANES = 128
SUB = 8
GROUP = 4
BATCH = 4
PLANES = 8
BLOCK = 2 * PLANES
CHUNK = 16
TILES = 8
VMEM_LIMIT = 8 * 2**20

WHOLE = pl.BlockSpec(memory_space=pltpu.VMEM)
SCALAR = pl.BlockSpec(memory_space=pltpu.SMEM)
ANYWHERE = pl.BlockSpec(memory_space=pl.ANY)


def params(limit=VMEM_LIMIT):
    return pltpu.CompilerParams(vmem_limit_bytes=limit)


def cost(flops, nbytes):
    return pl.CostEstimate(flops=flops, bytes_accessed=nbytes, transcendentals=0)


def resident(x):
    return pltpu.with_memory_space_constraint(x, pltpu.VMEM)


def streamed(x):
    return pltpu.with_memory_space_constraint(x, pltpu.HBM)


def split(x):
    high = x.astype(jnp.bfloat16)
    low = (x - high.astype(jnp.float32)).astype(jnp.bfloat16)
    return jnp.concatenate([high, low], axis=0)


def along_z(point_z, start):
    points = point_z.shape[-1]
    row = lax.broadcasted_iota(jnp.int32, (LANES, points), 0).astype(jnp.bfloat16)
    place = (point_z - start).astype(jnp.float32)
    place = jnp.broadcast_to(place, (LANES, points)).astype(jnp.bfloat16)
    dist = jnp.abs(row - place)
    near = [dist == float(d) for d in range(RAD + 1)]
    out = []
    for taps in (HIGH, LOW):
        value = jnp.zeros_like(row)
        for d in range(RAD, -1, -1):
            value = jnp.where(near[d], jnp.full_like(row, taps[d]), value)
        out.append(value)
    return out


def wrapped(point_y, base, total_y):
    near = point_y - base
    near = jnp.where(near > total_y // 2, near - total_y, near)
    return jnp.where(near < -(total_y // 2), near + total_y, near)


def along_y(point_y, base, cells_y, total_y):
    near = wrapped(point_y, base, total_y)
    dist = jnp.abs(lax.broadcasted_iota(jnp.int32, (cells_y, point_y.shape[-1]), 0) - near)
    return jnp.where(
        dist == 0, TAP[0], jnp.where(dist == 1, TAP[1], jnp.where(dist == 2, TAP[2], 0.0))
    )


def make_plan(hub, lowest, highest, tiles, live, table):
    f32, i32 = jnp.float32, jnp.int32
    tile_y = lax.axis_index("gy").astype(f32)
    groups_y = float(lax.axis_size("gy"))
    records, units = hub.shape[0], table.shape[1]
    square = (records, records)
    diagonal = lax.broadcasted_iota(i32, square, 0) == lax.broadcasted_iota(i32, square, 1)

    def turned(x, axis):
        kept = jnp.where(diagonal, jnp.broadcast_to(x, square), 0.0)
        return jnp.sum(kept, axis=axis, keepdims=True)

    first, count = turned(tiles[0:1].astype(f32), 1), turned(tiles[1:2].astype(f32), 1)
    offset = tile_y - first
    offset = jnp.where(offset < 0.0, offset + groups_y, offset)
    order = lax.broadcasted_iota(i32, (records, 1), 0).astype(f32)
    valid = jnp.logical_and(offset < count, order < live)
    valid = jnp.logical_and(valid, highest >= 0.0)
    low = jnp.right_shift(lowest.astype(i32) - RAD, 7)
    high = jnp.right_shift(highest.astype(i32) + RAD, 7)
    number = jnp.where(valid, (high - low + 1).astype(f32), 0.0)
    key = hub * float(records) + order
    before = turned(key, 0) < key
    place = jnp.sum(jnp.where(before, turned(number, 0), 0.0), axis=1, keepdims=True)
    lane = lax.broadcasted_iota(i32, (records, units), 1).astype(f32)
    mine = jnp.logical_and(lane >= place, lane < place + number)

    def pick(value):
        return jnp.sum(jnp.where(mine, value, 0.0), axis=0, keepdims=True).astype(i32)

    table[0:1] = pick(order)
    table[1:2] = pick(hub)
    table[2:3] = pick(low.astype(f32) + lane - place)
    total = jnp.sum(number, axis=0, keepdims=True).astype(i32)
    table[3:4] = jnp.broadcast_to(total, (1, units))


def found(plan):
    return plan[3, 0]


def group(plan, t):
    picks, keeps = [], []
    for k in range(GROUP):
        wanted = GROUP * t + k
        n = jnp.minimum(wanted, found(plan) - 1)
        cols = pl.ds(pl.multiple_of(plan[2, n] * LANES, LANES), LANES)
        picks.append((n, plan[0, n], plan[1, n], cols))
        keeps.append(wanted == n)
    return picks, keeps


def groups_of(plan):
    return (found(plan) + GROUP - 1) // GROUP


def sampled_rows(field, weight_y, weight_z, picks):
    cells_y = field.shape[2]
    rows = 3 * cells_y
    parts = []
    for t, r, hub, cols in picks:
        planes = []
        for c in range(3):
            plane = TAP[0] * field[c, hub, :, cols]
            plane += TAP[1] * (field[c, hub - 1, :, cols] + field[c, hub + 1, :, cols])
            plane += TAP[2] * (field[c, hub - 2, :, cols] + field[c, hub + 2, :, cols])
            planes.append(plane)
        part = split(jnp.concatenate(planes, axis=0))
        parts.append(jnp.concatenate([part, part], axis=1))
    out = []
    for (t, r, hub, cols), part in zip(picks, parts):
        picked = jnp.dot(part, weight_z[t], preferred_element_type=jnp.float32)
        picked = picked[:rows] + picked[rows:]
        weight = weight_y[t]
        out.append(
            [
                jnp.sum(picked[c * cells_y : (c + 1) * cells_y] * weight, axis=0, keepdims=True)
                for c in range(3)
            ]
        )
    return out


def add_rows(pack, first_row, picks, sampled, keeps):
    for (t, r, hub, cols), rows, keep in zip(picks, sampled, keeps):
        for c in range(3):
            n = first_row + 3 * r + c
            pack[n] = pack[n] + jnp.where(keep, rows[c], 0.0)


def pack_sides(field, edge_west, edge_east):
    for c in range(3):
        edge_west[c] = field[c, 0]
        edge_east[c] = field[c, field.shape[1] - 1]


def pack_rows(field, low_out, high_out, first, last):
    cells_x, cells_y = field.shape[1:3]

    def step(t, carry):
        cells = [(c, t * BATCH + k) for k in range(BATCH) for c in range(3)]
        rows = [
            (field[c, i, pl.ds(0, 1), :], field[c, i, pl.ds(cells_y - 1, 1), :]) for c, i in cells
        ]
        for (c, i), (low, high) in zip(cells, rows):
            low_out[c * cells_x + i] = low
            high_out[c * cells_x + i] = high
        return carry

    lax.fori_loop(first // BATCH, last // BATCH, step, 0)


def load_field(
    velocity, positions, tiles_hbm, coefs_hbm, counts,
    field, edge_low, edge_high, edge_west, edge_east, strength, point_y, point_z, plan,
    hubs, tiles, places, coefs, table, small_sems, plan_sem, sems,
):
    cells_x, cells_y, depth = field.shape[1:]
    records, points = coefs.shape
    chunks = cells_x // CHUNK
    start = lax.axis_index("gx") * cells_x

    def chunk(k):
        planes = pl.ds(k * CHUNK, CHUNK)
        return pltpu.make_async_copy(velocity.at[:, planes], field.at[:, planes], sems.at[k])

    small = [
        (positions.at[pl.ds(1, 2)], places),
        (positions.at[0, :, pl.ds(0, LANES)], hubs),
        (tiles_hbm, tiles),
        (coefs_hbm, coefs),
    ]
    small = [
        pltpu.make_async_copy(source, target, small_sems.at[n])
        for n, (source, target) in enumerate(small)
    ]
    total_y = cells_y * lax.axis_size("gy")
    base = lax.axis_index("gy") * cells_y
    for copy in small:
        copy.start()
    for k in range(chunks):
        chunk(k).start()
    for copy in small[:3]:
        copy.wait()
    near = wrapped(places[0], base, total_y)
    inside = jnp.logical_and(near >= -RAD, near < cells_y + RAD)
    height = places[1].astype(jnp.float32)
    lowest = jnp.min(jnp.where(inside, height, float(depth)), axis=1, keepdims=True)
    highest = jnp.max(jnp.where(inside, height, -1.0), axis=1, keepdims=True)
    hub = (hubs[:, 0:1] - start).astype(jnp.float32)
    make_plan(hub, lowest, highest, tiles, counts[0].astype(jnp.float32), table)
    plan_copy = pltpu.make_async_copy(table, plan, plan_sem)
    plan_copy.start()

    small[3].wait()
    for first in range(0, records, SUB):
        here = range(first, first + SUB)
        rows = [
            (places[0, pl.ds(r, 1), :], places[1, pl.ds(r, 1), :], coefs[pl.ds(r, 1), :])
            for r in here
        ]
        for r, (y, z, coef) in zip(here, rows):
            point_y[r], point_z[r], strength[r] = y, z, coef

    def arrived(k, carry):
        chunk(k).wait()
        pack_rows(field, edge_low, edge_high, k * CHUNK, (k + 1) * CHUNK)
        return carry

    lax.fori_loop(0, chunks, arrived, 0)
    pack_sides(field, edge_west, edge_east)
    plan_copy.wait()


def clear_rows(pack, first, last):
    def clear(n, carry):
        for k in range(SUB):
            pack[first + n * SUB + k] = jnp.zeros(pack.shape[1:], jnp.float32)
        return carry

    lax.fori_loop(0, (last - first) // SUB, clear, 0)


def sample_first(field, plan, point_y, point_z, weight_y, weight_z, partial):
    cells_y = field.shape[2]
    total_y = cells_y * lax.axis_size("gy")
    base = lax.axis_index("gy") * cells_y
    clear_rows(partial, 0, partial.shape[0])

    def weigh(t, carry):
        made = []
        for k in range(2):
            n = jnp.minimum(2 * t + k, found(plan) - 1)
            r, half = plan[0, n], plan[2, n]
            high, low = along_z(point_z[r], half * LANES)
            made.append((n, along_y(point_y[r], base, cells_y, total_y), high, low))
        for n, across, high, low in made:
            weight_y[n] = across
            weight_z[n, 0:LANES] = high
            weight_z[n, LANES:] = low
        return carry

    lax.fori_loop(0, (found(plan) + 1) // 2, weigh, 0)

    def step(t, carry):
        picks, keeps = group(plan, t)
        rows = sampled_rows(field, weight_y, weight_z, picks)
        add_rows(partial, 0, picks, rows, keeps)
        return carry

    lax.fori_loop(0, groups_of(plan), step, 0)


def fix_west(factor, target, own, inflow, ghost):
    first = lax.axis_index("gx") == 0
    for c in range(3):
        west = jnp.where(first, inflow[c], ghost[c])
        coef = factor * TIME_STEP * VISCOSITY + (0.5 * factor * TIME_STEP) * own[0]
        target[c, 0] = target[c, 0] + (west - own[c]) * coef


def fix_east(factor, target, own, ghost):
    last = lax.axis_index("gx") == lax.axis_size("gx") - 1
    end = target.shape[1] - 1
    for c in range(3):
        east = jnp.where(last, own[c], ghost[c])
        coef = factor * TIME_STEP * VISCOSITY - (0.5 * factor * TIME_STEP) * own[0]
        target[c, end] = target[c, end] + (east - own[c]) * coef


def fix_rows(factor, target, own_low, own_high, got_low, got_high, t):
    cells_x, cells_y = target.shape[1:3]
    spread = factor * TIME_STEP * VISCOSITY
    half = 0.5 * factor * TIME_STEP
    shape = (SUB, target.shape[3])
    row = lax.broadcasted_iota(jnp.int32, shape, 0)
    low, high = pl.ds(0, SUB), pl.ds(cells_y - SUB, SUB)

    def wide(x):
        return jnp.broadcast_to(x, shape)

    for first in range(0, SUB, 2):
        values = []
        for k in range(first, first + 2):
            i = t * SUB + k
            south = jnp.where(row == 0, spread + half * wide(own_low[cells_x + i]), 0.0)
            north = jnp.where(row == SUB - 1, spread - half * wide(own_high[cells_x + i]), 0.0)
            for c in range(3):
                n = c * cells_x + i
                values.append((c, i, low, target[c, i, low, :] + wide(got_low[n]) * south))
                values.append((c, i, high, target[c, i, high, :] + wide(got_high[n]) * north))
        for c, i, rows, value in values:
            target[c, i, rows, :] = value


def slabs_of(weight_of, weight_z, strength, first_row, own, low, high, cells_y, scales, picks):
    count = 3 * cells_y
    across = (((1,), (1,)), ((), ()))
    spread = []
    for (t, r, hub, cols), scale in zip(picks, scales):
        rows = [first_row + 3 * r + c for c in range(3)]
        total = [own[n] + (low[n] + high[n]) for n in rows]
        speed = jnp.sqrt(total[0] * total[0] + total[1] * total[1] + total[2] * total[2])
        pull = strength[r] * (-scale) * speed
        weight = weight_of(t, r)
        spread.append(split(jnp.concatenate([weight * (pull * x) for x in total], axis=0)))
    slabs = []
    for (t, r, hub, cols), part in zip(picks, spread):
        slab = lax.dot_general(part, weight_z[t], across, preferred_element_type=jnp.float32)
        slab = slab[:count] + slab[count:]
        slabs.append(slab[:, :LANES] + slab[:, LANES:])
    return slabs


def add_slab(field, slab, hub, cols):
    cells_y = field.shape[2]
    for c in range(3):
        part = slab[c * cells_y : (c + 1) * cells_y]
        terms = [tap * part for tap in TAP]
        reach = range(-RAD, RAD + 1)
        values = [field[c, hub + d, :, cols] + terms[abs(d)] for d in reach]
        for d, value in zip(reach, values):
            field[c, hub + d, :, cols] = value


def spread_group(t, scale, field, plan, points, first_row, own, low, high):
    picks, keeps = group(plan, t)
    scales = [jnp.where(keep, scale, 0.0) for keep in keeps]
    slabs = slabs_of(*points, first_row, own, low, high, field.shape[2], scales, picks)
    for (_, _, hub, cols), slab in zip(picks, slabs):
        add_slab(field, slab, hub, cols)


def spread_sample(
    section_in, inflow, ghost_low, ghost_high, own_low, own_high, own_west, own_east, got_low, got_high,
    own, part_low, part_high, plan, weight_y, weight_z, strength,
    section, section_out, stored_z, pack_low, pack_high, edge_west, edge_east,
    share_out, sem, sem_z,
):
    cells_x = section.shape[1]
    records = strength.shape[0]
    share = share_out.shape[2] // 3
    first_row = 3 * cells_x

    def store(t):
        some = pl.ds(t * TILES, TILES)
        return pltpu.make_async_copy(weight_z.at[some], stored_z.at[some], sem_z.at[t])

    def start_store(t, carry):
        store(t).start()
        return carry

    def wait_store(t, carry):
        store(t).wait()
        return carry

    stores = (found(plan) + TILES - 1) // TILES
    lax.fori_loop(0, stores, start_store, 0)

    def fix_step(t, carry):
        fix_rows(1.0, section, own_low, own_high, got_low, got_high, t)
        return carry

    fix_west(1.0, section, own_west, inflow, ghost_low)
    fix_east(1.0, section, own_east, ghost_high)
    lax.fori_loop(0, cells_x // SUB, fix_step, 0)

    def spread_step(t, carry):
        points = (lambda n, r: weight_y[n], weight_z, strength)
        spread_group(t, TIME_STEP, section, plan, points, 0, own, part_low, part_high)
        return carry

    lax.fori_loop(0, groups_of(plan), spread_step, 0)
    copy = pltpu.make_async_copy(section, section_out, sem)
    copy.start()
    pack_sides(section, edge_west, edge_east)
    pack_rows(section, pack_low, pack_high, 0, cells_x)
    clear_rows(pack_low, first_row, first_row + 3 * records)

    def sample_step(t, carry):
        picks, keeps = group(plan, t)
        rows = sampled_rows(section, weight_y, weight_z, picks)
        add_rows(pack_low, first_row, picks, rows, keeps)
        return carry

    lax.fori_loop(0, groups_of(plan), sample_step, 0)

    def copy_rows(r, carry):
        old = [own[3 * r + c] for c in range(3)]
        new = [pack_low[first_row + 3 * r + c] for c in range(3)]
        for c in range(3):
            pack_high[first_row + 3 * r + c] = new[c]
            share_out[r // share, 0, 3 * (r % share) + c] = old[c]
            share_out[r // share, 1, 3 * (r % share) + c] = new[c]
        return carry

    lax.fori_loop(0, records, copy_rows, 0)
    lax.fori_loop(0, stores, wait_store, 0)
    copy.wait()


def share_force(parts, strength, counts, after, after_low, after_high, result):
    groups, _, rows = parts.shape[:3]
    share = rows // 3
    mine = lax.axis_index("gy") * share
    values = []
    for s in range(share):
        live = mine + s < counts[0]
        pull = jnp.where(live, -0.5 * strength[mine + s], 0.0)
        total = [0.0, 0.0, 0.0]
        for stage in range(2):
            value = []
            for c in range(3):
                n = 3 * s + c
                x = parts[0, stage, n]
                for g in range(1, groups):
                    x += parts[g, stage, n]
                value.append(x)
            speed = jnp.sqrt(value[0] * value[0] + value[1] * value[1] + value[2] * value[2])
            total = [acc + speed * x for acc, x in zip(total, value)]
        values.extend((3 * s + c, pull * total[c]) for c in range(3))
        if s % 2 == 1 or s + 1 == share:
            for n, value in values:
                for g in range(groups):
                    result[g, n] = value
            values = []


def spread_next(
    following, inflow, ghost_low, ghost_high, own_low, own_high, own_west, own_east, got_low, got_high,
    plan, point_y, stored_z, strength, after,
    result, field, weight_z, in_sems, out_sems, sem_z,
):
    chunks = field.shape[1] // CHUNK
    factor = 0.5

    def chunk_in(k):
        planes = pl.ds(k * CHUNK, CHUNK)
        return pltpu.make_async_copy(following.at[:, planes], field.at[:, planes], in_sems.at[k])

    def chunk_out(k):
        planes = pl.ds(k * CHUNK, CHUNK)
        return pltpu.make_async_copy(field.at[:, planes], result.at[:, planes], out_sems.at[k])

    def wait_to(ready, wanted):
        def step(k, carry):
            chunk_in(k).wait()
            for n in range(CHUNK // SUB):
                t = k * (CHUNK // SUB) + n
                fix_rows(factor, field, own_low, own_high, got_low, got_high, t)

            @pl.when(k == 0)
            def _():
                fix_west(factor, field, own_west, inflow, ghost_low)

            @pl.when(k == chunks - 1)
            def _():
                fix_east(factor, field, own_east, ghost_high)

            return carry

        lax.fori_loop(ready, wanted, step, 0)
        return jnp.maximum(ready, wanted)

    def send_to(sent, done):
        def step(k, carry):
            chunk_out(k).start()
            return carry

        lax.fori_loop(sent, done, step, 0)
        return jnp.maximum(sent, done)

    def weights(t):
        some = pl.ds(t * TILES, TILES)
        return pltpu.make_async_copy(stored_z.at[some], weight_z.at[some], sem_z.at[t])

    def start_weights(t, carry):
        weights(t).start()
        return carry

    def weight_of(t, r):
        cells_y = field.shape[2]
        base = lax.axis_index("gy") * cells_y
        return along_y(point_y[r], base, cells_y, cells_y * lax.axis_size("gy"))

    loads = (found(plan) + TILES - 1) // TILES
    for k in range(chunks):
        chunk_in(k).start()
        lax.fori_loop(k * loads // chunks, (k + 1) * loads // chunks, start_weights, 0)

    def step(t, carry):
        ready, sent = carry
        picks, keeps = group(plan, t)
        @pl.when(t * GROUP % TILES == 0)
        def _():
            weights(t * GROUP // TILES).wait()

        ready = wait_to(ready, (picks[-1][2] + RAD) // CHUNK + 1)
        sent = send_to(sent, (picks[0][2] - RAD) // CHUNK)
        points = (weight_of, weight_z, strength)
        first_row = 3 * field.shape[1]
        packs = (own_low, got_low, got_high)
        spread_group(t, factor * TIME_STEP, field, plan, points, first_row, *packs)
        return ready, sent

    zero = jnp.int32(0)
    ready, sent = lax.fori_loop(0, groups_of(plan), step, (zero, zero))
    sent = send_to(sent, ready)

    def finish(k, carry):
        wait_to(k, k + 1)
        chunk_out(k).start()
        return carry

    lax.fori_loop(ready, chunks, finish, 0)
    for k in range(chunks):
        chunk_out(k).wait()


def fill_shifts(shifts):
    depth = shifts.shape[1]
    source = lax.broadcasted_iota(jnp.int32, (depth, depth), 0)
    cell = lax.broadcasted_iota(jnp.int32, (depth, depth), 1)
    upper = jnp.where(source == cell + 1, 1.0, 0.0)
    lower = jnp.where(source == cell - 1, 1.0, 0.0)
    difference = (upper - lower).astype(shifts.dtype)
    shifts[0:depth] = difference
    shifts[depth : 2 * depth] = difference
    shifts[2 * depth : 3 * depth] = (upper + lower).astype(shifts.dtype)


def along_depth(i, field, shifts, slot):
    depth = shifts.shape[1]
    x = jnp.concatenate([field[c, i + k] for k in range(PLANES) for c in range(3)], axis=0)
    high = x.astype(jnp.bfloat16)
    low = (x - high.astype(jnp.float32)).astype(jnp.bfloat16)
    slot[0] = jnp.dot(
        jnp.concatenate([high, low], axis=1),
        shifts[0 : 2 * depth],
        preferred_element_type=jnp.float32,
    )
    slot[1] = jnp.dot(
        high, shifts[2 * depth : 3 * depth], preferred_element_type=jnp.float32
    )


def advance(i, k, factor, field, slot, target, finish):
    cells_x, cells_y, depth = field.shape[1:]
    groups, halves = cells_y // SUB, depth // LANES
    row = lax.broadcasted_iota(jnp.int32, (SUB, LANES), 0)
    first_row, last_row = row == 0, row == SUB - 1
    spread = factor * TIME_STEP * VISCOSITY
    centre = factor * (1.0 - 6.0 * TIME_STEP * VISCOSITY)
    zero = jnp.zeros((SUB, LANES), jnp.float32)
    loaded = {}
    here = i + k
    west, east = jnp.maximum(here - 1, 0), jnp.minimum(here + 1, cells_x - 1)

    def at(c, g, h):
        if (c, g, h) not in loaded:
            loaded[c, g, h] = field[c, here, pl.ds(g * SUB, SUB), pl.ds(h * LANES, LANES)]
        return loaded[c, g, h]

    values = []
    for g in range(groups):
        for h in range(halves):
            rows, cols = pl.ds(g * SUB, SUB), pl.ds(h * LANES, LANES)
            q = [at(c, g, h) for c in range(3)]
            speeds = [(0.5 * factor * TIME_STEP) * x for x in q]
            less = [spread - s for s in speeds[:2]]
            more = [spread + s for s in speeds[:2]]
            if g == 0:
                more[1] = jnp.where(first_row, zero, more[1])
            if g == groups - 1:
                less[1] = jnp.where(last_row, zero, less[1])
            for c in range(3):
                x = q[c]
                above, below = x, x
                if g + 1 < groups:
                    above = jnp.where(first_row, at(c, g + 1, h), x)
                if g > 0:
                    below = jnp.where(last_row, at(c, g - 1, h), x)
                above, below = pltpu.roll(above, SUB - 1, 0), pltpu.roll(below, 1, 0)
                place = pl.ds((3 * k + c) * cells_y + g * SUB, SUB)
                total = centre * x
                total += field[c, east, rows, cols] * less[0]
                total += field[c, west, rows, cols] * more[0]
                total += above * less[1] + below * more[1]
                total += spread * slot[1, place, cols] - speeds[2] * slot[0, place, cols]
                values.append((c, rows, cols, finish(c, here, rows, cols, total)))
        if g % 2 == 1 or g + 1 == groups:
            for c, rows, cols, value in values:
                target[c, here, rows, cols] = value
            values = []


def advance_batch(i, n, factor, field, shifts, slots, target, finish):
    now, later = slots[n % 2], slots[1 - n % 2]
    along_depth(jnp.minimum(i + PLANES, field.shape[1] - PLANES), field, shifts, later)
    for k in range(PLANES):
        advance(i, k, factor, field, now, target, finish)


def advance_first(field, after, section, shifts, slot_a, slot_b):
    fill_shifts(shifts)
    along_depth(0, field, shifts, slot_a)

    def step(t, carry):
        for n in range(BLOCK // PLANES):
            advance_batch(
                BLOCK * t + PLANES * n, n, 1.0, field, shifts, (slot_a, slot_b), section,
                lambda c, i, rows, cols, value: value,
            )
        return carry

    lax.fori_loop(0, field.shape[1] // BLOCK, step, 0)


def advance_second(
    section_hbm, velocity, following, token,
    section, field, result, shifts, slot_a, slot_b, in_sems, old_sems, out_sems,
):
    cells_x = section.shape[1]
    blocks = cells_x // BLOCK

    def planes(k):
        return pl.ds(k * BLOCK, BLOCK)

    def section_in(k):
        if isinstance(k, int) and k in (0, blocks):
            some = pl.ds(0 if k == 0 else cells_x - PLANES, PLANES)
        else:
            some = pl.ds(k * BLOCK - PLANES, BLOCK)
        return pltpu.make_async_copy(section_hbm.at[:, some], section.at[:, some], in_sems.at[k])

    def old_in(k):
        return pltpu.make_async_copy(
            velocity.at[:, planes(k)], field.at[:, planes(k)], old_sems.at[k]
        )

    def block_out(k):
        return pltpu.make_async_copy(
            result.at[:, planes(k)], following.at[:, planes(k)], out_sems.at[k]
        )

    def finish(c, i, rows, cols, value):
        return value + 0.5 * field[c, i, rows, cols]

    for k in range(blocks + 1):
        section_in(k).start()
        if k > 0:
            old_in(k - 1).start()
    token[...] = jnp.zeros_like(token)
    fill_shifts(shifts)
    section_in(0).wait()
    along_depth(0, section, shifts, slot_a)

    def step(t, carry):
        @pl.when(t + 1 < blocks)
        def _():
            section_in(t + 1).wait()

        @pl.when(t + 1 == blocks)
        def _():
            section_in(blocks).wait()

        old_in(t).wait()
        for n in range(BLOCK // PLANES):
            advance_batch(
                t * BLOCK + n * PLANES, n, 0.5, section, shifts, (slot_a, slot_b), result, finish
            )
        block_out(t).start()
        return carry

    lax.fori_loop(0, blocks, step, 0)
    for k in range(blocks):
        block_out(k).wait()


def shifted(x, axis, step, periodic):
    count = lax.axis_size(axis)
    pairs = [(i, (i + step) % count) for i in range(count)]
    if not periodic:
        pairs = [(s, t) for s, t in pairs if t - s == step]
    return lax.ppermute(x, axis, pairs)


def exchange(low, high, west, east):
    got_low = shifted(high, "gy", 1, True)
    got_high = shifted(low, "gy", -1, True)
    ghost_low = shifted(east, "gx", 1, False)
    ghost_high = shifted(west, "gx", -1, False)
    return ghost_low, ghost_high, got_low, got_high


def local(velocity, inflow, positions, tiles, coefs, counts):
    f32, i32 = jnp.float32, jnp.int32
    whole = velocity.shape
    _, cells_x, cells_y, depth = whole
    groups_y = lax.axis_size("gy")
    positions = positions[0].transpose(1, 0, 2)
    tiles, coefs = tiles[0].T, coefs[0]
    records, points = coefs.shape
    share = records // groups_y
    chunks = cells_x // CHUNK
    size = 4 * math.prod(whole)
    held = pltpu.VMEM(whole, f32)
    stored = pltpu.HBM(whole, f32)
    array = jax.ShapeDtypeStruct
    pack = array((3 * cells_x + 3 * records, 1, points), f32)
    edge = array((3, cells_y, depth), f32)
    per_record = (records, 1, points)
    units = records * (depth // LANES)
    y_shape, z_shape = (units, cells_y, points), (units, 2 * LANES, points)
    z_bytes = 2 * math.prod(z_shape)
    products = [pltpu.VMEM((3 * depth, depth), jnp.bfloat16)]
    products += [pltpu.VMEM((2, 3 * PLANES * cells_y, depth), f32)] * 2
    unit_sems = pltpu.SemaphoreType.DMA((units // TILES,))
    chunk_sems = pltpu.SemaphoreType.DMA((chunks,))

    halo = array((3 * cells_x, 1, points), f32)
    field, *own_a, strength, point_y, point_z, plan = pl.pallas_call(
        load_field,
        out_shape=(
            held, halo, halo, edge, edge,
            array(per_record, f32), array(per_record, i32), array(per_record, i32),
            array((SUB, units), i32),
        ),
        in_specs=[ANYWHERE] * 4 + [SCALAR],
        out_specs=(WHOLE,) * 8 + (SCALAR,),
        scratch_shapes=[
            pltpu.VMEM((records, LANES), i32),
            pltpu.VMEM((2, records), i32),
            pltpu.VMEM((2, records, points), i32),
            pltpu.VMEM((records, points), f32),
            pltpu.VMEM((SUB, units), i32),
            pltpu.SemaphoreType.DMA((4,)),
            pltpu.SemaphoreType.DMA,
            chunk_sems,
        ],
        compiler_params=params(),
        cost_estimate=cost(10**9, size),
        name="load_field",
    )(streamed(velocity), streamed(positions), streamed(tiles), streamed(coefs), counts)
    field = resident(field)
    ghosts_a = exchange(*own_a)

    weight_y, weight_z, partial = pl.pallas_call(
        sample_first,
        out_shape=(
            pltpu.VMEM(y_shape, f32), pltpu.VMEM(z_shape, jnp.bfloat16),
            array((3 * records, 1, points), f32),
        ),
        in_specs=[WHOLE, SCALAR, WHOLE, WHOLE],
        out_specs=(WHOLE,) * 3,
        compiler_params=params(),
        cost_estimate=cost(2 * 10**9, size),
        name="sample_first",
    )(field, plan, point_y, point_z)
    weight_y, weight_z = resident(weight_y), resident(weight_z)
    parts_a = (partial, shifted(partial, "gy", 1, True), shifted(partial, "gy", -1, True))

    section = pl.pallas_call(
        advance_first,
        out_shape=held,
        in_specs=[WHOLE, ANYWHERE],
        out_specs=WHOLE,
        scratch_shapes=products,
        compiler_params=params(),
        cost_estimate=cost(10**9, 4 * size),
        name="advance_first",
    )(field, partial)

    _, section, stored_z, *own_b, shares = pl.pallas_call(
        spread_sample,
        out_shape=(
            held, stored, pltpu.HBM(z_shape, jnp.bfloat16),
            pack, pack, edge, edge,
            array((groups_y, 2, 3 * share, 1, points), f32),
        ),
        in_specs=[WHOLE] * 13 + [SCALAR] + [WHOLE] * 3,
        out_specs=(WHOLE,) + (ANYWHERE,) * 2 + (WHOLE,) * 5,
        input_output_aliases={0: 0},
        scratch_shapes=[pltpu.SemaphoreType.DMA, unit_sems],
        compiler_params=params(),
        cost_estimate=cost(2 * 10**9, 4 * size),
        name="spread_sample",
    )(
        resident(section), inflow, *ghosts_a[:2], *own_a, *ghosts_a[2:],
        *parts_a, plan, weight_y, weight_z, strength,
    )
    shares = lax.all_to_all(shares, "gy", 0, 0)
    ghosts_b = exchange(*own_b)

    following, token = pl.pallas_call(
        advance_second,
        out_shape=(stored, array((SUB, LANES), f32)),
        in_specs=[ANYWHERE] * 2,
        out_specs=(ANYWHERE, WHOLE),
        scratch_shapes=[pltpu.VMEM(whole, f32)] * 3
        + products
        + [pltpu.SemaphoreType.DMA((cells_x // BLOCK + 1,))] * 3,
        compiler_params=params(VMEM_LIMIT + 3 * size),
        cost_estimate=cost(10**9, 4 * size),
        name="advance_second",
    )(streamed(section), streamed(velocity))

    forces = pl.pallas_call(
        share_force,
        out_shape=array((groups_y, 3 * share, 1, points), f32),
        in_specs=[WHOLE, WHOLE, SCALAR] + [ANYWHERE] * 3,
        out_specs=WHOLE,
        compiler_params=params(),
        cost_estimate=cost(10**6, 10**6),
        name="share_force",
    )(shares, strength, counts, token, *ghosts_b[:2])
    all_forces = lax.all_to_all(forces, "gy", 0, 0)

    velocity_next = pl.pallas_call(
        spread_next,
        out_shape=stored,
        in_specs=[ANYWHERE] + [WHOLE] * 9 + [SCALAR, WHOLE, ANYWHERE, WHOLE, ANYWHERE],
        out_specs=ANYWHERE,
        scratch_shapes=[
            pltpu.VMEM(whole, f32),
            pltpu.VMEM(z_shape, jnp.bfloat16),
            chunk_sems, chunk_sems, unit_sems,
        ],
        compiler_params=params(VMEM_LIMIT + size + z_bytes),
        cost_estimate=cost(2 * 10**9, 4 * size),
        name="spread_next",
    )(
        streamed(following), inflow, *ghosts_b[:2], *own_b, *ghosts_b[2:],
        plan, point_y, streamed(stored_z), strength, forces,
    )
    return (velocity_next, all_forces.reshape(1, records, 3, points))


def solution(mesh):
    return jax.shard_map(
        local,
        mesh=mesh,
        in_specs=(
            P(None, "gx", "gy", None),
            P(None, "gy", None),
            P("gx", None, None, None),
            P("gx", None, None),
            P("gx", None, None),
            P("gx"),
        ),
        out_specs=(P(None, "gx", "gy", None), P("gx", None, None, None)),
        check_vma=False,
    )
```

```python
import math

import jax
import jax.numpy as jnp
from jax import lax
from jax.experimental import pallas as pl
from jax.experimental.pallas import tpu as pltpu
from jax.sharding import PartitionSpec as P

RAD = 2
VISCOSITY = 0.05
TIME_STEP = 0.1
WIDTH_EPS = 1.5
ROOT_PI = 1.7724538509055159
TAP = [math.exp(-((d / WIDTH_EPS) ** 2)) / (WIDTH_EPS * ROOT_PI) for d in range(RAD + 1)]
HIGH = [float(jnp.bfloat16(tap)) for tap in TAP]
LOW = [float(jnp.bfloat16(tap - high)) for tap, high in zip(TAP, HIGH)]
LANES = 128
SUB = 8
GROUP = 4
BATCH = 4
PLANES = 8
BLOCK = 2 * PLANES
CHUNK = 16
TILES = 8
VMEM_LIMIT = 8 * 2**20

WHOLE = pl.BlockSpec(memory_space=pltpu.VMEM)
SCALAR = pl.BlockSpec(memory_space=pltpu.SMEM)
ANYWHERE = pl.BlockSpec(memory_space=pl.ANY)


def params(limit=VMEM_LIMIT):
    return pltpu.CompilerParams(vmem_limit_bytes=limit)


def cost(flops, nbytes):
    return pl.CostEstimate(flops=flops, bytes_accessed=nbytes, transcendentals=0)


def resident(x):
    return pltpu.with_memory_space_constraint(x, pltpu.VMEM)


def streamed(x):
    return pltpu.with_memory_space_constraint(x, pltpu.HBM)


def split(x):
    high = x.astype(jnp.bfloat16)
    low = (x - high.astype(jnp.float32)).astype(jnp.bfloat16)
    return jnp.concatenate([high, low], axis=0)


def along_z(point_z, start):
    points = point_z.shape[-1]
    row = lax.broadcasted_iota(jnp.int32, (LANES, points), 0).astype(jnp.bfloat16)
    place = (point_z - start).astype(jnp.float32)
    place = jnp.broadcast_to(place, (LANES, points)).astype(jnp.bfloat16)
    dist = jnp.abs(row - place)
    near = [dist == float(d) for d in range(RAD + 1)]
    out = []
    for taps in (HIGH, LOW):
        value = jnp.zeros_like(row)
        for d in range(RAD, -1, -1):
            value = jnp.where(near[d], jnp.full_like(row, taps[d]), value)
        out.append(value)
    return out


def wrapped(point_y, base, total_y):
    near = point_y - base
    near = jnp.where(near > total_y // 2, near - total_y, near)
    return jnp.where(near < -(total_y // 2), near + total_y, near)


def along_y(point_y, base, cells_y, total_y):
    near = wrapped(point_y, base, total_y)
    dist = jnp.abs(lax.broadcasted_iota(jnp.int32, (cells_y, point_y.shape[-1]), 0) - near)
    return jnp.where(
        dist == 0, TAP[0], jnp.where(dist == 1, TAP[1], jnp.where(dist == 2, TAP[2], 0.0))
    )


def make_plan(hub, lowest, highest, tiles, live, table):
    f32, i32 = jnp.float32, jnp.int32
    tile_y = lax.axis_index("gy").astype(f32)
    groups_y = float(lax.axis_size("gy"))
    records, units = hub.shape[0], table.shape[1]
    square = (records, records)
    diagonal = lax.broadcasted_iota(i32, square, 0) == lax.broadcasted_iota(i32, square, 1)

    def turned(x, axis):
        kept = jnp.where(diagonal, jnp.broadcast_to(x, square), 0.0)
        return jnp.sum(kept, axis=axis, keepdims=True)

    first, count = turned(tiles[0:1].astype(f32), 1), turned(tiles[1:2].astype(f32), 1)
    offset = tile_y - first
    offset = jnp.where(offset < 0.0, offset + groups_y, offset)
    order = lax.broadcasted_iota(i32, (records, 1), 0).astype(f32)
    valid = jnp.logical_and(offset < count, order < live)
    valid = jnp.logical_and(valid, highest >= 0.0)
    low = jnp.right_shift(lowest.astype(i32) - RAD, 7)
    high = jnp.right_shift(highest.astype(i32) + RAD, 7)
    number = jnp.where(valid, (high - low + 1).astype(f32), 0.0)
    key = hub * float(records) + order
    before = turned(key, 0) < key
    place = jnp.sum(jnp.where(before, turned(number, 0), 0.0), axis=1, keepdims=True)
    lane = lax.broadcasted_iota(i32, (records, units), 1).astype(f32)
    mine = jnp.logical_and(lane >= place, lane < place + number)

    def pick(value):
        return jnp.sum(jnp.where(mine, value, 0.0), axis=0, keepdims=True).astype(i32)

    table[0:1] = pick(order)
    table[1:2] = pick(hub)
    table[2:3] = pick(low.astype(f32) + lane - place)
    total = jnp.sum(number, axis=0, keepdims=True).astype(i32)
    table[3:4] = jnp.broadcast_to(total, (1, units))


def found(plan):
    return plan[3, 0]


def group(plan, t):
    picks, keeps = [], []
    for k in range(GROUP):
        wanted = GROUP * t + k
        n = jnp.minimum(wanted, found(plan) - 1)
        cols = pl.ds(pl.multiple_of(plan[2, n] * LANES, LANES), LANES)
        picks.append((n, plan[0, n], plan[1, n], cols))
        keeps.append(wanted == n)
    return picks, keeps


def groups_of(plan):
    return (found(plan) + GROUP - 1) // GROUP


def sampled_rows(field, weight_y, weight_z, picks):
    cells_y = field.shape[2]
    rows = 3 * cells_y
    parts = []
    for t, r, hub, cols in picks:
        planes = []
        for c in range(3):
            plane = TAP[0] * field[c, hub, :, cols]
            plane += TAP[1] * (field[c, hub - 1, :, cols] + field[c, hub + 1, :, cols])
            plane += TAP[2] * (field[c, hub - 2, :, cols] + field[c, hub + 2, :, cols])
            planes.append(plane)
        part = split(jnp.concatenate(planes, axis=0))
        parts.append(jnp.concatenate([part, part], axis=1))
    out = []
    for (t, r, hub, cols), part in zip(picks, parts):
        picked = jnp.dot(part, weight_z[t], preferred_element_type=jnp.float32)
        picked = picked[:rows] + picked[rows:]
        weight = weight_y[t]
        out.append(
            [
                jnp.sum(picked[c * cells_y : (c + 1) * cells_y] * weight, axis=0, keepdims=True)
                for c in range(3)
            ]
        )
    return out


def add_rows(pack, first_row, picks, sampled, keeps):
    for (t, r, hub, cols), rows, keep in zip(picks, sampled, keeps):
        for c in range(3):
            n = first_row + 3 * r + c
            pack[n] = pack[n] + jnp.where(keep, rows[c], 0.0)


def pack_edges(field, edge_west, edge_east, pack_low, pack_high):
    cells_x, cells_y, depth = field.shape[1:]
    for c in range(3):
        edge_west[c] = field[c, 0]
        edge_east[c] = field[c, cells_x - 1]

    def step(t, carry):
        cells = [(c, t * BATCH + k) for k in range(BATCH) for c in range(3)]
        rows = [
            (field[c, i, pl.ds(0, 1), :], field[c, i, pl.ds(cells_y - 1, 1), :]) for c, i in cells
        ]
        for (c, i), (low, high) in zip(cells, rows):
            pack_low[c * cells_x + i] = low
            pack_high[c * cells_x + i] = high
        return carry

    lax.fori_loop(0, cells_x // BATCH, step, 0)


def load_sample(
    velocity, positions, tiles_hbm, coefs_hbm, counts,
    field, pack_low, pack_high, edge_west, edge_east, weight_y, weight_z, strength, point_y, plan,
    point_z, hubs, tiles, places, coefs, table, small_sems, plan_sem, sems,
):
    cells_x, cells_y, depth = field.shape[1:]
    records, points = coefs.shape
    chunks = cells_x // CHUNK
    first_row = 3 * cells_x
    start = lax.axis_index("gx") * cells_x

    def chunk(k):
        planes = pl.ds(k * CHUNK, CHUNK)
        return pltpu.make_async_copy(velocity.at[:, planes], field.at[:, planes], sems.at[k])

    small = [
        (positions.at[pl.ds(1, 2)], places),
        (positions.at[0, :, pl.ds(0, LANES)], hubs),
        (tiles_hbm, tiles),
        (coefs_hbm, coefs),
    ]
    small = [
        pltpu.make_async_copy(source, target, small_sems.at[n])
        for n, (source, target) in enumerate(small)
    ]
    total_y = cells_y * lax.axis_size("gy")
    base = lax.axis_index("gy") * cells_y
    for copy in small:
        copy.start()
    for k in range(chunks):
        chunk(k).start()
    for copy in small[:3]:
        copy.wait()
    near = wrapped(places[0], base, total_y)
    inside = jnp.logical_and(near >= -RAD, near < cells_y + RAD)
    height = places[1].astype(jnp.float32)
    lowest = jnp.min(jnp.where(inside, height, float(depth)), axis=1, keepdims=True)
    highest = jnp.max(jnp.where(inside, height, -1.0), axis=1, keepdims=True)
    hub = (hubs[:, 0:1] - start).astype(jnp.float32)
    make_plan(hub, lowest, highest, tiles, counts[0].astype(jnp.float32), table)
    plan_copy = pltpu.make_async_copy(table, plan, plan_sem)
    plan_copy.start()

    def clear(n, carry):
        for k in range(SUB):
            pack_low[first_row + n * SUB + k] = jnp.zeros((1, points), jnp.float32)
        return carry

    lax.fori_loop(0, 3 * records // SUB, clear, 0)
    small[3].wait()
    for first in range(0, records, SUB):
        here = range(first, first + SUB)
        rows = [
            (places[0, pl.ds(r, 1), :], places[1, pl.ds(r, 1), :], coefs[pl.ds(r, 1), :])
            for r in here
        ]
        for r, (y, z, coef) in zip(here, rows):
            point_y[r], point_z[r], strength[r] = y, z, coef
    plan_copy.wait()

    def weigh(t, carry):
        made = []
        for k in range(2):
            n = jnp.minimum(2 * t + k, found(plan) - 1)
            r, half = plan[0, n], plan[2, n]
            high, low = along_z(point_z[r], half * LANES)
            made.append((n, along_y(point_y[r], base, cells_y, total_y), high, low))
        for n, across, high, low in made:
            weight_y[n] = across
            weight_z[n, 0:LANES] = high
            weight_z[n, LANES:] = low
        return carry

    lax.fori_loop(0, (found(plan) + 1) // 2, weigh, 0)

    def wait_to(ready, wanted):
        def step(k, carry):
            chunk(k).wait()
            return carry

        lax.fori_loop(ready, wanted, step, 0)
        return jnp.maximum(ready, wanted)

    def step(t, ready):
        picks, keeps = group(plan, t)
        ready = wait_to(ready, (picks[-1][2] + RAD) // CHUNK + 1)
        rows = sampled_rows(field, weight_y, weight_z, picks)
        add_rows(pack_low, first_row, picks, rows, keeps)
        return ready

    ready = lax.fori_loop(0, groups_of(plan), step, jnp.int32(0))
    wait_to(ready, chunks)

    def copy_rows(t, carry):
        rows = [first_row + t * SUB + k for k in range(SUB)]
        values = [pack_low[n] for n in rows]
        for n, value in zip(rows, values):
            pack_high[n] = value
        return carry

    lax.fori_loop(0, 3 * records // SUB, copy_rows, 0)
    pack_edges(field, edge_west, edge_east, pack_low, pack_high)


def fix_west(factor, target, own, inflow, ghost):
    first = lax.axis_index("gx") == 0
    for c in range(3):
        west = jnp.where(first, inflow[c], ghost[c])
        coef = factor * TIME_STEP * VISCOSITY + (0.5 * factor * TIME_STEP) * own[0]
        target[c, 0] = target[c, 0] + (west - own[c]) * coef


def fix_east(factor, target, own, ghost):
    last = lax.axis_index("gx") == lax.axis_size("gx") - 1
    end = target.shape[1] - 1
    for c in range(3):
        east = jnp.where(last, own[c], ghost[c])
        coef = factor * TIME_STEP * VISCOSITY - (0.5 * factor * TIME_STEP) * own[0]
        target[c, end] = target[c, end] + (east - own[c]) * coef


def fix_rows(factor, target, own_low, own_high, got_low, got_high, t):
    cells_x, cells_y = target.shape[1:3]
    spread = factor * TIME_STEP * VISCOSITY
    half = 0.5 * factor * TIME_STEP
    shape = (SUB, target.shape[3])
    row = lax.broadcasted_iota(jnp.int32, shape, 0)
    low, high = pl.ds(0, SUB), pl.ds(cells_y - SUB, SUB)

    def wide(x):
        return jnp.broadcast_to(x, shape)

    for first in range(0, SUB, 2):
        values = []
        for k in range(first, first + 2):
            i = t * SUB + k
            south = jnp.where(row == 0, spread + half * wide(own_low[cells_x + i]), 0.0)
            north = jnp.where(row == SUB - 1, spread - half * wide(own_high[cells_x + i]), 0.0)
            for c in range(3):
                n = c * cells_x + i
                values.append((c, i, low, target[c, i, low, :] + wide(got_low[n]) * south))
                values.append((c, i, high, target[c, i, high, :] + wide(got_high[n]) * north))
        for c, i, rows, value in values:
            target[c, i, rows, :] = value


def slabs_of(weight_of, weight_z, strength, own, low, high, cells, scales, picks):
    cells_x, cells_y, depth = cells
    count = 3 * cells_y
    across = (((1,), (1,)), ((), ()))
    spread = []
    for (t, r, hub, cols), scale in zip(picks, scales):
        rows = [3 * cells_x + 3 * r + c for c in range(3)]
        total = [own[n] + (low[n] + high[n]) for n in rows]
        speed = jnp.sqrt(total[0] * total[0] + total[1] * total[1] + total[2] * total[2])
        pull = strength[r] * (-scale) * speed
        weight = weight_of(t, r)
        spread.append(split(jnp.concatenate([weight * (pull * x) for x in total], axis=0)))
    slabs = []
    for (t, r, hub, cols), part in zip(picks, spread):
        slab = lax.dot_general(part, weight_z[t], across, preferred_element_type=jnp.float32)
        slab = slab[:count] + slab[count:]
        slabs.append(slab[:, :LANES] + slab[:, LANES:])
    return slabs


def add_slab(field, slab, hub, cols):
    cells_y = field.shape[2]
    for c in range(3):
        part = slab[c * cells_y : (c + 1) * cells_y]
        terms = [tap * part for tap in TAP]
        reach = range(-RAD, RAD + 1)
        values = [field[c, hub + d, :, cols] + terms[abs(d)] for d in reach]
        for d, value in zip(reach, values):
            field[c, hub + d, :, cols] = value


def spread_group(t, scale, field, plan, points, own, low, high):
    picks, keeps = group(plan, t)
    scales = [jnp.where(keep, scale, 0.0) for keep in keeps]
    slabs = slabs_of(*points, own, low, high, field.shape[1:], scales, picks)
    for (_, _, hub, cols), slab in zip(picks, slabs):
        add_slab(field, slab, hub, cols)


def spread_sample(
    section_in, inflow, ghost_low, ghost_high, own_low, own_high, own_west, own_east, got_low, got_high,
    plan, weight_y, weight_z, strength,
    section, section_out, stored_z, pack_low, pack_high, edge_west, edge_east,
    share_out, sem, sem_z,
):
    cells_x = section.shape[1]
    records = strength.shape[0]
    share = share_out.shape[2] // 3
    first_row = 3 * cells_x

    def store(t):
        some = pl.ds(t * TILES, TILES)
        return pltpu.make_async_copy(weight_z.at[some], stored_z.at[some], sem_z.at[t])

    def start_store(t, carry):
        store(t).start()
        return carry

    def wait_store(t, carry):
        store(t).wait()
        return carry

    stores = (found(plan) + TILES - 1) // TILES
    lax.fori_loop(0, stores, start_store, 0)

    def fix_step(t, carry):
        fix_rows(1.0, section, own_low, own_high, got_low, got_high, t)
        return carry

    fix_west(1.0, section, own_west, inflow, ghost_low)
    fix_east(1.0, section, own_east, ghost_high)
    lax.fori_loop(0, cells_x // SUB, fix_step, 0)

    def spread_step(t, carry):
        points = (lambda n, r: weight_y[n], weight_z, strength)
        spread_group(t, TIME_STEP, section, plan, points, own_low, got_low, got_high)
        return carry

    lax.fori_loop(0, groups_of(plan), spread_step, 0)
    copy = pltpu.make_async_copy(section, section_out, sem)
    copy.start()
    pack_edges(section, edge_west, edge_east, pack_low, pack_high)

    def clear(n, carry):
        for k in range(SUB):
            pack_low[first_row + n * SUB + k] = jnp.zeros_like(own_low[0])
        return carry

    lax.fori_loop(0, 3 * records // SUB, clear, 0)

    def sample_step(t, carry):
        picks, keeps = group(plan, t)
        rows = sampled_rows(section, weight_y, weight_z, picks)
        add_rows(pack_low, first_row, picks, rows, keeps)
        return carry

    lax.fori_loop(0, groups_of(plan), sample_step, 0)

    def copy_rows(r, carry):
        old = [own_low[first_row + 3 * r + c] for c in range(3)]
        new = [pack_low[first_row + 3 * r + c] for c in range(3)]
        for c in range(3):
            pack_high[first_row + 3 * r + c] = new[c]
            share_out[r // share, 0, 3 * (r % share) + c] = old[c]
            share_out[r // share, 1, 3 * (r % share) + c] = new[c]
        return carry

    lax.fori_loop(0, records, copy_rows, 0)
    lax.fori_loop(0, stores, wait_store, 0)
    copy.wait()


def share_force(parts, strength, counts, after, after_low, after_high, result):
    groups, _, rows = parts.shape[:3]
    share = rows // 3
    mine = lax.axis_index("gy") * share
    values = []
    for s in range(share):
        live = mine + s < counts[0]
        pull = jnp.where(live, -0.5 * strength[mine + s], 0.0)
        total = [0.0, 0.0, 0.0]
        for stage in range(2):
            value = []
            for c in range(3):
                n = 3 * s + c
                x = parts[0, stage, n]
                for g in range(1, groups):
                    x += parts[g, stage, n]
                value.append(x)
            speed = jnp.sqrt(value[0] * value[0] + value[1] * value[1] + value[2] * value[2])
            total = [acc + speed * x for acc, x in zip(total, value)]
        values.extend((3 * s + c, pull * total[c]) for c in range(3))
        if s % 2 == 1 or s + 1 == share:
            for n, value in values:
                for g in range(groups):
                    result[g, n] = value
            values = []


def spread_next(
    following, inflow, ghost_low, ghost_high, own_low, own_high, own_west, own_east, got_low, got_high,
    plan, point_y, stored_z, strength, after,
    result, field, weight_z, in_sems, out_sems, sem_z,
):
    chunks = field.shape[1] // CHUNK
    factor = 0.5

    def chunk_in(k):
        planes = pl.ds(k * CHUNK, CHUNK)
        return pltpu.make_async_copy(following.at[:, planes], field.at[:, planes], in_sems.at[k])

    def chunk_out(k):
        planes = pl.ds(k * CHUNK, CHUNK)
        return pltpu.make_async_copy(field.at[:, planes], result.at[:, planes], out_sems.at[k])

    def wait_to(ready, wanted):
        def step(k, carry):
            chunk_in(k).wait()
            for n in range(CHUNK // SUB):
                t = k * (CHUNK // SUB) + n
                fix_rows(factor, field, own_low, own_high, got_low, got_high, t)

            @pl.when(k == 0)
            def _():
                fix_west(factor, field, own_west, inflow, ghost_low)

            @pl.when(k == chunks - 1)
            def _():
                fix_east(factor, field, own_east, ghost_high)

            return carry

        lax.fori_loop(ready, wanted, step, 0)
        return jnp.maximum(ready, wanted)

    def send_to(sent, done):
        def step(k, carry):
            chunk_out(k).start()
            return carry

        lax.fori_loop(sent, done, step, 0)
        return jnp.maximum(sent, done)

    def weights(t):
        some = pl.ds(t * TILES, TILES)
        return pltpu.make_async_copy(stored_z.at[some], weight_z.at[some], sem_z.at[t])

    def start_weights(t, carry):
        weights(t).start()
        return carry

    def weight_of(t, r):
        cells_y = field.shape[2]
        base = lax.axis_index("gy") * cells_y
        return along_y(point_y[r], base, cells_y, cells_y * lax.axis_size("gy"))

    loads = (found(plan) + TILES - 1) // TILES
    for k in range(chunks):
        chunk_in(k).start()
        lax.fori_loop(k * loads // chunks, (k + 1) * loads // chunks, start_weights, 0)

    def step(t, carry):
        ready, sent = carry
        picks, keeps = group(plan, t)
        @pl.when(t * GROUP % TILES == 0)
        def _():
            weights(t * GROUP // TILES).wait()

        ready = wait_to(ready, (picks[-1][2] + RAD) // CHUNK + 1)
        sent = send_to(sent, (picks[0][2] - RAD) // CHUNK)
        points = (weight_of, weight_z, strength)
        spread_group(t, factor * TIME_STEP, field, plan, points, own_low, got_low, got_high)
        return ready, sent

    zero = jnp.int32(0)
    ready, sent = lax.fori_loop(0, groups_of(plan), step, (zero, zero))
    sent = send_to(sent, ready)

    def finish(k, carry):
        wait_to(k, k + 1)
        chunk_out(k).start()
        return carry

    lax.fori_loop(ready, chunks, finish, 0)
    for k in range(chunks):
        chunk_out(k).wait()


def fill_shifts(shifts):
    depth = shifts.shape[1]
    source = lax.broadcasted_iota(jnp.int32, (depth, depth), 0)
    cell = lax.broadcasted_iota(jnp.int32, (depth, depth), 1)
    upper = jnp.where(source == cell + 1, 1.0, 0.0)
    lower = jnp.where(source == cell - 1, 1.0, 0.0)
    difference = (upper - lower).astype(shifts.dtype)
    shifts[0:depth] = difference
    shifts[depth : 2 * depth] = difference


def along_depth(i, field, shifts, slot):
    x = jnp.concatenate([field[c, i + k] for k in range(PLANES) for c in range(3)], axis=0)
    high = x.astype(jnp.bfloat16)
    low = (x - high.astype(jnp.float32)).astype(jnp.bfloat16)
    slot[...] = jnp.dot(
        jnp.concatenate([high, low], axis=1), shifts[...], preferred_element_type=jnp.float32
    )


def advance(i, k, factor, field, slot, target, finish):
    cells_x, cells_y, depth = field.shape[1:]
    groups, halves = cells_y // SUB, depth // LANES
    row = lax.broadcasted_iota(jnp.int32, (SUB, LANES), 0)
    lane = lax.broadcasted_iota(jnp.int32, (SUB, LANES), 1)
    first_row, last_row, first_lane = row == 0, row == SUB - 1, lane == 0
    spread = factor * TIME_STEP * VISCOSITY
    centre = factor * (1.0 - 6.0 * TIME_STEP * VISCOSITY)
    zero = jnp.zeros((SUB, LANES), jnp.float32)
    loaded = {}
    here = i + k
    west, east = jnp.maximum(here - 1, 0), jnp.minimum(here + 1, cells_x - 1)

    def at(c, g, h):
        if (c, g, h) not in loaded:
            loaded[c, g, h] = field[c, here, pl.ds(g * SUB, SUB), pl.ds(h * LANES, LANES)]
        return loaded[c, g, h]

    values = []
    for g in range(groups):
        turned = {}
        for h in range(halves):
            rows, cols = pl.ds(g * SUB, SUB), pl.ds(h * LANES, LANES)
            q = [at(c, g, h) for c in range(3)]
            speeds = [(0.5 * factor * TIME_STEP) * x for x in q]
            less = [spread - s for s in speeds]
            more = [spread + s for s in speeds[:2]]
            if g == 0:
                more[1] = jnp.where(first_row, zero, more[1])
            if g == groups - 1:
                less[1] = jnp.where(last_row, zero, less[1])
            for c in range(3):
                x = q[c]
                above, below = x, x
                if g + 1 < groups:
                    above = jnp.where(first_row, at(c, g + 1, h), x)
                if g > 0:
                    below = jnp.where(last_row, at(c, g - 1, h), x)
                above, below = pltpu.roll(above, SUB - 1, 0), pltpu.roll(below, 1, 0)
                place = pl.ds((3 * k + c) * cells_y + g * SUB, SUB)
                total = centre * x
                total += field[c, east, rows, cols] * less[0]
                total += field[c, west, rows, cols] * more[0]
                total += above * less[1] + below * more[1]
                lower = pltpu.roll(x, 1, 1)
                turned[c, h] = lower
                lower = jnp.where(first_lane, zero if h == 0 else turned[c, h - 1], lower)
                total += slot[place, cols] * less[2] + (2.0 * spread) * lower
                values.append((c, rows, cols, finish(c, here, rows, cols, total)))
        if g % 2 == 1 or g + 1 == groups:
            for c, rows, cols, value in values:
                target[c, here, rows, cols] = value
            values = []


def advance_batch(i, n, factor, field, shifts, slots, target, finish):
    now, later = slots[n % 2], slots[1 - n % 2]
    along_depth(jnp.minimum(i + PLANES, field.shape[1] - PLANES), field, shifts, later)
    for k in range(PLANES):
        advance(i, k, factor, field, now, target, finish)


def advance_first(field, section, shifts, slot_a, slot_b):
    fill_shifts(shifts)
    along_depth(0, field, shifts, slot_a)

    def step(t, carry):
        for n in range(BLOCK // PLANES):
            advance_batch(
                BLOCK * t + PLANES * n, n, 1.0, field, shifts, (slot_a, slot_b), section,
                lambda c, i, rows, cols, value: value,
            )
        return carry

    lax.fori_loop(0, field.shape[1] // BLOCK, step, 0)


def advance_second(
    section_hbm, velocity, following, token,
    section, field, result, shifts, slot_a, slot_b, in_sems, old_sems, out_sems,
):
    cells_x = section.shape[1]
    blocks = cells_x // BLOCK

    def planes(k):
        return pl.ds(k * BLOCK, BLOCK)

    def section_in(k):
        if isinstance(k, int) and k in (0, blocks):
            some = pl.ds(0 if k == 0 else cells_x - PLANES, PLANES)
        else:
            some = pl.ds(k * BLOCK - PLANES, BLOCK)
        return pltpu.make_async_copy(section_hbm.at[:, some], section.at[:, some], in_sems.at[k])

    def old_in(k):
        return pltpu.make_async_copy(
            velocity.at[:, planes(k)], field.at[:, planes(k)], old_sems.at[k]
        )

    def block_out(k):
        return pltpu.make_async_copy(
            result.at[:, planes(k)], following.at[:, planes(k)], out_sems.at[k]
        )

    def finish(c, i, rows, cols, value):
        return value + 0.5 * field[c, i, rows, cols]

    for k in range(blocks + 1):
        section_in(k).start()
        if k > 0:
            old_in(k - 1).start()
    token[...] = jnp.zeros_like(token)
    fill_shifts(shifts)
    section_in(0).wait()
    along_depth(0, section, shifts, slot_a)

    def step(t, carry):
        @pl.when(t + 1 < blocks)
        def _():
            section_in(t + 1).wait()

        @pl.when(t + 1 == blocks)
        def _():
            section_in(blocks).wait()

        old_in(t).wait()
        for n in range(BLOCK // PLANES):
            advance_batch(
                t * BLOCK + n * PLANES, n, 0.5, section, shifts, (slot_a, slot_b), result, finish
            )
        block_out(t).start()
        return carry

    lax.fori_loop(0, blocks, step, 0)
    for k in range(blocks):
        block_out(k).wait()


def shifted(x, axis, step, periodic):
    count = lax.axis_size(axis)
    pairs = [(i, (i + step) % count) for i in range(count)]
    if not periodic:
        pairs = [(s, t) for s, t in pairs if t - s == step]
    return lax.ppermute(x, axis, pairs)


def exchange(pack_low, pack_high, edge_west, edge_east):
    got_low = shifted(pack_high, "gy", 1, True)
    got_high = shifted(pack_low, "gy", -1, True)
    ghost_low = shifted(edge_east, "gx", 1, False)
    ghost_high = shifted(edge_west, "gx", -1, False)
    return ghost_low, ghost_high, got_low, got_high


def local(velocity, inflow, positions, tiles, coefs, counts):
    f32, i32 = jnp.float32, jnp.int32
    whole = velocity.shape
    _, cells_x, cells_y, depth = whole
    groups_y = lax.axis_size("gy")
    positions = positions[0].transpose(1, 0, 2)
    tiles, coefs = tiles[0].T, coefs[0]
    records, points = coefs.shape
    share = records // groups_y
    chunks = cells_x // CHUNK
    size = 4 * math.prod(whole)
    held = pltpu.VMEM(whole, f32)
    stored = pltpu.HBM(whole, f32)
    array = jax.ShapeDtypeStruct
    pack = array((3 * cells_x + 3 * records, 1, points), f32)
    edge = array((3, cells_y, depth), f32)
    per_record = (records, 1, points)
    units = records * (depth // LANES)
    y_shape, z_shape = (units, cells_y, points), (units, 2 * LANES, points)
    z_bytes = 2 * math.prod(z_shape)
    products = [pltpu.VMEM((2 * depth, depth), jnp.bfloat16)]
    products += [pltpu.VMEM((3 * PLANES * cells_y, depth), f32)] * 2
    unit_sems = pltpu.SemaphoreType.DMA((units // TILES,))
    chunk_sems = pltpu.SemaphoreType.DMA((chunks,))

    field, *own_a, weight_y, weight_z, strength, point_y, plan = pl.pallas_call(
        load_sample,
        out_shape=(
            held, pack, pack, edge, edge,
            pltpu.VMEM(y_shape, f32), pltpu.VMEM(z_shape, jnp.bfloat16),
            array(per_record, f32), array(per_record, i32),
            array((SUB, units), i32),
        ),
        in_specs=[ANYWHERE] * 4 + [SCALAR],
        out_specs=(WHOLE,) * 9 + (SCALAR,),
        scratch_shapes=[
            pltpu.VMEM(per_record, i32),
            pltpu.VMEM((records, LANES), i32),
            pltpu.VMEM((2, records), i32),
            pltpu.VMEM((2, records, points), i32),
            pltpu.VMEM((records, points), f32),
            pltpu.VMEM((SUB, units), i32),
            pltpu.SemaphoreType.DMA((4,)),
            pltpu.SemaphoreType.DMA,
            chunk_sems,
        ],
        compiler_params=params(),
        cost_estimate=cost(2 * 10**9, 4 * size),
        name="load_sample",
    )(streamed(velocity), streamed(positions), streamed(tiles), streamed(coefs), counts)
    weight_y, weight_z = resident(weight_y), resident(weight_z)
    ghosts_a = exchange(*own_a)

    section = pl.pallas_call(
        advance_first,
        out_shape=held,
        in_specs=[WHOLE],
        out_specs=WHOLE,
        scratch_shapes=products,
        compiler_params=params(),
        cost_estimate=cost(10**9, 4 * size),
        name="advance_first",
    )(resident(field))

    _, section, stored_z, *own_b, shares = pl.pallas_call(
        spread_sample,
        out_shape=(
            held, stored, pltpu.HBM(z_shape, jnp.bfloat16),
            pack, pack, edge, edge,
            array((groups_y, 2, 3 * share, 1, points), f32),
        ),
        in_specs=[WHOLE] * 10 + [SCALAR] + [WHOLE] * 3,
        out_specs=(WHOLE,) + (ANYWHERE,) * 2 + (WHOLE,) * 5,
        input_output_aliases={0: 0},
        scratch_shapes=[pltpu.SemaphoreType.DMA, unit_sems],
        compiler_params=params(),
        cost_estimate=cost(2 * 10**9, 4 * size),
        name="spread_sample",
    )(
        resident(section), inflow, *ghosts_a[:2], *own_a, *ghosts_a[2:],
        plan, weight_y, weight_z, strength,
    )
    shares = lax.all_to_all(shares, "gy", 0, 0)
    ghosts_b = exchange(*own_b)

    following, token = pl.pallas_call(
        advance_second,
        out_shape=(stored, array((SUB, LANES), f32)),
        in_specs=[ANYWHERE] * 2,
        out_specs=(ANYWHERE, WHOLE),
        scratch_shapes=[pltpu.VMEM(whole, f32)] * 3
        + products
        + [pltpu.SemaphoreType.DMA((cells_x // BLOCK + 1,))] * 3,
        compiler_params=params(VMEM_LIMIT + 3 * size),
        cost_estimate=cost(10**9, 4 * size),
        name="advance_second",
    )(streamed(section), streamed(velocity))

    forces = pl.pallas_call(
        share_force,
        out_shape=array((groups_y, 3 * share, 1, points), f32),
        in_specs=[WHOLE, WHOLE, SCALAR] + [ANYWHERE] * 3,
        out_specs=WHOLE,
        compiler_params=params(),
        cost_estimate=cost(10**6, 10**6),
        name="share_force",
    )(shares, strength, counts, token, *ghosts_b[:2])
    all_forces = lax.all_to_all(forces, "gy", 0, 0)

    velocity_next = pl.pallas_call(
        spread_next,
        out_shape=stored,
        in_specs=[ANYWHERE] + [WHOLE] * 9 + [SCALAR, WHOLE, ANYWHERE, WHOLE, ANYWHERE],
        out_specs=ANYWHERE,
        scratch_shapes=[
            pltpu.VMEM(whole, f32),
            pltpu.VMEM(z_shape, jnp.bfloat16),
            chunk_sems, chunk_sems, unit_sems,
        ],
        compiler_params=params(VMEM_LIMIT + size + z_bytes),
        cost_estimate=cost(2 * 10**9, 4 * size),
        name="spread_next",
    )(
        streamed(following), inflow, *ghosts_b[:2], *own_b, *ghosts_b[2:],
        plan, point_y, streamed(stored_z), strength, forces,
    )
    return (velocity_next, all_forces.reshape(1, records, 3, points))


def solution(mesh):
    return jax.shard_map(
        local,
        mesh=mesh,
        in_specs=(
            P(None, "gx", "gy", None),
            P(None, "gy", None),
            P("gx", None, None, None),
            P("gx", None, None),
            P("gx", None, None),
            P("gx"),
        ),
        out_specs=(P(None, "gx", "gy", None), P("gx", None, None, None)),
        check_vma=False,
    )
```

```python
import math

import jax
import jax.numpy as jnp
from jax import lax
from jax.experimental import pallas as pl
from jax.experimental.pallas import tpu as pltpu
from jax.sharding import PartitionSpec as P

RAD = 2
VISCOSITY = 0.05
TIME_STEP = 0.1
WIDTH_EPS = 1.5
ROOT_PI = 1.7724538509055159
TAP = [math.exp(-((d / WIDTH_EPS) ** 2)) / (WIDTH_EPS * ROOT_PI) for d in range(RAD + 1)]
HIGH = [float(jnp.bfloat16(tap)) for tap in TAP]
LOW = [float(jnp.bfloat16(tap - high)) for tap, high in zip(TAP, HIGH)]
LANES = 128
SUB = 8
GROUP = 4
BATCH = 4
PLANES = 8
BLOCK = 2 * PLANES
CHUNK = 16
TILES = 8
VMEM_LIMIT = 8 * 2**20

WHOLE = pl.BlockSpec(memory_space=pltpu.VMEM)
SCALAR = pl.BlockSpec(memory_space=pltpu.SMEM)
ANYWHERE = pl.BlockSpec(memory_space=pl.ANY)


def params(limit=VMEM_LIMIT):
    return pltpu.CompilerParams(vmem_limit_bytes=limit)


def cost(flops, nbytes):
    return pl.CostEstimate(flops=flops, bytes_accessed=nbytes, transcendentals=0)


def resident(x):
    return pltpu.with_memory_space_constraint(x, pltpu.VMEM)


def streamed(x):
    return pltpu.with_memory_space_constraint(x, pltpu.HBM)


def split(x):
    high = x.astype(jnp.bfloat16)
    low = (x - high.astype(jnp.float32)).astype(jnp.bfloat16)
    return jnp.concatenate([high, low], axis=0)


def along_z(point_z, start):
    points = point_z.shape[-1]
    row = lax.broadcasted_iota(jnp.int32, (LANES, points), 0).astype(jnp.bfloat16)
    place = (point_z - start).astype(jnp.float32)
    place = jnp.broadcast_to(place, (LANES, points)).astype(jnp.bfloat16)
    dist = jnp.abs(row - place)
    near = [dist == float(d) for d in range(RAD + 1)]
    out = []
    for taps in (HIGH, LOW):
        value = jnp.zeros_like(row)
        for d in range(RAD, -1, -1):
            value = jnp.where(near[d], jnp.full_like(row, taps[d]), value)
        out.append(value)
    return out


def wrapped(point_y, base, total_y):
    near = point_y - base
    near = jnp.where(near > total_y // 2, near - total_y, near)
    return jnp.where(near < -(total_y // 2), near + total_y, near)


def along_y(point_y, base, cells_y, total_y):
    near = wrapped(point_y, base, total_y)
    dist = jnp.abs(lax.broadcasted_iota(jnp.int32, (cells_y, point_y.shape[-1]), 0) - near)
    return jnp.where(
        dist == 0, TAP[0], jnp.where(dist == 1, TAP[1], jnp.where(dist == 2, TAP[2], 0.0))
    )


def make_plan(hub, lowest, highest, tiles, live, table):
    f32, i32 = jnp.float32, jnp.int32
    tile_y = lax.axis_index("gy").astype(f32)
    groups_y = float(lax.axis_size("gy"))
    records, units = hub.shape[0], table.shape[1]
    square = (records, records)
    diagonal = lax.broadcasted_iota(i32, square, 0) == lax.broadcasted_iota(i32, square, 1)

    def turned(x, axis):
        kept = jnp.where(diagonal, jnp.broadcast_to(x, square), 0.0)
        return jnp.sum(kept, axis=axis, keepdims=True)

    first, count = turned(tiles[0:1].astype(f32), 1), turned(tiles[1:2].astype(f32), 1)
    offset = tile_y - first
    offset = jnp.where(offset < 0.0, offset + groups_y, offset)
    order = lax.broadcasted_iota(i32, (records, 1), 0).astype(f32)
    valid = jnp.logical_and(offset < count, order < live)
    valid = jnp.logical_and(valid, highest >= 0.0)
    low = jnp.right_shift(lowest.astype(i32) - RAD, 7)
    high = jnp.right_shift(highest.astype(i32) + RAD, 7)
    number = jnp.where(valid, (high - low + 1).astype(f32), 0.0)
    key = hub * float(records) + order
    before = turned(key, 0) < key
    place = jnp.sum(jnp.where(before, turned(number, 0), 0.0), axis=1, keepdims=True)
    lane = lax.broadcasted_iota(i32, (records, units), 1).astype(f32)
    mine = jnp.logical_and(lane >= place, lane < place + number)

    def pick(value):
        return jnp.sum(jnp.where(mine, value, 0.0), axis=0, keepdims=True).astype(i32)

    table[0:1] = pick(order)
    table[1:2] = pick(hub)
    table[2:3] = pick(low.astype(f32) + lane - place)
    total = jnp.sum(number, axis=0, keepdims=True).astype(i32)
    table[3:4] = jnp.broadcast_to(total, (1, units))


def found(plan):
    return plan[3, 0]


def group(plan, t):
    picks, keeps = [], []
    for k in range(GROUP):
        wanted = GROUP * t + k
        n = jnp.minimum(wanted, found(plan) - 1)
        cols = pl.ds(pl.multiple_of(plan[2, n] * LANES, LANES), LANES)
        picks.append((n, plan[0, n], plan[1, n], cols))
        keeps.append(wanted == n)
    return picks, keeps


def groups_of(plan):
    return (found(plan) + GROUP - 1) // GROUP


def sampled_rows(field, weight_y, weight_z, picks):
    cells_y = field.shape[2]
    rows = 3 * cells_y
    parts = []
    for t, r, hub, cols in picks:
        planes = []
        for c in range(3):
            plane = TAP[0] * field[c, hub, :, cols]
            plane += TAP[1] * (field[c, hub - 1, :, cols] + field[c, hub + 1, :, cols])
            plane += TAP[2] * (field[c, hub - 2, :, cols] + field[c, hub + 2, :, cols])
            planes.append(plane)
        part = split(jnp.concatenate(planes, axis=0))
        parts.append(jnp.concatenate([part, part], axis=1))
    out = []
    for (t, r, hub, cols), part in zip(picks, parts):
        picked = jnp.dot(part, weight_z[t], preferred_element_type=jnp.float32)
        picked = picked[:rows] + picked[rows:]
        weight = weight_y[t]
        out.append(
            [
                jnp.sum(picked[c * cells_y : (c + 1) * cells_y] * weight, axis=0, keepdims=True)
                for c in range(3)
            ]
        )
    return out


def add_rows(pack, first_row, picks, sampled, keeps):
    for (t, r, hub, cols), rows, keep in zip(picks, sampled, keeps):
        for c in range(3):
            n = first_row + 3 * r + c
            pack[n] = pack[n] + jnp.where(keep, rows[c], 0.0)


def is_even(axis):
    return lax.rem(lax.axis_index(axis), 2) == 0


def pack_edges(field, edge_near, edge_far, pack_low, pack_high):
    cells_x, cells_y, depth = field.shape[1:]
    even = is_even("gx")
    for c in range(3):
        west, east = field[c, 0], field[c, cells_x - 1]
        edge_near[c] = jnp.where(even, east, west)
        edge_far[c] = jnp.where(even, west, east)

    def step(t, carry):
        cells = [(c, t * BATCH + k) for k in range(BATCH) for c in range(3)]
        rows = [
            (field[c, i, pl.ds(0, 1), :], field[c, i, pl.ds(cells_y - 1, 1), :]) for c, i in cells
        ]
        for (c, i), (low, high) in zip(cells, rows):
            pack_low[c * cells_x + i] = low
            pack_high[c * cells_x + i] = high
        return carry

    lax.fori_loop(0, cells_x // BATCH, step, 0)


def load_sample(
    velocity, positions, tiles_hbm, coefs_hbm, counts,
    field, pack_low, pack_high, edge_near, edge_far, weight_y, weight_z, strength, point_y, plan,
    point_z, hubs, tiles, places, coefs, table, small_sems, plan_sem, sems,
):
    cells_x, cells_y, depth = field.shape[1:]
    records, points = coefs.shape
    chunks = cells_x // CHUNK
    first_row = 3 * cells_x
    start = lax.axis_index("gx") * cells_x

    def chunk(k):
        planes = pl.ds(k * CHUNK, CHUNK)
        return pltpu.make_async_copy(velocity.at[:, planes], field.at[:, planes], sems.at[k])

    small = [
        (positions.at[pl.ds(1, 2)], places),
        (positions.at[0, :, pl.ds(0, LANES)], hubs),
        (tiles_hbm, tiles),
        (coefs_hbm, coefs),
    ]
    small = [
        pltpu.make_async_copy(source, target, small_sems.at[n])
        for n, (source, target) in enumerate(small)
    ]
    total_y = cells_y * lax.axis_size("gy")
    base = lax.axis_index("gy") * cells_y
    for copy in small:
        copy.start()
    for k in range(chunks):
        chunk(k).start()
    for copy in small[:3]:
        copy.wait()
    near = wrapped(places[0], base, total_y)
    inside = jnp.logical_and(near >= -RAD, near < cells_y + RAD)
    height = places[1].astype(jnp.float32)
    lowest = jnp.min(jnp.where(inside, height, float(depth)), axis=1, keepdims=True)
    highest = jnp.max(jnp.where(inside, height, -1.0), axis=1, keepdims=True)
    hub = (hubs[:, 0:1] - start).astype(jnp.float32)
    make_plan(hub, lowest, highest, tiles, counts[0].astype(jnp.float32), table)
    plan_copy = pltpu.make_async_copy(table, plan, plan_sem)
    plan_copy.start()

    def clear(n, carry):
        for k in range(SUB):
            pack_low[first_row + n * SUB + k] = jnp.zeros((1, points), jnp.float32)
        return carry

    lax.fori_loop(0, 3 * records // SUB, clear, 0)
    small[3].wait()
    for first in range(0, records, SUB):
        here = range(first, first + SUB)
        rows = [
            (places[0, pl.ds(r, 1), :], places[1, pl.ds(r, 1), :], coefs[pl.ds(r, 1), :])
            for r in here
        ]
        for r, (y, z, coef) in zip(here, rows):
            point_y[r], point_z[r], strength[r] = y, z, coef
    plan_copy.wait()

    def weigh(t, carry):
        made = []
        for k in range(2):
            n = jnp.minimum(2 * t + k, found(plan) - 1)
            r, half = plan[0, n], plan[2, n]
            high, low = along_z(point_z[r], half * LANES)
            made.append((n, along_y(point_y[r], base, cells_y, total_y), high, low))
        for n, across, high, low in made:
            weight_y[n] = across
            weight_z[n, 0:LANES] = high
            weight_z[n, LANES:] = low
        return carry

    lax.fori_loop(0, (found(plan) + 1) // 2, weigh, 0)

    def wait_to(ready, wanted):
        def step(k, carry):
            chunk(k).wait()
            return carry

        lax.fori_loop(ready, wanted, step, 0)
        return jnp.maximum(ready, wanted)

    def step(t, ready):
        picks, keeps = group(plan, t)
        ready = wait_to(ready, (picks[-1][2] + RAD) // CHUNK + 1)
        rows = sampled_rows(field, weight_y, weight_z, picks)
        add_rows(pack_low, first_row, picks, rows, keeps)
        return ready

    ready = lax.fori_loop(0, groups_of(plan), step, jnp.int32(0))
    wait_to(ready, chunks)

    def copy_rows(t, carry):
        rows = [first_row + t * SUB + k for k in range(SUB)]
        values = [pack_low[n] for n in rows]
        for n, value in zip(rows, values):
            pack_high[n] = value
        return carry

    lax.fori_loop(0, 3 * records // SUB, copy_rows, 0)
    pack_edges(field, edge_near, edge_far, pack_low, pack_high)


def fix_sides(factor, target, own_near, own_far, inflow, ghost_near, ghost_far, west_side):
    near = is_even("gx") != west_side

    def side(one, other, c):
        return jnp.where(near, one[c], other[c])

    sign = 1.0 if west_side else -1.0
    end = 0 if west_side else target.shape[1] - 1
    place = lax.axis_index("gx")
    spread = factor * TIME_STEP * VISCOSITY
    coef = spread + (sign * 0.5 * factor * TIME_STEP) * side(own_near, own_far, 0)
    for c in range(3):
        own, ghost = side(own_near, own_far, c), side(ghost_near, ghost_far, c)
        if west_side:
            ghost = jnp.where(place == 0, inflow[c], ghost)
        else:
            ghost = jnp.where(place == lax.axis_size("gx") - 1, own, ghost)
        target[c, end] = target[c, end] + (ghost - own) * coef


def fix_rows(factor, target, own_low, own_high, got_low, got_high, t):
    cells_x, cells_y = target.shape[1:3]
    spread = factor * TIME_STEP * VISCOSITY
    half = 0.5 * factor * TIME_STEP
    shape = (SUB, target.shape[3])
    row = lax.broadcasted_iota(jnp.int32, shape, 0)
    low, high = pl.ds(0, SUB), pl.ds(cells_y - SUB, SUB)

    def wide(x):
        return jnp.broadcast_to(x, shape)

    for first in range(0, SUB, 2):
        values = []
        for k in range(first, first + 2):
            i = t * SUB + k
            south = jnp.where(row == 0, spread + half * wide(own_low[cells_x + i]), 0.0)
            north = jnp.where(row == SUB - 1, spread - half * wide(own_high[cells_x + i]), 0.0)
            for c in range(3):
                n = c * cells_x + i
                values.append((c, i, low, target[c, i, low, :] + wide(got_low[n]) * south))
                values.append((c, i, high, target[c, i, high, :] + wide(got_high[n]) * north))
        for c, i, rows, value in values:
            target[c, i, rows, :] = value


def slabs_of(weight_of, weight_z, strength, own, low, high, cells, scales, picks):
    cells_x, cells_y, depth = cells
    count = 3 * cells_y
    across = (((1,), (1,)), ((), ()))
    spread = []
    for (t, r, hub, cols), scale in zip(picks, scales):
        rows = [3 * cells_x + 3 * r + c for c in range(3)]
        total = [own[n] + (low[n] + high[n]) for n in rows]
        speed = jnp.sqrt(total[0] * total[0] + total[1] * total[1] + total[2] * total[2])
        pull = strength[r] * (-scale) * speed
        weight = weight_of(t, r)
        spread.append(split(jnp.concatenate([weight * (pull * x) for x in total], axis=0)))
    slabs = []
    for (t, r, hub, cols), part in zip(picks, spread):
        slab = lax.dot_general(part, weight_z[t], across, preferred_element_type=jnp.float32)
        slab = slab[:count] + slab[count:]
        slabs.append(slab[:, :LANES] + slab[:, LANES:])
    return slabs


def add_slab(field, slab, hub, cols):
    cells_y = field.shape[2]
    for c in range(3):
        part = slab[c * cells_y : (c + 1) * cells_y]
        terms = [tap * part for tap in TAP]
        reach = range(-RAD, RAD + 1)
        values = [field[c, hub + d, :, cols] + terms[abs(d)] for d in reach]
        for d, value in zip(reach, values):
            field[c, hub + d, :, cols] = value


def spread_group(t, scale, field, plan, points, own, low, high):
    picks, keeps = group(plan, t)
    scales = [jnp.where(keep, scale, 0.0) for keep in keeps]
    slabs = slabs_of(*points, own, low, high, field.shape[1:], scales, picks)
    for (_, _, hub, cols), slab in zip(picks, slabs):
        add_slab(field, slab, hub, cols)


def spread_sample(
    section_in, inflow, ghost_near, ghost_far, own_low, own_high, own_near, own_far, got_low, got_high,
    plan, weight_y, weight_z, strength,
    section, section_out, stored_z, pack_low, pack_high, edge_near, edge_far,
    share_out, sem, sem_z,
):
    cells_x = section.shape[1]
    records = strength.shape[0]
    share = share_out.shape[2] // 3
    first_row = 3 * cells_x

    def store(t):
        some = pl.ds(t * TILES, TILES)
        return pltpu.make_async_copy(weight_z.at[some], stored_z.at[some], sem_z.at[t])

    def start_store(t, carry):
        store(t).start()
        return carry

    def wait_store(t, carry):
        store(t).wait()
        return carry

    stores = (found(plan) + TILES - 1) // TILES
    lax.fori_loop(0, stores, start_store, 0)

    def fix_step(t, carry):
        fix_rows(1.0, section, own_low, own_high, got_low, got_high, t)
        return carry

    sides = (own_near, own_far, inflow, ghost_near, ghost_far)
    fix_sides(1.0, section, *sides, True)
    fix_sides(1.0, section, *sides, False)
    lax.fori_loop(0, cells_x // SUB, fix_step, 0)

    def spread_step(t, carry):
        points = (lambda n, r: weight_y[n], weight_z, strength)
        spread_group(t, TIME_STEP, section, plan, points, own_low, got_low, got_high)
        return carry

    lax.fori_loop(0, groups_of(plan), spread_step, 0)
    copy = pltpu.make_async_copy(section, section_out, sem)
    copy.start()
    pack_edges(section, edge_near, edge_far, pack_low, pack_high)

    def clear(n, carry):
        for k in range(SUB):
            pack_low[first_row + n * SUB + k] = jnp.zeros_like(own_low[0])
        return carry

    lax.fori_loop(0, 3 * records // SUB, clear, 0)

    def sample_step(t, carry):
        picks, keeps = group(plan, t)
        rows = sampled_rows(section, weight_y, weight_z, picks)
        add_rows(pack_low, first_row, picks, rows, keeps)
        return carry

    lax.fori_loop(0, groups_of(plan), sample_step, 0)

    def copy_rows(r, carry):
        old = [own_low[first_row + 3 * r + c] for c in range(3)]
        new = [pack_low[first_row + 3 * r + c] for c in range(3)]
        for c in range(3):
            pack_high[first_row + 3 * r + c] = new[c]
            share_out[r // share, 0, 3 * (r % share) + c] = old[c]
            share_out[r // share, 1, 3 * (r % share) + c] = new[c]
        return carry

    lax.fori_loop(0, records, copy_rows, 0)
    lax.fori_loop(0, stores, wait_store, 0)
    copy.wait()


def share_force(parts, strength, counts, after, after_low, after_high, result):
    groups, _, rows = parts.shape[:3]
    share = rows // 3
    mine = lax.axis_index("gy") * share
    values = []
    for s in range(share):
        live = mine + s < counts[0]
        pull = jnp.where(live, -0.5 * strength[mine + s], 0.0)
        total = [0.0, 0.0, 0.0]
        for stage in range(2):
            value = []
            for c in range(3):
                n = 3 * s + c
                x = parts[0, stage, n]
                for g in range(1, groups):
                    x += parts[g, stage, n]
                value.append(x)
            speed = jnp.sqrt(value[0] * value[0] + value[1] * value[1] + value[2] * value[2])
            total = [acc + speed * x for acc, x in zip(total, value)]
        values.extend((3 * s + c, pull * total[c]) for c in range(3))
        if s % 2 == 1 or s + 1 == share:
            for n, value in values:
                for g in range(groups):
                    result[g, n] = value
            values = []


def spread_next(
    following, inflow, ghost_near, ghost_far, own_low, own_high, own_near, own_far, got_low, got_high,
    plan, point_y, stored_z, strength, after,
    result, field, weight_z, in_sems, out_sems, sem_z,
):
    chunks = field.shape[1] // CHUNK
    factor = 0.5
    sides = (own_near, own_far, inflow, ghost_near, ghost_far)

    def chunk_in(k):
        planes = pl.ds(k * CHUNK, CHUNK)
        return pltpu.make_async_copy(following.at[:, planes], field.at[:, planes], in_sems.at[k])

    def chunk_out(k):
        planes = pl.ds(k * CHUNK, CHUNK)
        return pltpu.make_async_copy(field.at[:, planes], result.at[:, planes], out_sems.at[k])

    def wait_to(ready, wanted):
        def step(k, carry):
            chunk_in(k).wait()
            for n in range(CHUNK // SUB):
                t = k * (CHUNK // SUB) + n
                fix_rows(factor, field, own_low, own_high, got_low, got_high, t)

            @pl.when(k == 0)
            def _():
                fix_sides(factor, field, *sides, True)

            @pl.when(k == chunks - 1)
            def _():
                fix_sides(factor, field, *sides, False)

            return carry

        lax.fori_loop(ready, wanted, step, 0)
        return jnp.maximum(ready, wanted)

    def send_to(sent, done):
        def step(k, carry):
            chunk_out(k).start()
            return carry

        lax.fori_loop(sent, done, step, 0)
        return jnp.maximum(sent, done)

    def weights(t):
        some = pl.ds(t * TILES, TILES)
        return pltpu.make_async_copy(stored_z.at[some], weight_z.at[some], sem_z.at[t])

    def start_weights(t, carry):
        weights(t).start()
        return carry

    def weight_of(t, r):
        cells_y = field.shape[2]
        base = lax.axis_index("gy") * cells_y
        return along_y(point_y[r], base, cells_y, cells_y * lax.axis_size("gy"))

    loads = (found(plan) + TILES - 1) // TILES
    for k in range(chunks):
        chunk_in(k).start()
        lax.fori_loop(k * loads // chunks, (k + 1) * loads // chunks, start_weights, 0)

    def step(t, carry):
        ready, sent = carry
        picks, keeps = group(plan, t)
        @pl.when(t * GROUP % TILES == 0)
        def _():
            weights(t * GROUP // TILES).wait()

        ready = wait_to(ready, (picks[-1][2] + RAD) // CHUNK + 1)
        sent = send_to(sent, (picks[0][2] - RAD) // CHUNK)
        points = (weight_of, weight_z, strength)
        spread_group(t, factor * TIME_STEP, field, plan, points, own_low, got_low, got_high)
        return ready, sent

    zero = jnp.int32(0)
    ready, sent = lax.fori_loop(0, groups_of(plan), step, (zero, zero))
    sent = send_to(sent, ready)

    def finish(k, carry):
        wait_to(k, k + 1)
        chunk_out(k).start()
        return carry

    lax.fori_loop(ready, chunks, finish, 0)
    for k in range(chunks):
        chunk_out(k).wait()


def fill_shifts(shifts):
    depth = shifts.shape[1]
    source = lax.broadcasted_iota(jnp.int32, (depth, depth), 0)
    cell = lax.broadcasted_iota(jnp.int32, (depth, depth), 1)
    upper = jnp.where(source == cell + 1, 1.0, 0.0)
    lower = jnp.where(source == cell - 1, 1.0, 0.0)
    difference = (upper - lower).astype(shifts.dtype)
    shifts[0:depth] = difference
    shifts[depth : 2 * depth] = difference


def along_depth(i, field, shifts, slot):
    x = jnp.concatenate([field[c, i + k] for k in range(PLANES) for c in range(3)], axis=0)
    high = x.astype(jnp.bfloat16)
    low = (x - high.astype(jnp.float32)).astype(jnp.bfloat16)
    slot[...] = jnp.dot(
        jnp.concatenate([high, low], axis=1), shifts[...], preferred_element_type=jnp.float32
    )


def advance(i, k, factor, field, slot, target, finish):
    cells_x, cells_y, depth = field.shape[1:]
    groups, halves = cells_y // SUB, depth // LANES
    row = lax.broadcasted_iota(jnp.int32, (SUB, LANES), 0)
    lane = lax.broadcasted_iota(jnp.int32, (SUB, LANES), 1)
    first_row, last_row, first_lane = row == 0, row == SUB - 1, lane == 0
    spread = factor * TIME_STEP * VISCOSITY
    centre = factor * (1.0 - 6.0 * TIME_STEP * VISCOSITY)
    zero = jnp.zeros((SUB, LANES), jnp.float32)
    loaded = {}
    here = i + k
    west, east = jnp.maximum(here - 1, 0), jnp.minimum(here + 1, cells_x - 1)

    def at(c, g, h):
        if (c, g, h) not in loaded:
            loaded[c, g, h] = field[c, here, pl.ds(g * SUB, SUB), pl.ds(h * LANES, LANES)]
        return loaded[c, g, h]

    values = []
    for g in range(groups):
        turned = {}
        for h in range(halves):
            rows, cols = pl.ds(g * SUB, SUB), pl.ds(h * LANES, LANES)
            q = [at(c, g, h) for c in range(3)]
            speeds = [(0.5 * factor * TIME_STEP) * x for x in q]
            less = [spread - s for s in speeds]
            more = [spread + s for s in speeds[:2]]
            if g == 0:
                more[1] = jnp.where(first_row, zero, more[1])
            if g == groups - 1:
                less[1] = jnp.where(last_row, zero, less[1])
            for c in range(3):
                x = q[c]
                above, below = x, x
                if g + 1 < groups:
                    above = jnp.where(first_row, at(c, g + 1, h), x)
                if g > 0:
                    below = jnp.where(last_row, at(c, g - 1, h), x)
                above, below = pltpu.roll(above, SUB - 1, 0), pltpu.roll(below, 1, 0)
                place = pl.ds((3 * k + c) * cells_y + g * SUB, SUB)
                total = centre * x
                total += field[c, east, rows, cols] * less[0]
                total += field[c, west, rows, cols] * more[0]
                total += above * less[1] + below * more[1]
                lower = pltpu.roll(x, 1, 1)
                turned[c, h] = lower
                lower = jnp.where(first_lane, zero if h == 0 else turned[c, h - 1], lower)
                total += slot[place, cols] * less[2] + (2.0 * spread) * lower
                values.append((c, rows, cols, finish(c, here, rows, cols, total)))
        if g % 2 == 1 or g + 1 == groups:
            for c, rows, cols, value in values:
                target[c, here, rows, cols] = value
            values = []


def advance_batch(i, n, factor, field, shifts, slots, target, finish):
    now, later = slots[n % 2], slots[1 - n % 2]
    along_depth(jnp.minimum(i + PLANES, field.shape[1] - PLANES), field, shifts, later)
    for k in range(PLANES):
        advance(i, k, factor, field, now, target, finish)


def advance_first(field, section, shifts, slot_a, slot_b):
    fill_shifts(shifts)
    along_depth(0, field, shifts, slot_a)

    def step(t, carry):
        for n in range(BLOCK // PLANES):
            advance_batch(
                BLOCK * t + PLANES * n, n, 1.0, field, shifts, (slot_a, slot_b), section,
                lambda c, i, rows, cols, value: value,
            )
        return carry

    lax.fori_loop(0, field.shape[1] // BLOCK, step, 0)


def advance_second(
    section_hbm, velocity, following, token,
    section, field, result, shifts, slot_a, slot_b, in_sems, old_sems, out_sems,
):
    cells_x = section.shape[1]
    blocks = cells_x // BLOCK

    def copy(source, target, first, count, sem):
        some = pl.ds(first, count)
        return pltpu.make_async_copy(source.at[:, some], target.at[:, some], sem)

    def section_in(k):
        return copy(section_hbm, section, k * BLOCK, BLOCK, in_sems.at[k])

    def old_in(k):
        return copy(velocity, field, k * BLOCK, BLOCK, old_sems.at[k])

    def block_out(k):
        return copy(result, following, k * BLOCK, BLOCK, out_sems.at[k])

    halves = range(BLOCK // PLANES)
    head = [
        (
            copy(section_hbm, section, n * PLANES, PLANES, in_sems.at[n * blocks]),
            copy(velocity, field, n * PLANES, PLANES, old_sems.at[n * blocks]),
        )
        for n in halves
    ]
    last = blocks - 1
    tail = [
        copy(result, following, last * BLOCK + n * PLANES, PLANES, out_sems.at[last + n])
        for n in halves
    ]

    def finish(c, i, rows, cols, value):
        return value + 0.5 * field[c, i, rows, cols]

    head[0][0].start()
    head[1][0].start()
    head[0][1].start()
    head[1][1].start()
    for k in range(1, blocks):
        section_in(k).start()
        old_in(k).start()
    token[...] = jnp.zeros_like(token)
    fill_shifts(shifts)

    def work(i, n):
        advance_batch(i, n, 0.5, section, shifts, (slot_a, slot_b), result, finish)

    head[0][0].wait()
    along_depth(0, section, shifts, slot_a)
    head[1][0].wait()
    head[0][1].wait()
    work(0, 0)
    section_in(1).wait()
    head[1][1].wait()
    work(PLANES, 1)
    block_out(0).start()

    def step(t, carry):
        section_in(t + 1).wait()
        old_in(t).wait()
        for n in halves:
            work(t * BLOCK + n * PLANES, n)
        block_out(t).start()
        return carry

    lax.fori_loop(1, last, step, 0)
    old_in(last).wait()
    for n in halves:
        work(last * BLOCK + n * PLANES, n)
        tail[n].start()
    for k in range(last):
        block_out(k).wait()
    for out in tail:
        out.wait()


def shifted(x, axis, step):
    count = lax.axis_size(axis)
    return lax.ppermute(x, axis, [(i, (i + step) % count) for i in range(count)])


def swapped(x, axis, first):
    count = lax.axis_size(axis)
    pairs = [(i, i + 1) for i in range(first, count - 1, 2)]
    return lax.ppermute(x, axis, pairs + [(t, s) for s, t in pairs])


def exchange(pack_low, pack_high, edge_near, edge_far):
    got_low = shifted(pack_high, "gy", 1)
    got_high = shifted(pack_low, "gy", -1)
    return swapped(edge_near, "gx", 0), swapped(edge_far, "gx", 1), got_low, got_high


def local(velocity, inflow, positions, tiles, coefs, counts):
    f32, i32 = jnp.float32, jnp.int32
    whole = velocity.shape
    _, cells_x, cells_y, depth = whole
    groups_y = lax.axis_size("gy")
    positions = positions[0].transpose(1, 0, 2)
    tiles, coefs = tiles[0].T, coefs[0]
    records, points = coefs.shape
    share = records // groups_y
    chunks = cells_x // CHUNK
    size = 4 * math.prod(whole)
    held = pltpu.VMEM(whole, f32)
    stored = pltpu.HBM(whole, f32)
    array = jax.ShapeDtypeStruct
    pack = array((3 * cells_x + 3 * records, 1, points), f32)
    edge = array((3, cells_y, depth), f32)
    per_record = (records, 1, points)
    units = records * (depth // LANES)
    y_shape, z_shape = (units, cells_y, points), (units, 2 * LANES, points)
    z_bytes = 2 * math.prod(z_shape)
    products = [pltpu.VMEM((2 * depth, depth), jnp.bfloat16)]
    products += [pltpu.VMEM((3 * PLANES * cells_y, depth), f32)] * 2
    unit_sems = pltpu.SemaphoreType.DMA((units // TILES,))
    chunk_sems = pltpu.SemaphoreType.DMA((chunks,))

    field, *own_a, weight_y, weight_z, strength, point_y, plan = pl.pallas_call(
        load_sample,
        out_shape=(
            held, pack, pack, edge, edge,
            pltpu.VMEM(y_shape, f32), pltpu.VMEM(z_shape, jnp.bfloat16),
            array(per_record, f32), array(per_record, i32),
            array((SUB, units), i32),
        ),
        in_specs=[ANYWHERE] * 4 + [SCALAR],
        out_specs=(WHOLE,) * 9 + (SCALAR,),
        scratch_shapes=[
            pltpu.VMEM(per_record, i32),
            pltpu.VMEM((records, LANES), i32),
            pltpu.VMEM((2, records), i32),
            pltpu.VMEM((2, records, points), i32),
            pltpu.VMEM((records, points), f32),
            pltpu.VMEM((SUB, units), i32),
            pltpu.SemaphoreType.DMA((4,)),
            pltpu.SemaphoreType.DMA,
            chunk_sems,
        ],
        compiler_params=params(),
        cost_estimate=cost(2 * 10**9, 4 * size),
        name="load_sample",
    )(streamed(velocity), streamed(positions), streamed(tiles), streamed(coefs), counts)
    weight_y, weight_z = resident(weight_y), resident(weight_z)
    ghosts_a = exchange(*own_a)

    section = pl.pallas_call(
        advance_first,
        out_shape=held,
        in_specs=[WHOLE],
        out_specs=WHOLE,
        scratch_shapes=products,
        compiler_params=params(),
        cost_estimate=cost(10**9, 4 * size),
        name="advance_first",
    )(resident(field))

    _, section, stored_z, *own_b, shares = pl.pallas_call(
        spread_sample,
        out_shape=(
            held, stored, pltpu.HBM(z_shape, jnp.bfloat16),
            pack, pack, edge, edge,
            array((groups_y, 2, 3 * share, 1, points), f32),
        ),
        in_specs=[WHOLE] * 10 + [SCALAR] + [WHOLE] * 3,
        out_specs=(WHOLE,) + (ANYWHERE,) * 2 + (WHOLE,) * 5,
        input_output_aliases={0: 0},
        scratch_shapes=[pltpu.SemaphoreType.DMA, unit_sems],
        compiler_params=params(),
        cost_estimate=cost(2 * 10**9, 4 * size),
        name="spread_sample",
    )(
        resident(section), inflow, *ghosts_a[:2], *own_a, *ghosts_a[2:],
        plan, weight_y, weight_z, strength,
    )
    shares = lax.all_to_all(shares, "gy", 0, 0)
    ghosts_b = exchange(*own_b)

    following, token = pl.pallas_call(
        advance_second,
        out_shape=(stored, array((SUB, LANES), f32)),
        in_specs=[ANYWHERE] * 2,
        out_specs=(ANYWHERE, WHOLE),
        scratch_shapes=[pltpu.VMEM(whole, f32)] * 3
        + products
        + [pltpu.SemaphoreType.DMA((cells_x // BLOCK + 1,))] * 3,
        compiler_params=params(VMEM_LIMIT + 3 * size),
        cost_estimate=cost(10**9, 4 * size),
        name="advance_second",
    )(streamed(section), streamed(velocity))

    forces = pl.pallas_call(
        share_force,
        out_shape=array((groups_y, 3 * share, 1, points), f32),
        in_specs=[WHOLE, WHOLE, SCALAR] + [ANYWHERE] * 3,
        out_specs=WHOLE,
        compiler_params=params(),
        cost_estimate=cost(10**6, 10**6),
        name="share_force",
    )(shares, strength, counts, token, *ghosts_b[:2])
    all_forces = lax.all_to_all(forces, "gy", 0, 0)

    velocity_next = pl.pallas_call(
        spread_next,
        out_shape=stored,
        in_specs=[ANYWHERE] + [WHOLE] * 9 + [SCALAR, WHOLE, ANYWHERE, WHOLE, ANYWHERE],
        out_specs=ANYWHERE,
        scratch_shapes=[
            pltpu.VMEM(whole, f32),
            pltpu.VMEM(z_shape, jnp.bfloat16),
            chunk_sems, chunk_sems, unit_sems,
        ],
        compiler_params=params(VMEM_LIMIT + size + z_bytes),
        cost_estimate=cost(2 * 10**9, 4 * size),
        name="spread_next",
    )(
        streamed(following), inflow, *ghosts_b[:2], *own_b, *ghosts_b[2:],
        plan, point_y, streamed(stored_z), strength, forces,
    )
    return (velocity_next, all_forces.reshape(1, records, 3, points))


def solution(mesh):
    return jax.shard_map(
        local,
        mesh=mesh,
        in_specs=(
            P(None, "gx", "gy", None),
            P(None, "gy", None),
            P("gx", None, None, None),
            P("gx", None, None),
            P("gx", None, None),
            P("gx"),
        ),
        out_specs=(P(None, "gx", "gy", None), P("gx", None, None, None)),
        check_vma=False,
    )
```

```python
import math

import jax
import jax.numpy as jnp
from jax import lax
from jax.experimental import pallas as pl
from jax.experimental.pallas import tpu as pltpu
from jax.sharding import PartitionSpec as P

RAD = 2
VISCOSITY = 0.05
TIME_STEP = 0.1
WIDTH_EPS = 1.5
ROOT_PI = 1.7724538509055159
TAP = [math.exp(-((d / WIDTH_EPS) ** 2)) / (WIDTH_EPS * ROOT_PI) for d in range(RAD + 1)]
HIGH = [float(jnp.bfloat16(tap)) for tap in TAP]
LOW = [float(jnp.bfloat16(tap - high)) for tap, high in zip(TAP, HIGH)]
LANES = 128
SUB = 8
GROUP = 4
BATCH = 4
PLANES = 8
BLOCK = 2 * PLANES
CHUNK = 16
TILES = 8
VMEM_LIMIT = 6 * 2**20

WHOLE = pl.BlockSpec(memory_space=pltpu.VMEM)
SCALAR = pl.BlockSpec(memory_space=pltpu.SMEM)
ANYWHERE = pl.BlockSpec(memory_space=pl.ANY)


def params(limit=VMEM_LIMIT):
    return pltpu.CompilerParams(vmem_limit_bytes=limit)


def cost(flops, nbytes):
    return pl.CostEstimate(flops=flops, bytes_accessed=nbytes, transcendentals=0)


def resident(x):
    return pltpu.with_memory_space_constraint(x, pltpu.VMEM)


def streamed(x):
    return pltpu.with_memory_space_constraint(x, pltpu.HBM)


def split(x):
    high = x.astype(jnp.bfloat16)
    low = (x - high.astype(jnp.float32)).astype(jnp.bfloat16)
    return jnp.concatenate([high, low], axis=0)


def along_z(point_z, start):
    points = point_z.shape[-1]
    row = lax.broadcasted_iota(jnp.int32, (LANES, points), 0).astype(jnp.bfloat16)
    place = (point_z - start).astype(jnp.float32)
    place = jnp.broadcast_to(place, (LANES, points)).astype(jnp.bfloat16)
    dist = jnp.abs(row - place)
    near = [dist == float(d) for d in range(RAD + 1)]
    out = []
    for taps in (HIGH, LOW):
        value = jnp.zeros_like(row)
        for d in range(RAD, -1, -1):
            value = jnp.where(near[d], jnp.full_like(row, taps[d]), value)
        out.append(value)
    return out


def wrapped(point_y, base, total_y):
    near = point_y - base
    near = jnp.where(near > total_y // 2, near - total_y, near)
    return jnp.where(near < -(total_y // 2), near + total_y, near)


def along_y(point_y, base, cells_y, total_y):
    near = wrapped(point_y, base, total_y)
    dist = jnp.abs(lax.broadcasted_iota(jnp.int32, (cells_y, point_y.shape[-1]), 0) - near)
    return jnp.where(
        dist == 0, TAP[0], jnp.where(dist == 1, TAP[1], jnp.where(dist == 2, TAP[2], 0.0))
    )


def make_plan(hub, lowest, highest, tiles, live, table):
    f32, i32 = jnp.float32, jnp.int32
    tile_y = lax.axis_index("gy").astype(f32)
    groups_y = float(lax.axis_size("gy"))
    records, units = hub.shape[0], table.shape[1]
    square = (records, records)
    diagonal = lax.broadcasted_iota(i32, square, 0) == lax.broadcasted_iota(i32, square, 1)

    def turned(x, axis):
        kept = jnp.where(diagonal, jnp.broadcast_to(x, square), 0.0)
        return jnp.sum(kept, axis=axis, keepdims=True)

    first, count = turned(tiles[0:1].astype(f32), 1), turned(tiles[1:2].astype(f32), 1)
    offset = tile_y - first
    offset = jnp.where(offset < 0.0, offset + groups_y, offset)
    order = lax.broadcasted_iota(i32, (records, 1), 0).astype(f32)
    valid = jnp.logical_and(offset < count, order < live)
    valid = jnp.logical_and(valid, highest >= 0.0)
    low = jnp.right_shift(lowest.astype(i32) - RAD, 7)
    high = jnp.right_shift(highest.astype(i32) + RAD, 7)
    number = jnp.where(valid, (high - low + 1).astype(f32), 0.0)
    key = hub * float(records) + order
    before = turned(key, 0) < key
    place = jnp.sum(jnp.where(before, turned(number, 0), 0.0), axis=1, keepdims=True)
    lane = lax.broadcasted_iota(i32, (records, units), 1).astype(f32)
    mine = jnp.logical_and(lane >= place, lane < place + number)

    def pick(value):
        return jnp.sum(jnp.where(mine, value, 0.0), axis=0, keepdims=True).astype(i32)

    table[0:1] = pick(order)
    table[1:2] = pick(hub)
    table[2:3] = pick(low.astype(f32) + lane - place)
    total = jnp.sum(number, axis=0, keepdims=True).astype(i32)
    table[3:4] = jnp.broadcast_to(total, (1, units))


def found(plan):
    return plan[3, 0]


def group(plan, t):
    picks, keeps = [], []
    for k in range(GROUP):
        wanted = GROUP * t + k
        n = jnp.minimum(wanted, found(plan) - 1)
        cols = pl.ds(pl.multiple_of(plan[2, n] * LANES, LANES), LANES)
        picks.append((n, plan[0, n], plan[1, n], cols))
        keeps.append(wanted == n)
    return picks, keeps


def groups_of(plan):
    return (found(plan) + GROUP - 1) // GROUP


def sampled_rows(field, weight_y, weight_z, picks):
    cells_y = field.shape[2]
    rows = 3 * cells_y
    parts = []
    for t, r, hub, cols in picks:
        planes = []
        for c in range(3):
            plane = TAP[0] * field[c, hub, :, cols]
            plane += TAP[1] * (field[c, hub - 1, :, cols] + field[c, hub + 1, :, cols])
            plane += TAP[2] * (field[c, hub - 2, :, cols] + field[c, hub + 2, :, cols])
            planes.append(plane)
        part = split(jnp.concatenate(planes, axis=0))
        parts.append(jnp.concatenate([part, part], axis=1))
    out = []
    for (t, r, hub, cols), part in zip(picks, parts):
        picked = jnp.dot(part, weight_z[t], preferred_element_type=jnp.float32)
        picked = picked[:rows] + picked[rows:]
        weight = weight_y[t]
        out.append(
            [
                jnp.sum(picked[c * cells_y : (c + 1) * cells_y] * weight, axis=0, keepdims=True)
                for c in range(3)
            ]
        )
    return out


def add_rows(pack, first_row, picks, sampled, keeps):
    for (t, r, hub, cols), rows, keep in zip(picks, sampled, keeps):
        for c in range(3):
            n = first_row + 3 * r + c
            pack[n] = pack[n] + jnp.where(keep, rows[c], 0.0)


def is_even(axis):
    return lax.rem(lax.axis_index(axis), 2) == 0


def pack_sides(field, edge_near, edge_far):
    even = is_even("gx")
    for c in range(3):
        west, east = field[c, 0], field[c, field.shape[1] - 1]
        edge_near[c] = jnp.where(even, east, west)
        edge_far[c] = jnp.where(even, west, east)


def pack_rows(field, low_out, high_out, first, last):
    cells_x, cells_y = field.shape[1:3]

    def step(t, carry):
        cells = [(c, t * BATCH + k) for k in range(BATCH) for c in range(3)]
        rows = [
            (field[c, i, pl.ds(0, 1), :], field[c, i, pl.ds(cells_y - 1, 1), :]) for c, i in cells
        ]
        for (c, i), (low, high) in zip(cells, rows):
            low_out[c * cells_x + i] = low
            high_out[c * cells_x + i] = high
        return carry

    lax.fori_loop(first // BATCH, last // BATCH, step, 0)


def load_field(
    velocity, positions, tiles_hbm, coefs_hbm, counts,
    field, edge_low, edge_high, edge_near, edge_far, strength, point_y, point_z, plan,
    hubs, tiles, places, coefs, table, small_sems, plan_sem, sems,
):
    cells_x, cells_y, depth = field.shape[1:]
    records, points = coefs.shape
    chunks = cells_x // CHUNK
    start = lax.axis_index("gx") * cells_x

    def chunk(k):
        planes = pl.ds(k * CHUNK, CHUNK)
        return pltpu.make_async_copy(velocity.at[:, planes], field.at[:, planes], sems.at[k])

    small = [
        (positions.at[pl.ds(1, 2)], places),
        (positions.at[0, :, pl.ds(0, LANES)], hubs),
        (tiles_hbm, tiles),
        (coefs_hbm, coefs),
    ]
    small = [
        pltpu.make_async_copy(source, target, small_sems.at[n])
        for n, (source, target) in enumerate(small)
    ]
    total_y = cells_y * lax.axis_size("gy")
    base = lax.axis_index("gy") * cells_y
    for copy in small:
        copy.start()
    for k in range(chunks):
        chunk(k).start()
    for copy in small[:3]:
        copy.wait()
    near = wrapped(places[0], base, total_y)
    inside = jnp.logical_and(near >= -RAD, near < cells_y + RAD)
    height = places[1].astype(jnp.float32)
    lowest = jnp.min(jnp.where(inside, height, float(depth)), axis=1, keepdims=True)
    highest = jnp.max(jnp.where(inside, height, -1.0), axis=1, keepdims=True)
    hub = (hubs[:, 0:1] - start).astype(jnp.float32)
    make_plan(hub, lowest, highest, tiles, counts[0].astype(jnp.float32), table)
    plan_copy = pltpu.make_async_copy(table, plan, plan_sem)
    plan_copy.start()

    small[3].wait()
    for first in range(0, records, SUB):
        here = range(first, first + SUB)
        rows = [
            (places[0, pl.ds(r, 1), :], places[1, pl.ds(r, 1), :], coefs[pl.ds(r, 1), :])
            for r in here
        ]
        for r, (y, z, coef) in zip(here, rows):
            point_y[r], point_z[r], strength[r] = y, z, coef

    def arrived(k, carry):
        chunk(k).wait()
        pack_rows(field, edge_low, edge_high, k * CHUNK, (k + 1) * CHUNK)
        return carry

    lax.fori_loop(0, chunks, arrived, 0)
    pack_sides(field, edge_near, edge_far)
    plan_copy.wait()


def clear_rows(pack, first, last):
    def clear(n, carry):
        for k in range(SUB):
            pack[first + n * SUB + k] = jnp.zeros(pack.shape[1:], jnp.float32)
        return carry

    lax.fori_loop(0, (last - first) // SUB, clear, 0)


def sample_first(field, plan, point_y, point_z, weight_y, weight_z, partial):
    cells_y = field.shape[2]
    total_y = cells_y * lax.axis_size("gy")
    base = lax.axis_index("gy") * cells_y
    clear_rows(partial, 0, partial.shape[0])

    def weigh(t, carry):
        made = []
        for k in range(2):
            n = jnp.minimum(2 * t + k, found(plan) - 1)
            r, half = plan[0, n], plan[2, n]
            high, low = along_z(point_z[r], half * LANES)
            made.append((n, along_y(point_y[r], base, cells_y, total_y), high, low))
        for n, across, high, low in made:
            weight_y[n] = across
            weight_z[n, 0:LANES] = high
            weight_z[n, LANES:] = low
        return carry

    lax.fori_loop(0, (found(plan) + 1) // 2, weigh, 0)

    def step(t, carry):
        picks, keeps = group(plan, t)
        rows = sampled_rows(field, weight_y, weight_z, picks)
        add_rows(partial, 0, picks, rows, keeps)
        return carry

    lax.fori_loop(0, groups_of(plan), step, 0)


def fix_sides(factor, target, own_near, own_far, inflow, ghost_near, ghost_far, west_side):
    near = is_even("gx") != west_side

    def side(one, other, c):
        return jnp.where(near, one[c], other[c])

    sign = 1.0 if west_side else -1.0
    end = 0 if west_side else target.shape[1] - 1
    place = lax.axis_index("gx")
    spread = factor * TIME_STEP * VISCOSITY
    coef = spread + (sign * 0.5 * factor * TIME_STEP) * side(own_near, own_far, 0)
    for c in range(3):
        own, ghost = side(own_near, own_far, c), side(ghost_near, ghost_far, c)
        if west_side:
            ghost = jnp.where(place == 0, inflow[c], ghost)
        else:
            ghost = jnp.where(place == lax.axis_size("gx") - 1, own, ghost)
        target[c, end] = target[c, end] + (ghost - own) * coef


def fix_rows(factor, target, own_low, own_high, got_low, got_high, t):
    cells_x, cells_y = target.shape[1:3]
    spread = factor * TIME_STEP * VISCOSITY
    half = 0.5 * factor * TIME_STEP
    shape = (SUB, target.shape[3])
    row = lax.broadcasted_iota(jnp.int32, shape, 0)
    low, high = pl.ds(0, SUB), pl.ds(cells_y - SUB, SUB)

    def wide(x):
        return jnp.broadcast_to(x, shape)

    for first in range(0, SUB, 2):
        values = []
        for k in range(first, first + 2):
            i = t * SUB + k
            south = jnp.where(row == 0, spread + half * wide(own_low[cells_x + i]), 0.0)
            north = jnp.where(row == SUB - 1, spread - half * wide(own_high[cells_x + i]), 0.0)
            for c in range(3):
                n = c * cells_x + i
                values.append((c, i, low, target[c, i, low, :] + wide(got_low[n]) * south))
                values.append((c, i, high, target[c, i, high, :] + wide(got_high[n]) * north))
        for c, i, rows, value in values:
            target[c, i, rows, :] = value


def slabs_of(weight_of, weight_z, strength, first_row, own, low, high, cells_y, scales, picks):
    count = 3 * cells_y
    across = (((1,), (1,)), ((), ()))
    spread = []
    for (t, r, hub, cols), scale in zip(picks, scales):
        rows = [first_row + 3 * r + c for c in range(3)]
        total = [own[n] + (low[n] + high[n]) for n in rows]
        speed = jnp.sqrt(total[0] * total[0] + total[1] * total[1] + total[2] * total[2])
        pull = strength[r] * (-scale) * speed
        weight = weight_of(t, r)
        spread.append(split(jnp.concatenate([weight * (pull * x) for x in total], axis=0)))
    slabs = []
    for (t, r, hub, cols), part in zip(picks, spread):
        slab = lax.dot_general(part, weight_z[t], across, preferred_element_type=jnp.float32)
        slab = slab[:count] + slab[count:]
        slabs.append(slab[:, :LANES] + slab[:, LANES:])
    return slabs


def add_slab(field, slab, hub, cols):
    cells_y = field.shape[2]
    for c in range(3):
        part = slab[c * cells_y : (c + 1) * cells_y]
        terms = [tap * part for tap in TAP]
        reach = range(-RAD, RAD + 1)
        values = [field[c, hub + d, :, cols] + terms[abs(d)] for d in reach]
        for d, value in zip(reach, values):
            field[c, hub + d, :, cols] = value


def spread_group(t, scale, field, plan, points, first_row, own, low, high):
    picks, keeps = group(plan, t)
    scales = [jnp.where(keep, scale, 0.0) for keep in keeps]
    slabs = slabs_of(*points, first_row, own, low, high, field.shape[2], scales, picks)
    for (_, _, hub, cols), slab in zip(picks, slabs):
        add_slab(field, slab, hub, cols)


def spread_sample(
    section_in, inflow, ghost_near, ghost_far, own_low, own_high, own_near, own_far, got_low, got_high,
    own, part_low, part_high, plan, weight_y, weight_z, strength,
    section, section_out, stored_z, pack_low, pack_high, edge_near, edge_far,
    share_out, sem, sem_z,
):
    cells_x = section.shape[1]
    records = strength.shape[0]
    share = share_out.shape[2] // 3
    first_row = 3 * cells_x

    def store(t):
        some = pl.ds(t * TILES, TILES)
        return pltpu.make_async_copy(weight_z.at[some], stored_z.at[some], sem_z.at[t])

    def start_store(t, carry):
        store(t).start()
        return carry

    def wait_store(t, carry):
        store(t).wait()
        return carry

    stores = (found(plan) + TILES - 1) // TILES
    lax.fori_loop(0, stores, start_store, 0)

    def fix_step(t, carry):
        fix_rows(1.0, section, own_low, own_high, got_low, got_high, t)
        return carry

    sides = (own_near, own_far, inflow, ghost_near, ghost_far)
    fix_sides(1.0, section, *sides, True)
    fix_sides(1.0, section, *sides, False)
    lax.fori_loop(0, cells_x // SUB, fix_step, 0)

    def spread_step(t, carry):
        points = (lambda n, r: weight_y[n], weight_z, strength)
        spread_group(t, TIME_STEP, section, plan, points, 0, own, part_low, part_high)
        return carry

    lax.fori_loop(0, groups_of(plan), spread_step, 0)
    copy = pltpu.make_async_copy(section, section_out, sem)
    copy.start()
    pack_sides(section, edge_near, edge_far)
    pack_rows(section, pack_low, pack_high, 0, cells_x)
    clear_rows(pack_low, first_row, first_row + 3 * records)

    def sample_step(t, carry):
        picks, keeps = group(plan, t)
        rows = sampled_rows(section, weight_y, weight_z, picks)
        add_rows(pack_low, first_row, picks, rows, keeps)
        return carry

    lax.fori_loop(0, groups_of(plan), sample_step, 0)

    def copy_rows(r, carry):
        old = [own[3 * r + c] for c in range(3)]
        new = [pack_low[first_row + 3 * r + c] for c in range(3)]
        for c in range(3):
            pack_high[first_row + 3 * r + c] = new[c]
            share_out[r // share, 0, 3 * (r % share) + c] = old[c]
            share_out[r // share, 1, 3 * (r % share) + c] = new[c]
        return carry

    lax.fori_loop(0, records, copy_rows, 0)
    lax.fori_loop(0, stores, wait_store, 0)
    copy.wait()


def share_force(parts, strength, counts, after, after_low, after_high, result):
    groups, _, rows = parts.shape[:3]
    share = rows // 3
    mine = lax.axis_index("gy") * share
    values = []
    for s in range(share):
        live = mine + s < counts[0]
        pull = jnp.where(live, -0.5 * strength[mine + s], 0.0)
        total = [0.0, 0.0, 0.0]
        for stage in range(2):
            value = []
            for c in range(3):
                n = 3 * s + c
                x = parts[0, stage, n]
                for g in range(1, groups):
                    x += parts[g, stage, n]
                value.append(x)
            speed = jnp.sqrt(value[0] * value[0] + value[1] * value[1] + value[2] * value[2])
            total = [acc + speed * x for acc, x in zip(total, value)]
        values.extend((3 * s + c, pull * total[c]) for c in range(3))
        if s % 2 == 1 or s + 1 == share:
            for n, value in values:
                for g in range(groups):
                    result[g, n] = value
            values = []


def spread_next(
    following, inflow, ghost_near, ghost_far, own_low, own_high, own_near, own_far, got_low, got_high,
    plan, point_y, stored_z, strength, after,
    result, field, weight_z, in_sems, out_sems, sem_z,
):
    chunks = field.shape[1] // CHUNK
    factor = 0.5
    sides = (own_near, own_far, inflow, ghost_near, ghost_far)

    def chunk_in(k):
        planes = pl.ds(k * CHUNK, CHUNK)
        return pltpu.make_async_copy(following.at[:, planes], field.at[:, planes], in_sems.at[k])

    def chunk_out(k):
        planes = pl.ds(k * CHUNK, CHUNK)
        return pltpu.make_async_copy(field.at[:, planes], result.at[:, planes], out_sems.at[k])

    def wait_to(ready, wanted):
        def step(k, carry):
            chunk_in(k).wait()
            for n in range(CHUNK // SUB):
                t = k * (CHUNK // SUB) + n
                fix_rows(factor, field, own_low, own_high, got_low, got_high, t)

            @pl.when(k == 0)
            def _():
                fix_sides(factor, field, *sides, True)

            @pl.when(k == chunks - 1)
            def _():
                fix_sides(factor, field, *sides, False)

            return carry

        lax.fori_loop(ready, wanted, step, 0)
        return jnp.maximum(ready, wanted)

    def send_to(sent, done):
        def step(k, carry):
            chunk_out(k).start()
            return carry

        lax.fori_loop(sent, done, step, 0)
        return jnp.maximum(sent, done)

    def weights(t):
        some = pl.ds(t * TILES, TILES)
        return pltpu.make_async_copy(stored_z.at[some], weight_z.at[some], sem_z.at[t])

    def start_weights(t, carry):
        weights(t).start()
        return carry

    def weight_of(t, r):
        cells_y = field.shape[2]
        base = lax.axis_index("gy") * cells_y
        return along_y(point_y[r], base, cells_y, cells_y * lax.axis_size("gy"))

    loads = (found(plan) + TILES - 1) // TILES
    for k in range(chunks):
        chunk_in(k).start()
        lax.fori_loop(k * loads // chunks, (k + 1) * loads // chunks, start_weights, 0)

    def step(t, carry):
        ready, sent = carry
        picks, keeps = group(plan, t)
        @pl.when(t * GROUP % TILES == 0)
        def _():
            weights(t * GROUP // TILES).wait()

        ready = wait_to(ready, (picks[-1][2] + RAD) // CHUNK + 1)
        sent = send_to(sent, (picks[0][2] - RAD) // CHUNK)
        points = (weight_of, weight_z, strength)
        first_row = 3 * field.shape[1]
        packs = (own_low, got_low, got_high)
        spread_group(t, factor * TIME_STEP, field, plan, points, first_row, *packs)
        return ready, sent

    zero = jnp.int32(0)
    ready, sent = lax.fori_loop(0, groups_of(plan), step, (zero, zero))
    sent = send_to(sent, ready)

    def finish(k, carry):
        wait_to(k, k + 1)
        chunk_out(k).start()
        return carry

    lax.fori_loop(ready, chunks, finish, 0)
    for k in range(chunks):
        chunk_out(k).wait()


def fill_shifts(shifts):
    depth = shifts.shape[1]
    source = lax.broadcasted_iota(jnp.int32, (depth, depth), 0)
    cell = lax.broadcasted_iota(jnp.int32, (depth, depth), 1)
    upper = jnp.where(source == cell + 1, 1.0, 0.0)
    lower = jnp.where(source == cell - 1, 1.0, 0.0)
    difference = (upper - lower).astype(shifts.dtype)
    shifts[0:depth] = difference
    shifts[depth : 2 * depth] = difference


def along_depth(i, field, shifts, slot):
    x = jnp.concatenate([field[c, i + k] for k in range(PLANES) for c in range(3)], axis=0)
    high = x.astype(jnp.bfloat16)
    low = (x - high.astype(jnp.float32)).astype(jnp.bfloat16)
    slot[...] = jnp.dot(
        jnp.concatenate([high, low], axis=1), shifts[...], preferred_element_type=jnp.float32
    )


def advance(i, k, factor, field, slot, target, finish):
    cells_x, cells_y, depth = field.shape[1:]
    groups, halves = cells_y // SUB, depth // LANES
    row = lax.broadcasted_iota(jnp.int32, (SUB, LANES), 0)
    lane = lax.broadcasted_iota(jnp.int32, (SUB, LANES), 1)
    first_row, last_row, first_lane = row == 0, row == SUB - 1, lane == 0
    spread = factor * TIME_STEP * VISCOSITY
    centre = factor * (1.0 - 6.0 * TIME_STEP * VISCOSITY)
    zero = jnp.zeros((SUB, LANES), jnp.float32)
    loaded = {}
    here = i + k
    west, east = jnp.maximum(here - 1, 0), jnp.minimum(here + 1, cells_x - 1)

    def at(c, g, h):
        if (c, g, h) not in loaded:
            loaded[c, g, h] = field[c, here, pl.ds(g * SUB, SUB), pl.ds(h * LANES, LANES)]
        return loaded[c, g, h]

    values = []
    for g in range(groups):
        turned = {}
        for h in range(halves):
            rows, cols = pl.ds(g * SUB, SUB), pl.ds(h * LANES, LANES)
            q = [at(c, g, h) for c in range(3)]
            speeds = [(0.5 * factor * TIME_STEP) * x for x in q]
            less = [spread - s for s in speeds]
            more = [spread + s for s in speeds[:2]]
            if g == 0:
                more[1] = jnp.where(first_row, zero, more[1])
            if g == groups - 1:
                less[1] = jnp.where(last_row, zero, less[1])
            for c in range(3):
                x = q[c]
                above, below = x, x
                if g + 1 < groups:
                    above = jnp.where(first_row, at(c, g + 1, h), x)
                if g > 0:
                    below = jnp.where(last_row, at(c, g - 1, h), x)
                above, below = pltpu.roll(above, SUB - 1, 0), pltpu.roll(below, 1, 0)
                place = pl.ds((3 * k + c) * cells_y + g * SUB, SUB)
                total = centre * x
                total += field[c, east, rows, cols] * less[0]
                total += field[c, west, rows, cols] * more[0]
                total += above * less[1] + below * more[1]
                lower = pltpu.roll(x, 1, 1)
                turned[c, h] = lower
                lower = jnp.where(first_lane, zero if h == 0 else turned[c, h - 1], lower)
                total += slot[place, cols] * less[2] + (2.0 * spread) * lower
                values.append((c, rows, cols, finish(c, here, rows, cols, total)))
        if g % 2 == 1 or g + 1 == groups:
            for c, rows, cols, value in values:
                target[c, here, rows, cols] = value
            values = []


def advance_batch(i, n, factor, field, shifts, slots, target, finish):
    now, later = slots[n % 2], slots[1 - n % 2]
    along_depth(jnp.minimum(i + PLANES, field.shape[1] - PLANES), field, shifts, later)
    for k in range(PLANES):
        advance(i, k, factor, field, now, target, finish)


def advance_first(field, after, section, shifts, slot_a, slot_b):
    fill_shifts(shifts)
    along_depth(0, field, shifts, slot_a)

    def step(t, carry):
        for n in range(BLOCK // PLANES):
            advance_batch(
                BLOCK * t + PLANES * n, n, 1.0, field, shifts, (slot_a, slot_b), section,
                lambda c, i, rows, cols, value: value,
            )
        return carry

    lax.fori_loop(0, field.shape[1] // BLOCK, step, 0)


def advance_second(
    section_hbm, velocity, following, token,
    section, field, result, shifts, slot_a, slot_b, in_sems, old_sems, out_sems,
):
    cells_x = section.shape[1]
    blocks = cells_x // BLOCK

    def copy(source, target, first, count, sem):
        some = pl.ds(first, count)
        return pltpu.make_async_copy(source.at[:, some], target.at[:, some], sem)

    def section_in(k):
        return copy(section_hbm, section, k * BLOCK, BLOCK, in_sems.at[k])

    def old_in(k):
        return copy(velocity, field, k * BLOCK, BLOCK, old_sems.at[k])

    def block_out(k):
        return copy(result, following, k * BLOCK, BLOCK, out_sems.at[k])

    halves = range(BLOCK // PLANES)
    head = [
        (
            copy(section_hbm, section, n * PLANES, PLANES, in_sems.at[n * blocks]),
            copy(velocity, field, n * PLANES, PLANES, old_sems.at[n * blocks]),
        )
        for n in halves
    ]
    last = blocks - 1
    tail = [
        copy(result, following, last * BLOCK + n * PLANES, PLANES, out_sems.at[last + n])
        for n in halves
    ]

    def finish(c, i, rows, cols, value):
        return value + 0.5 * field[c, i, rows, cols]

    head[0][0].start()
    head[1][0].start()
    head[0][1].start()
    head[1][1].start()
    for k in range(1, blocks):
        section_in(k).start()
        old_in(k).start()
    token[...] = jnp.zeros_like(token)
    fill_shifts(shifts)

    def work(i, n):
        advance_batch(i, n, 0.5, section, shifts, (slot_a, slot_b), result, finish)

    head[0][0].wait()
    along_depth(0, section, shifts, slot_a)
    head[1][0].wait()
    head[0][1].wait()
    work(0, 0)
    section_in(1).wait()
    head[1][1].wait()
    work(PLANES, 1)
    block_out(0).start()

    def step(t, carry):
        section_in(t + 1).wait()
        old_in(t).wait()
        for n in halves:
            work(t * BLOCK + n * PLANES, n)
        block_out(t).start()
        return carry

    lax.fori_loop(1, last, step, 0)
    old_in(last).wait()
    for n in halves:
        work(last * BLOCK + n * PLANES, n)
        tail[n].start()
    for k in range(last):
        block_out(k).wait()
    for out in tail:
        out.wait()


def shifted(x, axis, step):
    count = lax.axis_size(axis)
    return lax.ppermute(x, axis, [(i, (i + step) % count) for i in range(count)])


def swapped(x, axis, first):
    count = lax.axis_size(axis)
    pairs = [(i, i + 1) for i in range(first, count - 1, 2)]
    return lax.ppermute(x, axis, pairs + [(t, s) for s, t in pairs])


def exchange(pack_low, pack_high, edge_near, edge_far):
    got_low = shifted(pack_high, "gy", 1)
    got_high = shifted(pack_low, "gy", -1)
    return swapped(edge_near, "gx", 0), swapped(edge_far, "gx", 1), got_low, got_high


def local(velocity, inflow, positions, tiles, coefs, counts):
    f32, i32 = jnp.float32, jnp.int32
    whole = velocity.shape
    _, cells_x, cells_y, depth = whole
    groups_y = lax.axis_size("gy")
    positions = positions[0].transpose(1, 0, 2)
    tiles, coefs = tiles[0].T, coefs[0]
    records, points = coefs.shape
    share = records // groups_y
    chunks = cells_x // CHUNK
    size = 4 * math.prod(whole)
    held = pltpu.VMEM(whole, f32)
    stored = pltpu.HBM(whole, f32)
    array = jax.ShapeDtypeStruct
    pack = array((3 * cells_x + 3 * records, 1, points), f32)
    edge = array((3, cells_y, depth), f32)
    per_record = (records, 1, points)
    units = records * (depth // LANES)
    y_shape, z_shape = (units, cells_y, points), (units, 2 * LANES, points)
    z_bytes = 2 * math.prod(z_shape)
    products = [pltpu.VMEM((2 * depth, depth), jnp.bfloat16)]
    products += [pltpu.VMEM((3 * PLANES * cells_y, depth), f32)] * 2
    unit_sems = pltpu.SemaphoreType.DMA((units // TILES,))
    chunk_sems = pltpu.SemaphoreType.DMA((chunks,))

    halo = array((3 * cells_x, 1, points), f32)
    field, *own_a, strength, point_y, point_z, plan = pl.pallas_call(
        load_field,
        out_shape=(
            held, halo, halo, edge, edge,
            array(per_record, f32), array(per_record, i32), array(per_record, i32),
            array((SUB, units), i32),
        ),
        in_specs=[ANYWHERE] * 4 + [SCALAR],
        out_specs=(WHOLE,) * 8 + (SCALAR,),
        scratch_shapes=[
            pltpu.VMEM((records, LANES), i32),
            pltpu.VMEM((2, records), i32),
            pltpu.VMEM((2, records, points), i32),
            pltpu.VMEM((records, points), f32),
            pltpu.VMEM((SUB, units), i32),
            pltpu.SemaphoreType.DMA((4,)),
            pltpu.SemaphoreType.DMA,
            chunk_sems,
        ],
        compiler_params=params(),
        cost_estimate=cost(10**9, size),
        name="load_field",
    )(streamed(velocity), streamed(positions), streamed(tiles), streamed(coefs), counts)
    field = resident(field)
    ghosts_a = exchange(*own_a)

    weight_y, weight_z, partial = pl.pallas_call(
        sample_first,
        out_shape=(
            pltpu.VMEM(y_shape, f32), pltpu.VMEM(z_shape, jnp.bfloat16),
            array((3 * records, 1, points), f32),
        ),
        in_specs=[WHOLE, SCALAR, WHOLE, WHOLE],
        out_specs=(WHOLE,) * 3,
        compiler_params=params(),
        cost_estimate=cost(2 * 10**9, size),
        name="sample_first",
    )(field, plan, point_y, point_z)
    weight_y, weight_z = resident(weight_y), resident(weight_z)
    parts_a = (partial, shifted(partial, "gy", 1), shifted(partial, "gy", -1))

    section = pl.pallas_call(
        advance_first,
        out_shape=held,
        in_specs=[WHOLE, ANYWHERE],
        out_specs=WHOLE,
        scratch_shapes=products,
        compiler_params=params(),
        cost_estimate=cost(10**9, 4 * size),
        name="advance_first",
    )(field, partial)

    _, section, stored_z, *own_b, shares = pl.pallas_call(
        spread_sample,
        out_shape=(
            held, stored, pltpu.HBM(z_shape, jnp.bfloat16),
            pack, pack, edge, edge,
            array((groups_y, 2, 3 * share, 1, points), f32),
        ),
        in_specs=[WHOLE] * 13 + [SCALAR] + [WHOLE] * 3,
        out_specs=(WHOLE,) + (ANYWHERE,) * 2 + (WHOLE,) * 5,
        input_output_aliases={0: 0},
        scratch_shapes=[pltpu.SemaphoreType.DMA, unit_sems],
        compiler_params=params(),
        cost_estimate=cost(2 * 10**9, 4 * size),
        name="spread_sample",
    )(
        resident(section), inflow, *ghosts_a[:2], *own_a, *ghosts_a[2:],
        *parts_a, plan, weight_y, weight_z, strength,
    )
    shares = lax.all_to_all(shares, "gy", 0, 0)
    ghosts_b = exchange(*own_b)

    following, token = pl.pallas_call(
        advance_second,
        out_shape=(stored, array((SUB, LANES), f32)),
        in_specs=[ANYWHERE] * 2,
        out_specs=(ANYWHERE, WHOLE),
        scratch_shapes=[pltpu.VMEM(whole, f32)] * 3
        + products
        + [pltpu.SemaphoreType.DMA((cells_x // BLOCK + 1,))] * 3,
        compiler_params=params(VMEM_LIMIT + 3 * size),
        cost_estimate=cost(10**9, 4 * size),
        name="advance_second",
    )(streamed(section), streamed(velocity))

    forces = pl.pallas_call(
        share_force,
        out_shape=array((groups_y, 3 * share, 1, points), f32),
        in_specs=[WHOLE, WHOLE, SCALAR] + [ANYWHERE] * 3,
        out_specs=WHOLE,
        compiler_params=params(),
        cost_estimate=cost(10**6, 10**6),
        name="share_force",
    )(shares, strength, counts, token, *ghosts_b[:2])
    all_forces = lax.all_to_all(forces, "gy", 0, 0)

    velocity_next = pl.pallas_call(
        spread_next,
        out_shape=stored,
        in_specs=[ANYWHERE] + [WHOLE] * 9 + [SCALAR, WHOLE, ANYWHERE, WHOLE, ANYWHERE],
        out_specs=ANYWHERE,
        scratch_shapes=[
            pltpu.VMEM(whole, f32),
            pltpu.VMEM(z_shape, jnp.bfloat16),
            chunk_sems, chunk_sems, unit_sems,
        ],
        compiler_params=params(VMEM_LIMIT + size + z_bytes),
        cost_estimate=cost(2 * 10**9, 4 * size),
        name="spread_next",
    )(
        streamed(following), inflow, *ghosts_b[:2], *own_b, *ghosts_b[2:],
        plan, point_y, streamed(stored_z), strength, forces,
    )
    return (velocity_next, all_forces.reshape(1, records, 3, points))


def solution(mesh):
    return jax.shard_map(
        local,
        mesh=mesh,
        in_specs=(
            P(None, "gx", "gy", None),
            P(None, "gy", None),
            P("gx", None, None, None),
            P("gx", None, None),
            P("gx", None, None),
            P("gx"),
        ),
        out_specs=(P(None, "gx", "gy", None), P("gx", None, None, None)),
        check_vma=False,
    )
```
